32 devices in a mesh: dp: 4 (over y, x), tensor: 8 (over z, core).
Axes of the slice: x: 2, y: 2, z: 4, core: 2. Of those that a mesh axis runs over, the one named last changes fastest.
Arguments:
- tokens: bfloat16 [8192, 2048], P(('dp', 'tensor')), may hold values from -6 to 6
- cotangent: bfloat16 [8192, 2048], P(('dp', 'tensor')), may hold values from -6 to 6
- resets: int32 [8], P('dp'), may hold values 0 or 1
- init_state: float32 [8, 2752], P('dp', 'tensor'), may hold values from -4 to 4
- init_conv: float32 [8, 3, 2752], P('dp', None, 'tensor'), may hold values from -6 to 6
- norm_gain: bfloat16 [2048], replicated, may hold values from 0.5 to 1.5
- w_input: bfloat16 [2048, 2752], P(None, 'tensor'), may hold values from -0.125 to 0.125
- w_branch: bfloat16 [2048, 2752], P(None, 'tensor'), may hold values from -0.125 to 0.125
- conv_params: float32 [5, 2752], P(None, 'tensor'), may hold values from -3 to 3
- gate_weights: bfloat16 [2, 16, 172, 172], P(None, 'tensor'), may hold values from -0.4375 to 0.4375
- gate_bias: float32 [2, 2752], P(None, 'tensor'), may hold values from -4 to 4
- decay_rate: float32 [2752], P('tensor'), may hold values from 0.0002 to 0.3
- w_output: bfloat16 [2752, 2048], P('tensor'), may hold values from -0.4375 to 0.4375
- mlp_gain: bfloat16 [2048], replicated, may hold values from 0.5 to 1.5
- w_gelu: bfloat16 [2048, 6144], P(None, 'tensor'), may hold values from -0.125 to 0.125
- w_linear: bfloat16 [2048, 6144], P(None, 'tensor'), may hold values from -0.125 to 0.125
- w_down: bfloat16 [6144, 2048], P('tensor'), may hold values from -0.15625 to 0.15625
Outputs:
- output: bfloat16 [8192, 2048], P(('dp', 'tensor'))
- input_grad: float32 [8192, 2048], P(('dp', 'tensor'))
- final_state: float32 [8, 2752], P('dp', 'tensor')
- final_conv: float32 [8, 3, 2752], P('dp', None, 'tensor')
- grad_norm_gain: float32 [2048], P('tensor')
- grad_w_input: float32 [2048, 2752], P(None, 'tensor')
- grad_w_branch: float32 [2048, 2752], P(None, 'tensor')
- grad_conv_params: float32 [5, 2752], P(None, 'tensor')
- grad_gate_weights: float32 [2, 16, 172, 172], P(None, 'tensor')
- grad_gate_bias: float32 [2, 2752], P(None, 'tensor')
- grad_decay_rate: float32 [2752], P('tensor')
- grad_w_output: float32 [2752, 2048], P('tensor')
- grad_mlp_gain: float32 [2048], P('tensor')
- grad_w_gelu: float32 [2048, 6144], P(None, 'tensor')
- grad_w_linear: float32 [2048, 6144], P(None, 'tensor')
- grad_w_down: float32 [6144, 2048], P('tensor')
The draws below stay inside these ranges and needn't reach their ends.
All inputs are finite; a program needn't handle non-finite values. No bound on the sum of `resets` on one device may be relied on, other than what follows from the above.
Results may differ from the reference program's by a relative error of at most 0.029.
Values may be sent and summed in bfloat16 or wider, within the bound.
A program may use at most 256 MiB of HBM per device.

```python
import math
import jax
import jax.numpy as jnp
from jax import lax

D = 2048
BLOCKS = 16
BW = 172
F = 6144
LENGTH = 1024
R = 2752
ROWS = 8
TOKENS = 8192


def plant(entries, own_key, smallest, largest):
    longest = entries.shape.index(max(entries.shape))
    spots = []
    for shift in (0, 1):
        where = [jax.random.randint(jax.random.fold_in(own_key, axis), (), 0, length) for axis, length in enumerate(entries.shape)]
        where[longest] = (where[longest] + shift) % entries.shape[longest]
        spots.append(tuple(where))
    return entries.at[spots[0]].set(smallest).at[spots[1]].set(largest)


def shard_levels(rng, dims, shards, low, top_value):
    def one(position, shards_of):
        heights = jax.random.uniform(jax.random.fold_in(jax.random.fold_in(rng, 6), position), (shards_of,), jnp.float32, low / len(shards), top_value / len(shards))
        return jnp.repeat(jnp.exp(heights), dims[position] // shards_of).reshape((-1,) + (1,) * (len(dims) - position - 1))

    level = one(*shards[0])
    for cut in shards[1:]:
        level = level * one(*cut)
    return level


def normal_values(key, extent, width, reach, split=(), kind=jnp.bfloat16):
    values = jax.random.normal(key, extent, jnp.float32) * width
    if len(split) > 0:
        values = shard_levels(key, extent, split, -0.22, 0.18) * values
    return jnp.clip(values, min=-reach, max=reach).astype(kind)


def setup_inputs(seed: int = 0) -> dict:
    key_of = jax.random.split(jax.random.key(seed), 18)
    tokens = normal_values(key_of[0], (TOKENS, D), 1.0, 6.0, ((0, 32),))
    cotangent = normal_values(key_of[1], (TOKENS, D), 1.0, 6.0, ((0, 32),))
    resets = plant((jax.random.randint(key_of[2], (ROWS,), 0, 2) < 1).astype(jnp.int32), jax.random.fold_in(key_of[2], 1), 0, 1)
    init_state = normal_values(key_of[3], (ROWS, R), 0.5, 4.0, ((0, 4), (1, 8)), jnp.float32)
    init_conv = normal_values(key_of[4], (ROWS, 3, R), 1.0, 6.0, ((0, 4), (2, 8)), jnp.float32)
    norm_gain = jnp.clip(1.0 + 0.1 * jax.random.normal(key_of[5], (D,), jnp.float32), 0.5, 1.5).astype(jnp.bfloat16)
    w_input = normal_values(key_of[6], (D, R), D ** -0.5, 0.125, ((1, 8),))
    w_branch = normal_values(key_of[7], (D, R), D ** -0.5, 0.125, ((1, 8),))
    conv_params = normal_values(key_of[8], (5, R), 0.5, 3.0, ((1, 8),), jnp.float32)
    gate_weights = normal_values(key_of[9], (2, BLOCKS, BW, BW), BW ** -0.5, 0.4375, ((1, 8),))
    gate_bias = normal_values(key_of[10], (2, R), 1.0, 4.0, ((1, 8),), jnp.float32)
    decay_rate = jnp.clip(jnp.exp(math.log(0.3) - 7.3132205 * jax.random.uniform(key_of[11], (R,), jnp.float32) ** shard_levels(key_of[11], (R,), ((0, 8),), -0.2, 0.2)), 0.0002, 0.3)
    w_output = normal_values(key_of[12], (R, D), (R // 16) ** -0.5, 0.4375, ((0, 8),))
    mlp_gain = jnp.clip(1.0 + 0.1 * jax.random.normal(key_of[13], (D,), jnp.float32), 0.5, 1.5).astype(jnp.bfloat16)
    w_gelu = normal_values(key_of[14], (D, F), D ** -0.5, 0.125, ((1, 8),))
    w_linear = normal_values(key_of[15], (D, F), D ** -0.5, 0.125, ((1, 8),))
    w_down = normal_values(key_of[16], (F, D), (F // 4) ** -0.5, 0.15625, ((0, 8),))
    return dict(tokens=tokens, cotangent=cotangent, resets=resets, init_state=init_state, init_conv=init_conv, norm_gain=norm_gain, w_input=w_input, w_branch=w_branch, conv_params=conv_params, gate_weights=gate_weights, gate_bias=gate_bias, decay_rate=decay_rate, w_output=w_output, mlp_gain=mlp_gain, w_gelu=w_gelu, w_linear=w_linear, w_down=w_down)


HIGHEST = lax.Precision.HIGHEST
EPSILON = 1e-06

@jax.custom_vjp
def low(v):
    return lax.optimization_barrier(v.astype(jnp.bfloat16)).astype(jnp.float32)

@jax.custom_vjp
def low_back(v):
    return v

def low_keep(v):
    return (low(v), None)

def low_pass(kept, grad):
    return (grad,)

def back_keep(v):
    return (v, None)

def back_low(kept, grad):
    return (low(grad),)
low.defvjp(low_keep, low_pass)
low_back.defvjp(back_keep, back_low)

def product(left, right):
    return jnp.dot(left, right, precision=HIGHEST)

def normalize(values, gain_row):
    inv_rms = lax.rsqrt(lax.optimization_barrier(jnp.mean(values * values, axis=-1, keepdims=True)) + EPSILON)
    return values * inv_rms * gain_row

def advance(carried, element):
    updated = element[0] * carried + element[1]
    return (updated, updated)

def layer(sequence, weights, start_state, start_conv):
    norm_gain, w_input, w_branch, conv_params, gate_weights, gate_bias, decay_rate, w_output, mlp_gain, w_gelu, w_linear, w_down = weights
    length = sequence.shape[0]
    normed = low(normalize(sequence, norm_gain))
    recur_in = low_back(product(normed, w_input))
    branch = low_back(product(normed, w_branch))
    gating = jax.nn.gelu(branch, approximate=True)
    history = jnp.concatenate([start_conv, recur_in], axis=0)
    convolved = conv_params[4] + conv_params[0] * history[3:] + conv_params[1] * history[2:length + 2]
    convolved = convolved + conv_params[2] * history[1:length + 1] + conv_params[3] * history[:length]
    convolved = low(convolved)
    grouped = convolved.reshape(length, BLOCKS, BW)
    pre_recall = jnp.einsum('nkb,kbc->nkc', grouped, gate_weights[0], precision=HIGHEST).reshape(length, R)
    pre_recall = low_back(pre_recall + gate_bias[0])
    pre_input = jnp.einsum('nkb,kbc->nkc', grouped, gate_weights[1], precision=HIGHEST).reshape(length, R)
    pre_input = low_back(pre_input + gate_bias[1])
    recall = jax.nn.sigmoid(pre_recall)
    ingate = jax.nn.sigmoid(pre_input)
    log_decay = -8.0 * recall * decay_rate
    decay_step = jnp.exp(log_decay)
    driving = jnp.sqrt(-jnp.expm1(2.0 * log_decay)) * ingate * convolved
    final_h, states = lax.scan(advance, start_state, (decay_step, driving))
    mixture = low(states * gating)
    residual = sequence + low_back(product(mixture, w_output))
    normed_mlp = low(normalize(residual, mlp_gain))
    first_up = low_back(product(normed_mlp, w_gelu))
    second_up = low_back(product(normed_mlp, w_linear))
    hidden = low(jax.nn.gelu(first_up, approximate=True) * second_up)
    result = residual + product(hidden, w_down)
    return (result, final_h, history[length:])

def reference(tokens, cotangent, resets, init_state, init_conv, norm_gain, w_input, w_branch, conv_params, gate_weights, gate_bias, decay_rate, w_output, mlp_gain, w_gelu, w_linear, w_down):
    weights = tuple((weight.astype(jnp.float32) for weight in (norm_gain, w_input, w_branch, conv_params, gate_weights, gate_bias, decay_rate, w_output, mlp_gain, w_gelu, w_linear, w_down)))
    sequences = resets.shape[0]
    survive = (1 - resets).astype(jnp.float32)
    inputs_all = tokens.astype(jnp.float32).reshape(sequences, LENGTH, D)
    grads_all = cotangent.astype(jnp.float32).reshape(sequences, LENGTH, D)
    states_all = init_state * survive[:, None]
    convs_all = init_conv * survive[:, None, None]

    def per_sequence(totals, element):
        sequence, seq_grad, start_state, start_conv = element

        def forward(seq_in, weight_set):
            return layer(seq_in, weight_set, start_state, start_conv)
        (result, final_h, last_conv), pullback = jax.vjp(forward, sequence, weights)
        input_grad, weight_grads = pullback((seq_grad, jnp.zeros_like(final_h), jnp.zeros_like(last_conv)))
        totals = jax.tree.map(lambda held, fresh: held + fresh, totals, weight_grads)
        return (totals, (result.astype(jnp.bfloat16), input_grad, final_h, last_conv))
    initial = jax.tree.map(jnp.zeros_like, weights)
    totals, outputs = lax.scan(per_sequence, initial, (inputs_all, grads_all, states_all, convs_all))
    results, input_grads, final_states, final_convs = outputs
    return (results.reshape(-1, D), input_grads.reshape(-1, D), final_states, final_convs, totals[0], totals[1], totals[2], totals[3], totals[4], totals[5], totals[6], totals[7], totals[8], totals[9], totals[10], totals[11])
```

```python
import functools

import jax
import jax.numpy as jnp
from jax import lax
from jax.experimental import pallas as pl
from jax.experimental.pallas import tpu as pltpu
from jax.sharding import PartitionSpec as P

EPSILON = 1e-06
KAPPA = 0.7978845608028654
CUBIC = 0.044715
PIECES = 2
F32 = jnp.float32
BF16 = jnp.bfloat16
ANY = pl.BlockSpec(memory_space=pl.ANY)
VM = pl.BlockSpec(memory_space=pltpu.VMEM)
VMEM_LIMIT = 61 * 1024 * 1024
MESH = pl.DeviceIdType.MESH


def dot(a, b):
    return jnp.dot(a, b, preferred_element_type=F32)


def dot_nt(a, b):
    return lax.dot_general(a, b, (((1,), (1,)), ((), ())), preferred_element_type=F32)


def dot_tn(a, b):
    return lax.dot_general(a, b, (((0,), (0,)), ((), ())), preferred_element_type=F32)


def tile_of(extent, wanted):
    while extent % wanted:
        wanted //= 2
    return wanted


def span(i, size):
    return pl.ds(pl.multiple_of(i * size, size), size)


def loop(count, body):
    def step(i, carry):
        body(i)
        return carry

    lax.fori_loop(0, count, step, 0)


class Place:
    def __init__(self, n):
        self.n = n
        self.nz = n // 2
        self.t = lax.axis_index("tensor")
        self.c = lax.rem(self.t, 2)
        self.j = lax.div(self.t, 2)
        self.sib = self.t + 1 - 2 * self.c
        self.has_up = self.j < self.nz - 1
        self.has_down = self.j > 0

    def greet(self):
        barrier = pltpu.get_barrier_semaphore()

        def signal(t):
            pl.semaphore_signal(barrier, inc=1, device_id={"tensor": t}, device_id_type=MESH)

        signal(self.sib)
        pl.when(self.has_up)(lambda: signal(self.t + 2))
        pl.when(self.has_down)(lambda: signal(self.t - 2))
        pl.semaphore_wait(
            barrier, 1 + self.has_up.astype(jnp.int32) + self.has_down.astype(jnp.int32)
        )

    def copy(self, src, dst, send, recv, t):
        return pltpu.make_async_remote_copy(
            src_ref=src,
            dst_ref=dst,
            send_sem=send,
            recv_sem=recv,
            device_id={"tensor": t},
            device_id_type=MESH,
        )


class Gather:
    def __init__(self, place, full, sent, came):
        self.place, self.full, self.sent, self.came = place, full, sent, came
        self.pieces = full.shape[1]

    @staticmethod
    def scratch(n, rows, width):
        return [
            pltpu.VMEM((n, PIECES, rows // PIECES, width), BF16),
            pltpu.SemaphoreType.DMA((n, PIECES, 3)),
            pltpu.SemaphoreType.DMA((n, PIECES)),
        ]

    def copy(self, t, p, way, to):
        return self.place.copy(
            self.full.at[t, p],
            self.full.at[t, p],
            self.sent.at[t, p, way],
            self.came.at[t, p],
            to,
        )

    def start(self):
        g = self.place
        for p in range(self.pieces):
            pl.when(g.has_up)(lambda: self.copy(g.t, p, 0, g.t + 2).start())
            pl.when(g.has_down)(lambda: self.copy(g.t, p, 1, g.t - 2).start())
        for p in range(self.pieces):
            self.copy(g.t, p, 2, g.sib).start()

    def forward(self, d):
        g = self.place
        for p in range(self.pieces):

            @pl.when(g.j - d >= 0)
            def _():
                t = g.t - 2 * d
                self.copy(t, p, 0, g.sib).wait_recv()
                pl.when(g.has_up)(lambda: self.copy(t, p, 0, g.t + 2).start())
                self.copy(t, p, 2, g.sib).start()

            @pl.when(g.j + d < g.nz)
            def _():
                t = g.t + 2 * d
                self.copy(t, p, 1, g.sib).wait_recv()
                pl.when(g.has_down)(lambda: self.copy(t, p, 1, g.t - 2).start())
                self.copy(t, p, 2, g.sib).start()

    def each(self, d, use):
        g = self.place

        def visit(q):
            core, way = lax.div(q, 2), 2 * lax.rem(q, 2) - 1
            j = g.j + way * d
            there = jnp.logical_and(j >= 0, j < g.nz)

            @pl.when(jnp.logical_and(there, jnp.logical_or(d > 0, way > 0)))
            def _():
                t = 2 * j + lax.rem(g.c + core, 2)

                @pl.when(core > 0)
                def _():
                    for p in range(self.pieces):
                        self.copy(t, p, 2, g.sib).wait_recv()

                use(t)

        loop(4, visit)

    def finish(self):
        g = self.place

        def done(t):
            for p in range(self.pieces):
                self.copy(t, p, 2, g.sib).wait_send()

                @pl.when(jnp.logical_and(t <= g.t, g.has_up))
                def _():
                    self.copy(t, p, 0, g.sib).wait_send()

                @pl.when(jnp.logical_and(t >= g.t, g.has_down))
                def _():
                    self.copy(t, p, 1, g.sib).wait_send()

        loop(g.nz, lambda k: done(2 * k + g.c))


class Scatter:
    def __init__(self, place, partial, tile, bufs):
        self.place, self.partial, self.tile = place, partial, tile
        self.to_sib, self.from_sib, self.line, self.out, self.acc = bufs[:5]
        self.sib_send, self.sib_recv, self.line_send, self.line_recv = bufs[5:]
        self.tiles = self.acc.shape[1] // tile

    @staticmethod
    def scratch(n, rows, width):
        nz = n // 2
        return [
            pltpu.VMEM((nz, rows, width), BF16),
            pltpu.VMEM((nz, rows, width), BF16),
            pltpu.VMEM((nz + 1, rows, width), BF16),
            pltpu.VMEM((nz, rows, width), BF16),
            pltpu.VMEM((rows, width), F32),
            pltpu.SemaphoreType.DMA((nz,)),
            pltpu.SemaphoreType.DMA((nz,)),
            pltpu.SemaphoreType.DMA((nz,)),
            pltpu.SemaphoreType.DMA((nz + 1,)),
        ]

    def sib_copy(self, k):
        return self.place.copy(
            self.to_sib.at[k],
            self.from_sib.at[k],
            self.sib_send.at[k],
            self.sib_recv.at[k],
            self.place.sib,
        )

    def line_copy(self, k, slot, to):
        return self.place.copy(
            self.out.at[k], self.line.at[slot], self.line_send.at[k], self.line_recv.at[slot], to
        )

    def offer(self, k):
        t = 2 * k + 1 - self.place.c

        def part(i):
            cols = span(i, self.tile)
            self.to_sib[k, :, cols] = self.partial(t, cols).astype(BF16)

        loop(self.tiles, part)
        self.sib_copy(k).start()

    def pair(self, k):
        self.sib_copy(k).wait_recv()
        t = 2 * k + self.place.c

        def part(i):
            cols = span(i, self.tile)
            self.acc[:, cols] = self.partial(t, cols) + self.from_sib[k, :, cols].astype(F32)

        loop(self.tiles, part)

    def offers(self, d):
        g = self.place

        def way_of(w):
            k = g.j + (1 - 2 * w) * d

            @pl.when(jnp.logical_and(jnp.logical_and(k >= 0, k < g.nz), jnp.logical_or(d > 0, w == 0)))
            def _():
                self.offer(k)

        loop(2, way_of)

    def step(self, d):
        g = self.place

        def way_of(w):
            sign = 1 - 2 * w
            k = g.j + sign * d

            @pl.when(jnp.logical_and(k >= 0, k < g.nz))
            def _():
                self.pair(k)
                upstream = g.j - sign
                more = jnp.logical_and(upstream >= 0, upstream < g.nz)

                @pl.when(more)
                def _():
                    self.line_copy(k, k, g.sib).wait_recv()
                    self.out[k] = (self.acc[...] + self.line[k].astype(F32)).astype(BF16)

                @pl.when(jnp.logical_not(more))
                def _():
                    self.out[k] = self.acc[...].astype(BF16)

                slot = jnp.where(jnp.logical_and(d == 1, w == 1), g.nz, k)
                self.line_copy(k, slot, g.t + 2 * sign).start()

        loop(2, way_of)

    def last(self):
        g = self.place
        self.pair(g.j)

        @pl.when(g.has_down)
        def _():
            self.line_copy(g.j, g.j, g.sib).wait_recv()
            self.acc[...] += self.line[g.j].astype(F32)

        @pl.when(g.has_up)
        def _():
            self.line_copy(g.j, g.nz, g.sib).wait_recv()
            self.acc[...] += self.line[g.nz].astype(F32)

    def finish(self):
        g = self.place

        def done(k):
            self.sib_copy(k).wait_send()
            pl.when(g.j != k)(lambda: self.line_copy(k, k, g.sib).wait_send())

        loop(g.nz, done)


def comm_params(collective_id):
    return pltpu.CompilerParams(
        collective_id=collective_id, has_side_effects=True, vmem_limit_bytes=VMEM_LIMIT
    )


def cost(flops):
    return pl.CostEstimate(flops=int(flops), bytes_accessed=200_000_000, transcendentals=0)


def shape(*dims, dtype=F32):
    return jax.ShapeDtypeStruct(dims, dtype)


def inv_rms(values):
    return lax.rsqrt(jnp.mean(values * values, axis=-1, keepdims=True) + EPSILON)


def norm_grad(values, gain, gradient):
    inv = inv_rms(values)
    unit = values * inv
    scaled = gradient * gain
    centred = jnp.mean(scaled * unit, axis=-1, keepdims=True)
    return inv * (scaled - unit * centred), gradient * unit


def sigmoid(v):
    return 1.0 / (1.0 + jnp.exp(-v))


def gelu_parts(v):
    square = v * v
    bend = jnp.tanh(KAPPA * v * (1.0 + CUBIC * square))
    half = 0.5 * (1.0 + bend)
    slope = half + 0.5 * v * (1.0 - bend * bend) * (KAPPA * (1.0 + 3.0 * CUBIC * square))
    return v * half, slope


def one_minus_square(log_decay, decay):
    m = -2.0 * log_decay
    series = m * (
        1.0 - m * (1 / 2) * (1.0 - m * (1 / 3) * (1.0 - m * (1 / 4) * (1.0 - m * (1 / 5) * (1.0 - m * (1 / 6)))))
    )
    return jnp.where(m < 0.35, series, 1.0 - decay * decay)


def project_kernel(n, tokens, gain, w_in, w_br, normed, recur, branch, full, sent, came, held_a, held_b, saved):
    g = Place(n)
    gather = Gather(g, full, sent, came)
    size = full.shape[2]
    for p in range(PIECES):
        values = tokens[p * size : (p + 1) * size].astype(F32)
        full[g.t, p] = (values * inv_rms(values) * gain[...].astype(F32)).astype(BF16)
    g.greet()
    gather.start()

    def use(t):
        pltpu.make_async_copy(full.at[t], normed.at[t], saved.at[t, 0]).start()
        for p in range(PIECES):
            rows = slice(p * size, (p + 1) * size)
            held_a[t, rows] = dot(full[t, p], w_in[...])
            held_b[t, rows] = dot(full[t, p], w_br[...])
        pltpu.make_async_copy(held_a.at[t], recur.at[t], saved.at[t, 1]).start()
        pltpu.make_async_copy(held_b.at[t], branch.at[t], saved.at[t, 2]).start()

    gather.each(0, use)

    def away(i):
        gather.forward(i + 1)
        gather.each(i + 1, use)

    loop(g.nz - 1, away)

    def done(t):
        pltpu.make_async_copy(full.at[t], normed.at[t], saved.at[t, 0]).wait()
        pltpu.make_async_copy(held_a.at[t], recur.at[t], saved.at[t, 1]).wait()
        pltpu.make_async_copy(held_b.at[t], branch.at[t], saved.at[t, 2]).wait()

    loop(n, done)
    gather.finish()


def project(n, tokens, gain, w_in, w_br):
    rows, width = tokens.shape
    channels = w_in.shape[1]
    return pl.pallas_call(
        functools.partial(project_kernel, n),
        out_shape=(
            shape(n, PIECES, rows // PIECES, width, dtype=BF16),
            shape(n, rows, channels),
            shape(n, rows, channels),
        ),
        in_specs=[VM] * 4,
        out_specs=(ANY,) * 3,
        scratch_shapes=Gather.scratch(n, rows, width)
        + [pltpu.VMEM((n, rows, channels), F32)] * 2
        + [pltpu.SemaphoreType.DMA((n, 3))],
        compiler_params=comm_params(1),
        cost_estimate=cost(4 * n * rows * width * channels),
        name="project",
    )(tokens, gain, w_in, w_br)


def recur_kernel(
    u, branch, start_state, start_conv, conv, gate_w, bias, decay,
    states, mixture, conv_low, recall, ingate, final_state, final_conv,
    hist, decay_buf, drive_buf, carry,
):
    chunk = pl.program_id(1)
    rows, channels = u.shape
    tile = 32

    @pl.when(chunk == 0)
    def _():
        carry[...] = jnp.broadcast_to(start_state[0], (8, channels))
        hist[0:8] = jnp.concatenate([jnp.zeros((5, channels), F32), start_conv[0]], axis=0)

    @pl.when(chunk > 0)
    def _():
        hist[0:8] = hist[rows : rows + 8]

    hist[8:] = u[...]

    def convolve(i):
        window = hist[pl.ds(pl.multiple_of(i * tile, tile), tile + 8)]
        value = conv[4:5] + conv[0:1] * window[8:] + conv[1:2] * window[7 : tile + 7]
        value = value + conv[2:3] * window[6 : tile + 6] + conv[3:4] * window[5 : tile + 5]
        conv_low[span(i, tile)] = value.astype(BF16)

    loop(rows // tile, convolve)
    low = conv_low[...]
    recall[...] = dot(low, gate_w[0])
    ingate[...] = dot(low, gate_w[1])

    def gates(i):
        at = span(i, tile)
        r = sigmoid(recall[at] + bias[0:1])
        k = sigmoid(ingate[at] + bias[1:2])
        recall[at] = r
        ingate[at] = k
        log_decay = -8.0 * r * decay[...]
        step = jnp.exp(log_decay)
        decay_buf[at] = step
        drive_buf[at] = jnp.sqrt(one_minus_square(log_decay, step)) * k * conv_low[at].astype(F32)

    loop(rows // tile, gates)
    row = lax.broadcasted_iota(jnp.int32, (8, channels), 0)

    def scan(i, before):
        for part in range(4):
            at = pl.ds(pl.multiple_of(i * 32 + part * 8, 8), 8)
            a, b = decay_buf[at], drive_buf[at]
            for shift in (1, 2, 4):
                inside = row >= shift
                b = b + a * jnp.where(inside, pltpu.roll(b, shift, 0), 0.0)
                a = a * jnp.where(inside, pltpu.roll(a, shift, 0), 1.0)
            h = a * before + b
            states[at] = h
            before = jnp.broadcast_to(h[7:8], (8, channels))
        return before

    carry[...] = lax.fori_loop(0, rows // 32, scan, carry[...])

    def mix(i):
        at = span(i, tile)
        value, _ = gelu_parts(branch[at])
        mixture[at] = (states[at] * value).astype(BF16)

    loop(rows // tile, mix)

    @pl.when(chunk == pl.num_programs(1) - 1)
    def _():
        final_state[0] = carry[0:1]
        final_conv[0] = hist[rows + 5 : rows + 8]


def recur_forward(u, branch, start_state, start_conv, conv, gate_w, bias, decay):
    total, channels = u.shape
    sequences = start_state.shape[0]
    length = total // sequences
    rows = tile_of(length, 256)
    chunks = length // rows
    block = pl.BlockSpec((rows, channels), lambda s, c: (s * chunks + c, 0))

    def whole(x):
        return pl.BlockSpec(x.shape, lambda s, c: (0,) * x.ndim)

    return pl.pallas_call(
        recur_kernel,
        grid=(sequences, chunks),
        out_shape=(
            shape(total, channels),
            shape(total, channels, dtype=BF16),
            shape(total, channels, dtype=BF16),
            shape(total, channels),
            shape(total, channels),
            shape(sequences, 1, channels),
            shape(sequences, 3, channels),
        ),
        in_specs=[
            block,
            block,
            pl.BlockSpec((1, 1, channels), lambda s, c: (s, 0, 0)),
            pl.BlockSpec((1, 3, channels), lambda s, c: (s, 0, 0)),
            whole(conv),
            whole(gate_w),
            whole(bias),
            whole(decay),
        ],
        out_specs=(block,) * 5
        + (
            pl.BlockSpec((1, 1, channels), lambda s, c: (s, 0, 0)),
            pl.BlockSpec((1, 3, channels), lambda s, c: (s, 0, 0)),
        ),
        scratch_shapes=[
            pltpu.VMEM((rows + 8, channels), F32),
            pltpu.VMEM((rows, channels), F32),
            pltpu.VMEM((rows, channels), F32),
            pltpu.VMEM((8, channels), F32),
        ],
        compiler_params=pltpu.CompilerParams(vmem_limit_bytes=VMEM_LIMIT),
        name="recur_forward",
    )(u, branch, start_state, start_conv, conv, gate_w, bias, decay)


def mixer_out_kernel(
    n, mixture, w_output, cotangent, tokens, gain, cot_full, residual, normed,
    full, sent, came, saved, *bufs
):
    g = Place(n)
    gather = Gather(g, full, sent, came)
    scatter = Scatter(g, lambda t, cols: dot(mixture[t], w_output[:, cols]), tile_of(residual.shape[1], 512), bufs)
    size = full.shape[2]
    for p in range(PIECES):
        full[g.t, p] = cotangent[p * size : (p + 1) * size]
    g.greet()

    def use(t):
        pltpu.make_async_copy(full.at[t], cot_full.at[t], saved.at[t]).start()

    scatter.offers(g.nz - 1)
    gather.start()

    def around(i):
        d = g.nz - 1 - i
        scatter.offers(d - 1)
        scatter.step(d)
        gather.each(i, use)
        gather.forward(i + 1)

    loop(g.nz - 1, around)
    scatter.last()
    part = 64

    def rows_of(i):
        at = span(i, part)
        values = scatter.acc[at] + tokens[at].astype(F32)
        residual[at] = values
        normed[at] = (values * inv_rms(values) * gain[...].astype(F32)).astype(BF16)

    loop(residual.shape[0] // part, rows_of)
    gather.each(g.nz - 1, use)
    loop(n, lambda t: pltpu.make_async_copy(full.at[t], cot_full.at[t], saved.at[t]).wait())
    scatter.finish()
    gather.finish()


def mixer_out(n, mixture, w_output, cotangent, tokens, gain):
    rows, width = tokens.shape
    return pl.pallas_call(
        functools.partial(mixer_out_kernel, n),
        out_shape=(
            shape(n, PIECES, rows // PIECES, width, dtype=BF16),
            shape(rows, width),
            shape(rows, width, dtype=BF16),
        ),
        in_specs=[VM] * 5,
        out_specs=(ANY, VM, VM),
        scratch_shapes=Gather.scratch(n, rows, width)
        + [pltpu.SemaphoreType.DMA((n,))]
        + Scatter.scratch(n, rows, width),
        compiler_params=comm_params(2),
        cost_estimate=cost(2 * n * rows * width * mixture.shape[-1]),
        name="mixer_out",
    )(mixture, w_output, cotangent, tokens, gain)


def mlp_kernel(
    n, normed, cot_full, w_gelu, w_linear, w_down, hidden, g_first, g_second, grad_gelu, grad_linear, grad_down,
    full, sent, came, cot, keep_h, keep_f, keep_s, acc_g, acc_l, acc_d, stage_c, stage_w, saved, fetched, drained,
):
    g = Place(n)
    gather = Gather(g, full, sent, came)
    size = full.shape[2]
    rows = PIECES * size
    columns = w_gelu.shape[1]
    width = full.shape[3]
    tile = tile_of(columns, 256)
    wide = tile_of(width, 512)
    for p in range(PIECES):
        full[g.t, p] = normed[p * size : (p + 1) * size]
    g.greet()
    gather.start()
    acc_g[...] = jnp.zeros_like(acc_g)
    acc_l[...] = jnp.zeros_like(acc_l)
    acc_d[...] = jnp.zeros_like(acc_d)

    def save(t, i, start):
        for q, (held, out) in enumerate(((keep_h, hidden), (keep_f, g_first), (keep_s, g_second))):
            copy = pltpu.make_async_copy(held.at[t], out.at[t], saved.at[t, q])
            copy.start() if start else copy.wait()

    def use(t):
        fetch = pltpu.make_async_copy(cot_full.at[t], cot, fetched)
        fetch.start()
        fetch.wait()

        def piece(p):
            at = span(p, size)

            def part(i):
                cols = span(i, tile)
                first = dot(full[t, p], w_gelu[:, cols])
                second = dot(full[t, p], w_linear[:, cols])
                back = dot_nt(cot[p], w_down[cols])
                value, slope = gelu_parts(first)
                keep_h[t, at, cols] = (value * second).astype(BF16)
                keep_f[t, at, cols] = (back * second * slope).astype(BF16)
                keep_s[t, at, cols] = (back * value).astype(BF16)

            loop(columns // tile, part)

        loop(PIECES, piece)
        save(t, 0, True)

        def part(i):
            at = span(i, wide)
            for p in range(PIECES):
                rows_p = slice(p * size, (p + 1) * size)
                acc_g[at] += dot_tn(full[t, p, :, at], keep_f[t, rows_p])
                acc_l[at] += dot_tn(full[t, p, :, at], keep_s[t, rows_p])
                acc_d[:, at] += dot_tn(keep_h[t, rows_p], cot[p, :, at])

        loop(width // wide, part)

    gather.each(0, use)

    def away(i):
        gather.forward(i + 1)
        gather.each(i + 1, use)

    loop(g.nz - 1, away)
    loop(n, lambda t: save(t, 0, False))
    gather.finish()

    def drain(acc, stage, out, sem):
        part = stage.shape[1]

        def move(i):
            slot = lax.rem(i, 2)
            at = span(i, part)
            copy = pltpu.make_async_copy(stage.at[slot], out.at[at], sem.at[slot])
            pl.when(i >= 2)(copy.wait)
            stage[slot] = acc[at].astype(BF16)
            copy.start()

        count = acc.shape[0] // part
        loop(count, move)
        for slot in range(min(count, 2)):
            pltpu.make_async_copy(stage.at[slot], out.at[0:part], sem.at[slot]).wait()

    drain(acc_g, stage_c, grad_gelu, drained)
    drain(acc_l, stage_c, grad_linear, drained)
    drain(acc_d, stage_w, grad_down, drained)


def mlp(n, normed, cot_full, w_gelu, w_linear, w_down):
    rows, width = normed.shape
    columns = w_gelu.shape[1]
    kept = pltpu.VMEM((n, rows, columns), BF16)
    return pl.pallas_call(
        functools.partial(mlp_kernel, n),
        out_shape=(shape(n, rows, columns, dtype=BF16),) * 3
        + (shape(width, columns, dtype=BF16),) * 2
        + (shape(columns, width, dtype=BF16),),
        in_specs=[VM, ANY, VM, VM, VM],
        out_specs=(ANY,) * 6,
        scratch_shapes=Gather.scratch(n, rows, width)
        + [pltpu.VMEM((PIECES, rows // PIECES, width), BF16)]
        + [kept] * 3
        + [pltpu.VMEM((width, columns), F32)] * 2
        + [pltpu.VMEM((columns, width), F32)]
        + [pltpu.VMEM((2, tile_of(width, 256), columns), BF16)]
        + [pltpu.VMEM((2, tile_of(columns, 128), width), BF16)]
        + [pltpu.SemaphoreType.DMA((n, 3)), pltpu.SemaphoreType.DMA, pltpu.SemaphoreType.DMA((2,))],
        compiler_params=comm_params(3),
        cost_estimate=cost(12 * n * rows * width * columns),
        name="mlp",
    )(normed, cot_full, w_gelu, w_linear, w_down)


def mlp_back_kernel(n, g_first, g_second, w_gelu, w_linear, residual, cotangent, gain, g_residual, g_low, g_gain, *bufs):
    g = Place(n)

    def partial(t, cols):
        return dot_nt(g_first[t], w_gelu[cols]) + dot_nt(g_second[t], w_linear[cols])

    scatter = Scatter(g, partial, tile_of(residual.shape[1], 512), bufs)
    g.greet()
    scatter.offers(g.nz - 1)

    def around(i):
        d = g.nz - 1 - i
        scatter.offers(d - 1)
        scatter.step(d)

    loop(g.nz - 1, around)
    scatter.last()
    part = 32
    g_gain[...] = jnp.zeros_like(g_gain)

    def rows_of(i):
        at = span(i, part)
        back, terms = norm_grad(residual[at], gain[...].astype(F32), scatter.acc[at])
        value = cotangent[at].astype(F32) + back
        g_residual[at] = value
        g_low[at] = value.astype(BF16)
        g_gain[...] += jnp.sum(terms, axis=0, keepdims=True)

    loop(residual.shape[0] // part, rows_of)
    scatter.finish()


def mlp_back(n, g_first, g_second, w_gelu, w_linear, residual, cotangent, gain):
    rows, width = residual.shape
    return pl.pallas_call(
        functools.partial(mlp_back_kernel, n),
        out_shape=(shape(rows, width), shape(rows, width, dtype=BF16), shape(1, width)),
        in_specs=[VM] * 7,
        out_specs=(VM,) * 3,
        scratch_shapes=Scatter.scratch(n, rows, width),
        compiler_params=comm_params(4),
        cost_estimate=cost(4 * n * rows * width * w_gelu.shape[1]),
        name="mlp_back",
    )(g_first, g_second, w_gelu, w_linear, residual, cotangent, gain)


def down_kernel(
    n, hidden, w_down, residual, g_low, w_output, mixture, output, g_mixture, grad_output,
    full, sent, came, acc_o, *bufs
):
    g = Place(n)
    gather = Gather(g, full, sent, came)
    width = residual.shape[1]
    wide = tile_of(width, 512)
    scatter = Scatter(g, lambda t, cols: dot(hidden[t], w_down[:, cols]), wide, bufs)
    size = full.shape[2]
    for p in range(PIECES):
        full[g.t, p] = g_low[p * size : (p + 1) * size]
    g.greet()

    def use(t):
        for p in range(PIECES):
            rows = slice(p * size, (p + 1) * size)
            g_mixture[t, rows] = dot_nt(full[t, p], w_output[...])

        def part(i):
            at = span(i, wide)
            for p in range(PIECES):
                rows = slice(p * size, (p + 1) * size)
                acc_o[:, at] += dot_tn(mixture[t, rows], full[t, p, :, at])

        loop(width // wide, part)

    gather.start()
    acc_o[...] = jnp.zeros_like(acc_o)
    scatter.offers(g.nz - 1)

    def around(i):
        d = g.nz - 1 - i
        scatter.offers(d - 1)
        scatter.step(d)
        gather.each(i, use)
        gather.forward(i + 1)

    loop(g.nz - 1, around)
    gather.each(g.nz - 1, use)
    grad_output[...] = acc_o[...].astype(BF16)
    scatter.last()
    output[...] = (scatter.acc[...] + residual[...]).astype(BF16)
    scatter.finish()
    gather.finish()


def down(n, hidden, w_down, residual, g_low, w_output, mixture):
    rows, width = residual.shape
    channels = w_output.shape[0]
    return pl.pallas_call(
        functools.partial(down_kernel, n),
        out_shape=(
            shape(rows, width, dtype=BF16),
            shape(n, rows, channels),
            shape(channels, width, dtype=BF16),
        ),
        in_specs=[VM] * 6,
        out_specs=(VM,) * 3,
        scratch_shapes=Gather.scratch(n, rows, width)
        + [pltpu.VMEM((channels, width), F32)]
        + Scatter.scratch(n, rows, width),
        compiler_params=comm_params(5),
        cost_estimate=cost(2 * n * rows * width * (hidden.shape[-1] + 2 * channels)),
        name="down",
    )(hidden, w_down, residual, g_low, w_output, mixture)


def recur_back_kernel(
    g_mix, branch, states, states_before, u, u_before, conv_low, recall, ingate, start_state, start_conv,
    conv, gate_w, decay,
    g_recur, g_branch, small, g_gates,
    g_state, step_buf, root_buf, g_conv, pre_r, pre_i, carry, hist_s, hist_u, sums,
):
    sequence, back = pl.program_id(0), pl.program_id(1)
    last = pl.num_programs(1) - 1
    rows, channels = u.shape
    tile = 32

    @pl.when(jnp.logical_and(sequence == 0, back == 0))
    def _():
        sums[...] = jnp.zeros_like(sums)
        g_gates[...] = jnp.zeros_like(g_gates)

    @pl.when(back == 0)
    def _():
        carry[...] = jnp.zeros_like(carry)
        g_conv[rows : rows + 8] = jnp.zeros((8, channels), F32)

    @pl.when(back > 0)
    def _():
        g_conv[rows : rows + 8] = g_conv[0:8]

    @pl.when(back == last)
    def _():
        hist_s[0:8] = jnp.broadcast_to(start_state[0], (8, channels))
        hist_u[0:8] = jnp.concatenate([jnp.zeros((5, channels), F32), start_conv[0]], axis=0)

    @pl.when(back < last)
    def _():
        hist_s[0:8] = states_before[...]
        hist_u[0:8] = u_before[...]

    hist_s[8:] = states[...]
    hist_u[8:] = u[...]

    def first(i):
        at = span(i, tile)
        value, slope = gelu_parts(branch[at])
        gm = g_mix[at]
        g_state[at] = gm * value
        g_branch[at] = (gm * states[at] * slope).astype(BF16)
        log_decay = -8.0 * recall[at] * decay[...]
        step = jnp.exp(log_decay)
        step_buf[at] = step
        root_buf[at] = jnp.sqrt(one_minus_square(log_decay, step))

    loop(rows // tile, first)
    row = lax.broadcasted_iota(jnp.int32, (8, channels), 0)
    groups = rows // 32

    def scan(i, after):
        for part in range(4):
            at = pl.ds(pl.multiple_of((groups - 1 - i) * 32 + (3 - part) * 8, 8), 8)
            a, gs = step_buf[at], g_state[at]
            b = a * gs
            for shift in (1, 2, 4):
                inside = row < 8 - shift
                b = b + a * jnp.where(inside, pltpu.roll(b, 8 - shift, 0), 0.0)
                a = a * jnp.where(inside, pltpu.roll(a, 8 - shift, 0), 1.0)
            e = a * after + b
            g_state[at] = gs + jnp.where(row < 7, pltpu.roll(e, 7, 0), after)
            after = jnp.broadcast_to(e[0:1], (8, channels))
        return after

    carry[...] = lax.fori_loop(0, groups, scan, carry[...])

    def fold(x):
        return jnp.sum(x.reshape(tile // 8, 8, channels), axis=0)

    def second(i):
        at = span(i, tile)
        window = hist_s[pl.ds(pl.multiple_of(i * tile, tile), tile + 8)]
        before = window[7 : tile + 7]
        g, r, k = g_state[at], recall[at], ingate[at]
        c = conv_low[at].astype(F32)
        step, root = step_buf[at], root_buf[at]
        kc = k * c
        g_log = g * (before * step - kc * (step * step) / root)
        slow = -8.0 * r
        sums[7] += fold(g_log * slow)
        low_r = (g_log * (slow * decay[...]) * (1.0 - r)).astype(BF16)
        low_i = (g * root * kc * (1.0 - k)).astype(BF16)
        pre_r[at] = low_r
        pre_i[at] = low_i
        sums[5] += fold(low_r.astype(F32))
        sums[6] += fold(low_i.astype(F32))
        g_conv[at] = g * root * k

    loop(rows // tile, second)
    low_r, low_i, low_c = pre_r[...], pre_i[...], conv_low[...]
    g_gates[0] += dot_tn(low_c, low_r)
    g_gates[1] += dot_tn(low_c, low_i)
    g_conv[0:rows] += dot_nt(low_r, gate_w[0]) + dot_nt(low_i, gate_w[1])

    def third(i):
        at = span(i, tile)
        start = pl.multiple_of(i * tile, tile)
        window = g_conv[pl.ds(start, tile + 8)]
        value = conv[0:1] * window[0:tile]
        for k in (1, 2, 3):
            value = value + conv[k : k + 1] * window[k : tile + k]
        g_recur[at] = value.astype(BF16)
        past = hist_u[pl.ds(start, tile + 8)]
        gc = window[0:tile]
        for k in range(4):
            sums[k] += fold(gc * past[8 - k : tile + 8 - k])
        sums[4] += fold(gc)

    loop(rows // tile, third)

    @pl.when(jnp.logical_and(sequence == pl.num_programs(0) - 1, back == last))
    def _():
        small[...] = jnp.sum(sums[...], axis=1)


def recur_back(g_mix, branch, states, u, conv_low, recall, ingate, start_state, start_conv, conv, gate_w, decay):
    total, channels = u.shape
    sequences = start_state.shape[0]
    length = total // sequences
    rows = tile_of(length, 256)
    chunks = length // rows
    eights = rows // 8

    def at(s, c):
        return (s * chunks + chunks - 1 - c, 0)

    def earlier(s, c):
        return (jnp.maximum((s * chunks + chunks - 1 - c) * eights - 1, 0), 0)

    block = pl.BlockSpec((rows, channels), at)
    before = pl.BlockSpec((8, channels), earlier)

    def whole(x):
        return pl.BlockSpec(x.shape, lambda s, c: (0,) * x.ndim)

    wide = pltpu.VMEM((rows, channels), F32)
    narrow = pltpu.VMEM((rows, channels), BF16)
    long = pltpu.VMEM((rows + 8, channels), F32)
    return pl.pallas_call(
        recur_back_kernel,
        grid=(sequences, chunks),
        out_shape=(
            shape(total, channels, dtype=BF16),
            shape(total, channels, dtype=BF16),
            shape(8, channels),
            shape(2, channels, channels),
        ),
        in_specs=[
            block, block, block, before, block, before, block, block, block,
            pl.BlockSpec((1, 1, channels), lambda s, c: (s, 0, 0)),
            pl.BlockSpec((1, 3, channels), lambda s, c: (s, 0, 0)),
            whole(conv), whole(gate_w), whole(decay),
        ],
        out_specs=(
            block,
            block,
            pl.BlockSpec((8, channels), lambda s, c: (0, 0)),
            pl.BlockSpec((2, channels, channels), lambda s, c: (0, 0, 0)),
        ),
        scratch_shapes=[
            wide, wide, wide, long, narrow, narrow,
            pltpu.VMEM((8, channels), F32), long, long,
            pltpu.VMEM((8, 8, channels), F32),
        ],
        compiler_params=pltpu.CompilerParams(vmem_limit_bytes=VMEM_LIMIT),
        name="recur_back",
    )(g_mix, branch, states, states, u, u, conv_low, recall, ingate, start_state, start_conv, conv, gate_w, decay)


def input_back_kernel(n, g_recur, g_branch, w_in, w_br, tokens, g_residual, gain, input_grad, g_gain, *bufs):
    g = Place(n)

    def partial(t, cols):
        return dot_nt(g_recur[t], w_in[cols]) + dot_nt(g_branch[t], w_br[cols])

    scatter = Scatter(g, partial, tile_of(tokens.shape[1], 512), bufs)
    g.greet()
    scatter.offers(g.nz - 1)

    def around(i):
        d = g.nz - 1 - i
        scatter.offers(d - 1)
        scatter.step(d)

    loop(g.nz - 1, around)
    scatter.last()
    part = 32
    g_gain[...] = jnp.zeros_like(g_gain)

    def rows_of(i):
        at = span(i, part)
        back, terms = norm_grad(tokens[at].astype(F32), gain[...].astype(F32), scatter.acc[at])
        input_grad[at] = g_residual[at] + back
        g_gain[...] += jnp.sum(terms, axis=0, keepdims=True)

    loop(tokens.shape[0] // part, rows_of)
    scatter.finish()


def input_back(n, g_recur, g_branch, w_in, w_br, tokens, g_residual, gain):
    rows, width = tokens.shape
    return pl.pallas_call(
        functools.partial(input_back_kernel, n),
        out_shape=(shape(rows, width), shape(1, width)),
        in_specs=[VM] * 7,
        out_specs=(VM,) * 2,
        scratch_shapes=Scatter.scratch(n, rows, width),
        compiler_params=comm_params(6),
        cost_estimate=cost(4 * n * rows * width * w_in.shape[1]),
        name="input_back",
    )(g_recur, g_branch, w_in, w_br, tokens, g_residual, gain)


def after(first, *rest):
    return lax.optimization_barrier((first, *rest))[1:]


def body(
    n,
    tokens,
    cotangent,
    resets,
    init_state,
    init_conv,
    norm_gain,
    w_input,
    w_branch,
    conv_params,
    gate_weights,
    gate_bias,
    decay_rate,
    w_output,
    mlp_gain,
    w_gelu,
    w_linear,
    w_down,
):
    rows, width = tokens.shape
    total = rows * n
    channels = w_input.shape[1]
    blocks, block = gate_weights.shape[1], gate_weights.shape[2]
    survive = (1 - resets).astype(F32)
    start_state = (init_state * survive[:, None])[:, None]
    start_conv = init_conv * survive[:, None, None]
    gain_first, gain_second = norm_gain[None], mlp_gain[None]
    gate_w = (gate_weights[:, :, :, None] * jnp.eye(blocks, dtype=BF16)[None, :, None, :, None]).reshape(
        2, channels, channels
    )
    decay = decay_rate[None]

    def flat(x):
        return x.reshape(total, x.shape[-1])

    def blocked(x):
        return x.reshape(n, rows, x.shape[-1])

    normed, recur, branch = project(n, tokens, gain_first, w_input, w_branch)
    recur, branch = flat(recur), flat(branch)
    states, mixture, conv_low, recall, ingate, final_state, final_conv = recur_forward(
        recur, branch, start_state, start_conv, conv_params, gate_w, gate_bias, decay
    )
    mixture = blocked(mixture)
    cot_full, residual, normed_mlp = mixer_out(n, mixture, w_output, cotangent, tokens, gain_second)
    hidden, g_first, g_second, grad_gelu, grad_linear, grad_down = mlp(
        n, normed_mlp, cot_full, w_gelu, w_linear, w_down
    )
    mlp_sums = lax.psum((grad_gelu, grad_linear, grad_down), "dp")
    g_residual, g_low, gain_second_grad = mlp_back(
        n, g_first, g_second, w_gelu, w_linear, residual, cotangent, gain_second
    )
    output, g_mixture, grad_output = down(n, hidden, w_down, residual, g_low, w_output, mixture)
    g_recur, g_branch, small, g_gates = recur_back(
        flat(g_mixture), branch, states, recur, conv_low, recall, ingate, start_state, start_conv,
        conv_params, gate_w, decay,
    )
    whole = normed.reshape(total, width)
    grad_input = dot_tn(whole, g_recur).astype(BF16)
    grad_branch = dot_tn(whole, g_branch).astype(BF16)
    gates = g_gates.reshape(2, blocks, block, blocks, block)
    gates = jnp.stack([gates[:, i, :, i] for i in range(blocks)], axis=1)
    late = (grad_output, grad_input, grad_branch, gates.astype(BF16), small.astype(BF16))
    mlp_sums, late = lax.optimization_barrier((mlp_sums, late))
    late_sums = lax.psum(late, "dp")
    input_grad, gain_first_grad = input_back(
        n, blocked(g_recur), blocked(g_branch), w_input, w_branch, tokens, g_residual, gain_first
    )
    gains = jnp.concatenate([gain_first_grad, gain_second_grad], axis=0)
    gains = lax.psum_scatter(gains, "tensor", scatter_dimension=1, tiled=True)
    gains = lax.psum(gains, "dp")
    grad_gelu, grad_linear, grad_down = (x.astype(F32) for x in mlp_sums)
    grad_output, grad_input, grad_branch, gates, small = (x.astype(F32) for x in late_sums)
    return (
        output,
        input_grad,
        final_state[:, 0],
        final_conv,
        gains[0],
        grad_input,
        grad_branch,
        small[:5],
        gates,
        small[5:7],
        small[7],
        grad_output,
        gains[1],
        grad_gelu,
        grad_linear,
        grad_down,
    )


def solution(mesh):
    in_specs = (
        P(("dp", "tensor"), None),
        P(("dp", "tensor"), None),
        P("dp"),
        P("dp", "tensor"),
        P("dp", None, "tensor"),
        P(),
        P(None, "tensor"),
        P(None, "tensor"),
        P(None, "tensor"),
        P(None, "tensor", None, None),
        P(None, "tensor"),
        P("tensor"),
        P("tensor", None),
        P(),
        P(None, "tensor"),
        P(None, "tensor"),
        P("tensor", None),
    )
    out_specs = (
        P(("dp", "tensor"), None),
        P(("dp", "tensor"), None),
        P("dp", "tensor"),
        P("dp", None, "tensor"),
        P("tensor"),
        P(None, "tensor"),
        P(None, "tensor"),
        P(None, "tensor"),
        P(None, "tensor", None, None),
        P(None, "tensor"),
        P("tensor"),
        P("tensor", None),
        P("tensor"),
        P(None, "tensor"),
        P(None, "tensor"),
        P("tensor", None),
    )
    return jax.shard_map(
        functools.partial(body, mesh.shape["tensor"]),
        mesh=mesh,
        in_specs=in_specs,
        out_specs=out_specs,
        check_vma=False,
    )
```

```python
import functools

import jax
import jax.numpy as jnp
from jax import lax
from jax.experimental import pallas as pl
from jax.experimental.pallas import tpu as pltpu
from jax.sharding import PartitionSpec as P

EPSILON = 1e-06
KAPPA = 0.7978845608028654
CUBIC = 0.044715
PIECES = 2
F32 = jnp.float32
BF16 = jnp.bfloat16
ANY = pl.BlockSpec(memory_space=pl.ANY)
VM = pl.BlockSpec(memory_space=pltpu.VMEM)
VMEM_LIMIT = 61 * 1024 * 1024
MESH = pl.DeviceIdType.MESH


def dot(a, b):
    return jnp.dot(a, b, preferred_element_type=F32)


def dot_nt(a, b):
    return lax.dot_general(a, b, (((1,), (1,)), ((), ())), preferred_element_type=F32)


def dot_tn(a, b):
    return lax.dot_general(a, b, (((0,), (0,)), ((), ())), preferred_element_type=F32)


def tile_of(extent, wanted):
    while extent % wanted:
        wanted //= 2
    return wanted


def span(i, size):
    return pl.ds(pl.multiple_of(i * size, size), size)


def loop(count, body):
    def step(i, carry):
        body(i)
        return carry

    lax.fori_loop(0, count, step, 0)


class Place:
    def __init__(self, n):
        self.n = n
        self.nz = n // 2
        self.t = lax.axis_index("tensor")
        self.c = lax.rem(self.t, 2)
        self.j = lax.div(self.t, 2)
        self.sib = self.t + 1 - 2 * self.c
        self.has_up = self.j < self.nz - 1
        self.has_down = self.j > 0

    def greet(self):
        barrier = pltpu.get_barrier_semaphore()

        def signal(t):
            pl.semaphore_signal(barrier, inc=1, device_id={"tensor": t}, device_id_type=MESH)

        signal(self.sib)
        pl.when(self.has_up)(lambda: signal(self.t + 2))
        pl.when(self.has_down)(lambda: signal(self.t - 2))
        pl.semaphore_wait(
            barrier, 1 + self.has_up.astype(jnp.int32) + self.has_down.astype(jnp.int32)
        )

    def copy(self, src, dst, send, recv, t):
        return pltpu.make_async_remote_copy(
            src_ref=src,
            dst_ref=dst,
            send_sem=send,
            recv_sem=recv,
            device_id={"tensor": t},
            device_id_type=MESH,
        )


class Gather:
    def __init__(self, place, full, sent, came):
        self.place, self.full, self.sent, self.came = place, full, sent, came
        self.pieces = came.shape[1]
        self.size = full.shape[1] // self.pieces

    @staticmethod
    def scratch(n, rows, width):
        return [
            pltpu.VMEM((n, rows, width), BF16),
            pltpu.SemaphoreType.DMA((n, PIECES, 3)),
            pltpu.SemaphoreType.DMA((n, PIECES)),
        ]

    def copy(self, t, p, way, to):
        piece = self.full.at[t, pl.ds(p * self.size, self.size)]
        return self.place.copy(piece, piece, self.sent.at[t, p, way], self.came.at[t, p], to)

    def start(self):
        g = self.place
        for p in range(self.pieces):
            pl.when(g.has_up)(lambda: self.copy(g.t, p, 0, g.t + 2).start())
            pl.when(g.has_down)(lambda: self.copy(g.t, p, 1, g.t - 2).start())
        for p in range(self.pieces):
            self.copy(g.t, p, 2, g.sib).start()

    def forward(self, d):
        g = self.place
        for p in range(self.pieces):

            @pl.when(g.j - d >= 0)
            def _():
                t = g.t - 2 * d
                self.copy(t, p, 0, g.sib).wait_recv()
                pl.when(g.has_up)(lambda: self.copy(t, p, 0, g.t + 2).start())
                self.copy(t, p, 2, g.sib).start()

            @pl.when(g.j + d < g.nz)
            def _():
                t = g.t + 2 * d
                self.copy(t, p, 1, g.sib).wait_recv()
                pl.when(g.has_down)(lambda: self.copy(t, p, 1, g.t - 2).start())
                self.copy(t, p, 2, g.sib).start()

    def each(self, d, use):
        g = self.place

        def visit(q):
            core, way = lax.div(q, 2), 2 * lax.rem(q, 2) - 1
            j = g.j + way * d
            there = jnp.logical_and(j >= 0, j < g.nz)

            @pl.when(jnp.logical_and(there, jnp.logical_or(d > 0, way > 0)))
            def _():
                t = 2 * j + lax.rem(g.c + core, 2)

                @pl.when(core > 0)
                def _():
                    for p in range(self.pieces):
                        self.copy(t, p, 2, g.sib).wait_recv()

                use(t)

        loop(4, visit)

    def finish(self):
        g = self.place

        def done(t):
            for p in range(self.pieces):
                self.copy(t, p, 2, g.sib).wait_send()

                @pl.when(jnp.logical_and(t <= g.t, g.has_up))
                def _():
                    self.copy(t, p, 0, g.sib).wait_send()

                @pl.when(jnp.logical_and(t >= g.t, g.has_down))
                def _():
                    self.copy(t, p, 1, g.sib).wait_send()

        loop(g.nz, lambda k: done(2 * k + g.c))


class Scatter:
    def __init__(self, place, partial, tile, bufs):
        self.place, self.partial, self.tile = place, partial, tile
        self.to_sib, self.from_sib, self.line, self.out, self.acc = bufs[:5]
        self.sib_send, self.sib_recv, self.line_send, self.line_recv = bufs[5:]
        self.tiles = self.acc.shape[1] // tile

    @staticmethod
    def scratch(n, rows, width):
        nz = n // 2
        return [
            pltpu.VMEM((nz, rows, width), BF16),
            pltpu.VMEM((nz, rows, width), BF16),
            pltpu.VMEM((nz + 1, rows, width), BF16),
            pltpu.VMEM((nz, rows, width), BF16),
            pltpu.VMEM((rows, width), F32),
            pltpu.SemaphoreType.DMA((nz,)),
            pltpu.SemaphoreType.DMA((nz,)),
            pltpu.SemaphoreType.DMA((nz,)),
            pltpu.SemaphoreType.DMA((nz + 1,)),
        ]

    def sib_copy(self, k):
        return self.place.copy(
            self.to_sib.at[k],
            self.from_sib.at[k],
            self.sib_send.at[k],
            self.sib_recv.at[k],
            self.place.sib,
        )

    def line_copy(self, k, slot, to):
        return self.place.copy(
            self.out.at[k], self.line.at[slot], self.line_send.at[k], self.line_recv.at[slot], to
        )

    def offer(self, k):
        t = 2 * k + 1 - self.place.c

        def part(i):
            cols = span(i, self.tile)
            self.to_sib[k, :, cols] = self.partial(t, cols).astype(BF16)

        loop(self.tiles, part)
        self.sib_copy(k).start()

    def pair(self, k):
        self.sib_copy(k).wait_recv()
        t = 2 * k + self.place.c

        def part(i):
            cols = span(i, self.tile)
            self.acc[:, cols] = self.partial(t, cols) + self.from_sib[k, :, cols].astype(F32)

        loop(self.tiles, part)

    def offers(self, d):
        g = self.place

        def way_of(w):
            k = g.j + (1 - 2 * w) * d

            @pl.when(jnp.logical_and(jnp.logical_and(k >= 0, k < g.nz), jnp.logical_or(d > 0, w == 0)))
            def _():
                self.offer(k)

        loop(2, way_of)

    def step(self, d):
        g = self.place

        def way_of(w):
            sign = 1 - 2 * w
            k = g.j + sign * d

            @pl.when(jnp.logical_and(k >= 0, k < g.nz))
            def _():
                self.pair(k)
                upstream = g.j - sign
                more = jnp.logical_and(upstream >= 0, upstream < g.nz)

                @pl.when(more)
                def _():
                    self.line_copy(k, k, g.sib).wait_recv()
                    self.out[k] = (self.acc[...] + self.line[k].astype(F32)).astype(BF16)

                @pl.when(jnp.logical_not(more))
                def _():
                    self.out[k] = self.acc[...].astype(BF16)

                slot = jnp.where(jnp.logical_and(d == 1, w == 1), g.nz, k)
                self.line_copy(k, slot, g.t + 2 * sign).start()

        loop(2, way_of)

    def last(self):
        g = self.place
        self.pair(g.j)

        @pl.when(g.has_down)
        def _():
            self.line_copy(g.j, g.j, g.sib).wait_recv()
            self.acc[...] += self.line[g.j].astype(F32)

        @pl.when(g.has_up)
        def _():
            self.line_copy(g.j, g.nz, g.sib).wait_recv()
            self.acc[...] += self.line[g.nz].astype(F32)

    def finish(self):
        g = self.place

        def done(k):
            self.sib_copy(k).wait_send()
            pl.when(g.j != k)(lambda: self.line_copy(k, k, g.sib).wait_send())

        loop(g.nz, done)


def comm_params(collective_id):
    return pltpu.CompilerParams(
        collective_id=collective_id, has_side_effects=True, vmem_limit_bytes=VMEM_LIMIT
    )


def cost(flops):
    return pl.CostEstimate(flops=int(flops), bytes_accessed=200_000_000, transcendentals=0)


def shape(*dims, dtype=F32):
    return jax.ShapeDtypeStruct(dims, dtype)


def inv_rms(values):
    return lax.rsqrt(jnp.mean(values * values, axis=-1, keepdims=True) + EPSILON)


def norm_grad(values, gain, gradient):
    inv = inv_rms(values)
    unit = values * inv
    scaled = gradient * gain
    centred = jnp.mean(scaled * unit, axis=-1, keepdims=True)
    return inv * (scaled - unit * centred), gradient * unit


def sigmoid(v):
    return 1.0 / (1.0 + jnp.exp(-v))


def gelu_parts(v):
    square = v * v
    bend = jnp.tanh(KAPPA * v * (1.0 + CUBIC * square))
    half = 0.5 * (1.0 + bend)
    slope = half + 0.5 * v * (1.0 - bend * bend) * (KAPPA * (1.0 + 3.0 * CUBIC * square))
    return v * half, slope


def one_minus_square(log_decay, decay):
    m = -2.0 * log_decay
    series = m * (
        1.0 - m * (1 / 2) * (1.0 - m * (1 / 3) * (1.0 - m * (1 / 4) * (1.0 - m * (1 / 5) * (1.0 - m * (1 / 6)))))
    )
    return jnp.where(m < 0.35, series, 1.0 - decay * decay)


def project_kernel(n, tokens, gain, w_in, w_br, normed, recur, branch, full, sent, came, held_a, held_b, saved):
    g = Place(n)
    gather = Gather(g, full, sent, came)
    part = 64

    def normalize(i):
        at = span(i, part)
        values = tokens[at].astype(F32)
        full[g.t, at] = (values * inv_rms(values) * gain[...].astype(F32)).astype(BF16)

    loop(full.shape[1] // part, normalize)
    g.greet()
    gather.start()

    def use(t):
        pltpu.make_async_copy(full.at[t], normed.at[t], saved.at[t, 0]).start()
        held_a[t] = dot_nt(full[t], w_in[...])
        held_b[t] = dot_nt(full[t], w_br[...])
        pltpu.make_async_copy(held_a.at[t], recur.at[t], saved.at[t, 1]).start()
        pltpu.make_async_copy(held_b.at[t], branch.at[t], saved.at[t, 2]).start()

    gather.each(0, use)

    def away(i):
        gather.forward(i + 1)
        gather.each(i + 1, use)

    loop(g.nz - 1, away)

    def done(t):
        pltpu.make_async_copy(full.at[t], normed.at[t], saved.at[t, 0]).wait()
        pltpu.make_async_copy(held_a.at[t], recur.at[t], saved.at[t, 1]).wait()
        pltpu.make_async_copy(held_b.at[t], branch.at[t], saved.at[t, 2]).wait()

    loop(n, done)
    gather.finish()


def project(n, tokens, gain, w_in, w_br):
    rows, width = tokens.shape
    channels = w_in.shape[0]
    return pl.pallas_call(
        functools.partial(project_kernel, n),
        out_shape=(
            shape(n, rows, width, dtype=BF16),
            shape(n, rows, channels),
            shape(n, rows, channels),
        ),
        in_specs=[VM] * 4,
        out_specs=(ANY,) * 3,
        scratch_shapes=Gather.scratch(n, rows, width)
        + [pltpu.VMEM((n, rows, channels), F32)] * 2
        + [pltpu.SemaphoreType.DMA((n, 3))],
        compiler_params=comm_params(1),
        cost_estimate=cost(4 * n * rows * width * channels),
        name="project",
    )(tokens, gain, w_in, w_br)


def recur_kernel(
    u, branch, start_state, start_conv, conv, gate_w, bias, decay,
    states, mixture, conv_low, recall, ingate, final_state, final_conv,
    hist, decay_buf, drive_buf, carry,
):
    chunk = pl.program_id(1)
    rows, channels = u.shape
    tile = 32

    @pl.when(chunk == 0)
    def _():
        carry[...] = jnp.broadcast_to(start_state[0], (8, channels))
        hist[0:8] = jnp.concatenate([jnp.zeros((5, channels), F32), start_conv[0]], axis=0)

    @pl.when(chunk > 0)
    def _():
        hist[0:8] = hist[rows : rows + 8]

    hist[8:] = u[...]

    def convolve(i):
        window = hist[pl.ds(pl.multiple_of(i * tile, tile), tile + 8)]
        value = conv[4:5] + conv[0:1] * window[8:] + conv[1:2] * window[7 : tile + 7]
        value = value + conv[2:3] * window[6 : tile + 6] + conv[3:4] * window[5 : tile + 5]
        conv_low[span(i, tile)] = value.astype(BF16)

    loop(rows // tile, convolve)
    low = conv_low[...]
    recall[...] = dot(low, gate_w[0])
    ingate[...] = dot(low, gate_w[1])

    def gates(i):
        at = span(i, tile)
        r = sigmoid(recall[at] + bias[0:1])
        k = sigmoid(ingate[at] + bias[1:2])
        recall[at] = r
        ingate[at] = k
        log_decay = -8.0 * r * decay[...]
        step = jnp.exp(log_decay)
        decay_buf[at] = step
        drive_buf[at] = jnp.sqrt(one_minus_square(log_decay, step)) * k * conv_low[at].astype(F32)

    loop(rows // tile, gates)
    row = lax.broadcasted_iota(jnp.int32, (8, channels), 0)

    def scan(i, before):
        for part in range(4):
            at = pl.ds(pl.multiple_of(i * 32 + part * 8, 8), 8)
            a, b = decay_buf[at], drive_buf[at]
            for shift in (1, 2, 4):
                inside = row >= shift
                b = b + a * jnp.where(inside, pltpu.roll(b, shift, 0), 0.0)
                a = a * jnp.where(inside, pltpu.roll(a, shift, 0), 1.0)
            h = a * before + b
            states[at] = h
            before = jnp.broadcast_to(h[7:8], (8, channels))
        return before

    carry[...] = lax.fori_loop(0, rows // 32, scan, carry[...])

    def mix(i):
        at = span(i, tile)
        value, _ = gelu_parts(branch[at])
        mixture[at] = (states[at] * value).astype(BF16)

    loop(rows // tile, mix)

    @pl.when(chunk == pl.num_programs(1) - 1)
    def _():
        final_state[0] = carry[0:1]
        final_conv[0] = hist[rows + 5 : rows + 8]


def recur_forward(u, branch, start_state, start_conv, conv, gate_w, bias, decay):
    total, channels = u.shape
    sequences = start_state.shape[0]
    length = total // sequences
    rows = tile_of(length, 256)
    chunks = length // rows
    block = pl.BlockSpec((rows, channels), lambda s, c: (s * chunks + c, 0))

    def whole(x):
        return pl.BlockSpec(x.shape, lambda s, c: (0,) * x.ndim)

    return pl.pallas_call(
        recur_kernel,
        grid=(sequences, chunks),
        out_shape=(
            shape(total, channels),
            shape(total, channels, dtype=BF16),
            shape(total, channels, dtype=BF16),
            shape(total, channels),
            shape(total, channels),
            shape(sequences, 1, channels),
            shape(sequences, 3, channels),
        ),
        in_specs=[
            block,
            block,
            pl.BlockSpec((1, 1, channels), lambda s, c: (s, 0, 0)),
            pl.BlockSpec((1, 3, channels), lambda s, c: (s, 0, 0)),
            whole(conv),
            whole(gate_w),
            whole(bias),
            whole(decay),
        ],
        out_specs=(block,) * 5
        + (
            pl.BlockSpec((1, 1, channels), lambda s, c: (s, 0, 0)),
            pl.BlockSpec((1, 3, channels), lambda s, c: (s, 0, 0)),
        ),
        scratch_shapes=[
            pltpu.VMEM((rows + 8, channels), F32),
            pltpu.VMEM((rows, channels), F32),
            pltpu.VMEM((rows, channels), F32),
            pltpu.VMEM((8, channels), F32),
        ],
        compiler_params=pltpu.CompilerParams(vmem_limit_bytes=VMEM_LIMIT),
        name="recur_forward",
    )(u, branch, start_state, start_conv, conv, gate_w, bias, decay)


def mixer_out_kernel(
    n, mixture, w_output, cotangent, tokens, gain, cot_full, residual, normed,
    full, sent, came, saved, *bufs
):
    g = Place(n)
    gather = Gather(g, full, sent, came)
    scatter = Scatter(g, lambda t, cols: dot(mixture[t], w_output[:, cols]), tile_of(residual.shape[1], 512), bufs)
    full[g.t] = cotangent[...]
    g.greet()

    def use(t):
        pltpu.make_async_copy(full.at[t], cot_full.at[t], saved.at[t]).start()

    scatter.offers(g.nz - 1)
    gather.start()

    def around(i):
        d = g.nz - 1 - i
        scatter.offers(d - 1)
        scatter.step(d)
        gather.each(i, use)
        gather.forward(i + 1)

    loop(g.nz - 1, around)
    scatter.last()
    part = 64

    def rows_of(i):
        at = span(i, part)
        values = scatter.acc[at] + tokens[at].astype(F32)
        residual[at] = values
        normed[at] = (values * inv_rms(values) * gain[...].astype(F32)).astype(BF16)

    loop(residual.shape[0] // part, rows_of)
    gather.each(g.nz - 1, use)
    loop(n, lambda t: pltpu.make_async_copy(full.at[t], cot_full.at[t], saved.at[t]).wait())
    scatter.finish()
    gather.finish()


def mixer_out(n, mixture, w_output, cotangent, tokens, gain):
    rows, width = tokens.shape
    return pl.pallas_call(
        functools.partial(mixer_out_kernel, n),
        out_shape=(
            shape(n, rows, width, dtype=BF16),
            shape(rows, width),
            shape(rows, width, dtype=BF16),
        ),
        in_specs=[VM] * 5,
        out_specs=(ANY, VM, VM),
        scratch_shapes=Gather.scratch(n, rows, width)
        + [pltpu.SemaphoreType.DMA((n,))]
        + Scatter.scratch(n, rows, width),
        compiler_params=comm_params(2),
        cost_estimate=cost(2 * n * rows * width * mixture.shape[-1]),
        name="mixer_out",
    )(mixture, w_output, cotangent, tokens, gain)


def mlp_kernel(
    n, normed, cot_full, w_gelu, w_linear, w_down, hidden, g_first, g_second, grad_gelu, grad_linear, grad_down,
    full, sent, came, cot, keep_h, keep_f, keep_s, acc_g, acc_l, acc_d, stage_c, stage_w, saved, fetched, drained,
):
    g = Place(n)
    gather = Gather(g, full, sent, came)
    columns = w_gelu.shape[1]
    width = full.shape[2]
    tile = tile_of(columns, 256)
    wide = tile_of(width, 512)
    full[g.t] = normed[...]

    def fetch(t):
        return pltpu.make_async_copy(cot_full.at[t], cot.at[t], fetched.at[t])

    loop(n, lambda t: fetch(t).start())
    g.greet()
    gather.start()
    acc_g[...] = jnp.zeros_like(acc_g)
    acc_l[...] = jnp.zeros_like(acc_l)
    acc_d[...] = jnp.zeros_like(acc_d)

    def save(t, start):
        for q, (held, out) in enumerate(((keep_h, hidden), (keep_f, g_first), (keep_s, g_second))):
            copy = pltpu.make_async_copy(held.at[t], out.at[t], saved.at[t, q])
            copy.start() if start else copy.wait()

    def use(t):
        fetch(t).wait()

        def part(i):
            cols = span(i, tile)
            first = dot(full[t], w_gelu[:, cols])
            second = dot(full[t], w_linear[:, cols])
            back = dot_nt(cot[t], w_down[cols])
            value, slope = gelu_parts(first)
            keep_h[t, :, cols] = (value * second).astype(BF16)
            keep_f[t, :, cols] = (back * second * slope).astype(BF16)
            keep_s[t, :, cols] = (back * value).astype(BF16)

        loop(columns // tile, part)
        save(t, True)

        def part(i):
            at = span(i, wide)
            acc_g[at] += dot_tn(full[t, :, at], keep_f[t])
            acc_l[at] += dot_tn(full[t, :, at], keep_s[t])
            acc_d[:, at] += dot_tn(keep_h[t], cot[t, :, at])

        loop(width // wide, part)

    gather.each(0, use)

    def away(i):
        gather.forward(i + 1)
        gather.each(i + 1, use)

    loop(g.nz - 1, away)
    loop(n, lambda t: save(t, False))
    gather.finish()

    def drain(acc, stage, out, sem):
        part = stage.shape[1]

        def move(i):
            slot = lax.rem(i, 2)
            at = span(i, part)
            copy = pltpu.make_async_copy(stage.at[slot], out.at[at], sem.at[slot])
            pl.when(i >= 2)(copy.wait)
            stage[slot] = acc[at].astype(BF16)
            copy.start()

        count = acc.shape[0] // part
        loop(count, move)
        for slot in range(min(count, 2)):
            pltpu.make_async_copy(stage.at[slot], out.at[0:part], sem.at[slot]).wait()

    drain(acc_g, stage_c, grad_gelu, drained)
    drain(acc_l, stage_c, grad_linear, drained)
    drain(acc_d, stage_w, grad_down, drained)


def mlp(n, normed, cot_full, w_gelu, w_linear, w_down):
    rows, width = normed.shape
    columns = w_gelu.shape[1]
    kept = pltpu.VMEM((n, rows, columns), BF16)
    return pl.pallas_call(
        functools.partial(mlp_kernel, n),
        out_shape=(shape(n, rows, columns, dtype=BF16),) * 3
        + (shape(width, columns, dtype=BF16),) * 2
        + (shape(columns, width, dtype=BF16),),
        in_specs=[VM, ANY, VM, VM, VM],
        out_specs=(ANY,) * 6,
        scratch_shapes=Gather.scratch(n, rows, width)
        + [pltpu.VMEM((n, rows, width), BF16)]
        + [kept] * 3
        + [pltpu.VMEM((width, columns), F32)] * 2
        + [pltpu.VMEM((columns, width), F32)]
        + [pltpu.VMEM((2, tile_of(width, 128), columns), BF16)]
        + [pltpu.VMEM((2, tile_of(columns, 64), width), BF16)]
        + [pltpu.SemaphoreType.DMA((n, 3)), pltpu.SemaphoreType.DMA((n,)), pltpu.SemaphoreType.DMA((2,))],
        compiler_params=comm_params(3),
        cost_estimate=cost(12 * n * rows * width * columns),
        name="mlp",
    )(normed, cot_full, w_gelu, w_linear, w_down)


def mlp_back_kernel(n, g_first, g_second, w_gelu, w_linear, residual, cotangent, gain, g_residual, g_low, g_gain, *bufs):
    g = Place(n)

    def partial(t, cols):
        return dot_nt(g_first[t], w_gelu[cols]) + dot_nt(g_second[t], w_linear[cols])

    scatter = Scatter(g, partial, tile_of(residual.shape[1], 512), bufs)
    g.greet()
    scatter.offers(g.nz - 1)

    def around(i):
        d = g.nz - 1 - i
        scatter.offers(d - 1)
        scatter.step(d)

    loop(g.nz - 1, around)
    scatter.last()
    part = 32
    g_gain[...] = jnp.zeros_like(g_gain)

    def rows_of(i):
        at = span(i, part)
        back, terms = norm_grad(residual[at], gain[...].astype(F32), scatter.acc[at])
        value = cotangent[at].astype(F32) + back
        g_residual[at] = value
        g_low[at] = value.astype(BF16)
        g_gain[...] += jnp.sum(terms, axis=0, keepdims=True)

    loop(residual.shape[0] // part, rows_of)
    scatter.finish()


def mlp_back(n, g_first, g_second, w_gelu, w_linear, residual, cotangent, gain):
    rows, width = residual.shape
    return pl.pallas_call(
        functools.partial(mlp_back_kernel, n),
        out_shape=(shape(rows, width), shape(rows, width, dtype=BF16), shape(1, width)),
        in_specs=[VM] * 7,
        out_specs=(VM,) * 3,
        scratch_shapes=Scatter.scratch(n, rows, width),
        compiler_params=comm_params(4),
        cost_estimate=cost(4 * n * rows * width * w_gelu.shape[1]),
        name="mlp_back",
    )(g_first, g_second, w_gelu, w_linear, residual, cotangent, gain)


def down_kernel(
    n, hidden, w_down, residual, g_low, w_output, mixture, output, g_mixture, grad_output,
    full, sent, came, acc_o, *bufs
):
    g = Place(n)
    gather = Gather(g, full, sent, came)
    width = residual.shape[1]
    wide = tile_of(width, 512)
    scatter = Scatter(g, lambda t, cols: dot(hidden[t], w_down[:, cols]), wide, bufs)
    full[g.t] = g_low[...]
    g.greet()

    def use(t):
        g_mixture[t] = dot_nt(full[t], w_output[...])

        def part(i):
            at = span(i, wide)
            acc_o[:, at] += dot_tn(mixture[t], full[t, :, at])

        loop(width // wide, part)

    gather.start()
    acc_o[...] = jnp.zeros_like(acc_o)
    scatter.offers(g.nz - 1)

    def around(i):
        d = g.nz - 1 - i
        scatter.offers(d - 1)
        scatter.step(d)
        gather.each(i, use)
        gather.forward(i + 1)

    loop(g.nz - 1, around)
    gather.each(g.nz - 1, use)
    grad_output[...] = acc_o[...].astype(BF16)
    scatter.last()
    output[...] = (scatter.acc[...] + residual[...]).astype(BF16)
    scatter.finish()
    gather.finish()


def down(n, hidden, w_down, residual, g_low, w_output, mixture):
    rows, width = residual.shape
    channels = w_output.shape[0]
    return pl.pallas_call(
        functools.partial(down_kernel, n),
        out_shape=(
            shape(rows, width, dtype=BF16),
            shape(n, rows, channels),
            shape(channels, width, dtype=BF16),
        ),
        in_specs=[VM] * 6,
        out_specs=(VM,) * 3,
        scratch_shapes=Gather.scratch(n, rows, width)
        + [pltpu.VMEM((channels, width), F32)]
        + Scatter.scratch(n, rows, width),
        compiler_params=comm_params(5),
        cost_estimate=cost(2 * n * rows * width * (hidden.shape[-1] + 2 * channels)),
        name="down",
    )(hidden, w_down, residual, g_low, w_output, mixture)


def recur_back_kernel(
    g_mix, branch, states, states_before, u, u_before, conv_low, recall, ingate, start_state, start_conv,
    conv, gate_w, decay,
    g_recur, g_branch, small, g_gates,
    g_state, step_buf, root_buf, g_conv, pre_r, pre_i, carry, hist_s, hist_u, sums,
):
    sequence, back = pl.program_id(0), pl.program_id(1)
    last = pl.num_programs(1) - 1
    rows, channels = u.shape
    tile = 32

    @pl.when(jnp.logical_and(sequence == 0, back == 0))
    def _():
        sums[...] = jnp.zeros_like(sums)
        g_gates[...] = jnp.zeros_like(g_gates)

    @pl.when(back == 0)
    def _():
        carry[...] = jnp.zeros_like(carry)
        g_conv[rows : rows + 8] = jnp.zeros((8, channels), F32)

    @pl.when(back > 0)
    def _():
        g_conv[rows : rows + 8] = g_conv[0:8]

    @pl.when(back == last)
    def _():
        hist_s[0:8] = jnp.broadcast_to(start_state[0], (8, channels))
        hist_u[0:8] = jnp.concatenate([jnp.zeros((5, channels), F32), start_conv[0]], axis=0)

    @pl.when(back < last)
    def _():
        hist_s[0:8] = states_before[...]
        hist_u[0:8] = u_before[...]

    hist_s[8:] = states[...]
    hist_u[8:] = u[...]

    def first(i):
        at = span(i, tile)
        value, slope = gelu_parts(branch[at])
        gm = g_mix[at]
        g_state[at] = gm * value
        g_branch[at] = (gm * states[at] * slope).astype(BF16)
        log_decay = -8.0 * recall[at] * decay[...]
        step = jnp.exp(log_decay)
        step_buf[at] = step
        root_buf[at] = jnp.sqrt(one_minus_square(log_decay, step))

    loop(rows // tile, first)
    row = lax.broadcasted_iota(jnp.int32, (8, channels), 0)
    groups = rows // 32

    def scan(i, after):
        for part in range(4):
            at = pl.ds(pl.multiple_of((groups - 1 - i) * 32 + (3 - part) * 8, 8), 8)
            a, gs = step_buf[at], g_state[at]
            b = a * gs
            for shift in (1, 2, 4):
                inside = row < 8 - shift
                b = b + a * jnp.where(inside, pltpu.roll(b, 8 - shift, 0), 0.0)
                a = a * jnp.where(inside, pltpu.roll(a, 8 - shift, 0), 1.0)
            e = a * after + b
            g_state[at] = gs + jnp.where(row < 7, pltpu.roll(e, 7, 0), after)
            after = jnp.broadcast_to(e[0:1], (8, channels))
        return after

    carry[...] = lax.fori_loop(0, groups, scan, carry[...])

    def fold(x):
        return jnp.sum(x.reshape(tile // 8, 8, channels), axis=0)

    def second(i):
        at = span(i, tile)
        window = hist_s[pl.ds(pl.multiple_of(i * tile, tile), tile + 8)]
        before = window[7 : tile + 7]
        g, r, k = g_state[at], recall[at], ingate[at]
        c = conv_low[at].astype(F32)
        step, root = step_buf[at], root_buf[at]
        kc = k * c
        g_log = g * (before * step - kc * (step * step) / root)
        slow = -8.0 * r
        sums[7] += fold(g_log * slow)
        low_r = (g_log * (slow * decay[...]) * (1.0 - r)).astype(BF16)
        low_i = (g * root * kc * (1.0 - k)).astype(BF16)
        pre_r[at] = low_r
        pre_i[at] = low_i
        sums[5] += fold(low_r.astype(F32))
        sums[6] += fold(low_i.astype(F32))
        g_conv[at] = g * root * k

    loop(rows // tile, second)
    low_r, low_i, low_c = pre_r[...], pre_i[...], conv_low[...]
    g_gates[0] += dot_tn(low_c, low_r)
    g_gates[1] += dot_tn(low_c, low_i)
    g_conv[0:rows] += dot_nt(low_r, gate_w[0]) + dot_nt(low_i, gate_w[1])

    def third(i):
        at = span(i, tile)
        start = pl.multiple_of(i * tile, tile)
        window = g_conv[pl.ds(start, tile + 8)]
        value = conv[0:1] * window[0:tile]
        for k in (1, 2, 3):
            value = value + conv[k : k + 1] * window[k : tile + k]
        g_recur[at] = value.astype(BF16)
        past = hist_u[pl.ds(start, tile + 8)]
        gc = window[0:tile]
        for k in range(4):
            sums[k] += fold(gc * past[8 - k : tile + 8 - k])
        sums[4] += fold(gc)

    loop(rows // tile, third)

    @pl.when(jnp.logical_and(sequence == pl.num_programs(0) - 1, back == last))
    def _():
        small[...] = jnp.sum(sums[...], axis=1)


def recur_back(g_mix, branch, states, u, conv_low, recall, ingate, start_state, start_conv, conv, gate_w, decay):
    total, channels = u.shape
    sequences = start_state.shape[0]
    length = total // sequences
    rows = tile_of(length, 256)
    chunks = length // rows
    eights = rows // 8

    def at(s, c):
        return (s * chunks + chunks - 1 - c, 0)

    def earlier(s, c):
        return (jnp.maximum((s * chunks + chunks - 1 - c) * eights - 1, 0), 0)

    block = pl.BlockSpec((rows, channels), at)
    before = pl.BlockSpec((8, channels), earlier)

    def whole(x):
        return pl.BlockSpec(x.shape, lambda s, c: (0,) * x.ndim)

    wide = pltpu.VMEM((rows, channels), F32)
    narrow = pltpu.VMEM((rows, channels), BF16)
    long = pltpu.VMEM((rows + 8, channels), F32)
    return pl.pallas_call(
        recur_back_kernel,
        grid=(sequences, chunks),
        out_shape=(
            shape(total, channels, dtype=BF16),
            shape(total, channels, dtype=BF16),
            shape(8, channels),
            shape(2, channels, channels),
        ),
        in_specs=[
            block, block, block, before, block, before, block, block, block,
            pl.BlockSpec((1, 1, channels), lambda s, c: (s, 0, 0)),
            pl.BlockSpec((1, 3, channels), lambda s, c: (s, 0, 0)),
            whole(conv), whole(gate_w), whole(decay),
        ],
        out_specs=(
            block,
            block,
            pl.BlockSpec((8, channels), lambda s, c: (0, 0)),
            pl.BlockSpec((2, channels, channels), lambda s, c: (0, 0, 0)),
        ),
        scratch_shapes=[
            wide, wide, wide, long, narrow, narrow,
            pltpu.VMEM((8, channels), F32), long, long,
            pltpu.VMEM((8, 8, channels), F32),
        ],
        compiler_params=pltpu.CompilerParams(vmem_limit_bytes=VMEM_LIMIT),
        name="recur_back",
    )(g_mix, branch, states, states, u, u, conv_low, recall, ingate, start_state, start_conv, conv, gate_w, decay)


class Spread:
    def __init__(self, me, count, part, landed, summed, sems):
        self.me, self.count, self.part, self.landed, self.summed = me, count, part, landed, summed
        self.out_send, self.out_recv, self.back_send, self.back_recv = sems

    def others(self, act):
        loop(self.count, lambda i: pl.when(i != self.me)(lambda: act(i)))

    def out(self, i, slot):
        return pltpu.make_async_remote_copy(
            src_ref=self.part(i),
            dst_ref=self.landed.at[slot],
            send_sem=self.out_send.at[i],
            recv_sem=self.out_recv.at[slot],
            device_id={"dp": i},
            device_id_type=MESH,
        )

    def back(self, i, slot):
        return pltpu.make_async_remote_copy(
            src_ref=self.summed.at[slot],
            dst_ref=self.summed.at[slot],
            send_sem=self.back_send.at[i],
            recv_sem=self.back_recv.at[slot],
            device_id={"dp": i},
            device_id_type=MESH,
        )

    def start(self):
        self.others(lambda i: self.out(i, self.me).start())
        self.landed[self.me] = self.part(self.me)[...]

    def turn(self):
        self.others(lambda i: self.out(i, i).wait_recv())
        rows = self.landed.shape[1]
        tile = tile_of(rows, 32)

        def add(r):
            at = span(r, tile)
            value = self.landed[0, at].astype(F32)
            for i in range(1, self.count):
                value = value + self.landed[i, at].astype(F32)
            self.summed[self.me, at] = value.astype(BF16)

        loop(rows // tile, add)
        self.others(lambda i: self.back(i, self.me).start())

    def finish(self):
        self.others(lambda i: self.back(i, i).wait_recv())
        self.others(lambda i: self.out(i, i).wait_send())
        self.others(lambda i: self.back(i, self.me).wait_send())


def input_back_kernel(
    n, copies, g_recur, g_branch, w_in, w_br, normed, tokens, g_residual, gain, second_gain, g_gates, small,
    input_grad, pair_out, rest_out, gains_out,
    pair, pair_in, pair_all, rest, rest_in, rest_all, gain_row, gain_parts, gain_in, gain_sum, gain_dp,
    pair_sems, rest_sems, gain_sent, gain_came, gain_dp_sent, gain_dp_came, *bufs
):
    g = Place(n)
    me = lax.axis_index("dp")
    rows, width = tokens.shape
    channels = w_in.shape[0]
    part_width = width // copies
    padded = pair.shape[1] // 2
    gain_width = width // n

    def block(ref, t):
        return ref[span(t, rows)]

    def partial(t, cols):
        return dot(block(g_recur, t), w_in[:, cols]) + dot(block(g_branch, t), w_br[:, cols])

    scatter = Scatter(g, partial, tile_of(width, 512), bufs)
    pairs = Spread(me, copies, lambda i: pair.at[i], pair_in, pair_all, [pair_sems.at[q] for q in range(4)])
    rests = Spread(me, copies, lambda i: rest.at[i], rest_in, rest_all, [rest_sems.at[q] for q in range(4)])

    def gain_copy(t, slot):
        return g.copy(gain_parts.at[t], gain_in.at[slot], gain_sent.at[t], gain_came.at[slot], t)

    def gain_dp_copy(i, slot):
        return pltpu.make_async_remote_copy(
            src_ref=gain_sum,
            dst_ref=gain_dp.at[slot],
            send_sem=gain_dp_sent.at[i],
            recv_sem=gain_dp_came.at[slot],
            device_id={"dp": i},
            device_id_type=MESH,
        )

    def others(act):
        loop(n, lambda t: pl.when(t != g.t)(lambda: act(t)))

    barrier = pltpu.get_barrier_semaphore()
    others(
        lambda t: pl.semaphore_signal(barrier, inc=1, device_id={"tensor": t}, device_id_type=MESH)
    )
    pairs.others(
        lambda i: pl.semaphore_signal(barrier, inc=1, device_id={"dp": i}, device_id_type=MESH)
    )
    pl.semaphore_wait(barrier, n - 1 + copies - 1)

    scatter.offers(g.nz - 1)

    def around(i):
        d = g.nz - 1 - i
        scatter.offers(d - 1)
        scatter.step(d)

    pair[...] = jnp.zeros_like(pair)

    def weigh(q):
        cols = span(q, part_width)
        first = dot_tn(g_recur[...], normed[:, cols])
        pair[q, 0:channels] = first.astype(BF16)
        terms = jnp.sum(w_in[:, cols].astype(F32) * first, axis=0, keepdims=True)
        second = dot_tn(g_branch[...], normed[:, cols])
        pair[q, padded : padded + channels] = second.astype(BF16)
        terms += jnp.sum(w_br[:, cols].astype(F32) * second, axis=0, keepdims=True)
        gain_row[0:1, cols] = terms / gain[0:1, cols].astype(F32)

    loop(copies, weigh)
    pairs.start()
    gain_row[1:2] = second_gain[...]
    for t in range(n):
        gain_parts[t] = gain_row[:, t * gain_width : (t + 1) * gain_width]
    others(lambda t: gain_copy(t, g.t).start())
    gain_in[g.t] = gain_parts[g.t]

    flat = jnp.concatenate(
        [
            g_gates[0],
            g_gates[1],
            small[...],
            jnp.zeros((copies * rest.shape[1] - 2 * channels - 8, channels), F32),
        ],
        axis=0,
    ).astype(BF16)
    for i in range(copies):
        rest[i] = flat[i * rest.shape[1] : (i + 1) * rest.shape[1]]
    rests.start()

    loop(g.nz - 2, around)

    others(lambda t: gain_copy(t, t).wait_recv())
    total = gain_in[0]
    for t in range(1, n):
        total = total + gain_in[t]
    gain_sum[...] = total
    pairs.others(lambda i: gain_dp_copy(i, me).start())
    gain_dp[me] = total
    pairs.turn()
    rests.turn()

    around(g.nz - 2)
    scatter.last()
    part = 32

    def rows_of(i):
        at = span(i, part)
        back, _ = norm_grad(tokens[at].astype(F32), gain[...].astype(F32), scatter.acc[at])
        input_grad[at] = g_residual[at] + back

    loop(rows // part, rows_of)
    pairs.others(lambda i: gain_dp_copy(i, i).wait_recv())
    total = gain_dp[0]
    for i in range(1, copies):
        total = total + gain_dp[i]
    gains_out[...] = total
    pairs.finish()
    rests.finish()
    pair_out[...] = pair_all[...]
    rest_out[...] = rest_all[...]
    others(lambda t: gain_copy(t, t).wait_send())
    pairs.others(lambda i: gain_dp_copy(i, i).wait_send())
    scatter.finish()


def up_to(extent, multiple):
    return (extent + multiple - 1) // multiple * multiple


def input_back(n, copies, g_recur, g_branch, w_in, w_br, normed, tokens, g_residual, gain, second_gain, g_gates, small):
    rows, width = tokens.shape
    channels = w_in.shape[0]
    pair_shape = (copies, 2 * up_to(channels, 16), width // copies)
    rest_shape = (copies, up_to(2 * channels + 8, 16 * copies) // copies, channels)
    gain_shape = (8, width // n)
    sems = pltpu.SemaphoreType.DMA
    return pl.pallas_call(
        functools.partial(input_back_kernel, n, copies),
        out_shape=(
            shape(rows, width),
            shape(*pair_shape, dtype=BF16),
            shape(*rest_shape, dtype=BF16),
            shape(*gain_shape),
        ),
        in_specs=[VM] * 11,
        out_specs=(VM,) * 4,
        scratch_shapes=[pltpu.VMEM(pair_shape, BF16)] * 3
        + [pltpu.VMEM(rest_shape, BF16)] * 3
        + [
            pltpu.VMEM((8, width), F32),
            pltpu.VMEM((n, *gain_shape), F32),
            pltpu.VMEM((n, *gain_shape), F32),
            pltpu.VMEM(gain_shape, F32),
            pltpu.VMEM((copies, *gain_shape), F32),
            sems((4, copies)),
            sems((4, copies)),
            sems((n,)),
            sems((n,)),
            sems((copies,)),
            sems((copies,)),
        ]
        + Scatter.scratch(n, rows, width),
        compiler_params=comm_params(6),
        cost_estimate=cost(8 * n * rows * width * channels),
        name="input_back",
    )(g_recur, g_branch, w_in, w_br, normed, tokens, g_residual, gain, second_gain, g_gates, small)


def body(
    n,
    copies,
    tokens,
    cotangent,
    resets,
    init_state,
    init_conv,
    norm_gain,
    w_input,
    w_branch,
    conv_params,
    gate_weights,
    gate_bias,
    decay_rate,
    w_output,
    mlp_gain,
    w_gelu,
    w_linear,
    w_down,
):
    rows, width = tokens.shape
    total = rows * n
    channels = w_input.shape[1]
    blocks, block = gate_weights.shape[1], gate_weights.shape[2]
    survive = (1 - resets).astype(F32)
    start_state = (init_state * survive[:, None])[:, None]
    start_conv = init_conv * survive[:, None, None]
    gain_first, gain_second = norm_gain[None], mlp_gain[None]
    gate_w = (gate_weights[:, :, :, None] * jnp.eye(blocks, dtype=BF16)[None, :, None, :, None]).reshape(
        2, channels, channels
    )
    decay = decay_rate[None]
    w_in, w_br = w_input.T, w_branch.T

    def flat(x):
        return x.reshape(total, x.shape[-1])

    def blocked(x):
        return x.reshape(n, rows, x.shape[-1])

    normed, recur, branch = project(n, tokens, gain_first, w_in, w_br)
    recur, branch = flat(recur), flat(branch)
    states, mixture, conv_low, recall, ingate, final_state, final_conv = recur_forward(
        recur, branch, start_state, start_conv, conv_params, gate_w, gate_bias, decay
    )
    mixture = blocked(mixture)
    cot_full, residual, normed_mlp = mixer_out(n, mixture, w_output, cotangent, tokens, gain_second)
    hidden, g_first, g_second, grad_gelu, grad_linear, grad_down = mlp(
        n, normed_mlp, cot_full, w_gelu, w_linear, w_down
    )
    mlp_sums = lax.psum((grad_gelu, grad_linear, grad_down), "dp")
    g_residual, g_low, gain_second_grad = mlp_back(
        n, g_first, g_second, w_gelu, w_linear, residual, cotangent, gain_second
    )
    output, g_mixture, grad_output = down(n, hidden, w_down, residual, g_low, w_output, mixture)
    g_recur, g_branch, small, g_gates = recur_back(
        flat(g_mixture), branch, states, recur, conv_low, recall, ingate, start_state, start_conv,
        conv_params, gate_w, decay,
    )
    mlp_sums, grad_output = lax.optimization_barrier((mlp_sums, grad_output))
    output_sum = lax.psum(grad_output, "dp")
    input_grad, pair, rest, gains = input_back(
        n, copies, g_recur, g_branch, w_in, w_br, flat(normed), tokens, g_residual, gain_first,
        gain_second_grad, g_gates, small,
    )
    padded = pair.shape[1] // 2

    def whole(part):
        return part[:, :channels].astype(F32).transpose(1, 0, 2).reshape(channels, width).T

    rest = rest.astype(F32).reshape(-1, channels)
    gates = rest[: 2 * channels].reshape(2, blocks, block, blocks, block)
    gates = jnp.stack([gates[:, i, :, i] for i in range(blocks)], axis=1)
    small = rest[2 * channels : 2 * channels + 8]
    grad_gelu, grad_linear, grad_down = (x.astype(F32) for x in mlp_sums)
    grad_output = output_sum.astype(F32)
    return (
        output,
        input_grad,
        final_state[:, 0],
        final_conv,
        gains[0],
        whole(pair[:, :padded]),
        whole(pair[:, padded:]),
        small[:5],
        gates,
        small[5:7],
        small[7],
        grad_output,
        gains[1],
        grad_gelu,
        grad_linear,
        grad_down,
    )


def solution(mesh):
    in_specs = (
        P(("dp", "tensor"), None),
        P(("dp", "tensor"), None),
        P("dp"),
        P("dp", "tensor"),
        P("dp", None, "tensor"),
        P(),
        P(None, "tensor"),
        P(None, "tensor"),
        P(None, "tensor"),
        P(None, "tensor", None, None),
        P(None, "tensor"),
        P("tensor"),
        P("tensor", None),
        P(),
        P(None, "tensor"),
        P(None, "tensor"),
        P("tensor", None),
    )
    out_specs = (
        P(("dp", "tensor"), None),
        P(("dp", "tensor"), None),
        P("dp", "tensor"),
        P("dp", None, "tensor"),
        P("tensor"),
        P(None, "tensor"),
        P(None, "tensor"),
        P(None, "tensor"),
        P(None, "tensor", None, None),
        P(None, "tensor"),
        P("tensor"),
        P("tensor", None),
        P("tensor"),
        P(None, "tensor"),
        P(None, "tensor"),
        P("tensor", None),
    )
    return jax.shard_map(
        functools.partial(body, mesh.shape["tensor"], mesh.shape["dp"]),
        mesh=mesh,
        in_specs=in_specs,
        out_specs=out_specs,
        check_vma=False,
    )
```

```python
import functools

import jax
import jax.numpy as jnp
from jax import lax
from jax.experimental import pallas as pl
from jax.experimental.pallas import tpu as pltpu
from jax.sharding import PartitionSpec as P

EPSILON = 1e-06
KAPPA = 0.7978845608028654
CUBIC = 0.044715
PIECES = 2
F32 = jnp.float32
BF16 = jnp.bfloat16
ANY = pl.BlockSpec(memory_space=pl.ANY)
VM = pl.BlockSpec(memory_space=pltpu.VMEM)
VMEM_LIMIT = 61 * 1024 * 1024
MESH = pl.DeviceIdType.MESH


def dot(a, b):
    return jnp.dot(a, b, preferred_element_type=F32)


def dot_nt(a, b):
    return lax.dot_general(a, b, (((1,), (1,)), ((), ())), preferred_element_type=F32)


def dot_tn(a, b):
    return lax.dot_general(a, b, (((0,), (0,)), ((), ())), preferred_element_type=F32)


def tile_of(extent, wanted):
    while extent % wanted:
        wanted //= 2
    return wanted


def span(i, size):
    return pl.ds(pl.multiple_of(i * size, size), size)


def loop(count, body):
    def step(i, carry):
        body(i)
        return carry

    lax.fori_loop(0, count, step, 0)


class Place:
    def __init__(self, n):
        self.n = n
        self.nz = n // 2
        self.t = lax.axis_index("tensor")
        self.c = lax.rem(self.t, 2)
        self.j = lax.div(self.t, 2)
        self.sib = self.t + 1 - 2 * self.c
        self.has_up = self.j < self.nz - 1
        self.has_down = self.j > 0

    def greet(self):
        barrier = pltpu.get_barrier_semaphore()

        def signal(t):
            pl.semaphore_signal(barrier, inc=1, device_id={"tensor": t}, device_id_type=MESH)

        signal(self.sib)
        pl.when(self.has_up)(lambda: signal(self.t + 2))
        pl.when(self.has_down)(lambda: signal(self.t - 2))
        pl.semaphore_wait(
            barrier, 1 + self.has_up.astype(jnp.int32) + self.has_down.astype(jnp.int32)
        )

    def copy(self, src, dst, send, recv, t):
        return pltpu.make_async_remote_copy(
            src_ref=src,
            dst_ref=dst,
            send_sem=send,
            recv_sem=recv,
            device_id={"tensor": t},
            device_id_type=MESH,
        )


class Gather:
    def __init__(self, place, full, sent, came):
        self.place, self.full, self.sent, self.came = place, full, sent, came
        self.pieces = came.shape[1]
        self.size = full.shape[1] // self.pieces

    @staticmethod
    def scratch(n, rows, width):
        return [
            pltpu.VMEM((n, rows, width), BF16),
            pltpu.SemaphoreType.DMA((n, PIECES, 3)),
            pltpu.SemaphoreType.DMA((n, PIECES)),
        ]

    def copy(self, t, p, way, to):
        piece = self.full.at[t, pl.ds(p * self.size, self.size)]
        return self.place.copy(piece, piece, self.sent.at[t, p, way], self.came.at[t, p], to)

    def start(self):
        g = self.place
        for p in range(self.pieces):
            pl.when(g.has_up)(lambda: self.copy(g.t, p, 0, g.t + 2).start())
            pl.when(g.has_down)(lambda: self.copy(g.t, p, 1, g.t - 2).start())
        for p in range(self.pieces):
            self.copy(g.t, p, 2, g.sib).start()

    def forward(self, d, pieces=None):
        g = self.place
        for p in range(self.pieces) if pieces is None else pieces:

            @pl.when(g.j - d >= 0)
            def _():
                t = g.t - 2 * d
                self.copy(t, p, 0, g.sib).wait_recv()
                pl.when(g.has_up)(lambda: self.copy(t, p, 0, g.t + 2).start())
                self.copy(t, p, 2, g.sib).start()

            @pl.when(g.j + d < g.nz)
            def _():
                t = g.t + 2 * d
                self.copy(t, p, 1, g.sib).wait_recv()
                pl.when(g.has_down)(lambda: self.copy(t, p, 1, g.t - 2).start())
                self.copy(t, p, 2, g.sib).start()

    def each(self, d, use):
        g = self.place

        def visit(q):
            core, way = lax.div(q, 2), 2 * lax.rem(q, 2) - 1
            j = g.j + way * d
            there = jnp.logical_and(j >= 0, j < g.nz)

            @pl.when(jnp.logical_and(there, jnp.logical_or(d > 0, way > 0)))
            def _():
                t = 2 * j + lax.rem(g.c + core, 2)

                @pl.when(core > 0)
                def _():
                    for p in range(self.pieces):
                        self.copy(t, p, 2, g.sib).wait_recv()

                use(t)

        loop(4, visit)

    def finish(self):
        g = self.place

        def done(t):
            for p in range(self.pieces):
                self.copy(t, p, 2, g.sib).wait_send()

                @pl.when(jnp.logical_and(t <= g.t, g.has_up))
                def _():
                    self.copy(t, p, 0, g.sib).wait_send()

                @pl.when(jnp.logical_and(t >= g.t, g.has_down))
                def _():
                    self.copy(t, p, 1, g.sib).wait_send()

        loop(g.nz, lambda k: done(2 * k + g.c))


class Scatter:
    def __init__(self, place, partial, tile, bufs):
        self.place, self.partial, self.tile = place, partial, tile
        self.to_sib, self.from_sib, self.line, self.out, self.acc = bufs[:5]
        self.sib_send, self.sib_recv, self.line_send, self.line_recv = bufs[5:]
        self.tiles = self.acc.shape[1] // tile

    @staticmethod
    def scratch(n, rows, width):
        nz = n // 2
        return [
            pltpu.VMEM((nz, rows, width), BF16),
            pltpu.VMEM((nz, rows, width), BF16),
            pltpu.VMEM((nz + 1, rows, width), BF16),
            pltpu.VMEM((nz, rows, width), BF16),
            pltpu.VMEM((rows, width), F32),
            pltpu.SemaphoreType.DMA((nz,)),
            pltpu.SemaphoreType.DMA((nz,)),
            pltpu.SemaphoreType.DMA((nz,)),
            pltpu.SemaphoreType.DMA((nz + 1,)),
        ]

    def sib_copy(self, k):
        return self.place.copy(
            self.to_sib.at[k],
            self.from_sib.at[k],
            self.sib_send.at[k],
            self.sib_recv.at[k],
            self.place.sib,
        )

    def line_copy(self, k, slot, to):
        return self.place.copy(
            self.out.at[k], self.line.at[slot], self.line_send.at[k], self.line_recv.at[slot], to
        )

    def offer(self, k):
        t = 2 * k + 1 - self.place.c

        def part(i):
            cols = span(i, self.tile)
            self.to_sib[k, :, cols] = self.partial(t, cols).astype(BF16)

        loop(self.tiles, part)
        self.sib_copy(k).start()

    def pair(self, k):
        self.sib_copy(k).wait_recv()
        t = 2 * k + self.place.c

        def part(i):
            cols = span(i, self.tile)
            self.acc[:, cols] = self.partial(t, cols) + self.from_sib[k, :, cols].astype(F32)

        loop(self.tiles, part)

    def offers(self, d):
        g = self.place

        def way_of(w):
            k = g.j + (1 - 2 * w) * d

            @pl.when(jnp.logical_and(jnp.logical_and(k >= 0, k < g.nz), jnp.logical_or(d > 0, w == 0)))
            def _():
                self.offer(k)

        loop(2, way_of)

    def step(self, d):
        g = self.place

        def way_of(w):
            sign = 1 - 2 * w
            k = g.j + sign * d

            @pl.when(jnp.logical_and(k >= 0, k < g.nz))
            def _():
                self.pair(k)
                upstream = g.j - sign
                more = jnp.logical_and(upstream >= 0, upstream < g.nz)

                @pl.when(more)
                def _():
                    self.line_copy(k, k, g.sib).wait_recv()
                    self.out[k] = (self.acc[...] + self.line[k].astype(F32)).astype(BF16)

                @pl.when(jnp.logical_not(more))
                def _():
                    self.out[k] = self.acc[...].astype(BF16)

                slot = jnp.where(jnp.logical_and(d == 1, w == 1), g.nz, k)
                self.line_copy(k, slot, g.t + 2 * sign).start()

        loop(2, way_of)

    def last(self):
        g = self.place
        self.pair(g.j)

        @pl.when(g.has_down)
        def _():
            self.line_copy(g.j, g.j, g.sib).wait_recv()
            self.acc[...] += self.line[g.j].astype(F32)

        @pl.when(g.has_up)
        def _():
            self.line_copy(g.j, g.nz, g.sib).wait_recv()
            self.acc[...] += self.line[g.nz].astype(F32)

    def finish(self):
        g = self.place

        def done(k):
            self.sib_copy(k).wait_send()
            pl.when(g.j != k)(lambda: self.line_copy(k, k, g.sib).wait_send())

        loop(g.nz, done)


def comm_params(collective_id):
    return pltpu.CompilerParams(
        collective_id=collective_id, has_side_effects=True, vmem_limit_bytes=VMEM_LIMIT
    )


def cost(flops):
    return pl.CostEstimate(flops=int(flops), bytes_accessed=200_000_000, transcendentals=0)


def shape(*dims, dtype=F32):
    return jax.ShapeDtypeStruct(dims, dtype)


def inv_rms(values):
    return lax.rsqrt(jnp.mean(values * values, axis=-1, keepdims=True) + EPSILON)


def norm_grad(values, gain, gradient):
    inv = inv_rms(values)
    unit = values * inv
    scaled = gradient * gain
    centred = jnp.mean(scaled * unit, axis=-1, keepdims=True)
    return inv * (scaled - unit * centred), gradient * unit


def sigmoid(v):
    return 1.0 / (1.0 + jnp.exp(-v))


def gelu_parts(v):
    square = v * v
    bend = jnp.tanh(KAPPA * v * (1.0 + CUBIC * square))
    half = 0.5 * (1.0 + bend)
    slope = half + 0.5 * v * (1.0 - bend * bend) * (KAPPA * (1.0 + 3.0 * CUBIC * square))
    return v * half, slope


def one_minus_square(log_decay, decay):
    m = -2.0 * log_decay
    series = m * (
        1.0 - m * (1 / 2) * (1.0 - m * (1 / 3) * (1.0 - m * (1 / 4) * (1.0 - m * (1 / 5) * (1.0 - m * (1 / 6)))))
    )
    return jnp.where(m < 0.35, series, 1.0 - decay * decay)


def project_kernel(n, tokens, gain, w_in, w_br, normed, recur, branch, full, sent, came, held_a, held_b, saved):
    g = Place(n)
    gather = Gather(g, full, sent, came)
    part = 64

    def normalize(i):
        at = span(i, part)
        values = tokens[at].astype(F32)
        full[g.t, at] = (values * inv_rms(values) * gain[...].astype(F32)).astype(BF16)

    loop(full.shape[1] // part, normalize)
    g.greet()
    gather.start()

    def use(t):
        pltpu.make_async_copy(full.at[t], normed.at[t], saved.at[t, 0]).start()
        held_a[t] = dot_nt(full[t], w_in[...])
        held_b[t] = dot_nt(full[t], w_br[...])
        pltpu.make_async_copy(held_a.at[t], recur.at[t], saved.at[t, 1]).start()
        pltpu.make_async_copy(held_b.at[t], branch.at[t], saved.at[t, 2]).start()

    gather.each(0, use)

    def away(i):
        gather.forward(i + 1)
        gather.each(i + 1, use)

    loop(g.nz - 1, away)

    def done(t):
        pltpu.make_async_copy(full.at[t], normed.at[t], saved.at[t, 0]).wait()
        pltpu.make_async_copy(held_a.at[t], recur.at[t], saved.at[t, 1]).wait()
        pltpu.make_async_copy(held_b.at[t], branch.at[t], saved.at[t, 2]).wait()

    loop(n, done)
    gather.finish()


def project(n, tokens, gain, w_in, w_br):
    rows, width = tokens.shape
    channels = w_in.shape[0]
    return pl.pallas_call(
        functools.partial(project_kernel, n),
        out_shape=(
            shape(n, rows, width, dtype=BF16),
            shape(n, rows, channels),
            shape(n, rows, channels),
        ),
        in_specs=[VM] * 4,
        out_specs=(ANY,) * 3,
        scratch_shapes=Gather.scratch(n, rows, width)
        + [pltpu.VMEM((n, rows, channels), F32)] * 2
        + [pltpu.SemaphoreType.DMA((n, 3))],
        compiler_params=comm_params(1),
        cost_estimate=cost(4 * n * rows * width * channels),
        name="project",
    )(tokens, gain, w_in, w_br)


def recur_kernel(
    u, branch, start_state, start_conv, conv, gate_w, bias, decay,
    states, mixture, conv_low, recall, ingate, final_state, final_conv,
    hist, decay_buf, drive_buf, carry,
):
    chunk = pl.program_id(1)
    rows, channels = u.shape
    tile = 32

    @pl.when(chunk == 0)
    def _():
        carry[...] = jnp.broadcast_to(start_state[0], (8, channels))
        hist[0:8] = jnp.concatenate([jnp.zeros((5, channels), F32), start_conv[0]], axis=0)

    @pl.when(chunk > 0)
    def _():
        hist[0:8] = hist[rows : rows + 8]

    hist[8:] = u[...]

    def convolve(i):
        window = hist[pl.ds(pl.multiple_of(i * tile, tile), tile + 8)]
        value = conv[4:5] + conv[0:1] * window[8:] + conv[1:2] * window[7 : tile + 7]
        value = value + conv[2:3] * window[6 : tile + 6] + conv[3:4] * window[5 : tile + 5]
        conv_low[span(i, tile)] = value.astype(BF16)

    loop(rows // tile, convolve)
    low = conv_low[...]
    recall[...] = dot(low, gate_w[0])
    ingate[...] = dot(low, gate_w[1])

    def gates(i):
        at = span(i, tile)
        r = sigmoid(recall[at] + bias[0:1])
        k = sigmoid(ingate[at] + bias[1:2])
        recall[at] = r
        ingate[at] = k
        log_decay = -8.0 * r * decay[...]
        step = jnp.exp(log_decay)
        decay_buf[at] = step
        drive_buf[at] = jnp.sqrt(one_minus_square(log_decay, step)) * k * conv_low[at].astype(F32)

    loop(rows // tile, gates)
    row = lax.broadcasted_iota(jnp.int32, (8, channels), 0)

    def scan(i, before):
        for part in range(4):
            at = pl.ds(pl.multiple_of(i * 32 + part * 8, 8), 8)
            a, b = decay_buf[at], drive_buf[at]
            for shift in (1, 2, 4):
                inside = row >= shift
                b = b + a * jnp.where(inside, pltpu.roll(b, shift, 0), 0.0)
                a = a * jnp.where(inside, pltpu.roll(a, shift, 0), 1.0)
            h = a * before + b
            states[at] = h
            before = jnp.broadcast_to(h[7:8], (8, channels))
        return before

    carry[...] = lax.fori_loop(0, rows // 32, scan, carry[...])

    def mix(i):
        at = span(i, tile)
        value, _ = gelu_parts(branch[at])
        mixture[at] = (states[at] * value).astype(BF16)

    loop(rows // tile, mix)

    @pl.when(chunk == pl.num_programs(1) - 1)
    def _():
        final_state[0] = carry[0:1]
        final_conv[0] = hist[rows + 5 : rows + 8]


def recur_forward(u, branch, start_state, start_conv, conv, gate_w, bias, decay):
    total, channels = u.shape
    sequences = start_state.shape[0]
    length = total // sequences
    rows = tile_of(length, 256)
    chunks = length // rows
    block = pl.BlockSpec((rows, channels), lambda s, c: (s * chunks + c, 0))

    def whole(x):
        return pl.BlockSpec(x.shape, lambda s, c: (0,) * x.ndim)

    return pl.pallas_call(
        recur_kernel,
        grid=(sequences, chunks),
        out_shape=(
            shape(total, channels),
            shape(total, channels, dtype=BF16),
            shape(total, channels, dtype=BF16),
            shape(total, channels),
            shape(total, channels),
            shape(sequences, 1, channels),
            shape(sequences, 3, channels),
        ),
        in_specs=[
            block,
            block,
            pl.BlockSpec((1, 1, channels), lambda s, c: (s, 0, 0)),
            pl.BlockSpec((1, 3, channels), lambda s, c: (s, 0, 0)),
            whole(conv),
            whole(gate_w),
            whole(bias),
            whole(decay),
        ],
        out_specs=(block,) * 5
        + (
            pl.BlockSpec((1, 1, channels), lambda s, c: (s, 0, 0)),
            pl.BlockSpec((1, 3, channels), lambda s, c: (s, 0, 0)),
        ),
        scratch_shapes=[
            pltpu.VMEM((rows + 8, channels), F32),
            pltpu.VMEM((rows, channels), F32),
            pltpu.VMEM((rows, channels), F32),
            pltpu.VMEM((8, channels), F32),
        ],
        compiler_params=pltpu.CompilerParams(vmem_limit_bytes=VMEM_LIMIT),
        name="recur_forward",
    )(u, branch, start_state, start_conv, conv, gate_w, bias, decay)


def mixer_out_kernel(
    n, mixture, w_output, cotangent, tokens, gain, cot_full, residual, normed,
    full, sent, came, saved, *bufs
):
    g = Place(n)
    gather = Gather(g, full, sent, came)
    scatter = Scatter(g, lambda t, cols: dot(mixture[t], w_output[:, cols]), tile_of(residual.shape[1], 512), bufs)
    full[g.t] = cotangent[...]
    g.greet()

    def use(t):
        pltpu.make_async_copy(full.at[t], cot_full.at[t], saved.at[t]).start()

    scatter.offers(g.nz - 1)
    gather.start()

    def around(i):
        d = g.nz - 1 - i
        scatter.offers(d - 1)
        scatter.step(d)
        gather.each(i, use)
        gather.forward(i + 1)

    loop(g.nz - 1, around)
    scatter.last()
    part = 64

    def rows_of(i):
        at = span(i, part)
        values = scatter.acc[at] + tokens[at].astype(F32)
        residual[at] = values
        normed[at] = (values * inv_rms(values) * gain[...].astype(F32)).astype(BF16)

    loop(residual.shape[0] // part, rows_of)
    gather.each(g.nz - 1, use)
    loop(n, lambda t: pltpu.make_async_copy(full.at[t], cot_full.at[t], saved.at[t]).wait())
    scatter.finish()
    gather.finish()


def mixer_out(n, mixture, w_output, cotangent, tokens, gain):
    rows, width = tokens.shape
    return pl.pallas_call(
        functools.partial(mixer_out_kernel, n),
        out_shape=(
            shape(n, rows, width, dtype=BF16),
            shape(rows, width),
            shape(rows, width, dtype=BF16),
        ),
        in_specs=[VM] * 5,
        out_specs=(ANY, VM, VM),
        scratch_shapes=Gather.scratch(n, rows, width)
        + [pltpu.SemaphoreType.DMA((n,))]
        + Scatter.scratch(n, rows, width),
        compiler_params=comm_params(2),
        cost_estimate=cost(2 * n * rows * width * mixture.shape[-1]),
        name="mixer_out",
    )(mixture, w_output, cotangent, tokens, gain)


PARTS = 8


def mlp_kernel(
    n, normed, cot_full, w_gelu, w_linear, w_down, residual, cotangent, gain,
    hidden, grad_gelu, grad_linear, grad_down, g_residual, g_low, g_gain,
    full, sent, came, cot, keep_h, keep_f, keep_s, acc_g, acc_l, acc_d,
    to_sib, sums, line, acc, saved, fetched, drained, sib_sent, sib_came, line_sent, line_came,
):
    g = Place(n)
    gather = Gather(g, full, sent, came)
    columns = w_gelu.shape[1]
    rows, width = acc.shape
    tile = tile_of(columns, 256)
    wide = tile_of(width, 512)
    strip = rows // PARTS
    full[g.t] = normed[...]
    g.greet()
    gather.start()
    acc_g[...] = jnp.zeros_like(acc_g)
    acc_l[...] = jnp.zeros_like(acc_l)
    acc_d[...] = jnp.zeros_like(acc_d)

    def fetch(t, q):
        return pltpu.make_async_copy(cot_full.at[t], cot.at[q], fetched.at[q])

    def save(t, q):
        return pltpu.make_async_copy(keep_h.at[q], hidden.at[t], saved.at[q])

    def layer(t, q):
        fetch(t, q).wait()

        def part(i):
            cols = span(i, tile)
            first = dot(full[t], w_gelu[:, cols])
            second = dot(full[t], w_linear[:, cols])
            back = dot_nt(cot[q], w_down[cols])
            value, slope = gelu_parts(first)
            keep_h[q, :, cols] = (value * second).astype(BF16)
            keep_f[q, :, cols] = (back * second * slope).astype(BF16)
            keep_s[q, :, cols] = (back * value).astype(BF16)

        loop(columns // tile, part)
        save(t, q).start()

    def partial(q, cols):
        return dot_nt(keep_f[q], w_gelu[cols]) + dot_nt(keep_s[q], w_linear[cols])

    def sib_copy(k):
        return g.copy(to_sib, sums.at[k], sib_sent, sib_came.at[k], g.sib)

    def line_copy(k, slot, p, to):
        at = pl.ds(pl.multiple_of(p * strip, strip), strip)
        return g.copy(
            sums.at[k, at], line.at[slot, at], line_sent.at[k, p], line_came.at[slot, p], to
        )

    def chip(d, way):
        k = g.j + way * d
        mine, its = g.c, 1 - g.c
        own, other = 2 * k + mine, 2 * k + its
        fetch(other, its).start()
        fetch(own, mine).start()
        for p in range(gather.pieces):
            gather.copy(other, p, 2, g.sib).wait_recv()
        layer(other, its)

        def offer(i):
            cols = span(i, wide)
            to_sib[:, cols] = partial(its, cols).astype(BF16)

        loop(width // wide, offer)
        sib_copy(k).start()
        layer(own, mine)
        sib_copy(k).wait()

        @pl.when(d == 0)
        def _():
            def part(i):
                cols = span(i, wide)
                acc[:, cols] = partial(mine, cols) + sums[k, :, cols].astype(F32)

            loop(width // wide, part)

        @pl.when(d > 0)
        def _():
            def part(i):
                cols = span(i, wide)
                sums[k, :, cols] = (partial(mine, cols) + sums[k, :, cols].astype(F32)).astype(BF16)

            loop(width // wide, part)
            first = jnp.logical_or(
                jnp.logical_and(way > 0, jnp.logical_not(g.has_down)),
                jnp.logical_and(way < 0, jnp.logical_not(g.has_up)),
            )

            @pl.when(first)
            def _():
                slot = jnp.where(jnp.logical_and(way < 0, d == 1), g.nz, k)
                for p in range(PARTS):
                    line_copy(k, slot, p, g.t + 2 * way).start()

        def part(i):
            at = span(i, wide)
            both = full[pl.ds(2 * k, 2), :, at].reshape(2 * rows, wide)
            acc_g[at] += dot_tn(both, keep_f[...].reshape(2 * rows, columns))
            acc_l[at] += dot_tn(both, keep_s[...].reshape(2 * rows, columns))
            acc_d[:, at] += dot_tn(
                keep_h[...].reshape(2 * rows, columns), cot[:, :, at].reshape(2 * rows, wide)
            )

        loop(width // wide, part)
        save(other, its).wait()
        save(own, mine).wait()

    def relay(m):
        def take(k, slot, sign, p):
            at = pl.ds(pl.multiple_of(p * strip, strip), strip)
            line_copy(k, slot, p, g.sib).wait_recv()

            @pl.when(k == g.j)
            def _():
                acc[at] += line[slot, at].astype(F32)

            @pl.when(k != g.j)
            def _():
                sums[k, at] = (sums[k, at].astype(F32) + line[slot, at].astype(F32)).astype(BF16)
                there = jnp.where(jnp.logical_and(sign < 0, k == g.j - 1), g.nz, k)
                line_copy(k, there, p, g.t + 2 * sign).start()

        def rise(p):
            pl.when(jnp.logical_and(g.has_down, m >= g.j))(lambda: take(m, m, 1, p))

        def fall(p):
            k = g.nz - 1 - m
            pl.when(jnp.logical_and(g.has_up, k <= g.j))(
                lambda: take(k, jnp.where(k == g.j, g.nz, k), -1, p)
            )

        lower = 2 * g.j < g.nz

        def strips(i):
            @pl.when(i < PARTS)
            def _():
                pl.when(lower)(lambda: rise(i))
                pl.when(jnp.logical_not(lower))(lambda: fall(i))

            @pl.when(i > 0)
            def _():
                pl.when(lower)(lambda: fall(i - 1))
                pl.when(jnp.logical_not(lower))(lambda: rise(i - 1))

        loop(PARTS + 1, strips)

    def step(d):
        up, down = g.j + d < g.nz, g.j - d >= 0

        def way_of(w):
            both = jnp.logical_and(up, down)
            way = jnp.where(jnp.logical_and(w == 0, up), 1, -1)
            wanted = jnp.where(w == 0, jnp.logical_or(up, down), jnp.logical_and(both, d > 0))
            pl.when(wanted)(lambda: chip(d, way))

            @pl.when(d < g.nz - 1)
            def _():
                for p in range(gather.pieces):
                    pl.when(w == min(p, 1))(lambda: gather.forward(d + 1, (p,)))

        loop(2, way_of)
        pl.when(d > 1)(lambda: relay(d - 1))

    loop(g.nz, step)
    gather.finish()

    stages = [held.at[q] for held in (keep_h, keep_f, keep_s) for q in (0, 1)]
    leaving = []

    def leave(i, value, out):
        slot = i % len(stages)
        if len(leaving) >= len(stages):
            leaving[i - len(stages)].wait()
        stages[slot][...] = value.astype(BF16)
        copy = pltpu.make_async_copy(stages[slot], out, drained.at[slot])
        copy.start()
        leaving.append(copy)

    count = width // rows
    for i in range(count):
        at = pl.ds(i * rows, rows)
        leave(2 * i, acc_g[at], grad_gelu.at[at])
        leave(2 * i + 1, acc_l[at], grad_linear.at[at])
    wider = []
    for i in range(columns // rows):
        at = pl.ds(i * rows, rows)
        full[i] = acc_d[at].astype(BF16)
        wider.append(pltpu.make_async_copy(full.at[i], grad_down.at[at], drained.at[len(stages) + i]))
        wider[-1].start()
    relay(g.nz - 1)
    lines = 32
    g_gain[...] = jnp.zeros_like(g_gain)

    def rows_of(i):
        at = span(i, lines)
        back, terms = norm_grad(residual[at], gain[...].astype(F32), acc[at])
        value = cotangent[at].astype(F32) + back
        g_residual[at] = value
        g_low[at] = value.astype(BF16)
        g_gain[...] += jnp.sum(terms, axis=0, keepdims=True)

    loop(rows // lines, rows_of)
    for copy in leaving[-len(stages):] + wider:
        copy.wait()

    def done(k):
        @pl.when(k != g.j)
        def _():
            for p in range(PARTS):
                line_copy(k, k, p, g.sib).wait_send()

    loop(g.nz, done)


def mlp(n, normed, cot_full, w_gelu, w_linear, w_down, residual, cotangent, gain):
    rows, width = normed.shape
    columns = w_gelu.shape[1]
    kept = pltpu.VMEM((2, rows, columns), BF16)
    sems = pltpu.SemaphoreType.DMA
    return pl.pallas_call(
        functools.partial(mlp_kernel, n),
        out_shape=(shape(n, rows, columns, dtype=BF16),)
        + (shape(width, columns, dtype=BF16),) * 2
        + (
            shape(columns, width, dtype=BF16),
            shape(rows, width),
            shape(rows, width, dtype=BF16),
            shape(1, width),
        ),
        in_specs=[VM, ANY] + [VM] * 6,
        out_specs=(ANY,) * 4 + (VM,) * 3,
        scratch_shapes=Gather.scratch(n, rows, width)
        + [pltpu.VMEM((2, rows, width), BF16)]
        + [kept] * 3
        + [pltpu.VMEM((width, columns), F32)] * 2
        + [
            pltpu.VMEM((columns, width), F32),
            pltpu.VMEM((rows, width), BF16),
            pltpu.VMEM((n // 2, rows, width), BF16),
            pltpu.VMEM((n // 2 + 1, rows, width), BF16),
            pltpu.VMEM((rows, width), F32),
            sems((2,)),
            sems((2,)),
            sems((6 + columns // rows,)),
            sems,
            sems((n // 2,)),
            sems((n // 2, PARTS)),
            sems((n // 2 + 1, PARTS)),
        ],
        compiler_params=comm_params(3),
        cost_estimate=cost(16 * n * rows * width * columns),
        name="mlp",
    )(normed, cot_full, w_gelu, w_linear, w_down, residual, cotangent, gain)


def down_kernel(
    n, hidden, w_down, residual, g_low, w_output, mixture, output, g_mixture, grad_output,
    full, sent, came, acc_o, *bufs
):
    g = Place(n)
    gather = Gather(g, full, sent, came)
    width = residual.shape[1]
    wide = tile_of(width, 512)
    scatter = Scatter(g, lambda t, cols: dot(hidden[t], w_down[:, cols]), wide, bufs)
    full[g.t] = g_low[...]
    g.greet()

    def use(t):
        g_mixture[t] = dot_nt(full[t], w_output[...])

        def part(i):
            at = span(i, wide)
            acc_o[:, at] += dot_tn(mixture[t], full[t, :, at])

        loop(width // wide, part)

    gather.start()
    acc_o[...] = jnp.zeros_like(acc_o)
    scatter.offers(g.nz - 1)

    def around(i):
        d = g.nz - 1 - i
        scatter.offers(d - 1)
        scatter.step(d)
        gather.each(i, use)
        gather.forward(i + 1)

    loop(g.nz - 1, around)
    gather.each(g.nz - 1, use)
    grad_output[...] = acc_o[...].astype(BF16)
    scatter.last()
    output[...] = (scatter.acc[...] + residual[...]).astype(BF16)
    scatter.finish()
    gather.finish()


def down(n, hidden, w_down, residual, g_low, w_output, mixture):
    rows, width = residual.shape
    channels = w_output.shape[0]
    return pl.pallas_call(
        functools.partial(down_kernel, n),
        out_shape=(
            shape(rows, width, dtype=BF16),
            shape(n, rows, channels),
            shape(channels, width, dtype=BF16),
        ),
        in_specs=[VM] * 6,
        out_specs=(VM,) * 3,
        scratch_shapes=Gather.scratch(n, rows, width)
        + [pltpu.VMEM((channels, width), F32)]
        + Scatter.scratch(n, rows, width),
        compiler_params=comm_params(5),
        cost_estimate=cost(2 * n * rows * width * (hidden.shape[-1] + 2 * channels)),
        name="down",
    )(hidden, w_down, residual, g_low, w_output, mixture)


def recur_back_kernel(
    g_mix, branch, states, states_before, u, u_before, conv_low, recall, ingate, start_state, start_conv,
    conv, gate_w, decay,
    g_recur, g_branch, small, g_gates,
    g_state, step_buf, root_buf, g_conv, pre_r, pre_i, carry, hist_s, hist_u, sums,
):
    sequence, back = pl.program_id(0), pl.program_id(1)
    last = pl.num_programs(1) - 1
    rows, channels = u.shape
    tile = 32

    @pl.when(jnp.logical_and(sequence == 0, back == 0))
    def _():
        sums[...] = jnp.zeros_like(sums)
        g_gates[...] = jnp.zeros_like(g_gates)

    @pl.when(back == 0)
    def _():
        carry[...] = jnp.zeros_like(carry)
        g_conv[rows : rows + 8] = jnp.zeros((8, channels), F32)

    @pl.when(back > 0)
    def _():
        g_conv[rows : rows + 8] = g_conv[0:8]

    @pl.when(back == last)
    def _():
        hist_s[0:8] = jnp.broadcast_to(start_state[0], (8, channels))
        hist_u[0:8] = jnp.concatenate([jnp.zeros((5, channels), F32), start_conv[0]], axis=0)

    @pl.when(back < last)
    def _():
        hist_s[0:8] = states_before[...]
        hist_u[0:8] = u_before[...]

    hist_s[8:] = states[...]
    hist_u[8:] = u[...]

    def first(i):
        at = span(i, tile)
        value, slope = gelu_parts(branch[at])
        gm = g_mix[at]
        g_state[at] = gm * value
        g_branch[at] = (gm * states[at] * slope).astype(BF16)
        log_decay = -8.0 * recall[at] * decay[...]
        step = jnp.exp(log_decay)
        step_buf[at] = step
        root_buf[at] = jnp.sqrt(one_minus_square(log_decay, step))

    loop(rows // tile, first)
    row = lax.broadcasted_iota(jnp.int32, (8, channels), 0)
    groups = rows // 32

    def scan(i, after):
        for part in range(4):
            at = pl.ds(pl.multiple_of((groups - 1 - i) * 32 + (3 - part) * 8, 8), 8)
            a, gs = step_buf[at], g_state[at]
            b = a * gs
            for shift in (1, 2, 4):
                inside = row < 8 - shift
                b = b + a * jnp.where(inside, pltpu.roll(b, 8 - shift, 0), 0.0)
                a = a * jnp.where(inside, pltpu.roll(a, 8 - shift, 0), 1.0)
            e = a * after + b
            g_state[at] = gs + jnp.where(row < 7, pltpu.roll(e, 7, 0), after)
            after = jnp.broadcast_to(e[0:1], (8, channels))
        return after

    carry[...] = lax.fori_loop(0, groups, scan, carry[...])

    def fold(x):
        return jnp.sum(x.reshape(tile // 8, 8, channels), axis=0)

    def second(i):
        at = span(i, tile)
        window = hist_s[pl.ds(pl.multiple_of(i * tile, tile), tile + 8)]
        before = window[7 : tile + 7]
        g, r, k = g_state[at], recall[at], ingate[at]
        c = conv_low[at].astype(F32)
        step, root = step_buf[at], root_buf[at]
        kc = k * c
        g_log = g * (before * step - kc * (step * step) / root)
        slow = -8.0 * r
        sums[7] += fold(g_log * slow)
        low_r = (g_log * (slow * decay[...]) * (1.0 - r)).astype(BF16)
        low_i = (g * root * kc * (1.0 - k)).astype(BF16)
        pre_r[at] = low_r
        pre_i[at] = low_i
        sums[5] += fold(low_r.astype(F32))
        sums[6] += fold(low_i.astype(F32))
        g_conv[at] = g * root * k

    loop(rows // tile, second)
    low_r, low_i, low_c = pre_r[...], pre_i[...], conv_low[...]
    g_gates[0] += dot_tn(low_c, low_r)
    g_gates[1] += dot_tn(low_c, low_i)
    g_conv[0:rows] += dot_nt(low_r, gate_w[0]) + dot_nt(low_i, gate_w[1])

    def third(i):
        at = span(i, tile)
        start = pl.multiple_of(i * tile, tile)
        window = g_conv[pl.ds(start, tile + 8)]
        value = conv[0:1] * window[0:tile]
        for k in (1, 2, 3):
            value = value + conv[k : k + 1] * window[k : tile + k]
        g_recur[at] = value.astype(BF16)
        past = hist_u[pl.ds(start, tile + 8)]
        gc = window[0:tile]
        for k in range(4):
            sums[k] += fold(gc * past[8 - k : tile + 8 - k])
        sums[4] += fold(gc)

    loop(rows // tile, third)

    @pl.when(jnp.logical_and(sequence == pl.num_programs(0) - 1, back == last))
    def _():
        small[...] = jnp.sum(sums[...], axis=1)


def recur_back(g_mix, branch, states, u, conv_low, recall, ingate, start_state, start_conv, conv, gate_w, decay):
    total, channels = u.shape
    sequences = start_state.shape[0]
    length = total // sequences
    rows = tile_of(length, 256)
    chunks = length // rows
    eights = rows // 8

    def at(s, c):
        return (s * chunks + chunks - 1 - c, 0)

    def earlier(s, c):
        return (jnp.maximum((s * chunks + chunks - 1 - c) * eights - 1, 0), 0)

    block = pl.BlockSpec((rows, channels), at)
    before = pl.BlockSpec((8, channels), earlier)

    def whole(x):
        return pl.BlockSpec(x.shape, lambda s, c: (0,) * x.ndim)

    wide = pltpu.VMEM((rows, channels), F32)
    narrow = pltpu.VMEM((rows, channels), BF16)
    long = pltpu.VMEM((rows + 8, channels), F32)
    return pl.pallas_call(
        recur_back_kernel,
        grid=(sequences, chunks),
        out_shape=(
            shape(total, channels, dtype=BF16),
            shape(total, channels, dtype=BF16),
            shape(8, channels),
            shape(2, channels, channels),
        ),
        in_specs=[
            block, block, block, before, block, before, block, block, block,
            pl.BlockSpec((1, 1, channels), lambda s, c: (s, 0, 0)),
            pl.BlockSpec((1, 3, channels), lambda s, c: (s, 0, 0)),
            whole(conv), whole(gate_w), whole(decay),
        ],
        out_specs=(
            block,
            block,
            pl.BlockSpec((8, channels), lambda s, c: (0, 0)),
            pl.BlockSpec((2, channels, channels), lambda s, c: (0, 0, 0)),
        ),
        scratch_shapes=[
            wide, wide, wide, long, narrow, narrow,
            pltpu.VMEM((8, channels), F32), long, long,
            pltpu.VMEM((8, 8, channels), F32),
        ],
        compiler_params=pltpu.CompilerParams(vmem_limit_bytes=VMEM_LIMIT),
        name="recur_back",
    )(g_mix, branch, states, states, u, u, conv_low, recall, ingate, start_state, start_conv, conv, gate_w, decay)


class Spread:
    def __init__(self, me, count, part, landed, summed, sems):
        self.me, self.count, self.part, self.landed, self.summed = me, count, part, landed, summed
        self.out_send, self.out_recv, self.back_send, self.back_recv = sems

    def others(self, act):
        loop(self.count, lambda i: pl.when(i != self.me)(lambda: act(i)))

    def out(self, i, slot):
        return pltpu.make_async_remote_copy(
            src_ref=self.part(i),
            dst_ref=self.landed.at[slot],
            send_sem=self.out_send.at[i],
            recv_sem=self.out_recv.at[slot],
            device_id={"dp": i},
            device_id_type=MESH,
        )

    def back(self, i, slot):
        return pltpu.make_async_remote_copy(
            src_ref=self.summed.at[slot],
            dst_ref=self.summed.at[slot],
            send_sem=self.back_send.at[i],
            recv_sem=self.back_recv.at[slot],
            device_id={"dp": i},
            device_id_type=MESH,
        )

    def start(self):
        self.others(lambda i: self.out(i, self.me).start())
        self.landed[self.me] = self.part(self.me)[...]

    def turn(self):
        self.others(lambda i: self.out(i, i).wait_recv())
        rows = self.landed.shape[1]
        tile = tile_of(rows, 32)

        def add(r):
            at = span(r, tile)
            value = self.landed[0, at].astype(F32)
            for i in range(1, self.count):
                value = value + self.landed[i, at].astype(F32)
            self.summed[self.me, at] = value.astype(BF16)

        loop(rows // tile, add)
        self.others(lambda i: self.back(i, self.me).start())

    def finish(self):
        self.others(lambda i: self.back(i, i).wait_recv())
        self.others(lambda i: self.out(i, i).wait_send())
        self.others(lambda i: self.back(i, self.me).wait_send())


def input_back_kernel(
    n, copies, g_recur, g_branch, w_in, w_br, normed, tokens, g_residual, gain, second_gain, g_gates, small,
    input_grad, pair_out, rest_out, gains_out,
    pair, pair_in, pair_all, rest, rest_in, rest_all, gain_row, gain_parts, gain_in, gain_sum, gain_dp,
    pair_sems, rest_sems, gain_sent, gain_came, gain_dp_sent, gain_dp_came, *bufs
):
    g = Place(n)
    me = lax.axis_index("dp")
    rows, width = tokens.shape
    channels = w_in.shape[0]
    part_width = width // copies
    padded = pair.shape[1] // 2
    gain_width = width // n

    def block(ref, t):
        return ref[span(t, rows)]

    def partial(t, cols):
        return dot(block(g_recur, t), w_in[:, cols]) + dot(block(g_branch, t), w_br[:, cols])

    scatter = Scatter(g, partial, tile_of(width, 512), bufs)
    pairs = Spread(me, copies, lambda i: pair.at[i], pair_in, pair_all, [pair_sems.at[q] for q in range(4)])
    rests = Spread(me, copies, lambda i: rest.at[i], rest_in, rest_all, [rest_sems.at[q] for q in range(4)])

    def gain_copy(t, slot):
        return g.copy(gain_parts.at[t], gain_in.at[slot], gain_sent.at[t], gain_came.at[slot], t)

    def gain_dp_copy(i, slot):
        return pltpu.make_async_remote_copy(
            src_ref=gain_sum,
            dst_ref=gain_dp.at[slot],
            send_sem=gain_dp_sent.at[i],
            recv_sem=gain_dp_came.at[slot],
            device_id={"dp": i},
            device_id_type=MESH,
        )

    def others(act):
        loop(n, lambda t: pl.when(t != g.t)(lambda: act(t)))

    barrier = pltpu.get_barrier_semaphore()
    others(
        lambda t: pl.semaphore_signal(barrier, inc=1, device_id={"tensor": t}, device_id_type=MESH)
    )
    pairs.others(
        lambda i: pl.semaphore_signal(barrier, inc=1, device_id={"dp": i}, device_id_type=MESH)
    )
    pl.semaphore_wait(barrier, n - 1 + copies - 1)

    scatter.offers(g.nz - 1)

    def around(i):
        d = g.nz - 1 - i
        scatter.offers(d - 1)
        scatter.step(d)

    pair[...] = jnp.zeros_like(pair)

    def weigh(q):
        cols = span(q, part_width)
        first = dot_tn(g_recur[...], normed[:, cols])
        pair[q, 0:channels] = first.astype(BF16)
        terms = jnp.sum(w_in[:, cols].astype(F32) * first, axis=0, keepdims=True)
        second = dot_tn(g_branch[...], normed[:, cols])
        pair[q, padded : padded + channels] = second.astype(BF16)
        terms += jnp.sum(w_br[:, cols].astype(F32) * second, axis=0, keepdims=True)
        gain_row[0:1, cols] = terms / gain[0:1, cols].astype(F32)

    loop(copies, weigh)
    pairs.start()
    gain_row[1:2] = second_gain[...]
    for t in range(n):
        gain_parts[t] = gain_row[:, t * gain_width : (t + 1) * gain_width]
    others(lambda t: gain_copy(t, g.t).start())
    gain_in[g.t] = gain_parts[g.t]

    flat = jnp.concatenate(
        [
            g_gates[0],
            g_gates[1],
            small[...],
            jnp.zeros((copies * rest.shape[1] - 2 * channels - 8, channels), F32),
        ],
        axis=0,
    ).astype(BF16)
    for i in range(copies):
        rest[i] = flat[i * rest.shape[1] : (i + 1) * rest.shape[1]]
    rests.start()

    loop(g.nz - 2, around)

    others(lambda t: gain_copy(t, t).wait_recv())
    total = gain_in[0]
    for t in range(1, n):
        total = total + gain_in[t]
    gain_sum[...] = total
    pairs.others(lambda i: gain_dp_copy(i, me).start())
    gain_dp[me] = total
    pairs.turn()
    rests.turn()

    around(g.nz - 2)
    scatter.last()
    part = 32

    def rows_of(i):
        at = span(i, part)
        back, _ = norm_grad(tokens[at].astype(F32), gain[...].astype(F32), scatter.acc[at])
        input_grad[at] = g_residual[at] + back

    loop(rows // part, rows_of)
    pairs.others(lambda i: gain_dp_copy(i, i).wait_recv())
    total = gain_dp[0]
    for i in range(1, copies):
        total = total + gain_dp[i]
    gains_out[...] = total
    pairs.finish()
    rests.finish()
    pair_out[...] = pair_all[...]
    rest_out[...] = rest_all[...]
    others(lambda t: gain_copy(t, t).wait_send())
    pairs.others(lambda i: gain_dp_copy(i, i).wait_send())
    scatter.finish()


def up_to(extent, multiple):
    return (extent + multiple - 1) // multiple * multiple


def input_back(n, copies, g_recur, g_branch, w_in, w_br, normed, tokens, g_residual, gain, second_gain, g_gates, small):
    rows, width = tokens.shape
    channels = w_in.shape[0]
    pair_shape = (copies, 2 * up_to(channels, 16), width // copies)
    rest_shape = (copies, up_to(2 * channels + 8, 16 * copies) // copies, channels)
    gain_shape = (8, width // n)
    sems = pltpu.SemaphoreType.DMA
    return pl.pallas_call(
        functools.partial(input_back_kernel, n, copies),
        out_shape=(
            shape(rows, width),
            shape(*pair_shape, dtype=BF16),
            shape(*rest_shape, dtype=BF16),
            shape(*gain_shape),
        ),
        in_specs=[VM] * 11,
        out_specs=(VM,) * 4,
        scratch_shapes=[pltpu.VMEM(pair_shape, BF16)] * 3
        + [pltpu.VMEM(rest_shape, BF16)] * 3
        + [
            pltpu.VMEM((8, width), F32),
            pltpu.VMEM((n, *gain_shape), F32),
            pltpu.VMEM((n, *gain_shape), F32),
            pltpu.VMEM(gain_shape, F32),
            pltpu.VMEM((copies, *gain_shape), F32),
            sems((4, copies)),
            sems((4, copies)),
            sems((n,)),
            sems((n,)),
            sems((copies,)),
            sems((copies,)),
        ]
        + Scatter.scratch(n, rows, width),
        compiler_params=comm_params(6),
        cost_estimate=cost(8 * n * rows * width * channels),
        name="input_back",
    )(g_recur, g_branch, w_in, w_br, normed, tokens, g_residual, gain, second_gain, g_gates, small)


def body(
    n,
    copies,
    tokens,
    cotangent,
    resets,
    init_state,
    init_conv,
    norm_gain,
    w_input,
    w_branch,
    conv_params,
    gate_weights,
    gate_bias,
    decay_rate,
    w_output,
    mlp_gain,
    w_gelu,
    w_linear,
    w_down,
):
    rows, width = tokens.shape
    total = rows * n
    channels = w_input.shape[1]
    blocks, block = gate_weights.shape[1], gate_weights.shape[2]
    survive = (1 - resets).astype(F32)
    start_state = (init_state * survive[:, None])[:, None]
    start_conv = init_conv * survive[:, None, None]
    gain_first, gain_second = norm_gain[None], mlp_gain[None]
    gate_w = (gate_weights[:, :, :, None] * jnp.eye(blocks, dtype=BF16)[None, :, None, :, None]).reshape(
        2, channels, channels
    )
    decay = decay_rate[None]
    w_in, w_br = w_input.T, w_branch.T

    def flat(x):
        return x.reshape(total, x.shape[-1])

    def blocked(x):
        return x.reshape(n, rows, x.shape[-1])

    normed, recur, branch = project(n, tokens, gain_first, w_in, w_br)
    recur, branch = flat(recur), flat(branch)
    states, mixture, conv_low, recall, ingate, final_state, final_conv = recur_forward(
        recur, branch, start_state, start_conv, conv_params, gate_w, gate_bias, decay
    )
    mixture = blocked(mixture)
    cot_full, residual, normed_mlp = mixer_out(n, mixture, w_output, cotangent, tokens, gain_second)
    hidden, grad_gelu, grad_linear, grad_down, g_residual, g_low, gain_second_grad = mlp(
        n, normed_mlp, cot_full, w_gelu, w_linear, w_down, residual, cotangent, gain_second
    )
    mlp_sums = lax.psum((grad_gelu, grad_linear, grad_down), "dp")
    output, g_mixture, grad_output = down(n, hidden, w_down, residual, g_low, w_output, mixture)
    g_recur, g_branch, small, g_gates = recur_back(
        flat(g_mixture), branch, states, recur, conv_low, recall, ingate, start_state, start_conv,
        conv_params, gate_w, decay,
    )
    mlp_sums, grad_output = lax.optimization_barrier((mlp_sums, grad_output))
    output_sum = lax.psum(grad_output, "dp")
    input_grad, pair, rest, gains = input_back(
        n, copies, g_recur, g_branch, w_in, w_br, flat(normed), tokens, g_residual, gain_first,
        gain_second_grad, g_gates, small,
    )
    padded = pair.shape[1] // 2

    def whole(part):
        return part[:, :channels].astype(F32).transpose(1, 0, 2).reshape(channels, width).T

    rest = rest.astype(F32).reshape(-1, channels)
    gates = rest[: 2 * channels].reshape(2, blocks, block, blocks, block)
    gates = jnp.stack([gates[:, i, :, i] for i in range(blocks)], axis=1)
    small = rest[2 * channels : 2 * channels + 8]
    grad_gelu, grad_linear, grad_down = (x.astype(F32) for x in mlp_sums)
    grad_output = output_sum.astype(F32)
    return (
        output,
        input_grad,
        final_state[:, 0],
        final_conv,
        gains[0],
        whole(pair[:, :padded]),
        whole(pair[:, padded:]),
        small[:5],
        gates,
        small[5:7],
        small[7],
        grad_output,
        gains[1],
        grad_gelu,
        grad_linear,
        grad_down,
    )


def solution(mesh):
    in_specs = (
        P(("dp", "tensor"), None),
        P(("dp", "tensor"), None),
        P("dp"),
        P("dp", "tensor"),
        P("dp", None, "tensor"),
        P(),
        P(None, "tensor"),
        P(None, "tensor"),
        P(None, "tensor"),
        P(None, "tensor", None, None),
        P(None, "tensor"),
        P("tensor"),
        P("tensor", None),
        P(),
        P(None, "tensor"),
        P(None, "tensor"),
        P("tensor", None),
    )
    out_specs = (
        P(("dp", "tensor"), None),
        P(("dp", "tensor"), None),
        P("dp", "tensor"),
        P("dp", None, "tensor"),
        P("tensor"),
        P(None, "tensor"),
        P(None, "tensor"),
        P(None, "tensor"),
        P(None, "tensor", None, None),
        P(None, "tensor"),
        P("tensor"),
        P("tensor", None),
        P("tensor"),
        P(None, "tensor"),
        P(None, "tensor"),
        P("tensor", None),
    )
    return jax.shard_map(
        functools.partial(body, mesh.shape["tensor"], mesh.shape["dp"]),
        mesh=mesh,
        in_specs=in_specs,
        out_specs=out_specs,
        check_vma=False,
    )
```

```python
import functools

import jax
import jax.numpy as jnp
from jax import lax
from jax.experimental import pallas as pl
from jax.experimental.pallas import tpu as pltpu
from jax.sharding import PartitionSpec as P

EPSILON = 1e-06
KAPPA = 0.7978845608028654
CUBIC = 0.044715
PIECES = 2
F32 = jnp.float32
BF16 = jnp.bfloat16
ANY = pl.BlockSpec(memory_space=pl.ANY)
VM = pl.BlockSpec(memory_space=pltpu.VMEM)
VMEM_LIMIT = 61 * 1024 * 1024
MESH = pl.DeviceIdType.MESH


def dot(a, b):
    return jnp.dot(a, b, preferred_element_type=F32)


def dot_nt(a, b):
    return lax.dot_general(a, b, (((1,), (1,)), ((), ())), preferred_element_type=F32)


def dot_tn(a, b):
    return lax.dot_general(a, b, (((0,), (0,)), ((), ())), preferred_element_type=F32)


def tile_of(extent, wanted):
    while extent % wanted:
        wanted //= 2
    return wanted


def span(i, size):
    return pl.ds(pl.multiple_of(i * size, size), size)


def loop(count, body):
    def step(i, carry):
        body(i)
        return carry

    lax.fori_loop(0, count, step, 0)


class Place:
    def __init__(self, n):
        self.n = n
        self.nz = n // 2
        self.t = lax.axis_index("tensor")
        self.c = lax.rem(self.t, 2)
        self.j = lax.div(self.t, 2)
        self.sib = self.t + 1 - 2 * self.c
        self.has_up = self.j < self.nz - 1
        self.has_down = self.j > 0

    def greet(self):
        barrier = pltpu.get_barrier_semaphore()

        def signal(t):
            pl.semaphore_signal(barrier, inc=1, device_id={"tensor": t}, device_id_type=MESH)

        signal(self.sib)
        pl.when(self.has_up)(lambda: signal(self.t + 2))
        pl.when(self.has_down)(lambda: signal(self.t - 2))
        pl.semaphore_wait(
            barrier, 1 + self.has_up.astype(jnp.int32) + self.has_down.astype(jnp.int32)
        )

    def copy(self, src, dst, send, recv, t):
        return pltpu.make_async_remote_copy(
            src_ref=src,
            dst_ref=dst,
            send_sem=send,
            recv_sem=recv,
            device_id={"tensor": t},
            device_id_type=MESH,
        )


class Gather:
    def __init__(self, place, full, sent, came):
        self.place, self.full, self.sent, self.came = place, full, sent, came
        self.pieces = came.shape[1]
        self.size = full.shape[1] // self.pieces

    @staticmethod
    def scratch(n, rows, width):
        return [
            pltpu.VMEM((n, rows, width), BF16),
            pltpu.SemaphoreType.DMA((n, PIECES, 3)),
            pltpu.SemaphoreType.DMA((n, PIECES)),
        ]

    def copy(self, t, p, way, to):
        piece = self.full.at[t, pl.ds(p * self.size, self.size)]
        return self.place.copy(piece, piece, self.sent.at[t, p, way], self.came.at[t, p], to)

    def start(self):
        g = self.place
        for p in range(self.pieces):
            pl.when(g.has_up)(lambda: self.copy(g.t, p, 0, g.t + 2).start())
            pl.when(g.has_down)(lambda: self.copy(g.t, p, 1, g.t - 2).start())
        for p in range(self.pieces):
            self.copy(g.t, p, 2, g.sib).start()

    def forward(self, d, pieces=None):
        g = self.place
        for p in range(self.pieces) if pieces is None else pieces:

            @pl.when(g.j - d >= 0)
            def _():
                t = g.t - 2 * d
                self.copy(t, p, 0, g.sib).wait_recv()
                pl.when(g.has_up)(lambda: self.copy(t, p, 0, g.t + 2).start())
                self.copy(t, p, 2, g.sib).start()

            @pl.when(g.j + d < g.nz)
            def _():
                t = g.t + 2 * d
                self.copy(t, p, 1, g.sib).wait_recv()
                pl.when(g.has_down)(lambda: self.copy(t, p, 1, g.t - 2).start())
                self.copy(t, p, 2, g.sib).start()

    def each(self, d, use):
        g = self.place

        def visit(q):
            core, way = lax.div(q, 2), 2 * lax.rem(q, 2) - 1
            j = g.j + way * d
            there = jnp.logical_and(j >= 0, j < g.nz)

            @pl.when(jnp.logical_and(there, jnp.logical_or(d > 0, way > 0)))
            def _():
                t = 2 * j + lax.rem(g.c + core, 2)

                @pl.when(core > 0)
                def _():
                    for p in range(self.pieces):
                        self.copy(t, p, 2, g.sib).wait_recv()

                use(t)

        loop(4, visit)

    def finish(self):
        g = self.place

        def done(t):
            for p in range(self.pieces):
                self.copy(t, p, 2, g.sib).wait_send()

                @pl.when(jnp.logical_and(t <= g.t, g.has_up))
                def _():
                    self.copy(t, p, 0, g.sib).wait_send()

                @pl.when(jnp.logical_and(t >= g.t, g.has_down))
                def _():
                    self.copy(t, p, 1, g.sib).wait_send()

        loop(g.nz, lambda k: done(2 * k + g.c))


class Scatter:
    def __init__(self, place, partial, tile, bufs):
        self.place, self.partial, self.tile = place, partial, tile
        self.to_sib, self.from_sib, self.line, self.acc = bufs[:4]
        self.sib_send, self.sib_recv, self.line_send, self.line_recv = bufs[4:]
        self.out = self.from_sib
        self.tiles = self.acc.shape[1] // tile

    @staticmethod
    def scratch(n, rows, width):
        nz = n // 2
        return [
            pltpu.VMEM((nz, rows, width), BF16),
            pltpu.VMEM((nz, rows, width), BF16),
            pltpu.VMEM((nz + 1, rows, width), BF16),
            pltpu.VMEM((rows, width), F32),
            pltpu.SemaphoreType.DMA((nz,)),
            pltpu.SemaphoreType.DMA((nz,)),
            pltpu.SemaphoreType.DMA((nz,)),
            pltpu.SemaphoreType.DMA((nz + 1,)),
        ]

    def sib_copy(self, k):
        return self.place.copy(
            self.to_sib.at[k],
            self.from_sib.at[k],
            self.sib_send.at[k],
            self.sib_recv.at[k],
            self.place.sib,
        )

    def line_copy(self, k, slot, to):
        return self.place.copy(
            self.out.at[k], self.line.at[slot], self.line_send.at[k], self.line_recv.at[slot], to
        )

    def offer(self, k):
        t = 2 * k + 1 - self.place.c

        def part(i):
            cols = span(i, self.tile)
            self.to_sib[k, :, cols] = self.partial(t, cols).astype(BF16)

        loop(self.tiles, part)
        self.sib_copy(k).start()

    def pair(self, k):
        self.sib_copy(k).wait_recv()
        t = 2 * k + self.place.c

        def part(i):
            cols = span(i, self.tile)
            self.acc[:, cols] = self.partial(t, cols) + self.from_sib[k, :, cols].astype(F32)

        loop(self.tiles, part)

    def offers(self, d):
        g = self.place

        def way_of(w):
            k = g.j + (1 - 2 * w) * d

            @pl.when(jnp.logical_and(jnp.logical_and(k >= 0, k < g.nz), jnp.logical_or(d > 0, w == 0)))
            def _():
                self.offer(k)

        loop(2, way_of)

    def step(self, d):
        g = self.place

        def way_of(w):
            sign = 1 - 2 * w
            k = g.j + sign * d

            @pl.when(jnp.logical_and(k >= 0, k < g.nz))
            def _():
                self.pair(k)
                upstream = g.j - sign
                more = jnp.logical_and(upstream >= 0, upstream < g.nz)

                @pl.when(more)
                def _():
                    self.line_copy(k, k, g.sib).wait_recv()
                    self.out[k] = (self.acc[...] + self.line[k].astype(F32)).astype(BF16)

                @pl.when(jnp.logical_not(more))
                def _():
                    self.out[k] = self.acc[...].astype(BF16)

                slot = jnp.where(jnp.logical_and(d == 1, w == 1), g.nz, k)
                self.line_copy(k, slot, g.t + 2 * sign).start()

        loop(2, way_of)

    def last(self):
        g = self.place
        self.pair(g.j)

        @pl.when(g.has_down)
        def _():
            self.line_copy(g.j, g.j, g.sib).wait_recv()
            self.acc[...] += self.line[g.j].astype(F32)

        @pl.when(g.has_up)
        def _():
            self.line_copy(g.j, g.nz, g.sib).wait_recv()
            self.acc[...] += self.line[g.nz].astype(F32)

    def finish(self):
        g = self.place

        def done(k):
            self.sib_copy(k).wait_send()
            pl.when(g.j != k)(lambda: self.line_copy(k, k, g.sib).wait_send())

        loop(g.nz, done)


def comm_params(collective_id):
    return pltpu.CompilerParams(
        collective_id=collective_id, has_side_effects=True, vmem_limit_bytes=VMEM_LIMIT
    )


def cost(flops):
    return pl.CostEstimate(flops=int(flops), bytes_accessed=200_000_000, transcendentals=0)


def shape(*dims, dtype=F32):
    return jax.ShapeDtypeStruct(dims, dtype)


def inv_rms(values):
    return lax.rsqrt(jnp.mean(values * values, axis=-1, keepdims=True) + EPSILON)


def norm_grad(values, gain, gradient):
    inv = inv_rms(values)
    unit = values * inv
    scaled = gradient * gain
    centred = jnp.mean(scaled * unit, axis=-1, keepdims=True)
    return inv * (scaled - unit * centred), gradient * unit


def sigmoid(v):
    return 1.0 / (1.0 + jnp.exp(-v))


def gelu_parts(v):
    square = v * v
    bend = jnp.tanh(KAPPA * v * (1.0 + CUBIC * square))
    half = 0.5 * (1.0 + bend)
    slope = half + 0.5 * v * (1.0 - bend * bend) * (KAPPA * (1.0 + 3.0 * CUBIC * square))
    return v * half, slope


def one_minus_square(log_decay, decay):
    m = -2.0 * log_decay
    series = m * (
        1.0 - m * (1 / 2) * (1.0 - m * (1 / 3) * (1.0 - m * (1 / 4) * (1.0 - m * (1 / 5) * (1.0 - m * (1 / 6)))))
    )
    return jnp.where(m < 0.35, series, 1.0 - decay * decay)


def project_kernel(n, tokens, gain, w_in, w_br, normed, recur, branch, full, sent, came, held_a, held_b, saved):
    g = Place(n)
    gather = Gather(g, full, sent, came)
    part = 64

    def normalize(i):
        at = span(i, part)
        values = tokens[at].astype(F32)
        full[g.t, at] = (values * inv_rms(values) * gain[...].astype(F32)).astype(BF16)

    loop(full.shape[1] // part, normalize)
    g.greet()
    gather.start()

    def use(t):
        pltpu.make_async_copy(full.at[t], normed.at[t], saved.at[t, 0]).start()
        held_a[t] = dot_nt(full[t], w_in[...])
        held_b[t] = dot_nt(full[t], w_br[...])
        pltpu.make_async_copy(held_a.at[t], recur.at[t], saved.at[t, 1]).start()
        pltpu.make_async_copy(held_b.at[t], branch.at[t], saved.at[t, 2]).start()

    gather.each(0, use)

    def away(i):
        gather.forward(i + 1)
        gather.each(i + 1, use)

    loop(g.nz - 1, away)

    def done(t):
        pltpu.make_async_copy(full.at[t], normed.at[t], saved.at[t, 0]).wait()
        pltpu.make_async_copy(held_a.at[t], recur.at[t], saved.at[t, 1]).wait()
        pltpu.make_async_copy(held_b.at[t], branch.at[t], saved.at[t, 2]).wait()

    loop(n, done)
    gather.finish()


def project(n, tokens, gain, w_in, w_br):
    rows, width = tokens.shape
    channels = w_in.shape[0]
    return pl.pallas_call(
        functools.partial(project_kernel, n),
        out_shape=(
            shape(n, rows, width, dtype=BF16),
            shape(n, rows, channels),
            shape(n, rows, channels),
        ),
        in_specs=[VM] * 4,
        out_specs=(ANY,) * 3,
        scratch_shapes=Gather.scratch(n, rows, width)
        + [pltpu.VMEM((n, rows, channels), F32)] * 2
        + [pltpu.SemaphoreType.DMA((n, 3))],
        compiler_params=comm_params(1),
        cost_estimate=cost(4 * n * rows * width * channels),
        name="project",
    )(tokens, gain, w_in, w_br)


def recur_kernel(
    u, branch, start_state, start_conv, conv, gate_w, bias, decay,
    states, mixture, conv_low, recall, ingate, final_state, final_conv,
    hist, decay_buf, drive_buf, carry,
):
    chunk = pl.program_id(1)
    rows, channels = u.shape
    tile = 32

    @pl.when(chunk == 0)
    def _():
        carry[...] = jnp.broadcast_to(start_state[0], (8, channels))
        hist[0:8] = jnp.concatenate([jnp.zeros((5, channels), F32), start_conv[0]], axis=0)

    @pl.when(chunk > 0)
    def _():
        hist[0:8] = hist[rows : rows + 8]

    hist[8:] = u[...]

    def convolve(i):
        window = hist[pl.ds(pl.multiple_of(i * tile, tile), tile + 8)]
        value = conv[4:5] + conv[0:1] * window[8:] + conv[1:2] * window[7 : tile + 7]
        value = value + conv[2:3] * window[6 : tile + 6] + conv[3:4] * window[5 : tile + 5]
        conv_low[span(i, tile)] = value.astype(BF16)

    loop(rows // tile, convolve)
    low = conv_low[...]
    recall[...] = dot(low, gate_w[0])
    ingate[...] = dot(low, gate_w[1])

    def gates(i):
        at = span(i, tile)
        r = sigmoid(recall[at] + bias[0:1])
        k = sigmoid(ingate[at] + bias[1:2])
        recall[at] = r
        ingate[at] = k
        log_decay = -8.0 * r * decay[...]
        step = jnp.exp(log_decay)
        decay_buf[at] = step
        drive_buf[at] = jnp.sqrt(one_minus_square(log_decay, step)) * k * conv_low[at].astype(F32)

    loop(rows // tile, gates)
    row = lax.broadcasted_iota(jnp.int32, (8, channels), 0)

    def scan(i, before):
        for part in range(4):
            at = pl.ds(pl.multiple_of(i * 32 + part * 8, 8), 8)
            a, b = decay_buf[at], drive_buf[at]
            for shift in (1, 2, 4):
                inside = row >= shift
                b = b + a * jnp.where(inside, pltpu.roll(b, shift, 0), 0.0)
                a = a * jnp.where(inside, pltpu.roll(a, shift, 0), 1.0)
            h = a * before + b
            states[at] = h
            before = jnp.broadcast_to(h[7:8], (8, channels))
        return before

    carry[...] = lax.fori_loop(0, rows // 32, scan, carry[...])

    def mix(i):
        at = span(i, tile)
        value, _ = gelu_parts(branch[at])
        mixture[at] = (states[at] * value).astype(BF16)

    loop(rows // tile, mix)

    @pl.when(chunk == pl.num_programs(1) - 1)
    def _():
        final_state[0] = carry[0:1]
        final_conv[0] = hist[rows + 5 : rows + 8]


def recur_forward(u, branch, start_state, start_conv, conv, gate_w, bias, decay):
    total, channels = u.shape
    sequences = start_state.shape[0]
    length = total // sequences
    rows = tile_of(length, 256)
    chunks = length // rows
    block = pl.BlockSpec((rows, channels), lambda s, c: (s * chunks + c, 0))

    def whole(x):
        return pl.BlockSpec(x.shape, lambda s, c: (0,) * x.ndim)

    return pl.pallas_call(
        recur_kernel,
        grid=(sequences, chunks),
        out_shape=(
            shape(total, channels),
            shape(total, channels, dtype=BF16),
            shape(total, channels, dtype=BF16),
            shape(total, channels),
            shape(total, channels),
            shape(sequences, 1, channels),
            shape(sequences, 3, channels),
        ),
        in_specs=[
            block,
            block,
            pl.BlockSpec((1, 1, channels), lambda s, c: (s, 0, 0)),
            pl.BlockSpec((1, 3, channels), lambda s, c: (s, 0, 0)),
            whole(conv),
            whole(gate_w),
            whole(bias),
            whole(decay),
        ],
        out_specs=(block,) * 5
        + (
            pl.BlockSpec((1, 1, channels), lambda s, c: (s, 0, 0)),
            pl.BlockSpec((1, 3, channels), lambda s, c: (s, 0, 0)),
        ),
        scratch_shapes=[
            pltpu.VMEM((rows + 8, channels), F32),
            pltpu.VMEM((rows, channels), F32),
            pltpu.VMEM((rows, channels), F32),
            pltpu.VMEM((8, channels), F32),
        ],
        compiler_params=pltpu.CompilerParams(vmem_limit_bytes=VMEM_LIMIT),
        name="recur_forward",
    )(u, branch, start_state, start_conv, conv, gate_w, bias, decay)


def mixer_out_kernel(
    n, mixture, w_output, cotangent, tokens, gain, cot_full, residual, normed,
    full, sent, came, saved, *bufs
):
    g = Place(n)
    gather = Gather(g, full, sent, came)
    scatter = Scatter(g, lambda t, cols: dot(mixture[t], w_output[:, cols]), tile_of(residual.shape[1], 512), bufs)
    full[g.t] = cotangent[...]
    g.greet()

    def use(t):
        pltpu.make_async_copy(full.at[t], cot_full.at[t], saved.at[t]).start()

    scatter.offers(g.nz - 1)
    gather.start()

    def around(i):
        d = g.nz - 1 - i
        scatter.offers(d - 1)
        scatter.step(d)
        gather.each(i, use)
        gather.forward(i + 1)

    loop(g.nz - 1, around)
    scatter.last()
    part = 64

    def rows_of(i):
        at = span(i, part)
        values = scatter.acc[at] + tokens[at].astype(F32)
        residual[at] = values
        normed[at] = (values * inv_rms(values) * gain[...].astype(F32)).astype(BF16)

    loop(residual.shape[0] // part, rows_of)
    gather.each(g.nz - 1, use)
    loop(n, lambda t: pltpu.make_async_copy(full.at[t], cot_full.at[t], saved.at[t]).wait())
    scatter.finish()
    gather.finish()


def mixer_out(n, mixture, w_output, cotangent, tokens, gain):
    rows, width = tokens.shape
    return pl.pallas_call(
        functools.partial(mixer_out_kernel, n),
        out_shape=(
            shape(n, rows, width, dtype=BF16),
            shape(rows, width),
            shape(rows, width, dtype=BF16),
        ),
        in_specs=[VM] * 5,
        out_specs=(ANY, VM, VM),
        scratch_shapes=Gather.scratch(n, rows, width)
        + [pltpu.SemaphoreType.DMA((n,))]
        + Scatter.scratch(n, rows, width),
        compiler_params=comm_params(2),
        cost_estimate=cost(2 * n * rows * width * mixture.shape[-1]),
        name="mixer_out",
    )(mixture, w_output, cotangent, tokens, gain)


PARTS = 8


def mlp_kernel(
    n, normed, cot_full, w_gelu, w_linear, w_down, residual, cotangent, gain,
    hidden, grad_gelu, grad_linear, grad_down, g_residual, g_low, g_gain,
    full, sent, came, cot, keep_h, keep_f, keep_s, acc_g, acc_l, acc_d,
    to_sib, sums, line, acc, saved, fetched, drained, sib_sent, sib_came, line_sent, line_came,
):
    g = Place(n)
    gather = Gather(g, full, sent, came)
    columns = w_gelu.shape[1]
    rows, width = acc.shape
    tile = tile_of(columns, 256)
    wide = tile_of(width, 512)
    strip = rows // PARTS
    full[g.t] = normed[...]
    g.greet()
    gather.start()
    acc_g[...] = jnp.zeros_like(acc_g)
    acc_l[...] = jnp.zeros_like(acc_l)
    acc_d[...] = jnp.zeros_like(acc_d)

    def fetch(t, q):
        return pltpu.make_async_copy(cot_full.at[t], cot.at[q], fetched.at[q])

    def save(t, q):
        return pltpu.make_async_copy(keep_h.at[q], hidden.at[t], saved.at[q])

    def layer(t, q):
        fetch(t, q).wait()

        def part(i):
            cols = span(i, tile)
            first = dot(full[t], w_gelu[:, cols])
            second = dot(full[t], w_linear[:, cols])
            back = dot_nt(cot[q], w_down[cols])
            value, slope = gelu_parts(first)
            keep_h[q, :, cols] = (value * second).astype(BF16)
            keep_f[q, :, cols] = (back * second * slope).astype(BF16)
            keep_s[q, :, cols] = (back * value).astype(BF16)

        loop(columns // tile, part)
        save(t, q).start()

    def partial(q, cols):
        return dot_nt(keep_f[q], w_gelu[cols]) + dot_nt(keep_s[q], w_linear[cols])

    def sib_copy(k):
        return g.copy(to_sib, sums.at[k], sib_sent, sib_came.at[k], g.sib)

    def line_copy(k, slot, p, to):
        at = pl.ds(pl.multiple_of(p * strip, strip), strip)
        return g.copy(
            sums.at[k, at], line.at[slot, at], line_sent.at[k, p], line_came.at[slot, p], to
        )

    def chip(d, way):
        k = g.j + way * d
        mine, its = g.c, 1 - g.c
        own, other = 2 * k + mine, 2 * k + its
        fetch(other, its).start()
        fetch(own, mine).start()
        for p in range(gather.pieces):
            gather.copy(other, p, 2, g.sib).wait_recv()
        layer(other, its)

        def offer(i):
            cols = span(i, wide)
            to_sib[:, cols] = partial(its, cols).astype(BF16)

        loop(width // wide, offer)
        sib_copy(k).start()
        layer(own, mine)
        sib_copy(k).wait()

        @pl.when(d == 0)
        def _():
            def part(i):
                cols = span(i, wide)
                acc[:, cols] = partial(mine, cols) + sums[k, :, cols].astype(F32)

            loop(width // wide, part)

        @pl.when(d > 0)
        def _():
            def part(i):
                cols = span(i, wide)
                sums[k, :, cols] = (partial(mine, cols) + sums[k, :, cols].astype(F32)).astype(BF16)

            loop(width // wide, part)
            first = jnp.logical_or(
                jnp.logical_and(way > 0, jnp.logical_not(g.has_down)),
                jnp.logical_and(way < 0, jnp.logical_not(g.has_up)),
            )

            @pl.when(first)
            def _():
                slot = jnp.where(jnp.logical_and(way < 0, d == 1), g.nz, k)
                for p in range(PARTS):
                    line_copy(k, slot, p, g.t + 2 * way).start()

        def part(i):
            at = span(i, wide)
            both = full[pl.ds(2 * k, 2), :, at].reshape(2 * rows, wide)
            acc_g[at] += dot_tn(both, keep_f[...].reshape(2 * rows, columns))
            acc_l[at] += dot_tn(both, keep_s[...].reshape(2 * rows, columns))
            acc_d[:, at] += dot_tn(
                keep_h[...].reshape(2 * rows, columns), cot[:, :, at].reshape(2 * rows, wide)
            )

        loop(width // wide, part)
        save(other, its).wait()
        save(own, mine).wait()

    def relay(m):
        def take(k, slot, sign, p):
            at = pl.ds(pl.multiple_of(p * strip, strip), strip)
            line_copy(k, slot, p, g.sib).wait_recv()

            @pl.when(k == g.j)
            def _():
                acc[at] += line[slot, at].astype(F32)

            @pl.when(k != g.j)
            def _():
                sums[k, at] = (sums[k, at].astype(F32) + line[slot, at].astype(F32)).astype(BF16)
                there = jnp.where(jnp.logical_and(sign < 0, k == g.j - 1), g.nz, k)
                line_copy(k, there, p, g.t + 2 * sign).start()

        def rise(p):
            pl.when(jnp.logical_and(g.has_down, m >= g.j))(lambda: take(m, m, 1, p))

        def fall(p):
            k = g.nz - 1 - m
            pl.when(jnp.logical_and(g.has_up, k <= g.j))(
                lambda: take(k, jnp.where(k == g.j, g.nz, k), -1, p)
            )

        lower = 2 * g.j < g.nz

        def strips(i):
            @pl.when(i < PARTS)
            def _():
                pl.when(lower)(lambda: rise(i))
                pl.when(jnp.logical_not(lower))(lambda: fall(i))

            @pl.when(i > 0)
            def _():
                pl.when(lower)(lambda: fall(i - 1))
                pl.when(jnp.logical_not(lower))(lambda: rise(i - 1))

        loop(PARTS + 1, strips)

    def step(d):
        up, down = g.j + d < g.nz, g.j - d >= 0

        def way_of(w):
            both = jnp.logical_and(up, down)
            way = jnp.where(jnp.logical_and(w == 0, up), 1, -1)
            wanted = jnp.where(w == 0, jnp.logical_or(up, down), jnp.logical_and(both, d > 0))
            pl.when(wanted)(lambda: chip(d, way))

            @pl.when(d < g.nz - 1)
            def _():
                for p in range(gather.pieces):
                    pl.when(w == min(p, 1))(lambda: gather.forward(d + 1, (p,)))

        loop(2, way_of)
        pl.when(d > 1)(lambda: relay(d - 1))

    loop(g.nz, step)
    gather.finish()

    stages = [held.at[q] for held in (keep_h, keep_f, keep_s) for q in (0, 1)]
    leaving = []

    def leave(i, value, out):
        slot = i % len(stages)
        if len(leaving) >= len(stages):
            leaving[i - len(stages)].wait()
        stages[slot][...] = value.astype(BF16)
        copy = pltpu.make_async_copy(stages[slot], out, drained.at[slot])
        copy.start()
        leaving.append(copy)

    count = width // rows
    for i in range(count):
        at = pl.ds(i * rows, rows)
        leave(2 * i, acc_g[at], grad_gelu.at[at])
        leave(2 * i + 1, acc_l[at], grad_linear.at[at])
    wider = []
    for i in range(columns // rows):
        at = pl.ds(i * rows, rows)
        full[i] = acc_d[at].astype(BF16)
        wider.append(pltpu.make_async_copy(full.at[i], grad_down.at[at], drained.at[len(stages) + i]))
        wider[-1].start()
    relay(g.nz - 1)
    lines = 32
    g_gain[...] = jnp.zeros_like(g_gain)

    def rows_of(i):
        at = span(i, lines)
        back, terms = norm_grad(residual[at], gain[...].astype(F32), acc[at])
        value = cotangent[at].astype(F32) + back
        g_residual[at] = value
        g_low[at] = value.astype(BF16)
        g_gain[...] += jnp.sum(terms, axis=0, keepdims=True)

    loop(rows // lines, rows_of)
    for copy in leaving[-len(stages):] + wider:
        copy.wait()

    def done(k):
        @pl.when(k != g.j)
        def _():
            for p in range(PARTS):
                line_copy(k, k, p, g.sib).wait_send()

    loop(g.nz, done)


def mlp(n, normed, cot_full, w_gelu, w_linear, w_down, residual, cotangent, gain):
    rows, width = normed.shape
    columns = w_gelu.shape[1]
    kept = pltpu.VMEM((2, rows, columns), BF16)
    sems = pltpu.SemaphoreType.DMA
    return pl.pallas_call(
        functools.partial(mlp_kernel, n),
        out_shape=(shape(n, rows, columns, dtype=BF16),)
        + (shape(width, columns, dtype=BF16),) * 2
        + (
            shape(columns, width, dtype=BF16),
            shape(rows, width),
            shape(rows, width, dtype=BF16),
            shape(1, width),
        ),
        in_specs=[VM, ANY] + [VM] * 6,
        out_specs=(ANY,) * 4 + (VM,) * 3,
        scratch_shapes=Gather.scratch(n, rows, width)
        + [pltpu.VMEM((2, rows, width), BF16)]
        + [kept] * 3
        + [pltpu.VMEM((width, columns), F32)] * 2
        + [
            pltpu.VMEM((columns, width), F32),
            pltpu.VMEM((rows, width), BF16),
            pltpu.VMEM((n // 2, rows, width), BF16),
            pltpu.VMEM((n // 2 + 1, rows, width), BF16),
            pltpu.VMEM((rows, width), F32),
            sems((2,)),
            sems((2,)),
            sems((6 + columns // rows,)),
            sems,
            sems((n // 2,)),
            sems((n // 2, PARTS)),
            sems((n // 2 + 1, PARTS)),
        ],
        compiler_params=comm_params(3),
        cost_estimate=cost(16 * n * rows * width * columns),
        name="mlp",
    )(normed, cot_full, w_gelu, w_linear, w_down, residual, cotangent, gain)


def down_kernel(
    n, hidden, w_down, residual, g_low, w_output, mixture, output, g_mixture, grad_output,
    full, sent, came, acc_o, *bufs
):
    g = Place(n)
    gather = Gather(g, full, sent, came)
    width = residual.shape[1]
    wide = tile_of(width, 512)
    scatter = Scatter(g, lambda t, cols: dot(hidden[t], w_down[:, cols]), wide, bufs)
    full[g.t] = g_low[...]
    g.greet()

    def use(t):
        g_mixture[t] = dot_nt(full[t], w_output[...])

        def part(i):
            at = span(i, wide)
            acc_o[:, at] += dot_tn(mixture[t], full[t, :, at])

        loop(width // wide, part)

    gather.start()
    acc_o[...] = jnp.zeros_like(acc_o)
    scatter.offers(g.nz - 1)

    def around(i):
        d = g.nz - 1 - i
        scatter.offers(d - 1)
        scatter.step(d)
        gather.each(i, use)
        gather.forward(i + 1)

    loop(g.nz - 1, around)
    gather.each(g.nz - 1, use)
    grad_output[...] = acc_o[...].astype(BF16)
    scatter.last()
    output[...] = (scatter.acc[...] + residual[...]).astype(BF16)
    scatter.finish()
    gather.finish()


def down(n, hidden, w_down, residual, g_low, w_output, mixture):
    rows, width = residual.shape
    channels = w_output.shape[0]
    return pl.pallas_call(
        functools.partial(down_kernel, n),
        out_shape=(
            shape(rows, width, dtype=BF16),
            shape(n, rows, channels),
            shape(channels, width, dtype=BF16),
        ),
        in_specs=[VM] * 6,
        out_specs=(VM,) * 3,
        scratch_shapes=Gather.scratch(n, rows, width)
        + [pltpu.VMEM((channels, width), F32)]
        + Scatter.scratch(n, rows, width),
        compiler_params=comm_params(5),
        cost_estimate=cost(2 * n * rows * width * (hidden.shape[-1] + 2 * channels)),
        name="down",
    )(hidden, w_down, residual, g_low, w_output, mixture)


def recur_back_kernel(
    g_mix, branch, states, states_before, u, u_before, conv_low, recall, ingate, start_state, start_conv,
    conv, gate_w, decay,
    g_recur, g_branch, small, g_gates,
    g_state, step_buf, root_buf, g_conv, pre_r, pre_i, carry, hist_s, hist_u, sums,
):
    sequence, back = pl.program_id(0), pl.program_id(1)
    last = pl.num_programs(1) - 1
    rows, channels = u.shape
    tile = 32

    @pl.when(jnp.logical_and(sequence == 0, back == 0))
    def _():
        sums[...] = jnp.zeros_like(sums)
        g_gates[...] = jnp.zeros_like(g_gates)

    @pl.when(back == 0)
    def _():
        carry[...] = jnp.zeros_like(carry)
        g_conv[rows : rows + 8] = jnp.zeros((8, channels), F32)

    @pl.when(back > 0)
    def _():
        g_conv[rows : rows + 8] = g_conv[0:8]

    @pl.when(back == last)
    def _():
        hist_s[0:8] = jnp.broadcast_to(start_state[0], (8, channels))
        hist_u[0:8] = jnp.concatenate([jnp.zeros((5, channels), F32), start_conv[0]], axis=0)

    @pl.when(back < last)
    def _():
        hist_s[0:8] = states_before[...]
        hist_u[0:8] = u_before[...]

    hist_s[8:] = states[...]
    hist_u[8:] = u[...]

    def first(i):
        at = span(i, tile)
        value, slope = gelu_parts(branch[at])
        gm = g_mix[at]
        g_state[at] = gm * value
        g_branch[at] = (gm * states[at] * slope).astype(BF16)
        log_decay = -8.0 * recall[at] * decay[...]
        step = jnp.exp(log_decay)
        step_buf[at] = step
        root_buf[at] = jnp.sqrt(one_minus_square(log_decay, step))

    loop(rows // tile, first)
    row = lax.broadcasted_iota(jnp.int32, (8, channels), 0)
    groups = rows // 32

    def scan(i, after):
        for part in range(4):
            at = pl.ds(pl.multiple_of((groups - 1 - i) * 32 + (3 - part) * 8, 8), 8)
            a, gs = step_buf[at], g_state[at]
            b = a * gs
            for shift in (1, 2, 4):
                inside = row < 8 - shift
                b = b + a * jnp.where(inside, pltpu.roll(b, 8 - shift, 0), 0.0)
                a = a * jnp.where(inside, pltpu.roll(a, 8 - shift, 0), 1.0)
            e = a * after + b
            g_state[at] = gs + jnp.where(row < 7, pltpu.roll(e, 7, 0), after)
            after = jnp.broadcast_to(e[0:1], (8, channels))
        return after

    carry[...] = lax.fori_loop(0, groups, scan, carry[...])

    def fold(x):
        return jnp.sum(x.reshape(tile // 8, 8, channels), axis=0)

    def second(i):
        at = span(i, tile)
        window = hist_s[pl.ds(pl.multiple_of(i * tile, tile), tile + 8)]
        before = window[7 : tile + 7]
        g, r, k = g_state[at], recall[at], ingate[at]
        c = conv_low[at].astype(F32)
        step, root = step_buf[at], root_buf[at]
        kc = k * c
        g_log = g * (before * step - kc * (step * step) / root)
        slow = -8.0 * r
        sums[7] += fold(g_log * slow)
        low_r = (g_log * (slow * decay[...]) * (1.0 - r)).astype(BF16)
        low_i = (g * root * kc * (1.0 - k)).astype(BF16)
        pre_r[at] = low_r
        pre_i[at] = low_i
        sums[5] += fold(low_r.astype(F32))
        sums[6] += fold(low_i.astype(F32))
        g_conv[at] = g * root * k

    loop(rows // tile, second)
    low_r, low_i, low_c = pre_r[...], pre_i[...], conv_low[...]
    g_gates[0] += dot_tn(low_c, low_r)
    g_gates[1] += dot_tn(low_c, low_i)
    g_conv[0:rows] += dot_nt(low_r, gate_w[0]) + dot_nt(low_i, gate_w[1])

    def third(i):
        at = span(i, tile)
        start = pl.multiple_of(i * tile, tile)
        window = g_conv[pl.ds(start, tile + 8)]
        value = conv[0:1] * window[0:tile]
        for k in (1, 2, 3):
            value = value + conv[k : k + 1] * window[k : tile + k]
        g_recur[at] = value.astype(BF16)
        past = hist_u[pl.ds(start, tile + 8)]
        gc = window[0:tile]
        for k in range(4):
            sums[k] += fold(gc * past[8 - k : tile + 8 - k])
        sums[4] += fold(gc)

    loop(rows // tile, third)

    @pl.when(jnp.logical_and(sequence == pl.num_programs(0) - 1, back == last))
    def _():
        small[...] = jnp.sum(sums[...], axis=1)


def recur_back(g_mix, branch, states, u, conv_low, recall, ingate, start_state, start_conv, conv, gate_w, decay):
    total, channels = u.shape
    sequences = start_state.shape[0]
    length = total // sequences
    rows = tile_of(length, 256)
    chunks = length // rows
    eights = rows // 8

    def at(s, c):
        return (s * chunks + chunks - 1 - c, 0)

    def earlier(s, c):
        return (jnp.maximum((s * chunks + chunks - 1 - c) * eights - 1, 0), 0)

    block = pl.BlockSpec((rows, channels), at)
    before = pl.BlockSpec((8, channels), earlier)

    def whole(x):
        return pl.BlockSpec(x.shape, lambda s, c: (0,) * x.ndim)

    wide = pltpu.VMEM((rows, channels), F32)
    narrow = pltpu.VMEM((rows, channels), BF16)
    long = pltpu.VMEM((rows + 8, channels), F32)
    return pl.pallas_call(
        recur_back_kernel,
        grid=(sequences, chunks),
        out_shape=(
            shape(total, channels, dtype=BF16),
            shape(total, channels, dtype=BF16),
            shape(8, channels),
            shape(2, channels, channels),
        ),
        in_specs=[
            block, block, block, before, block, before, block, block, block,
            pl.BlockSpec((1, 1, channels), lambda s, c: (s, 0, 0)),
            pl.BlockSpec((1, 3, channels), lambda s, c: (s, 0, 0)),
            whole(conv), whole(gate_w), whole(decay),
        ],
        out_specs=(
            block,
            block,
            pl.BlockSpec((8, channels), lambda s, c: (0, 0)),
            pl.BlockSpec((2, channels, channels), lambda s, c: (0, 0, 0)),
        ),
        scratch_shapes=[
            wide, wide, wide, long, narrow, narrow,
            pltpu.VMEM((8, channels), F32), long, long,
            pltpu.VMEM((8, 8, channels), F32),
        ],
        compiler_params=pltpu.CompilerParams(vmem_limit_bytes=VMEM_LIMIT),
        name="recur_back",
    )(g_mix, branch, states, states, u, u, conv_low, recall, ingate, start_state, start_conv, conv, gate_w, decay)


class Halving:
    def __init__(self, me, count, data, landed, final, sems):
        self.me, self.count = me, count
        self.data, self.landed, self.final = data, landed, final
        self.out_send, self.out_recv, self.back_send, self.back_recv = (sems.at[q] for q in range(4))
        self.bits = count.bit_length() - 1
        assert count == 1 << self.bits

    @staticmethod
    def scratch(count, rows, columns):
        slots = max(count - 1, 1)
        return [
            pltpu.VMEM((2, count, rows, columns), BF16),
            pltpu.VMEM((2, slots, rows, columns), BF16),
            pltpu.VMEM((2, count, rows, columns), BF16),
            pltpu.SemaphoreType.DMA((4, 2, slots)),
        ]

    def own(self, bit):
        return lax.rem(lax.div(self.me, 1 << bit), 2)

    def swaps(self, s):
        for track in (0, 1):
            order = [(i + track) % self.bits for i in range(self.bits)]
            bit = order[s]
            partner = self.me + (1 - 2 * self.own(bit)) * (1 << bit)
            fixed = sum(self.own(b) * (1 << b) for b in order[:s])
            for u in range(self.count >> (s + 1)):
                free = sum(((u >> i) & 1) << b for i, b in enumerate(order[s + 1 :]))
                slot = self.count - (self.count >> s) + u
                kept = fixed + free + self.own(bit) * (1 << bit)
                yield track, slot, partner, fixed + free + (1 - self.own(bit)) * (1 << bit), kept

    def out(self, track, slot, partner, given):
        return pltpu.make_async_remote_copy(
            src_ref=self.data.at[track, given],
            dst_ref=self.landed.at[track, slot],
            send_sem=self.out_send.at[track, slot],
            recv_sem=self.out_recv.at[track, slot],
            device_id={"dp": partner},
            device_id_type=MESH,
        )

    def back(self, track, slot, partner, segment):
        return pltpu.make_async_remote_copy(
            src_ref=self.final.at[track, segment],
            dst_ref=self.final.at[track, segment],
            send_sem=self.back_send.at[track, slot],
            recv_sem=self.back_recv.at[track, slot],
            device_id={"dp": partner},
            device_id_type=MESH,
        )

    def start(self, s=0):
        for track, slot, partner, given, _ in self.swaps(s):
            self.out(track, slot, partner, given).start()

    def turn(self, s):
        rows = self.data.shape[2]
        tile = tile_of(rows, 32)
        for track, slot, partner, given, kept in self.swaps(s):
            self.out(track, slot, partner, given).wait_recv()
            result = self.final if s == self.bits - 1 else self.data

            def add(r):
                at = span(r, tile)
                value = self.data[track, kept, at].astype(F32) + self.landed[track, slot, at].astype(F32)
                result[track, kept, at] = value.astype(BF16)

            loop(rows // tile, add)
        if s < self.bits - 1:
            self.start(s + 1)
        else:
            self.start_back(s)

    def start_back(self, s):
        for track, slot, partner, _, kept in self.swaps(s):
            self.back(track, slot, partner, kept).start()

    def turn_back(self, s):
        for track, slot, partner, given, _ in self.swaps(s):
            self.back(track, slot, partner, given).wait_recv()
        if s > 0:
            self.start_back(s - 1)

    def events(self):
        steps = [functools.partial(self.turn, s) for s in range(self.bits)]
        return steps + [functools.partial(self.turn_back, s) for s in range(self.bits - 1, 0, -1)]

    def finish(self):
        self.turn_back(0)
        for s in range(self.bits):
            for track, slot, partner, given, kept in self.swaps(s):
                self.out(track, slot, partner, given).wait_send()
                self.back(track, slot, partner, kept).wait_send()


def input_back_kernel(
    n, copies, g_recur, g_branch, w_in, w_br, normed, tokens, g_residual, gain, second_gain, g_gates, small, g_out,
    input_grad, in_out, br_out, out_out, gates_out, conv_out, bias_out, decay_out, gains_out,
    gain_row, gain_parts, gain_in, gain_sum, gain_dp, gain_sent, gain_came, gain_dp_sent, gain_dp_came, *bufs
):
    g = Place(n)
    me = lax.axis_index("dp")
    rows, width = tokens.shape
    channels = w_in.shape[0]
    blocks, block_width = gates_out.shape[1], gates_out.shape[2]
    segment = width // (2 * copies)
    gain_width = width // n
    weights = Halving(me, copies, *bufs[:4])
    rest = Halving(me, copies, *bufs[4:8])
    padded = bufs[0].shape[2] // 3
    rest_rows = bufs[4].shape[2]

    def block(ref, t):
        return ref[span(t, rows)]

    def partial(t, cols):
        return dot(block(g_recur, t), w_in[:, cols]) + dot(block(g_branch, t), w_br[:, cols])

    scatter = Scatter(g, partial, tile_of(width, 512), bufs[8:])

    def gain_copy(t, slot):
        return g.copy(gain_parts.at[t], gain_in.at[slot], gain_sent.at[t], gain_came.at[slot], t)

    def gain_dp_copy(i, slot):
        return pltpu.make_async_remote_copy(
            src_ref=gain_sum,
            dst_ref=gain_dp.at[slot],
            send_sem=gain_dp_sent.at[i],
            recv_sem=gain_dp_came.at[slot],
            device_id={"dp": i},
            device_id_type=MESH,
        )

    def others(act):
        loop(n, lambda t: pl.when(t != g.t)(lambda: act(t)))

    def copies_of(act):
        loop(copies, lambda i: pl.when(i != me)(lambda: act(i)))

    barrier = pltpu.get_barrier_semaphore()
    others(
        lambda t: pl.semaphore_signal(barrier, inc=1, device_id={"tensor": t}, device_id_type=MESH)
    )
    copies_of(lambda i: pl.semaphore_signal(barrier, inc=1, device_id={"dp": i}, device_id_type=MESH))
    pl.semaphore_wait(barrier, n - 1 + copies - 1)

    scatter.offers(g.nz - 1)

    def around(i):
        d = g.nz - 1 - i
        scatter.offers(d - 1)
        scatter.step(d)

    around(0)

    data = bufs[0]

    def weigh(q):
        cols = span(q, 2 * segment)
        first = dot_tn(g_recur[...], normed[:, cols])
        second = dot_tn(g_branch[...], normed[:, cols])
        third = g_out[:, cols]
        for half in (0, 1):
            index = 2 * q + half
            track, part = lax.div(index, copies), lax.rem(index, copies)
            for i, value in enumerate((first, second, third)):
                piece = value[:, half * segment : (half + 1) * segment].astype(BF16)
                data[track, part, i * padded : i * padded + channels] = piece
                if padded > channels:
                    data[track, part, i * padded + channels : (i + 1) * padded] = jnp.zeros(
                        (padded - channels, segment), BF16
                    )
        terms = jnp.sum(w_in[:, cols].astype(F32) * first + w_br[:, cols].astype(F32) * second, axis=0, keepdims=True)
        gain_row[0:1, cols] = terms / gain[0:1, cols].astype(F32)

    loop(copies, weigh)
    weights.start()
    gain_row[1:2] = second_gain[...]
    gain_row[2:8] = jnp.zeros((6, width), F32)
    for t in range(n):
        gain_parts[t] = gain_row[:, t * gain_width : (t + 1) * gain_width]
    others(lambda t: gain_copy(t, g.t).start())
    gain_in[g.t] = gain_parts[g.t]

    flat = jnp.concatenate(
        [
            g_gates[0],
            g_gates[1],
            small[...],
            jnp.zeros((2 * copies * rest_rows - 2 * channels - 8, channels), F32),
        ],
        axis=0,
    ).astype(BF16)
    for i in range(2 * copies):
        bufs[4][i // copies, i % copies] = flat[i * rest_rows : (i + 1) * rest_rows]
    rest.start()

    events = [lambda a=a, b=b: (a(), b()) for a, b in zip(weights.events(), rest.events())]
    for i in range(1, g.nz - 1):
        around(i)
        if events:
            events.pop(0)()
        if i == 1:
            others(lambda t: gain_copy(t, t).wait_recv())
            total = gain_in[0]
            for t in range(1, n):
                total = total + gain_in[t]
            gain_sum[...] = total
            copies_of(lambda i: gain_dp_copy(i, me).start())
            gain_dp[me] = total
    for event in events:
        event()
    scatter.last()
    part = 32

    def rows_of(i):
        at = span(i, part)
        back, _ = norm_grad(tokens[at].astype(F32), gain[...].astype(F32), scatter.acc[at])
        input_grad[at] = g_residual[at] + back

    loop(rows // part, rows_of)
    copies_of(lambda i: gain_dp_copy(i, i).wait_recv())
    total = gain_dp[0]
    for i in range(1, copies):
        total = total + gain_dp[i]
    gains_out[...] = total
    rest.finish()
    flat = jnp.concatenate([bufs[6][i // copies, i % copies].astype(F32) for i in range(2 * copies)], axis=0)
    for q in (0, 1):
        for i in range(blocks):
            start = q * channels + i * block_width
            gates_out[q, i] = flat[start : start + block_width, i * block_width : (i + 1) * block_width]
    conv_out[...] = flat[2 * channels : 2 * channels + 5]
    bias_out[...] = flat[2 * channels + 5 : 2 * channels + 7]
    decay_out[...] = flat[2 * channels + 7 : 2 * channels + 8]
    weights.finish()
    for i in range(2 * copies):
        for q, out in enumerate((in_out, br_out, out_out)):
            out[:, i * segment : (i + 1) * segment] = bufs[2][
                i // copies, i % copies, q * padded : q * padded + channels
            ]
    others(lambda t: gain_copy(t, t).wait_send())
    copies_of(lambda i: gain_dp_copy(i, i).wait_send())
    scatter.finish()


def up_to(extent, multiple):
    return (extent + multiple - 1) // multiple * multiple


def input_back(
    n, copies, g_recur, g_branch, w_in, w_br, normed, tokens, g_residual, gain, second_gain, g_gates, small, g_out,
    blocks,
):
    rows, width = tokens.shape
    channels = w_in.shape[0]
    block = channels // blocks
    rest_rows = up_to((2 * channels + 8 + 2 * copies - 1) // (2 * copies), 16)
    gain_shape = (8, width // n)
    sems = pltpu.SemaphoreType.DMA
    return pl.pallas_call(
        functools.partial(input_back_kernel, n, copies),
        out_shape=(shape(rows, width),)
        + (shape(channels, width, dtype=BF16),) * 3
        + (
            shape(2, blocks, block, block),
            shape(5, channels),
            shape(2, channels),
            shape(1, channels),
            shape(*gain_shape),
        ),
        in_specs=[VM] * 12,
        out_specs=(VM,) * 9,
        scratch_shapes=[
            pltpu.VMEM((8, width), F32),
            pltpu.VMEM((n, *gain_shape), F32),
            pltpu.VMEM((n, *gain_shape), F32),
            pltpu.VMEM(gain_shape, F32),
            pltpu.VMEM((copies, *gain_shape), F32),
            sems((n,)),
            sems((n,)),
            sems((copies,)),
            sems((copies,)),
        ]
        + Halving.scratch(copies, 3 * up_to(channels, 16), width // (2 * copies))
        + Halving.scratch(copies, rest_rows, channels)
        + Scatter.scratch(n, rows, width),
        compiler_params=comm_params(6),
        cost_estimate=cost(8 * n * rows * width * channels),
        name="input_back",
    )(g_recur, g_branch, w_in, w_br, normed, tokens, g_residual, gain, second_gain, g_gates, small, g_out)


def body(
    n,
    copies,
    tokens,
    cotangent,
    resets,
    init_state,
    init_conv,
    norm_gain,
    w_input,
    w_branch,
    conv_params,
    gate_weights,
    gate_bias,
    decay_rate,
    w_output,
    mlp_gain,
    w_gelu,
    w_linear,
    w_down,
):
    rows, width = tokens.shape
    total = rows * n
    channels = w_input.shape[1]
    blocks, block = gate_weights.shape[1], gate_weights.shape[2]
    survive = (1 - resets).astype(F32)
    start_state = (init_state * survive[:, None])[:, None]
    start_conv = init_conv * survive[:, None, None]
    gain_first, gain_second = norm_gain[None], mlp_gain[None]
    gate_w = (gate_weights[:, :, :, None] * jnp.eye(blocks, dtype=BF16)[None, :, None, :, None]).reshape(
        2, channels, channels
    )
    decay = decay_rate[None]
    w_in, w_br = w_input.T, w_branch.T

    def flat(x):
        return x.reshape(total, x.shape[-1])

    def blocked(x):
        return x.reshape(n, rows, x.shape[-1])

    normed, recur, branch = project(n, tokens, gain_first, w_in, w_br)
    recur, branch = flat(recur), flat(branch)
    states, mixture, conv_low, recall, ingate, final_state, final_conv = recur_forward(
        recur, branch, start_state, start_conv, conv_params, gate_w, gate_bias, decay
    )
    mixture = blocked(mixture)
    cot_full, residual, normed_mlp = mixer_out(n, mixture, w_output, cotangent, tokens, gain_second)
    hidden, grad_gelu, grad_linear, grad_down, g_residual, g_low, gain_second_grad = mlp(
        n, normed_mlp, cot_full, w_gelu, w_linear, w_down, residual, cotangent, gain_second
    )
    mlp_sums = lax.psum((grad_gelu, grad_linear, grad_down), "dp")
    output, g_mixture, grad_output = down(n, hidden, w_down, residual, g_low, w_output, mixture)
    g_recur, g_branch, small, g_gates = recur_back(
        flat(g_mixture), branch, states, recur, conv_low, recall, ingate, start_state, start_conv,
        conv_params, gate_w, decay,
    )
    input_grad, grad_input, grad_branch, grad_output, gates, g_conv, g_bias, g_decay, gains = input_back(
        n, copies, g_recur, g_branch, w_in, w_br, flat(normed), tokens, g_residual, gain_first,
        gain_second_grad, g_gates, small, grad_output, blocks,
    )
    grad_gelu, grad_linear, grad_down = (x.astype(F32) for x in mlp_sums)
    return (
        output,
        input_grad,
        final_state[:, 0],
        final_conv,
        gains[0],
        grad_input.astype(F32).T,
        grad_branch.astype(F32).T,
        g_conv,
        gates,
        g_bias,
        g_decay[0],
        grad_output.astype(F32),
        gains[1],
        grad_gelu,
        grad_linear,
        grad_down,
    )


def solution(mesh):
    in_specs = (
        P(("dp", "tensor"), None),
        P(("dp", "tensor"), None),
        P("dp"),
        P("dp", "tensor"),
        P("dp", None, "tensor"),
        P(),
        P(None, "tensor"),
        P(None, "tensor"),
        P(None, "tensor"),
        P(None, "tensor", None, None),
        P(None, "tensor"),
        P("tensor"),
        P("tensor", None),
        P(),
        P(None, "tensor"),
        P(None, "tensor"),
        P("tensor", None),
    )
    out_specs = (
        P(("dp", "tensor"), None),
        P(("dp", "tensor"), None),
        P("dp", "tensor"),
        P("dp", None, "tensor"),
        P("tensor"),
        P(None, "tensor"),
        P(None, "tensor"),
        P(None, "tensor"),
        P(None, "tensor", None, None),
        P(None, "tensor"),
        P("tensor"),
        P("tensor", None),
        P("tensor"),
        P(None, "tensor"),
        P(None, "tensor"),
        P("tensor", None),
    )
    return jax.shard_map(
        functools.partial(body, mesh.shape["tensor"], mesh.shape["dp"]),
        mesh=mesh,
        in_specs=in_specs,
        out_specs=out_specs,
        check_vma=False,
    )
```

```python
import functools

import jax
import jax.numpy as jnp
from jax import lax
from jax.experimental import pallas as pl
from jax.experimental.pallas import tpu as pltpu
from jax.sharding import PartitionSpec as P

EPSILON = 1e-06
KAPPA = 0.7978845608028654
CUBIC = 0.044715
PIECES = 2
STRIPS = 4
PARTS = 8
F32 = jnp.float32
BF16 = jnp.bfloat16
ANY = pl.BlockSpec(memory_space=pl.ANY)
VM = pl.BlockSpec(memory_space=pltpu.VMEM)
VMEM_LIMIT = 61 * 1024 * 1024
MESH = pl.DeviceIdType.MESH


def dot(a, b):
    return jnp.dot(a, b, preferred_element_type=F32)


def dot_nt(a, b):
    return lax.dot_general(a, b, (((1,), (1,)), ((), ())), preferred_element_type=F32)


def dot_tn(a, b):
    return lax.dot_general(a, b, (((0,), (0,)), ((), ())), preferred_element_type=F32)


def tile_of(extent, wanted):
    while extent % wanted:
        wanted //= 2
    return wanted


def span(i, size):
    return pl.ds(pl.multiple_of(i * size, size), size)


def loop(count, body):
    def step(i, carry):
        body(i)
        return carry

    lax.fori_loop(0, count, step, 0)


class Place:
    def __init__(self, n):
        self.n = n
        self.nz = n // 2
        self.t = lax.axis_index("tensor")
        self.c = lax.rem(self.t, 2)
        self.j = lax.div(self.t, 2)
        self.sib = self.t + 1 - 2 * self.c
        self.has_up = self.j < self.nz - 1
        self.has_down = self.j > 0

    def greet(self, partners=()):
        barrier = pltpu.get_barrier_semaphore()

        def signal(t):
            pl.semaphore_signal(barrier, inc=1, device_id={"tensor": t}, device_id_type=MESH)

        for i in partners:
            pl.semaphore_signal(barrier, inc=1, device_id={"dp": i}, device_id_type=MESH)

        signal(self.sib)
        pl.when(self.has_up)(lambda: signal(self.t + 2))
        pl.when(self.has_down)(lambda: signal(self.t - 2))
        pl.semaphore_wait(
            barrier,
            1 + len(partners) + self.has_up.astype(jnp.int32) + self.has_down.astype(jnp.int32),
        )

    def copy(self, src, dst, send, recv, t):
        return pltpu.make_async_remote_copy(
            src_ref=src,
            dst_ref=dst,
            send_sem=send,
            recv_sem=recv,
            device_id={"tensor": t},
            device_id_type=MESH,
        )


class Gather:
    def __init__(self, place, full, sent, came):
        self.place, self.full, self.sent, self.came = place, full, sent, came
        self.pieces = came.shape[1]
        self.size = full.shape[1] // self.pieces

    @staticmethod
    def scratch(n, rows, width):
        return [
            pltpu.VMEM((n, rows, width), BF16),
            pltpu.SemaphoreType.DMA((n, PIECES, 3)),
            pltpu.SemaphoreType.DMA((n, PIECES)),
        ]

    def copy(self, t, p, way, to):
        piece = self.full.at[t, pl.ds(p * self.size, self.size)]
        return self.place.copy(piece, piece, self.sent.at[t, p, way], self.came.at[t, p], to)

    def start(self):
        g = self.place
        for p in range(self.pieces):
            pl.when(g.has_up)(lambda: self.copy(g.t, p, 0, g.t + 2).start())
            pl.when(g.has_down)(lambda: self.copy(g.t, p, 1, g.t - 2).start())
        for p in range(self.pieces):
            self.copy(g.t, p, 2, g.sib).start()

    def forward(self, d, pieces=None):
        g = self.place
        for p in range(self.pieces) if pieces is None else pieces:

            @pl.when(g.j - d >= 0)
            def _():
                t = g.t - 2 * d
                self.copy(t, p, 0, g.sib).wait_recv()
                pl.when(g.has_up)(lambda: self.copy(t, p, 0, g.t + 2).start())
                self.copy(t, p, 2, g.sib).start()

            @pl.when(g.j + d < g.nz)
            def _():
                t = g.t + 2 * d
                self.copy(t, p, 1, g.sib).wait_recv()
                pl.when(g.has_down)(lambda: self.copy(t, p, 1, g.t - 2).start())
                self.copy(t, p, 2, g.sib).start()

    def each(self, d, use):
        g = self.place

        def visit(q):
            core, way = lax.div(q, 2), 2 * lax.rem(q, 2) - 1
            j = g.j + way * d
            there = jnp.logical_and(j >= 0, j < g.nz)

            @pl.when(jnp.logical_and(there, jnp.logical_or(d > 0, way > 0)))
            def _():
                t = 2 * j + lax.rem(g.c + core, 2)

                @pl.when(core > 0)
                def _():
                    for p in range(self.pieces):
                        self.copy(t, p, 2, g.sib).wait_recv()

                use(t)

        loop(4, visit)

    def finish(self):
        g = self.place

        def done(t):
            for p in range(self.pieces):
                self.copy(t, p, 2, g.sib).wait_send()

                @pl.when(jnp.logical_and(t <= g.t, g.has_up))
                def _():
                    self.copy(t, p, 0, g.sib).wait_send()

                @pl.when(jnp.logical_and(t >= g.t, g.has_down))
                def _():
                    self.copy(t, p, 1, g.sib).wait_send()

        loop(g.nz, lambda k: done(2 * k + g.c))


class Scatter:
    def __init__(self, place, partial, tile, bufs):
        self.place, self.partial, self.tile = place, partial, tile
        self.to_sib, self.from_sib, self.line, self.acc = bufs[:4]
        self.sib_send, self.sib_recv, self.line_send, self.line_recv = bufs[4:]
        self.out = self.from_sib
        self.tiles = self.acc.shape[1] // tile

    @staticmethod
    def scratch(n, rows, width):
        nz = n // 2
        return [
            pltpu.VMEM((nz, rows, width), BF16),
            pltpu.VMEM((nz, rows, width), BF16),
            pltpu.VMEM((nz + 1, rows, width), BF16),
            pltpu.VMEM((rows, width), F32),
            pltpu.SemaphoreType.DMA((nz,)),
            pltpu.SemaphoreType.DMA((nz,)),
            pltpu.SemaphoreType.DMA((nz, STRIPS)),
            pltpu.SemaphoreType.DMA((nz + 1, STRIPS)),
        ]

    def sib_copy(self, k):
        return self.place.copy(
            self.to_sib.at[k],
            self.from_sib.at[k],
            self.sib_send.at[k],
            self.sib_recv.at[k],
            self.place.sib,
        )

    def line_copy(self, k, slot, p, to):
        at = self.strip(p)
        return self.place.copy(
            self.out.at[k, at], self.line.at[slot, at], self.line_send.at[k, p], self.line_recv.at[slot, p], to
        )

    def strip(self, p):
        return span(p, self.acc.shape[0] // STRIPS)

    def offer(self, k):
        t = 2 * k + 1 - self.place.c

        def part(i):
            cols = span(i, self.tile)
            self.to_sib[k, :, cols] = self.partial(t, cols).astype(BF16)

        loop(self.tiles, part)
        self.sib_copy(k).start()

    def pair(self, k):
        self.sib_copy(k).wait_recv()
        t = 2 * k + self.place.c

        def part(i):
            cols = span(i, self.tile)
            self.acc[:, cols] = self.partial(t, cols) + self.from_sib[k, :, cols].astype(F32)

        loop(self.tiles, part)

    def offers(self, d):
        g = self.place

        def way_of(w):
            k = g.j + (1 - 2 * w) * d

            @pl.when(jnp.logical_and(jnp.logical_and(k >= 0, k < g.nz), jnp.logical_or(d > 0, w == 0)))
            def _():
                self.offer(k)

        loop(2, way_of)

    def step(self, d):
        g = self.place

        def way_of(w):
            sign = 1 - 2 * w
            k = g.j + sign * d

            @pl.when(jnp.logical_and(k >= 0, k < g.nz))
            def _():
                self.pair(k)
                upstream = g.j - sign
                more = jnp.logical_and(upstream >= 0, upstream < g.nz)

                slot = jnp.where(jnp.logical_and(d == 1, w == 1), g.nz, k)

                def pass_on(p):
                    at = self.strip(p)

                    @pl.when(more)
                    def _():
                        self.line_copy(k, k, p, g.sib).wait_recv()
                        self.out[k, at] = (self.acc[at] + self.line[k, at].astype(F32)).astype(BF16)

                    @pl.when(jnp.logical_not(more))
                    def _():
                        self.out[k, at] = self.acc[at].astype(BF16)

                    self.line_copy(k, slot, p, g.t + 2 * sign).start()

                loop(STRIPS, pass_on)

        loop(2, way_of)

    def last(self):
        g = self.place
        self.pair(g.j)

        def take(p):
            at = self.strip(p)

            @pl.when(g.has_down)
            def _():
                self.line_copy(g.j, g.j, p, g.sib).wait_recv()
                self.acc[at] += self.line[g.j, at].astype(F32)

            @pl.when(g.has_up)
            def _():
                self.line_copy(g.j, g.nz, p, g.sib).wait_recv()
                self.acc[at] += self.line[g.nz, at].astype(F32)

        loop(STRIPS, take)

    def finish(self):
        g = self.place

        def done(k):
            self.sib_copy(k).wait_send()
            pl.when(g.j != k)(
                lambda: loop(STRIPS, lambda p: self.line_copy(k, k, p, g.sib).wait_send())
            )

        loop(g.nz, done)


class Halving:
    def __init__(self, me, count, data, landed, final, sems):
        self.me, self.count = me, count
        self.data, self.landed, self.final = data, landed, final
        self.out_send, self.out_recv, self.back_send, self.back_recv = (sems.at[q] for q in range(4))
        self.bits = count.bit_length() - 1
        assert count == 1 << self.bits

    @staticmethod
    def scratch(count, rows, columns):
        return [
            pltpu.VMEM((2, count, 1, rows, columns), BF16),
            pltpu.VMEM((2, count - 1, 1, rows, columns), BF16),
            pltpu.VMEM((2, count, 1, rows, columns), BF16),
            pltpu.SemaphoreType.DMA((4, 2, count - 1)),
        ]

    @staticmethod
    def over(me, count, data, landed, final, sems):
        def at(ref):
            return lambda track, index: ref.at[track, index]

        return Halving(me, count, at(data), at(landed), at(final), sems)

    def partners(self):
        return [self.me + (1 - 2 * self.own(b)) * (1 << b) for b in range(self.bits)]

    def own(self, bit):
        return lax.rem(lax.div(self.me, 1 << bit), 2)

    def swaps(self, s):
        for track in (0, 1):
            order = [(i + track) % self.bits for i in range(self.bits)]
            bit = order[s]
            partner = self.me + (1 - 2 * self.own(bit)) * (1 << bit)
            fixed = sum(self.own(b) * (1 << b) for b in order[:s])
            for u in range(self.count >> (s + 1)):
                free = sum(((u >> i) & 1) << b for i, b in enumerate(order[s + 1 :]))
                slot = self.count - (self.count >> s) + u
                kept = fixed + free + self.own(bit) * (1 << bit)
                yield track, slot, partner, fixed + free + (1 - self.own(bit)) * (1 << bit), kept

    def out(self, track, slot, partner, given):
        return pltpu.make_async_remote_copy(
            src_ref=self.data(track, given),
            dst_ref=self.landed(track, slot),
            send_sem=self.out_send.at[track, slot],
            recv_sem=self.out_recv.at[track, slot],
            device_id={"dp": partner},
            device_id_type=MESH,
        )

    def back(self, track, slot, partner, segment):
        return pltpu.make_async_remote_copy(
            src_ref=self.final(track, segment),
            dst_ref=self.final(track, segment),
            send_sem=self.back_send.at[track, slot],
            recv_sem=self.back_recv.at[track, slot],
            device_id={"dp": partner},
            device_id_type=MESH,
        )

    def start(self, s=0):
        for track, slot, partner, given, _ in self.swaps(s):
            self.out(track, slot, partner, given).start()

    def turn(self, s):
        for track, slot, partner, given, kept in self.swaps(s):
            self.out(track, slot, partner, given).wait_recv()
            mine, theirs = self.data(track, kept), self.landed(track, slot)
            result = self.final(track, kept) if s == self.bits - 1 else mine
            blocks, rows, _ = mine.shape
            tile = tile_of(rows, 32)

            def add(r):
                block, at = lax.div(r, rows // tile), span(lax.rem(r, rows // tile), tile)
                result[block, at] = (mine[block, at].astype(F32) + theirs[block, at].astype(F32)).astype(BF16)

            loop(blocks * (rows // tile), add)
        if s < self.bits - 1:
            self.start(s + 1)
        else:
            self.start_back(s)

    def start_back(self, s):
        for track, slot, partner, _, kept in self.swaps(s):
            self.back(track, slot, partner, kept).start()

    def turn_back(self, s):
        for track, slot, partner, given, _ in self.swaps(s):
            self.back(track, slot, partner, given).wait_recv()
        if s > 0:
            self.start_back(s - 1)

    def events(self):
        steps = [functools.partial(self.turn, s) for s in range(self.bits)]
        return steps + [functools.partial(self.turn_back, s) for s in range(self.bits - 1, 0, -1)]

    def finish(self):
        self.turn_back(0)
        for s in range(self.bits):
            for track, slot, partner, given, kept in self.swaps(s):
                self.out(track, slot, partner, given).wait_send()
                self.back(track, slot, partner, kept).wait_send()


def fetching(kernel, which):
    def wrapped(*refs):
        refs = list(refs)
        sems = refs.pop()
        kept = refs[len(refs) - len(which) :]
        del refs[len(refs) - len(which) :]
        copies = {}
        for q, i in enumerate(which):
            copies[i] = pltpu.make_async_copy(refs[i], kept[q], sems.at[q])
            copies[i].start()
            refs[i] = kept[q]

        def arrive(*wanted):
            for i in wanted:
                copies[i].wait()

        return kernel(arrive, *refs)

    return wrapped


def fetched_specs(inputs, which, plain=()):
    specs = [ANY if i in which or i in plain else VM for i in range(len(inputs))]
    scratch = [pltpu.VMEM(inputs[i].shape, inputs[i].dtype) for i in which]
    return specs, scratch + [pltpu.SemaphoreType.DMA((len(which),))]


def comm_params(collective_id):
    return pltpu.CompilerParams(
        collective_id=collective_id, has_side_effects=True, vmem_limit_bytes=VMEM_LIMIT
    )


def cost(flops):
    return pl.CostEstimate(flops=int(flops), bytes_accessed=200_000_000, transcendentals=0)


def shape(*dims, dtype=F32):
    return jax.ShapeDtypeStruct(dims, dtype)


def inv_rms(values):
    return lax.rsqrt(jnp.mean(values * values, axis=-1, keepdims=True) + EPSILON)


def norm_grad(values, gain, gradient):
    inv = inv_rms(values)
    unit = values * inv
    scaled = gradient * gain
    centred = jnp.mean(scaled * unit, axis=-1, keepdims=True)
    return inv * (scaled - unit * centred), gradient * unit


def sigmoid(v):
    return 1.0 / (1.0 + jnp.exp(-v))


def gelu_parts(v):
    square = v * v
    bend = jnp.tanh(KAPPA * v * (1.0 + CUBIC * square))
    half = 0.5 * (1.0 + bend)
    slope = half + 0.5 * v * (1.0 - bend * bend) * (KAPPA * (1.0 + 3.0 * CUBIC * square))
    return v * half, slope


def one_minus_square(log_decay, decay):
    m = -2.0 * log_decay
    series = m * (
        1.0 - m * (1 / 2) * (1.0 - m * (1 / 3) * (1.0 - m * (1 / 4) * (1.0 - m * (1 / 5) * (1.0 - m * (1 / 6)))))
    )
    return jnp.where(m < 0.35, series, 1.0 - decay * decay)


def project_kernel(n, arrive, tokens, gain, w_in, w_br, normed, recur, branch, full, sent, came, held_a, held_b, saved):
    g = Place(n)
    gather = Gather(g, full, sent, came)
    part = 64

    def normalize(i):
        at = span(i, part)
        values = tokens[at].astype(F32)
        full[g.t, at] = (values * inv_rms(values) * gain[...].astype(F32)).astype(BF16)

    loop(full.shape[1] // part, normalize)
    g.greet()
    gather.start()
    arrive(2, 3)

    def use(t):
        pltpu.make_async_copy(full.at[t], normed.at[t], saved.at[t, 0]).start()
        held_a[t] = dot_nt(full[t], w_in[...])
        held_b[t] = dot_nt(full[t], w_br[...])
        pltpu.make_async_copy(held_a.at[t], recur.at[t], saved.at[t, 1]).start()
        pltpu.make_async_copy(held_b.at[t], branch.at[t], saved.at[t, 2]).start()

    gather.each(0, use)

    def away(i):
        gather.forward(i + 1)
        gather.each(i + 1, use)

    loop(g.nz - 1, away)

    def done(t):
        pltpu.make_async_copy(full.at[t], normed.at[t], saved.at[t, 0]).wait()
        pltpu.make_async_copy(held_a.at[t], recur.at[t], saved.at[t, 1]).wait()
        pltpu.make_async_copy(held_b.at[t], branch.at[t], saved.at[t, 2]).wait()

    loop(n, done)
    gather.finish()


def project(n, tokens, gain, w_in, w_br):
    rows, width = tokens.shape
    channels = w_in.shape[0]
    inputs = (tokens, gain, w_in, w_br)
    specs, kept = fetched_specs(inputs, (2, 3))
    return pl.pallas_call(
        fetching(functools.partial(project_kernel, n), (2, 3)),
        out_shape=(
            shape(n, rows, width, dtype=BF16),
            shape(n, rows, channels),
            shape(n, rows, channels),
        ),
        in_specs=specs,
        out_specs=(ANY,) * 3,
        scratch_shapes=Gather.scratch(n, rows, width)
        + [pltpu.VMEM((n, rows, channels), F32)] * 2
        + [pltpu.SemaphoreType.DMA((n, 3))]
        + kept,
        compiler_params=comm_params(1),
        cost_estimate=cost(4 * n * rows * width * channels),
        name="project",
    )(*inputs)


def recur_kernel(
    u, branch, start_state, start_conv, conv, gate_w, bias, decay,
    states, mixture, conv_low, recall, ingate, final_state, final_conv,
    hist, decay_buf, drive_buf, carry,
):
    chunk = pl.program_id(1)
    rows, channels = u.shape
    tile = 32

    @pl.when(chunk == 0)
    def _():
        carry[...] = jnp.broadcast_to(start_state[0], (8, channels))
        hist[0:8] = jnp.concatenate([jnp.zeros((5, channels), F32), start_conv[0]], axis=0)

    @pl.when(chunk > 0)
    def _():
        hist[0:8] = hist[rows : rows + 8]

    hist[8:] = u[...]

    def convolve(i):
        window = hist[pl.ds(pl.multiple_of(i * tile, tile), tile + 8)]
        value = conv[4:5] + conv[0:1] * window[8:] + conv[1:2] * window[7 : tile + 7]
        value = value + conv[2:3] * window[6 : tile + 6] + conv[3:4] * window[5 : tile + 5]
        conv_low[span(i, tile)] = value.astype(BF16)

    loop(rows // tile, convolve)
    low = conv_low[...]
    recall[...] = dot(low, gate_w[0])
    ingate[...] = dot(low, gate_w[1])

    def gates(i):
        at = span(i, tile)
        r = sigmoid(recall[at] + bias[0:1])
        k = sigmoid(ingate[at] + bias[1:2])
        recall[at] = r
        ingate[at] = k
        log_decay = -8.0 * r * decay[...]
        step = jnp.exp(log_decay)
        decay_buf[at] = step
        drive_buf[at] = jnp.sqrt(one_minus_square(log_decay, step)) * k * conv_low[at].astype(F32)

    loop(rows // tile, gates)
    row = lax.broadcasted_iota(jnp.int32, (8, channels), 0)

    def scan(i, before):
        for part in range(4):
            at = pl.ds(pl.multiple_of(i * 32 + part * 8, 8), 8)
            a, b = decay_buf[at], drive_buf[at]
            for shift in (1, 2, 4):
                inside = row >= shift
                b = b + a * jnp.where(inside, pltpu.roll(b, shift, 0), 0.0)
                a = a * jnp.where(inside, pltpu.roll(a, shift, 0), 1.0)
            h = a * before + b
            states[at] = h
            before = jnp.broadcast_to(h[7:8], (8, channels))
        return before

    carry[...] = lax.fori_loop(0, rows // 32, scan, carry[...])

    def mix(i):
        at = span(i, tile)
        value, _ = gelu_parts(branch[at])
        mixture[at] = (states[at] * value).astype(BF16)

    loop(rows // tile, mix)

    @pl.when(chunk == pl.num_programs(1) - 1)
    def _():
        final_state[0] = carry[0:1]
        final_conv[0] = hist[rows + 5 : rows + 8]


def recur_forward(u, branch, start_state, start_conv, conv, gate_w, bias, decay):
    total, channels = u.shape
    sequences = start_state.shape[0]
    length = total // sequences
    rows = tile_of(length, 256)
    chunks = length // rows
    block = pl.BlockSpec((rows, channels), lambda s, c: (s * chunks + c, 0))

    def whole(x):
        return pl.BlockSpec(x.shape, lambda s, c: (0,) * x.ndim)

    return pl.pallas_call(
        recur_kernel,
        grid=(sequences, chunks),
        out_shape=(
            shape(total, channels),
            shape(total, channels, dtype=BF16),
            shape(total, channels, dtype=BF16),
            shape(total, channels),
            shape(total, channels),
            shape(sequences, 1, channels),
            shape(sequences, 3, channels),
        ),
        in_specs=[
            block,
            block,
            pl.BlockSpec((1, 1, channels), lambda s, c: (s, 0, 0)),
            pl.BlockSpec((1, 3, channels), lambda s, c: (s, 0, 0)),
            whole(conv),
            whole(gate_w),
            whole(bias),
            whole(decay),
        ],
        out_specs=(block,) * 5
        + (
            pl.BlockSpec((1, 1, channels), lambda s, c: (s, 0, 0)),
            pl.BlockSpec((1, 3, channels), lambda s, c: (s, 0, 0)),
        ),
        scratch_shapes=[
            pltpu.VMEM((rows + 8, channels), F32),
            pltpu.VMEM((rows, channels), F32),
            pltpu.VMEM((rows, channels), F32),
            pltpu.VMEM((8, channels), F32),
        ],
        compiler_params=pltpu.CompilerParams(vmem_limit_bytes=VMEM_LIMIT),
        name="recur_forward",
    )(u, branch, start_state, start_conv, conv, gate_w, bias, decay)


def mixer_out_kernel(
    n, arrive, mixture, w_output, cotangent, tokens, gain, cot_full, residual, normed,
    full, sent, came, saved, *bufs
):
    g = Place(n)
    gather = Gather(g, full, sent, came)
    scatter = Scatter(g, lambda t, cols: dot(mixture[t], w_output[:, cols]), tile_of(residual.shape[1], 512), bufs)
    first = pltpu.make_async_copy(cotangent, full.at[g.t], saved.at[0])
    first.start()
    g.greet()
    first.wait()
    gather.start()
    arrive(0, 1)

    def use(t):
        pltpu.make_async_copy(full.at[t], cot_full.at[t], saved.at[t]).start()

    scatter.offers(g.nz - 1)

    def around(i):
        d = g.nz - 1 - i
        scatter.offers(d - 1)
        scatter.step(d)
        gather.each(i, use)
        gather.forward(i + 1)

    loop(g.nz - 1, around)
    scatter.last()
    arrive(3)
    part = 64

    def rows_of(i):
        at = span(i, part)
        values = scatter.acc[at] + tokens[at].astype(F32)
        residual[at] = values
        normed[at] = (values * inv_rms(values) * gain[...].astype(F32)).astype(BF16)

    loop(residual.shape[0] // part, rows_of)
    gather.each(g.nz - 1, use)
    loop(n, lambda t: pltpu.make_async_copy(full.at[t], cot_full.at[t], saved.at[t]).wait())
    scatter.finish()
    gather.finish()


def mixer_out(n, mixture, w_output, cotangent, tokens, gain):
    rows, width = tokens.shape
    inputs, which = (mixture, w_output, cotangent, tokens, gain), (0, 1, 3)
    specs, kept = fetched_specs(inputs, which, (2,))
    return pl.pallas_call(
        fetching(functools.partial(mixer_out_kernel, n), which),
        out_shape=(
            shape(n, rows, width, dtype=BF16),
            shape(rows, width),
            shape(rows, width, dtype=BF16),
        ),
        in_specs=specs,
        out_specs=(ANY, VM, VM),
        scratch_shapes=Gather.scratch(n, rows, width)
        + [pltpu.SemaphoreType.DMA((n,))]
        + Scatter.scratch(n, rows, width)
        + kept,
        compiler_params=comm_params(2),
        cost_estimate=cost(2 * n * rows * width * mixture.shape[-1]),
        name="mixer_out",
    )(*inputs)


def mlp_kernel(
    n, copies, arrive, normed, cot_full, w_gelu, w_linear, w_down, residual, gain,
    hidden, grad_gelu, grad_linear, grad_down, g_residual, g_low, g_gain,
    full, sent, came, cot, keep_h, keep_f, keep_s, acc_g, acc_l, acc_d,
    to_sib, sums, line, acc, landed, swap_sems, saved, fetched, drained, sib_sent, sib_came, line_sent, line_came,
):
    g = Place(n)
    gather = Gather(g, full, sent, came)
    columns = w_gelu.shape[1]
    rows, width = acc.shape
    tile = tile_of(columns, 256)
    wide = tile_of(width, 512)
    strip = rows // PARTS
    me = lax.axis_index("dp")
    start = pltpu.make_async_copy(normed, full.at[g.t], saved.at[0])
    start.start()
    part_width = width // (2 * copies)
    depth = columns // rows

    def segment(track, index):
        return pl.ds(pl.multiple_of((track * copies + index) * part_width, part_width), part_width)

    swap = Halving(
        me,
        copies,
        lambda track, index: full.at[0:depth, :, segment(track, index)],
        lambda track, slot: landed.at[track, slot],
        lambda track, index: full.at[depth : 2 * depth, :, segment(track, index)],
        swap_sems,
    )
    def fetch(t, q):
        return pltpu.make_async_copy(cot_full.at[t], cot.at[q], fetched.at[q])

    g.greet(swap.partners())
    start.wait()
    gather.start()
    fetch(2 * g.j, 0).start()
    fetch(2 * g.j + 1, 1).start()
    arrive(2, 3, 4)
    acc_g[...] = jnp.zeros_like(acc_g)
    acc_l[...] = jnp.zeros_like(acc_l)
    acc_d[...] = jnp.zeros_like(acc_d)

    def save(t, q):
        return pltpu.make_async_copy(keep_h.at[q], hidden.at[t], saved.at[q])

    def layer(t, q):
        fetch(t, q).wait()

        def part(i):
            cols = span(i, tile)
            first = dot(full[t], w_gelu[:, cols])
            second = dot(full[t], w_linear[:, cols])
            back = dot_nt(cot[q], w_down[cols])
            value, slope = gelu_parts(first)
            keep_h[q, :, cols] = (value * second).astype(BF16)
            keep_f[q, :, cols] = (back * second * slope).astype(BF16)
            keep_s[q, :, cols] = (back * value).astype(BF16)

        loop(columns // tile, part)
        save(t, q).start()

    def partial(q, cols):
        return dot_nt(keep_f[q], w_gelu[cols]) + dot_nt(keep_s[q], w_linear[cols])

    def sib_copy(k):
        return g.copy(to_sib, sums.at[k], sib_sent, sib_came.at[k], g.sib)

    def line_copy(k, slot, p, to):
        at = pl.ds(pl.multiple_of(p * strip, strip), strip)
        return g.copy(
            sums.at[k, at], line.at[slot, at], line_sent.at[k, p], line_came.at[slot, p], to
        )

    def chip(d, way):
        k = g.j + way * d
        mine, its = g.c, 1 - g.c
        own, other = 2 * k + mine, 2 * k + its
        for p in range(gather.pieces):
            gather.copy(other, p, 2, g.sib).wait_recv()
        layer(other, its)

        def offer(i):
            cols = span(i, wide)
            to_sib[:, cols] = partial(its, cols).astype(BF16)

        loop(width // wide, offer)
        sib_copy(k).start()
        layer(own, mine)
        sib_copy(k).wait()

        @pl.when(d == 0)
        def _():
            def part(i):
                cols = span(i, wide)
                acc[:, cols] = partial(mine, cols) + sums[k, :, cols].astype(F32)

            loop(width // wide, part)

        @pl.when(d > 0)
        def _():
            def part(i):
                cols = span(i, wide)
                sums[k, :, cols] = (partial(mine, cols) + sums[k, :, cols].astype(F32)).astype(BF16)

            loop(width // wide, part)
            first = jnp.logical_or(
                jnp.logical_and(way > 0, jnp.logical_not(g.has_down)),
                jnp.logical_and(way < 0, jnp.logical_not(g.has_up)),
            )

            @pl.when(first)
            def _():
                slot = jnp.where(jnp.logical_and(way < 0, d == 1), g.nz, k)
                for p in range(PARTS):
                    line_copy(k, slot, p, g.t + 2 * way).start()

        def part(i):
            at = span(i, wide)
            both = full[pl.ds(2 * k, 2), :, at].reshape(2 * rows, wide)
            acc_g[at] += dot_tn(both, keep_f[...].reshape(2 * rows, columns))
            acc_l[at] += dot_tn(both, keep_s[...].reshape(2 * rows, columns))
            acc_d[:, at] += dot_tn(
                keep_h[...].reshape(2 * rows, columns), cot[:, :, at].reshape(2 * rows, wide)
            )

        loop(width // wide, part)
        both_ways = jnp.logical_and(g.j + d < g.nz, g.j - d >= 0)
        again = jnp.logical_and(both_ways, jnp.logical_and(way > 0, d > 0))
        later = jnp.where(g.j + d + 1 < g.nz, g.j + d + 1, g.j - d - 1)
        following = jnp.where(again, g.j - d, later)

        @pl.when(following >= 0)
        def _():
            fetch(2 * following, 0).start()
            fetch(2 * following + 1, 1).start()

        save(other, its).wait()
        save(own, mine).wait()

    def relay(m, events=()):
        def take(k, slot, sign, p):
            at = pl.ds(pl.multiple_of(p * strip, strip), strip)
            line_copy(k, slot, p, g.sib).wait_recv()

            @pl.when(k == g.j)
            def _():
                acc[at] += line[slot, at].astype(F32)

            @pl.when(k != g.j)
            def _():
                sums[k, at] = (sums[k, at].astype(F32) + line[slot, at].astype(F32)).astype(BF16)
                there = jnp.where(jnp.logical_and(sign < 0, k == g.j - 1), g.nz, k)
                line_copy(k, there, p, g.t + 2 * sign).start()

        def rise(p):
            pl.when(jnp.logical_and(g.has_down, m >= g.j))(lambda: take(m, m, 1, p))

        def fall(p):
            k = g.nz - 1 - m
            pl.when(jnp.logical_and(g.has_up, k <= g.j))(
                lambda: take(k, jnp.where(k == g.j, g.nz, k), -1, p)
            )

        lower = 2 * g.j < g.nz

        def strips(i):
            @pl.when(i < PARTS)
            def _():
                pl.when(lower)(lambda: rise(i))
                pl.when(jnp.logical_not(lower))(lambda: fall(i))

            @pl.when(i > 0)
            def _():
                pl.when(lower)(lambda: fall(i - 1))
                pl.when(jnp.logical_not(lower))(lambda: rise(i - 1))

        def between(i):
            strips(i)
            for q, event in enumerate(events):
                pl.when(i == (q + 1) * PARTS // len(events))(event)

        loop(PARTS + 1, between)

    def cores(d):
        up, down = g.j + d < g.nz, g.j - d >= 0

        def way_of(w):
            both = jnp.logical_and(up, down)
            way = jnp.where(jnp.logical_and(w == 0, up), 1, -1)
            wanted = jnp.where(w == 0, jnp.logical_or(up, down), jnp.logical_and(both, d > 0))
            pl.when(wanted)(lambda: chip(d, way))

            @pl.when(d < g.nz - 1)
            def _():
                for p in range(gather.pieces):
                    pl.when(w == min(p, 1))(lambda: gather.forward(d + 1, (p,)))

        loop(2, way_of)

    def step(d):
        @pl.when(d < g.nz)
        def _():
            cores(d)

        @pl.when(d == g.nz - 1)
        def _():
            gather.finish()
            for i in range(depth):
                full[i] = acc_d[pl.ds(i * rows, rows)].astype(BF16)
            swap.start()

        pl.when(d > 1)(lambda: relay(d - 1))

    loop(g.nz, step)

    stages = [held.at[q] for held in (keep_h, keep_f, keep_s) for q in (0, 1)]
    leaving = []

    def leave(i, value, out):
        slot = i % len(stages)
        if len(leaving) >= len(stages):
            leaving[i - len(stages)].wait()
        stages[slot][...] = value.astype(BF16)
        copy = pltpu.make_async_copy(stages[slot], out, drained.at[slot])
        copy.start()
        leaving.append(copy)

    for i in range(width // rows):
        at = pl.ds(i * rows, rows)
        leave(2 * i, acc_g[at], grad_gelu.at[at])
        leave(2 * i + 1, acc_l[at], grad_linear.at[at])
    events = swap.events()
    events.pop(0)()
    relay(g.nz - 1, events)
    own = pltpu.make_async_copy(cot_full.at[g.t], cot.at[0], fetched.at[0])
    own.start()
    own.wait()
    arrive(5)
    lines = 32
    g_gain[...] = jnp.zeros_like(g_gain)

    def rows_of(i):
        at = span(i, lines)
        back, terms = norm_grad(residual[at], gain[...].astype(F32), acc[at])
        value = cot[0, at].astype(F32) + back
        acc[at] = value
        cot[1, at] = value.astype(BF16)
        g_gain[...] += jnp.sum(terms, axis=0, keepdims=True)

    loop(rows // lines, rows_of)
    last = [
        pltpu.make_async_copy(acc, g_residual, saved.at[0]),
        pltpu.make_async_copy(cot.at[1], g_low, saved.at[1]),
    ]
    swap.finish()
    for i in range(depth):
        at = pl.ds(i * rows, rows)
        last.append(pltpu.make_async_copy(full.at[depth + i], grad_down.at[at], drained.at[len(stages) + i]))
    for copy in last:
        copy.start()
    for copy in leaving[-len(stages) :] + last:
        copy.wait()

    def done(k):
        @pl.when(k != g.j)
        def _():
            for p in range(PARTS):
                line_copy(k, k, p, g.sib).wait_send()

    loop(g.nz, done)


def mlp(n, copies, normed, cot_full, w_gelu, w_linear, w_down, residual, gain):
    rows, width = normed.shape
    columns = w_gelu.shape[1]
    kept = pltpu.VMEM((2, rows, columns), BF16)
    sems = pltpu.SemaphoreType.DMA
    inputs, which = (normed, cot_full, w_gelu, w_linear, w_down, residual, gain), (2, 3, 4, 5)
    specs, held = fetched_specs(inputs, which, (0, 1))
    return pl.pallas_call(
        fetching(functools.partial(mlp_kernel, n, copies), which),
        out_shape=(shape(n, rows, columns, dtype=BF16),)
        + (shape(width, columns, dtype=BF16),) * 2
        + (
            shape(columns, width, dtype=BF16),
            shape(rows, width),
            shape(rows, width, dtype=BF16),
            shape(1, width),
        ),
        in_specs=specs,
        out_specs=(ANY,) * 6 + (VM,),
        scratch_shapes=Gather.scratch(n, rows, width)
        + [pltpu.VMEM((2, rows, width), BF16)]
        + [kept] * 3
        + [pltpu.VMEM((width, columns), F32)] * 2
        + [
            pltpu.VMEM((columns, width), F32),
            pltpu.VMEM((rows, width), BF16),
            pltpu.VMEM((n // 2, rows, width), BF16),
            pltpu.VMEM((n // 2 + 1, rows, width), BF16),
            pltpu.VMEM((rows, width), F32),
            pltpu.VMEM((2, copies - 1, columns // rows, rows, width // (2 * copies)), BF16),
            sems((4, 2, copies - 1)),
            sems((2,)),
            sems((2,)),
            sems((6 + columns // rows,)),
            sems,
            sems((n // 2,)),
            sems((n // 2, PARTS)),
            sems((n // 2 + 1, PARTS)),
        ]
        + held,
        compiler_params=comm_params(3),
        cost_estimate=cost(16 * n * rows * width * columns),
        name="mlp",
    )(*inputs)


def down_kernel(
    n, arrive, hidden, w_down, residual, g_low, w_output, mixture, output, g_mixture, grad_output,
    full, sent, came, acc_o, start_sem, *bufs
):
    g = Place(n)
    gather = Gather(g, full, sent, came)
    width = residual.shape[1]
    wide = tile_of(width, 512)
    scatter = Scatter(g, lambda t, cols: dot(hidden[t], w_down[:, cols]), wide, bufs)
    first = pltpu.make_async_copy(g_low, full.at[g.t], start_sem)
    first.start()
    g.greet()
    first.wait()

    def use(t):
        g_mixture[t] = dot_nt(full[t], w_output[...])

        def part(i):
            at = span(i, wide)
            acc_o[:, at] += dot_tn(mixture[t], full[t, :, at])

        loop(width // wide, part)

    gather.start()
    acc_o[...] = jnp.zeros_like(acc_o)
    arrive(0, 1)
    scatter.offers(g.nz - 1)
    arrive(4, 5)

    def around(i):
        d = g.nz - 1 - i
        scatter.offers(d - 1)
        scatter.step(d)
        gather.each(i, use)
        gather.forward(i + 1)

    loop(g.nz - 1, around)
    gather.each(g.nz - 1, use)
    grad_output[...] = acc_o[...].astype(BF16)
    scatter.last()
    arrive(2)
    output[...] = (scatter.acc[...] + residual[...]).astype(BF16)
    scatter.finish()
    gather.finish()


def down(n, hidden, w_down, residual, g_low, w_output, mixture):
    rows, width = residual.shape
    channels = w_output.shape[0]
    inputs, which = (hidden, w_down, residual, g_low, w_output, mixture), (0, 1, 4, 5, 2)
    specs, kept = fetched_specs(inputs, which, (3,))
    return pl.pallas_call(
        fetching(functools.partial(down_kernel, n), which),
        out_shape=(
            shape(rows, width, dtype=BF16),
            shape(n, rows, channels),
            shape(channels, width, dtype=BF16),
        ),
        in_specs=specs,
        out_specs=(VM,) * 3,
        scratch_shapes=Gather.scratch(n, rows, width)
        + [pltpu.VMEM((channels, width), F32), pltpu.SemaphoreType.DMA]
        + Scatter.scratch(n, rows, width)
        + kept,
        compiler_params=comm_params(5),
        cost_estimate=cost(2 * n * rows * width * (hidden.shape[-1] + 2 * channels)),
        name="down",
    )(*inputs)


def recur_back_kernel(
    g_mix, branch, states, states_before, u, u_before, conv_low, recall, ingate, start_state, start_conv,
    conv, gate_w, decay,
    g_recur, g_branch, small, g_gates,
    g_state, step_buf, root_buf, g_conv, pre_r, pre_i, carry, hist_s, hist_u, sums,
):
    sequence, back = pl.program_id(0), pl.program_id(1)
    last = pl.num_programs(1) - 1
    rows, channels = u.shape
    tile = 32

    @pl.when(jnp.logical_and(sequence == 0, back == 0))
    def _():
        sums[...] = jnp.zeros_like(sums)
        g_gates[...] = jnp.zeros_like(g_gates)

    @pl.when(back == 0)
    def _():
        carry[...] = jnp.zeros_like(carry)
        g_conv[rows : rows + 8] = jnp.zeros((8, channels), F32)

    @pl.when(back > 0)
    def _():
        g_conv[rows : rows + 8] = g_conv[0:8]

    @pl.when(back == last)
    def _():
        hist_s[0:8] = jnp.broadcast_to(start_state[0], (8, channels))
        hist_u[0:8] = jnp.concatenate([jnp.zeros((5, channels), F32), start_conv[0]], axis=0)

    @pl.when(back < last)
    def _():
        hist_s[0:8] = states_before[...]
        hist_u[0:8] = u_before[...]

    hist_s[8:] = states[...]
    hist_u[8:] = u[...]

    def first(i):
        at = span(i, tile)
        value, slope = gelu_parts(branch[at])
        gm = g_mix[at]
        g_state[at] = gm * value
        g_branch[at] = (gm * states[at] * slope).astype(BF16)
        log_decay = -8.0 * recall[at] * decay[...]
        step = jnp.exp(log_decay)
        step_buf[at] = step
        root_buf[at] = jnp.sqrt(one_minus_square(log_decay, step))

    loop(rows // tile, first)
    row = lax.broadcasted_iota(jnp.int32, (8, channels), 0)
    groups = rows // 32

    def scan(i, after):
        for part in range(4):
            at = pl.ds(pl.multiple_of((groups - 1 - i) * 32 + (3 - part) * 8, 8), 8)
            a, gs = step_buf[at], g_state[at]
            b = a * gs
            for shift in (1, 2, 4):
                inside = row < 8 - shift
                b = b + a * jnp.where(inside, pltpu.roll(b, 8 - shift, 0), 0.0)
                a = a * jnp.where(inside, pltpu.roll(a, 8 - shift, 0), 1.0)
            e = a * after + b
            g_state[at] = gs + jnp.where(row < 7, pltpu.roll(e, 7, 0), after)
            after = jnp.broadcast_to(e[0:1], (8, channels))
        return after

    carry[...] = lax.fori_loop(0, groups, scan, carry[...])

    def fold(x):
        return jnp.sum(x.reshape(tile // 8, 8, channels), axis=0)

    def second(i):
        at = span(i, tile)
        window = hist_s[pl.ds(pl.multiple_of(i * tile, tile), tile + 8)]
        before = window[7 : tile + 7]
        g, r, k = g_state[at], recall[at], ingate[at]
        c = conv_low[at].astype(F32)
        step, root = step_buf[at], root_buf[at]
        kc = k * c
        g_log = g * (before * step - kc * (step * step) / root)
        slow = -8.0 * r
        sums[7] += fold(g_log * slow)
        low_r = (g_log * (slow * decay[...]) * (1.0 - r)).astype(BF16)
        low_i = (g * root * kc * (1.0 - k)).astype(BF16)
        pre_r[at] = low_r
        pre_i[at] = low_i
        sums[5] += fold(low_r.astype(F32))
        sums[6] += fold(low_i.astype(F32))
        g_conv[at] = g * root * k

    loop(rows // tile, second)
    low_r, low_i, low_c = pre_r[...], pre_i[...], conv_low[...]
    g_gates[0] += dot_tn(low_c, low_r)
    g_gates[1] += dot_tn(low_c, low_i)
    g_conv[0:rows] += dot_nt(low_r, gate_w[0]) + dot_nt(low_i, gate_w[1])

    def third(i):
        at = span(i, tile)
        start = pl.multiple_of(i * tile, tile)
        window = g_conv[pl.ds(start, tile + 8)]
        value = conv[0:1] * window[0:tile]
        for k in (1, 2, 3):
            value = value + conv[k : k + 1] * window[k : tile + k]
        g_recur[at] = value.astype(BF16)
        past = hist_u[pl.ds(start, tile + 8)]
        gc = window[0:tile]
        for k in range(4):
            sums[k] += fold(gc * past[8 - k : tile + 8 - k])
        sums[4] += fold(gc)

    loop(rows // tile, third)

    @pl.when(jnp.logical_and(sequence == pl.num_programs(0) - 1, back == last))
    def _():
        small[...] = jnp.sum(sums[...], axis=1)


def recur_back(g_mix, branch, states, u, conv_low, recall, ingate, start_state, start_conv, conv, gate_w, decay):
    total, channels = u.shape
    sequences = start_state.shape[0]
    length = total // sequences
    rows = tile_of(length, 256)
    chunks = length // rows
    eights = rows // 8

    def at(s, c):
        return (s * chunks + chunks - 1 - c, 0)

    def earlier(s, c):
        return (jnp.maximum((s * chunks + chunks - 1 - c) * eights - 1, 0), 0)

    block = pl.BlockSpec((rows, channels), at)
    before = pl.BlockSpec((8, channels), earlier)

    def whole(x):
        return pl.BlockSpec(x.shape, lambda s, c: (0,) * x.ndim)

    wide = pltpu.VMEM((rows, channels), F32)
    narrow = pltpu.VMEM((rows, channels), BF16)
    long = pltpu.VMEM((rows + 8, channels), F32)
    return pl.pallas_call(
        recur_back_kernel,
        grid=(sequences, chunks),
        out_shape=(
            shape(total, channels, dtype=BF16),
            shape(total, channels, dtype=BF16),
            shape(8, channels),
            shape(2, channels, channels),
        ),
        in_specs=[
            block, block, block, before, block, before, block, block, block,
            pl.BlockSpec((1, 1, channels), lambda s, c: (s, 0, 0)),
            pl.BlockSpec((1, 3, channels), lambda s, c: (s, 0, 0)),
            whole(conv), whole(gate_w), whole(decay),
        ],
        out_specs=(
            block,
            block,
            pl.BlockSpec((8, channels), lambda s, c: (0, 0)),
            pl.BlockSpec((2, channels, channels), lambda s, c: (0, 0, 0)),
        ),
        scratch_shapes=[
            wide, wide, wide, long, narrow, narrow,
            pltpu.VMEM((8, channels), F32), long, long,
            pltpu.VMEM((8, 8, channels), F32),
        ],
        compiler_params=pltpu.CompilerParams(vmem_limit_bytes=VMEM_LIMIT),
        name="recur_back",
    )(g_mix, branch, states, states, u, u, conv_low, recall, ingate, start_state, start_conv, conv, gate_w, decay)


def input_back_kernel(
    n, copies, arrive, g_recur, g_branch, w_in, w_br, normed, tokens, g_residual, gain, second_gain, g_gates, small, g_out,
    input_grad, in_out, br_out, out_out, gates_out, conv_out, bias_out, decay_out, gains_out,
    gain_row, gain_parts, gain_in, gain_sum, gain_dp, gain_sent, gain_came, gain_dp_sent, gain_dp_came, *bufs
):
    g = Place(n)
    me = lax.axis_index("dp")
    rows, width = tokens.shape
    channels = w_in.shape[0]
    blocks, block_width = gates_out.shape[1], gates_out.shape[2]
    segment = width // (2 * copies)
    gain_width = width // n
    weights = Halving.over(me, copies, *bufs[:4])
    rest = Halving.over(me, copies, *bufs[4:8])
    padded = bufs[0].shape[3] // 3
    rest_rows = bufs[4].shape[3]

    def block(ref, t):
        return ref[span(t, rows)]

    def partial(t, cols):
        return dot(block(g_recur, t), w_in[:, cols]) + dot(block(g_branch, t), w_br[:, cols])

    scatter = Scatter(g, partial, tile_of(width, 512), bufs[8:])

    def gain_copy(t, slot):
        return g.copy(gain_parts.at[t], gain_in.at[slot], gain_sent.at[t], gain_came.at[slot], t)

    def gain_dp_copy(i, slot):
        return pltpu.make_async_remote_copy(
            src_ref=gain_sum,
            dst_ref=gain_dp.at[slot],
            send_sem=gain_dp_sent.at[i],
            recv_sem=gain_dp_came.at[slot],
            device_id={"dp": i},
            device_id_type=MESH,
        )

    def others(act):
        loop(n, lambda t: pl.when(t != g.t)(lambda: act(t)))

    def copies_of(act):
        loop(copies, lambda i: pl.when(i != me)(lambda: act(i)))

    barrier = pltpu.get_barrier_semaphore()
    others(
        lambda t: pl.semaphore_signal(barrier, inc=1, device_id={"tensor": t}, device_id_type=MESH)
    )
    copies_of(lambda i: pl.semaphore_signal(barrier, inc=1, device_id={"dp": i}, device_id_type=MESH))
    pl.semaphore_wait(barrier, n - 1 + copies - 1)

    arrive(0, 1, 2, 3)
    scatter.offers(g.nz - 1)

    def around(i):
        d = g.nz - 1 - i
        scatter.offers(d - 1)
        scatter.step(d)

    around(0)
    arrive(4, 11, 9)

    data = bufs[0]

    def weigh(q):
        cols = span(q, 2 * segment)
        first = dot_tn(g_recur[...], normed[:, cols])
        second = dot_tn(g_branch[...], normed[:, cols])
        third = g_out[:, cols]
        for half in (0, 1):
            index = 2 * q + half
            track, part = lax.div(index, copies), lax.rem(index, copies)
            for i, value in enumerate((first, second, third)):
                piece = value[:, half * segment : (half + 1) * segment].astype(BF16)
                data[track, part, 0, i * padded : i * padded + channels] = piece
                if padded > channels:
                    data[track, part, 0, i * padded + channels : (i + 1) * padded] = jnp.zeros(
                        (padded - channels, segment), BF16
                    )
        terms = jnp.sum(w_in[:, cols].astype(F32) * first + w_br[:, cols].astype(F32) * second, axis=0, keepdims=True)
        gain_row[0:1, cols] = terms / gain[0:1, cols].astype(F32)

    loop(copies, weigh)
    weights.start()
    gain_row[1:2] = second_gain[...]
    gain_row[2:8] = jnp.zeros((6, width), F32)
    for t in range(n):
        gain_parts[t] = gain_row[:, t * gain_width : (t + 1) * gain_width]
    others(lambda t: gain_copy(t, g.t).start())
    gain_in[g.t] = gain_parts[g.t]

    flat = jnp.concatenate(
        [
            g_gates[0],
            g_gates[1],
            small[...],
            jnp.zeros((2 * copies * rest_rows - 2 * channels - 8, channels), F32),
        ],
        axis=0,
    ).astype(BF16)
    for i in range(2 * copies):
        bufs[4][i // copies, i % copies, 0] = flat[i * rest_rows : (i + 1) * rest_rows]
    rest.start()

    events = [lambda a=a, b=b: (a(), b()) for a, b in zip(weights.events(), rest.events())]
    for i in range(1, g.nz - 1):
        around(i)
        if events:
            events.pop(0)()
        if i == 1:
            others(lambda t: gain_copy(t, t).wait_recv())
            total = gain_in[0]
            for t in range(1, n):
                total = total + gain_in[t]
            gain_sum[...] = total
            copies_of(lambda i: gain_dp_copy(i, me).start())
            gain_dp[me] = total
    for event in events:
        event()
    scatter.last()
    arrive(5, 6)
    part = 32

    def rows_of(i):
        at = span(i, part)
        back, _ = norm_grad(tokens[at].astype(F32), gain[...].astype(F32), scatter.acc[at])
        input_grad[at] = g_residual[at] + back

    loop(rows // part, rows_of)
    copies_of(lambda i: gain_dp_copy(i, i).wait_recv())
    total = gain_dp[0]
    for i in range(1, copies):
        total = total + gain_dp[i]
    gains_out[...] = total
    rest.finish()
    flat = jnp.concatenate([bufs[6][i // copies, i % copies, 0].astype(F32) for i in range(2 * copies)], axis=0)
    for q in (0, 1):
        for i in range(blocks):
            start = q * channels + i * block_width
            gates_out[q, i] = flat[start : start + block_width, i * block_width : (i + 1) * block_width]
    conv_out[...] = flat[2 * channels : 2 * channels + 5]
    bias_out[...] = flat[2 * channels + 5 : 2 * channels + 7]
    decay_out[...] = flat[2 * channels + 7 : 2 * channels + 8]
    weights.finish()
    for i in range(2 * copies):
        for q, out in enumerate((in_out, br_out, out_out)):
            out[:, i * segment : (i + 1) * segment] = bufs[2][
                i // copies, i % copies, 0, q * padded : q * padded + channels
            ]
    others(lambda t: gain_copy(t, t).wait_send())
    copies_of(lambda i: gain_dp_copy(i, i).wait_send())
    scatter.finish()


def up_to(extent, multiple):
    return (extent + multiple - 1) // multiple * multiple


def input_back(
    n, copies, g_recur, g_branch, w_in, w_br, normed, tokens, g_residual, gain, second_gain, g_gates, small, g_out,
    blocks,
):
    rows, width = tokens.shape
    channels = w_in.shape[0]
    block = channels // blocks
    rest_rows = up_to((2 * channels + 8 + 2 * copies - 1) // (2 * copies), 16)
    gain_shape = (8, width // n)
    sems = pltpu.SemaphoreType.DMA
    inputs = (g_recur, g_branch, w_in, w_br, normed, tokens, g_residual, gain, second_gain, g_gates, small, g_out)
    which = (0, 1, 2, 3, 4, 11, 9, 5, 6)
    specs, kept = fetched_specs(inputs, which)
    return pl.pallas_call(
        fetching(functools.partial(input_back_kernel, n, copies), which),
        out_shape=(shape(rows, width),)
        + (shape(channels, width, dtype=BF16),) * 3
        + (
            shape(2, blocks, block, block),
            shape(5, channels),
            shape(2, channels),
            shape(1, channels),
            shape(*gain_shape),
        ),
        in_specs=specs,
        out_specs=(VM,) * 9,
        scratch_shapes=[
            pltpu.VMEM((8, width), F32),
            pltpu.VMEM((n, *gain_shape), F32),
            pltpu.VMEM((n, *gain_shape), F32),
            pltpu.VMEM(gain_shape, F32),
            pltpu.VMEM((copies, *gain_shape), F32),
            sems((n,)),
            sems((n,)),
            sems((copies,)),
            sems((copies,)),
        ]
        + Halving.scratch(copies, 3 * up_to(channels, 16), width // (2 * copies))
        + Halving.scratch(copies, rest_rows, channels)
        + Scatter.scratch(n, rows, width)
        + kept,
        compiler_params=comm_params(6),
        cost_estimate=cost(8 * n * rows * width * channels),
        name="input_back",
    )(*inputs)


def body(
    n,
    copies,
    tokens,
    cotangent,
    resets,
    init_state,
    init_conv,
    norm_gain,
    w_input,
    w_branch,
    conv_params,
    gate_weights,
    gate_bias,
    decay_rate,
    w_output,
    mlp_gain,
    w_gelu,
    w_linear,
    w_down,
):
    rows, width = tokens.shape
    total = rows * n
    channels = w_input.shape[1]
    blocks, block = gate_weights.shape[1], gate_weights.shape[2]
    survive = (1 - resets).astype(F32)
    start_state = (init_state * survive[:, None])[:, None]
    start_conv = init_conv * survive[:, None, None]
    gain_first, gain_second = norm_gain[None], mlp_gain[None]
    gate_w = (gate_weights[:, :, :, None] * jnp.eye(blocks, dtype=BF16)[None, :, None, :, None]).reshape(
        2, channels, channels
    )
    decay = decay_rate[None]
    w_in, w_br = w_input.T, w_branch.T

    def flat(x):
        return x.reshape(total, x.shape[-1])

    def blocked(x):
        return x.reshape(n, rows, x.shape[-1])

    normed, recur, branch = project(n, tokens, gain_first, w_in, w_br)
    recur, branch = flat(recur), flat(branch)
    states, mixture, conv_low, recall, ingate, final_state, final_conv = recur_forward(
        recur, branch, start_state, start_conv, conv_params, gate_w, gate_bias, decay
    )
    mixture = blocked(mixture)
    cot_full, residual, normed_mlp = mixer_out(n, mixture, w_output, cotangent, tokens, gain_second)
    hidden, grad_gelu, grad_linear, grad_down, g_residual, g_low, gain_second_grad = mlp(
        n, copies, normed_mlp, cot_full, w_gelu, w_linear, w_down, residual, gain_second
    )
    mlp_sums = lax.psum((grad_gelu, grad_linear), "dp")
    output, g_mixture, grad_output = down(n, hidden, w_down, residual, g_low, w_output, mixture)
    g_recur, g_branch, small, g_gates = recur_back(
        flat(g_mixture), branch, states, recur, conv_low, recall, ingate, start_state, start_conv,
        conv_params, gate_w, decay,
    )
    input_grad, grad_input, grad_branch, grad_output, gates, g_conv, g_bias, g_decay, gains = input_back(
        n, copies, g_recur, g_branch, w_in, w_br, flat(normed), tokens, g_residual, gain_first,
        gain_second_grad, g_gates, small, grad_output, blocks,
    )
    grad_gelu, grad_linear = (x.astype(F32) for x in mlp_sums)
    grad_down = grad_down.astype(F32)
    return (
        output,
        input_grad,
        final_state[:, 0],
        final_conv,
        gains[0],
        grad_input.astype(F32).T,
        grad_branch.astype(F32).T,
        g_conv,
        gates,
        g_bias,
        g_decay[0],
        grad_output.astype(F32),
        gains[1],
        grad_gelu,
        grad_linear,
        grad_down,
    )


def solution(mesh):
    in_specs = (
        P(("dp", "tensor"), None),
        P(("dp", "tensor"), None),
        P("dp"),
        P("dp", "tensor"),
        P("dp", None, "tensor"),
        P(),
        P(None, "tensor"),
        P(None, "tensor"),
        P(None, "tensor"),
        P(None, "tensor", None, None),
        P(None, "tensor"),
        P("tensor"),
        P("tensor", None),
        P(),
        P(None, "tensor"),
        P(None, "tensor"),
        P("tensor", None),
    )
    out_specs = (
        P(("dp", "tensor"), None),
        P(("dp", "tensor"), None),
        P("dp", "tensor"),
        P("dp", None, "tensor"),
        P("tensor"),
        P(None, "tensor"),
        P(None, "tensor"),
        P(None, "tensor"),
        P(None, "tensor", None, None),
        P(None, "tensor"),
        P("tensor"),
        P("tensor", None),
        P("tensor"),
        P(None, "tensor"),
        P(None, "tensor"),
        P("tensor", None),
    )
    return jax.shard_map(
        functools.partial(body, mesh.shape["tensor"], mesh.shape["dp"]),
        mesh=mesh,
        in_specs=in_specs,
        out_specs=out_specs,
        check_vma=False,
    )
```

```python
import functools

import jax
import jax.numpy as jnp
from jax import lax
from jax.experimental import pallas as pl
from jax.experimental.pallas import tpu as pltpu
from jax.sharding import PartitionSpec as P

EPSILON = 1e-06
KAPPA = 0.7978845608028654
CUBIC = 0.044715
PIECES = 2
STRIPS = 4
PARTS = 8
F32 = jnp.float32
BF16 = jnp.bfloat16
ANY = pl.BlockSpec(memory_space=pl.ANY)
VM = pl.BlockSpec(memory_space=pltpu.VMEM)
VMEM_LIMIT = 61 * 1024 * 1024
MESH = pl.DeviceIdType.MESH


def dot(a, b):
    return jnp.dot(a, b, preferred_element_type=F32)


def dot_nt(a, b):
    return lax.dot_general(a, b, (((1,), (1,)), ((), ())), preferred_element_type=F32)


def dot_tn(a, b):
    return lax.dot_general(a, b, (((0,), (0,)), ((), ())), preferred_element_type=F32)


def tile_of(extent, wanted):
    while extent % wanted:
        wanted //= 2
    return wanted


def span(i, size):
    return pl.ds(pl.multiple_of(i * size, size), size)


def loop(count, body):
    def step(i, carry):
        body(i)
        return carry

    lax.fori_loop(0, count, step, 0)


class Place:
    def __init__(self, n):
        self.n = n
        self.nz = n // 2
        self.t = lax.axis_index("tensor")
        self.c = lax.rem(self.t, 2)
        self.j = lax.div(self.t, 2)
        self.sib = self.t + 1 - 2 * self.c
        self.has_up = self.j < self.nz - 1
        self.has_down = self.j > 0

    def greet(self, partners=()):
        barrier = pltpu.get_barrier_semaphore()

        def signal(t):
            pl.semaphore_signal(barrier, inc=1, device_id={"tensor": t}, device_id_type=MESH)

        for i in partners:
            pl.semaphore_signal(barrier, inc=1, device_id={"dp": i}, device_id_type=MESH)

        signal(self.sib)
        pl.when(self.has_up)(lambda: signal(self.t + 2))
        pl.when(self.has_down)(lambda: signal(self.t - 2))
        pl.semaphore_wait(
            barrier,
            1 + len(partners) + self.has_up.astype(jnp.int32) + self.has_down.astype(jnp.int32),
        )

    def copy(self, src, dst, send, recv, t):
        return pltpu.make_async_remote_copy(
            src_ref=src,
            dst_ref=dst,
            send_sem=send,
            recv_sem=recv,
            device_id={"tensor": t},
            device_id_type=MESH,
        )


class Gather:
    def __init__(self, place, full, sent, came):
        self.place, self.full, self.sent, self.came = place, full, sent, came
        self.pieces = came.shape[1]
        self.size = full.shape[1] // self.pieces

    @staticmethod
    def scratch(n, rows, width):
        return [
            pltpu.VMEM((n, rows, width), BF16),
            pltpu.SemaphoreType.DMA((n, PIECES, 3)),
            pltpu.SemaphoreType.DMA((n, PIECES)),
        ]

    def copy(self, t, p, way, to):
        piece = self.full.at[t, pl.ds(p * self.size, self.size)]
        return self.place.copy(piece, piece, self.sent.at[t, p, way], self.came.at[t, p], to)

    def start(self):
        g = self.place
        for p in range(self.pieces):
            pl.when(g.has_up)(lambda: self.copy(g.t, p, 0, g.t + 2).start())
            pl.when(g.has_down)(lambda: self.copy(g.t, p, 1, g.t - 2).start())
        for p in range(self.pieces):
            self.copy(g.t, p, 2, g.sib).start()

    def forward(self, d, pieces=None):
        g = self.place
        for p in range(self.pieces) if pieces is None else pieces:

            @pl.when(g.j - d >= 0)
            def _():
                t = g.t - 2 * d
                self.copy(t, p, 0, g.sib).wait_recv()
                pl.when(g.has_up)(lambda: self.copy(t, p, 0, g.t + 2).start())
                self.copy(t, p, 2, g.sib).start()

            @pl.when(g.j + d < g.nz)
            def _():
                t = g.t + 2 * d
                self.copy(t, p, 1, g.sib).wait_recv()
                pl.when(g.has_down)(lambda: self.copy(t, p, 1, g.t - 2).start())
                self.copy(t, p, 2, g.sib).start()

    def each(self, d, use):
        g = self.place

        def visit(q):
            core, way = lax.div(q, 2), 2 * lax.rem(q, 2) - 1
            j = g.j + way * d
            there = jnp.logical_and(j >= 0, j < g.nz)

            @pl.when(jnp.logical_and(there, jnp.logical_or(d > 0, way > 0)))
            def _():
                t = 2 * j + lax.rem(g.c + core, 2)

                @pl.when(core > 0)
                def _():
                    for p in range(self.pieces):
                        self.copy(t, p, 2, g.sib).wait_recv()

                use(t)

        loop(4, visit)

    def finish(self):
        g = self.place

        def done(t):
            for p in range(self.pieces):
                self.copy(t, p, 2, g.sib).wait_send()

                @pl.when(jnp.logical_and(t <= g.t, g.has_up))
                def _():
                    self.copy(t, p, 0, g.sib).wait_send()

                @pl.when(jnp.logical_and(t >= g.t, g.has_down))
                def _():
                    self.copy(t, p, 1, g.sib).wait_send()

        loop(g.nz, lambda k: done(2 * k + g.c))


class Scatter:
    def __init__(self, place, partial, tile, bufs):
        self.place, self.partial, self.tile = place, partial, tile
        self.to_sib, self.from_sib, self.line, self.acc = bufs[:4]
        self.sib_send, self.sib_recv, self.line_send, self.line_recv = bufs[4:]
        self.out = self.from_sib
        self.tiles = self.acc.shape[1] // tile

    @staticmethod
    def scratch(n, rows, width):
        nz = n // 2
        return [
            pltpu.VMEM((nz, rows, width), BF16),
            pltpu.VMEM((nz, rows, width), BF16),
            pltpu.VMEM((nz + 1, rows, width), BF16),
            pltpu.VMEM((rows, width), F32),
            pltpu.SemaphoreType.DMA((nz,)),
            pltpu.SemaphoreType.DMA((nz,)),
            pltpu.SemaphoreType.DMA((nz, STRIPS)),
            pltpu.SemaphoreType.DMA((nz + 1, STRIPS)),
        ]

    def sib_copy(self, k):
        return self.place.copy(
            self.to_sib.at[k],
            self.from_sib.at[k],
            self.sib_send.at[k],
            self.sib_recv.at[k],
            self.place.sib,
        )

    def line_copy(self, k, slot, p, to):
        at = self.strip(p)
        return self.place.copy(
            self.out.at[k, at], self.line.at[slot, at], self.line_send.at[k, p], self.line_recv.at[slot, p], to
        )

    def strip(self, p):
        return span(p, self.acc.shape[0] // STRIPS)

    def offer(self, k):
        t = 2 * k + 1 - self.place.c

        def part(i):
            cols = span(i, self.tile)
            self.to_sib[k, :, cols] = self.partial(t, cols).astype(BF16)

        loop(self.tiles, part)
        self.sib_copy(k).start()

    def pair(self, k):
        self.sib_copy(k).wait_recv()
        t = 2 * k + self.place.c

        def part(i):
            cols = span(i, self.tile)
            self.acc[:, cols] = self.partial(t, cols) + self.from_sib[k, :, cols].astype(F32)

        loop(self.tiles, part)

    def offers(self, d):
        g = self.place

        def way_of(w):
            k = g.j + (1 - 2 * w) * d

            @pl.when(jnp.logical_and(jnp.logical_and(k >= 0, k < g.nz), jnp.logical_or(d > 0, w == 0)))
            def _():
                self.offer(k)

        loop(2, way_of)

    def step(self, d):
        g = self.place

        def way_of(w):
            sign = 1 - 2 * w
            k = g.j + sign * d

            @pl.when(jnp.logical_and(k >= 0, k < g.nz))
            def _():
                self.pair(k)
                upstream = g.j - sign
                more = jnp.logical_and(upstream >= 0, upstream < g.nz)

                slot = jnp.where(jnp.logical_and(d == 1, w == 1), g.nz, k)

                def pass_on(p):
                    at = self.strip(p)

                    @pl.when(more)
                    def _():
                        self.line_copy(k, k, p, g.sib).wait_recv()
                        self.out[k, at] = (self.acc[at] + self.line[k, at].astype(F32)).astype(BF16)

                    @pl.when(jnp.logical_not(more))
                    def _():
                        self.out[k, at] = self.acc[at].astype(BF16)

                    self.line_copy(k, slot, p, g.t + 2 * sign).start()

                loop(STRIPS, pass_on)

        loop(2, way_of)

    def last(self):
        g = self.place
        self.pair(g.j)

        def take(p):
            at = self.strip(p)

            @pl.when(g.has_down)
            def _():
                self.line_copy(g.j, g.j, p, g.sib).wait_recv()
                self.acc[at] += self.line[g.j, at].astype(F32)

            @pl.when(g.has_up)
            def _():
                self.line_copy(g.j, g.nz, p, g.sib).wait_recv()
                self.acc[at] += self.line[g.nz, at].astype(F32)

        loop(STRIPS, take)

    def finish(self):
        g = self.place

        def done(k):
            self.sib_copy(k).wait_send()
            pl.when(g.j != k)(
                lambda: loop(STRIPS, lambda p: self.line_copy(k, k, p, g.sib).wait_send())
            )

        loop(g.nz, done)


class Halving:
    def __init__(self, me, count, data, landed, final, sems):
        self.me, self.count = me, count
        self.data, self.landed, self.final = data, landed, final
        self.out_send, self.out_recv, self.back_send, self.back_recv = (sems.at[q] for q in range(4))
        self.bits = count.bit_length() - 1
        assert count == 1 << self.bits

    @staticmethod
    def scratch(count, rows, columns):
        return [
            pltpu.VMEM((2, count, 1, rows, columns), BF16),
            pltpu.VMEM((2, count - 1, 1, rows, columns), BF16),
            pltpu.VMEM((2, count, 1, rows, columns), BF16),
            pltpu.SemaphoreType.DMA((4, 2, count - 1)),
        ]

    @staticmethod
    def over(me, count, data, landed, final, sems):
        def at(ref):
            return lambda track, index: ref.at[track, index]

        return Halving(me, count, at(data), at(landed), at(final), sems)

    def partners(self):
        return [self.me + (1 - 2 * self.own(b)) * (1 << b) for b in range(self.bits)]

    def own(self, bit):
        return lax.rem(lax.div(self.me, 1 << bit), 2)

    def swaps(self, s):
        for track in (0, 1):
            order = [(i + track) % self.bits for i in range(self.bits)]
            bit = order[s]
            partner = self.me + (1 - 2 * self.own(bit)) * (1 << bit)
            fixed = sum(self.own(b) * (1 << b) for b in order[:s])
            for u in range(self.count >> (s + 1)):
                free = sum(((u >> i) & 1) << b for i, b in enumerate(order[s + 1 :]))
                slot = self.count - (self.count >> s) + u
                kept = fixed + free + self.own(bit) * (1 << bit)
                yield track, slot, partner, fixed + free + (1 - self.own(bit)) * (1 << bit), kept

    def out(self, track, slot, partner, given):
        return pltpu.make_async_remote_copy(
            src_ref=self.data(track, given),
            dst_ref=self.landed(track, slot),
            send_sem=self.out_send.at[track, slot],
            recv_sem=self.out_recv.at[track, slot],
            device_id={"dp": partner},
            device_id_type=MESH,
        )

    def back(self, track, slot, partner, segment):
        return pltpu.make_async_remote_copy(
            src_ref=self.final(track, segment),
            dst_ref=self.final(track, segment),
            send_sem=self.back_send.at[track, slot],
            recv_sem=self.back_recv.at[track, slot],
            device_id={"dp": partner},
            device_id_type=MESH,
        )

    def start(self, s=0):
        for track, slot, partner, given, _ in self.swaps(s):
            self.out(track, slot, partner, given).start()

    def turn(self, s):
        for track, slot, partner, given, kept in self.swaps(s):
            self.out(track, slot, partner, given).wait_recv()
            mine, theirs = self.data(track, kept), self.landed(track, slot)
            result = self.final(track, kept) if s == self.bits - 1 else mine
            blocks, rows, _ = mine.shape
            tile = tile_of(rows, 32)

            def add(r):
                block, at = lax.div(r, rows // tile), span(lax.rem(r, rows // tile), tile)
                result[block, at] = (mine[block, at].astype(F32) + theirs[block, at].astype(F32)).astype(BF16)

            loop(blocks * (rows // tile), add)
        if s < self.bits - 1:
            self.start(s + 1)
        else:
            self.start_back(s)

    def start_back(self, s):
        for track, slot, partner, _, kept in self.swaps(s):
            self.back(track, slot, partner, kept).start()

    def turn_back(self, s):
        for track, slot, partner, given, _ in self.swaps(s):
            self.back(track, slot, partner, given).wait_recv()
        if s > 0:
            self.start_back(s - 1)

    def events(self):
        steps = [functools.partial(self.turn, s) for s in range(self.bits)]
        return steps + [functools.partial(self.turn_back, s) for s in range(self.bits - 1, 0, -1)]

    def finish(self):
        self.turn_back(0)
        for s in range(self.bits):
            for track, slot, partner, given, kept in self.swaps(s):
                self.out(track, slot, partner, given).wait_send()
                self.back(track, slot, partner, kept).wait_send()


def fetching(kernel, which):
    def wrapped(*refs):
        refs = list(refs)
        sems = refs.pop()
        kept = refs[len(refs) - len(which) :]
        del refs[len(refs) - len(which) :]
        copies = {}
        for q, i in enumerate(which):
            copies[i] = pltpu.make_async_copy(refs[i], kept[q], sems.at[q])
            copies[i].start()
            refs[i] = kept[q]

        def arrive(*wanted):
            for i in wanted:
                copies[i].wait()

        return kernel(arrive, *refs)

    return wrapped


def fetched_specs(inputs, which, plain=()):
    specs = [ANY if i in which or i in plain else VM for i in range(len(inputs))]
    scratch = [pltpu.VMEM(inputs[i].shape, inputs[i].dtype) for i in which]
    return specs, scratch + [pltpu.SemaphoreType.DMA((len(which),))]


def comm_params(collective_id):
    return pltpu.CompilerParams(
        collective_id=collective_id, has_side_effects=True, vmem_limit_bytes=VMEM_LIMIT
    )


def cost(flops):
    return pl.CostEstimate(flops=int(flops), bytes_accessed=200_000_000, transcendentals=0)


def shape(*dims, dtype=F32):
    return jax.ShapeDtypeStruct(dims, dtype)


def inv_rms(values):
    return lax.rsqrt(jnp.mean(values * values, axis=-1, keepdims=True) + EPSILON)


def norm_grad(values, gain, gradient):
    inv = inv_rms(values)
    unit = values * inv
    scaled = gradient * gain
    centred = jnp.mean(scaled * unit, axis=-1, keepdims=True)
    return inv * (scaled - unit * centred), gradient * unit


def sigmoid(v):
    return 1.0 / (1.0 + jnp.exp(-v))


def gelu_parts(v):
    square = v * v
    bend = jnp.tanh(KAPPA * v * (1.0 + CUBIC * square))
    half = 0.5 * (1.0 + bend)
    slope = half + 0.5 * v * (1.0 - bend * bend) * (KAPPA * (1.0 + 3.0 * CUBIC * square))
    return v * half, slope


def one_minus_square(log_decay, decay):
    m = -2.0 * log_decay
    series = m * (
        1.0 - m * (1 / 2) * (1.0 - m * (1 / 3) * (1.0 - m * (1 / 4) * (1.0 - m * (1 / 5) * (1.0 - m * (1 / 6)))))
    )
    return jnp.where(m < 0.35, series, 1.0 - decay * decay)


def project_kernel(n, arrive, tokens, gain, w_in, w_br, normed, recur, branch, full, sent, came, held_a, held_b, saved):
    g = Place(n)
    gather = Gather(g, full, sent, came)
    part = 64

    def normalize(i):
        at = span(i, part)
        values = tokens[at].astype(F32)
        full[g.t, at] = (values * inv_rms(values) * gain[...].astype(F32)).astype(BF16)

    loop(full.shape[1] // part, normalize)
    g.greet()
    gather.start()
    arrive(2, 3)

    def use(t):
        pltpu.make_async_copy(full.at[t], normed.at[t], saved.at[t, 0]).start()
        held_a[t] = dot_nt(full[t], w_in[...])
        held_b[t] = dot_nt(full[t], w_br[...])
        pltpu.make_async_copy(held_a.at[t], recur.at[t], saved.at[t, 1]).start()
        pltpu.make_async_copy(held_b.at[t], branch.at[t], saved.at[t, 2]).start()

    gather.each(0, use)

    def away(i):
        gather.forward(i + 1)
        gather.each(i + 1, use)

    loop(g.nz - 1, away)

    def done(t):
        pltpu.make_async_copy(full.at[t], normed.at[t], saved.at[t, 0]).wait()
        pltpu.make_async_copy(held_a.at[t], recur.at[t], saved.at[t, 1]).wait()
        pltpu.make_async_copy(held_b.at[t], branch.at[t], saved.at[t, 2]).wait()

    loop(n, done)
    gather.finish()


def project(n, tokens, gain, w_in, w_br):
    rows, width = tokens.shape
    channels = w_in.shape[0]
    inputs = (tokens, gain, w_in, w_br)
    specs, kept = fetched_specs(inputs, (2, 3))
    return pl.pallas_call(
        fetching(functools.partial(project_kernel, n), (2, 3)),
        out_shape=(
            shape(n, rows, width, dtype=BF16),
            shape(n, rows, channels),
            shape(n, rows, channels),
        ),
        in_specs=specs,
        out_specs=(ANY,) * 3,
        scratch_shapes=Gather.scratch(n, rows, width)
        + [pltpu.VMEM((n, rows, channels), F32)] * 2
        + [pltpu.SemaphoreType.DMA((n, 3))]
        + kept,
        compiler_params=comm_params(1),
        cost_estimate=cost(4 * n * rows * width * channels),
        name="project",
    )(*inputs)


def starts(reset, here, init_state, init_conv, state, hist):
    keep = (1 - reset).astype(F32)
    state[...] = jnp.broadcast_to(init_state[here] * keep, state.shape)
    before = [init_conv[q, here] * keep for q in range(3)]
    hist[0:8] = jnp.concatenate([jnp.zeros((5, hist.shape[1]), F32)] + before, axis=0)


def recur_kernel(
    resets, u, branch, init_state, init_conv, conv, gate_w, bias, decay,
    states, mixture, conv_low, recall, ingate, final_state, final_conv,
    hist, decay_buf, drive_buf, carry,
):
    sequence, chunk = pl.program_id(0), pl.program_id(1)
    rows, channels = u.shape
    tile = 32
    here = pl.ds(sequence, 1)

    @pl.when(chunk == 0)
    def _():
        starts(resets[sequence], here, init_state, init_conv, carry, hist)

    @pl.when(chunk > 0)
    def _():
        hist[0:8] = hist[rows : rows + 8]

    hist[8:] = u[...]

    def convolve(i):
        window = hist[pl.ds(pl.multiple_of(i * tile, tile), tile + 8)]
        value = conv[4:5] + conv[0:1] * window[8:] + conv[1:2] * window[7 : tile + 7]
        value = value + conv[2:3] * window[6 : tile + 6] + conv[3:4] * window[5 : tile + 5]
        conv_low[span(i, tile)] = value.astype(BF16)

    loop(rows // tile, convolve)
    low = conv_low[...]
    recall[...] = dot(low, gate_w[0])
    ingate[...] = dot(low, gate_w[1])

    def gates(i):
        at = span(i, tile)
        r = sigmoid(recall[at] + bias[0:1])
        k = sigmoid(ingate[at] + bias[1:2])
        recall[at] = r
        ingate[at] = k
        log_decay = -8.0 * r * decay[...][None]
        step = jnp.exp(log_decay)
        decay_buf[at] = step
        drive_buf[at] = jnp.sqrt(one_minus_square(log_decay, step)) * k * conv_low[at].astype(F32)

    loop(rows // tile, gates)
    row = lax.broadcasted_iota(jnp.int32, (8, channels), 0)

    def scan(i, before):
        for part in range(4):
            at = pl.ds(pl.multiple_of(i * 32 + part * 8, 8), 8)
            a, b = decay_buf[at], drive_buf[at]
            for shift in (1, 2, 4):
                inside = row >= shift
                b = b + a * jnp.where(inside, pltpu.roll(b, shift, 0), 0.0)
                a = a * jnp.where(inside, pltpu.roll(a, shift, 0), 1.0)
            h = a * before + b
            states[at] = h
            before = jnp.broadcast_to(h[7:8], (8, channels))
        return before

    carry[...] = lax.fori_loop(0, rows // 32, scan, carry[...])

    def mix(i):
        at = span(i, tile)
        value, _ = gelu_parts(branch[at])
        mixture[at] = (states[at] * value).astype(BF16)

    loop(rows // tile, mix)

    @pl.when(chunk == pl.num_programs(1) - 1)
    def _():
        final_state[here] = carry[0:1]
        for q in range(3):
            final_conv[q, here] = hist[rows + 5 + q : rows + 6 + q]


def recur_forward(resets, u, branch, init_state, init_conv, conv, gate_w, bias, decay):
    total, channels = u.shape
    sequences = init_state.shape[0]
    length = total // sequences
    rows = tile_of(length, 256)
    chunks = length // rows
    block = pl.BlockSpec((rows, channels), lambda s, c: (s * chunks + c, 0))

    def whole(x):
        return pl.BlockSpec(x.shape, lambda s, c: (0,) * x.ndim)

    return pl.pallas_call(
        recur_kernel,
        grid=(sequences, chunks),
        out_shape=(
            shape(total, channels),
            shape(total, channels, dtype=BF16),
            shape(total, channels, dtype=BF16),
            shape(total, channels),
            shape(total, channels),
            shape(sequences, channels),
            shape(3, sequences, channels),
        ),
        in_specs=[
            pl.BlockSpec(memory_space=pltpu.SMEM),
            block,
            block,
            whole(init_state),
            whole(init_conv),
            whole(conv),
            whole(gate_w),
            whole(bias),
            whole(decay),
        ],
        out_specs=(block,) * 5
        + (
            whole(init_state),
            whole(init_conv),
        ),
        scratch_shapes=[
            pltpu.VMEM((rows + 8, channels), F32),
            pltpu.VMEM((rows, channels), F32),
            pltpu.VMEM((rows, channels), F32),
            pltpu.VMEM((8, channels), F32),
        ],
        compiler_params=pltpu.CompilerParams(vmem_limit_bytes=VMEM_LIMIT),
        name="recur_forward",
    )(resets, u, branch, init_state, init_conv, conv, gate_w, bias, decay)


def mixer_out_kernel(
    n, arrive, mixture, w_output, cotangent, tokens, gain, cot_full, residual, normed,
    full, sent, came, saved, *bufs
):
    g = Place(n)
    gather = Gather(g, full, sent, came)
    scatter = Scatter(g, lambda t, cols: dot(mixture[t], w_output[:, cols]), tile_of(residual.shape[1], 512), bufs)
    first = pltpu.make_async_copy(cotangent, full.at[g.t], saved.at[0])
    first.start()
    g.greet()
    first.wait()
    gather.start()
    arrive(0, 1)

    def use(t):
        pltpu.make_async_copy(full.at[t], cot_full.at[t], saved.at[t]).start()

    scatter.offers(g.nz - 1)

    def around(i):
        d = g.nz - 1 - i
        scatter.offers(d - 1)
        scatter.step(d)
        gather.each(i, use)
        gather.forward(i + 1)

    loop(g.nz - 1, around)
    scatter.last()
    arrive(3)
    part = 64

    def rows_of(i):
        at = span(i, part)
        values = scatter.acc[at] + tokens[at].astype(F32)
        residual[at] = values
        normed[at] = (values * inv_rms(values) * gain[...].astype(F32)).astype(BF16)

    loop(residual.shape[0] // part, rows_of)
    gather.each(g.nz - 1, use)
    loop(n, lambda t: pltpu.make_async_copy(full.at[t], cot_full.at[t], saved.at[t]).wait())
    scatter.finish()
    gather.finish()


def mixer_out(n, mixture, w_output, cotangent, tokens, gain):
    rows, width = tokens.shape
    inputs, which = (mixture, w_output, cotangent, tokens, gain), (0, 1, 3)
    specs, kept = fetched_specs(inputs, which, (2,))
    return pl.pallas_call(
        fetching(functools.partial(mixer_out_kernel, n), which),
        out_shape=(
            shape(n, rows, width, dtype=BF16),
            shape(rows, width),
            shape(rows, width, dtype=BF16),
        ),
        in_specs=specs,
        out_specs=(ANY, VM, VM),
        scratch_shapes=Gather.scratch(n, rows, width)
        + [pltpu.SemaphoreType.DMA((n,))]
        + Scatter.scratch(n, rows, width)
        + kept,
        compiler_params=comm_params(2),
        cost_estimate=cost(2 * n * rows * width * mixture.shape[-1]),
        name="mixer_out",
    )(*inputs)


def mlp_kernel(
    n, copies, arrive, normed, cot_full, w_gelu, w_linear, w_down, residual, gain,
    hidden, grad_gelu, grad_linear, grad_down, g_residual, g_low, g_gain,
    full, sent, came, cot, keep_h, keep_f, keep_s, acc_g, acc_l, acc_d,
    to_sib, sums, line, acc, landed, swap_sems, saved, fetched, drained, sib_sent, sib_came, line_sent, line_came,
):
    g = Place(n)
    gather = Gather(g, full, sent, came)
    columns = w_gelu.shape[1]
    rows, width = acc.shape
    tile = tile_of(columns, 256)
    wide = tile_of(width, 512)
    strip = rows // PARTS
    me = lax.axis_index("dp")
    start = pltpu.make_async_copy(normed, full.at[g.t], saved.at[0])
    start.start()
    part_width = width // (2 * copies)
    depth = columns // rows

    def segment(track, index):
        return pl.ds(pl.multiple_of((track * copies + index) * part_width, part_width), part_width)

    swap = Halving(
        me,
        copies,
        lambda track, index: full.at[0:depth, :, segment(track, index)],
        lambda track, slot: landed.at[track, slot],
        lambda track, index: full.at[depth : 2 * depth, :, segment(track, index)],
        swap_sems,
    )
    def fetch(t, q):
        return pltpu.make_async_copy(cot_full.at[t], cot.at[q], fetched.at[q])

    g.greet(swap.partners())
    start.wait()
    gather.start()
    fetch(2 * g.j, 0).start()
    fetch(2 * g.j + 1, 1).start()
    arrive(2, 3, 4)
    acc_g[...] = jnp.zeros_like(acc_g)
    acc_l[...] = jnp.zeros_like(acc_l)
    acc_d[...] = jnp.zeros_like(acc_d)

    def save(t, q):
        return pltpu.make_async_copy(keep_h.at[q], hidden.at[t], saved.at[q])

    def layer(t, q):
        fetch(t, q).wait()

        def part(i):
            cols = span(i, tile)
            first = dot(full[t], w_gelu[:, cols])
            second = dot(full[t], w_linear[:, cols])
            back = dot_nt(cot[q], w_down[cols])
            value, slope = gelu_parts(first)
            keep_h[q, :, cols] = (value * second).astype(BF16)
            keep_f[q, :, cols] = (back * second * slope).astype(BF16)
            keep_s[q, :, cols] = (back * value).astype(BF16)

        loop(columns // tile, part)
        save(t, q).start()

    def partial(q, cols):
        return dot_nt(keep_f[q], w_gelu[cols]) + dot_nt(keep_s[q], w_linear[cols])

    def sib_copy(k):
        return g.copy(to_sib, sums.at[k], sib_sent, sib_came.at[k], g.sib)

    def line_copy(k, slot, p, to):
        at = pl.ds(pl.multiple_of(p * strip, strip), strip)
        return g.copy(
            sums.at[k, at], line.at[slot, at], line_sent.at[k, p], line_came.at[slot, p], to
        )

    def chip(d, way):
        k = g.j + way * d
        mine, its = g.c, 1 - g.c
        own, other = 2 * k + mine, 2 * k + its
        for p in range(gather.pieces):
            gather.copy(other, p, 2, g.sib).wait_recv()
        layer(other, its)

        def offer(i):
            cols = span(i, wide)
            to_sib[:, cols] = partial(its, cols).astype(BF16)

        loop(width // wide, offer)
        sib_copy(k).start()
        layer(own, mine)
        sib_copy(k).wait()

        @pl.when(d == 0)
        def _():
            def part(i):
                cols = span(i, wide)
                acc[:, cols] = partial(mine, cols) + sums[k, :, cols].astype(F32)

            loop(width // wide, part)

        @pl.when(d > 0)
        def _():
            def part(i):
                cols = span(i, wide)
                sums[k, :, cols] = (partial(mine, cols) + sums[k, :, cols].astype(F32)).astype(BF16)

            loop(width // wide, part)
            first = jnp.logical_or(
                jnp.logical_and(way > 0, jnp.logical_not(g.has_down)),
                jnp.logical_and(way < 0, jnp.logical_not(g.has_up)),
            )

            @pl.when(first)
            def _():
                slot = jnp.where(jnp.logical_and(way < 0, d == 1), g.nz, k)
                for p in range(PARTS):
                    line_copy(k, slot, p, g.t + 2 * way).start()

        def part(i):
            at = span(i, wide)
            both = full[pl.ds(2 * k, 2), :, at].reshape(2 * rows, wide)
            acc_g[at] += dot_tn(both, keep_f[...].reshape(2 * rows, columns))
            acc_l[at] += dot_tn(both, keep_s[...].reshape(2 * rows, columns))
            acc_d[:, at] += dot_tn(
                keep_h[...].reshape(2 * rows, columns), cot[:, :, at].reshape(2 * rows, wide)
            )

        loop(width // wide, part)
        both_ways = jnp.logical_and(g.j + d < g.nz, g.j - d >= 0)
        again = jnp.logical_and(both_ways, jnp.logical_and(way > 0, d > 0))
        later = jnp.where(g.j + d + 1 < g.nz, g.j + d + 1, g.j - d - 1)
        following = jnp.where(again, g.j - d, later)

        @pl.when(following >= 0)
        def _():
            fetch(2 * following, 0).start()
            fetch(2 * following + 1, 1).start()

        save(other, its).wait()
        save(own, mine).wait()

    def relay(m, events=()):
        def take(k, slot, sign, p):
            at = pl.ds(pl.multiple_of(p * strip, strip), strip)
            line_copy(k, slot, p, g.sib).wait_recv()

            @pl.when(k == g.j)
            def _():
                acc[at] += line[slot, at].astype(F32)

            @pl.when(k != g.j)
            def _():
                sums[k, at] = (sums[k, at].astype(F32) + line[slot, at].astype(F32)).astype(BF16)
                there = jnp.where(jnp.logical_and(sign < 0, k == g.j - 1), g.nz, k)
                line_copy(k, there, p, g.t + 2 * sign).start()

        def rise(p):
            pl.when(jnp.logical_and(g.has_down, m >= g.j))(lambda: take(m, m, 1, p))

        def fall(p):
            k = g.nz - 1 - m
            pl.when(jnp.logical_and(g.has_up, k <= g.j))(
                lambda: take(k, jnp.where(k == g.j, g.nz, k), -1, p)
            )

        lower = 2 * g.j < g.nz

        def strips(i):
            @pl.when(i < PARTS)
            def _():
                pl.when(lower)(lambda: rise(i))
                pl.when(jnp.logical_not(lower))(lambda: fall(i))

            @pl.when(i > 0)
            def _():
                pl.when(lower)(lambda: fall(i - 1))
                pl.when(jnp.logical_not(lower))(lambda: rise(i - 1))

        def between(i):
            strips(i)
            for q, event in enumerate(events):
                pl.when(i == (q + 1) * PARTS // len(events))(event)

        loop(PARTS + 1, between)

    def cores(d):
        up, down = g.j + d < g.nz, g.j - d >= 0

        def way_of(w):
            both = jnp.logical_and(up, down)
            way = jnp.where(jnp.logical_and(w == 0, up), 1, -1)
            wanted = jnp.where(w == 0, jnp.logical_or(up, down), jnp.logical_and(both, d > 0))
            pl.when(wanted)(lambda: chip(d, way))

            @pl.when(d < g.nz - 1)
            def _():
                for p in range(gather.pieces):
                    pl.when(w == min(p, 1))(lambda: gather.forward(d + 1, (p,)))

        loop(2, way_of)

    def step(d):
        @pl.when(d < g.nz)
        def _():
            cores(d)

        @pl.when(d == g.nz - 1)
        def _():
            gather.finish()
            for i in range(depth):
                full[i] = acc_d[pl.ds(i * rows, rows)].astype(BF16)
            swap.start()

        pl.when(d > 1)(lambda: relay(d - 1))

    loop(g.nz, step)

    stages = [held.at[q] for held in (keep_h, keep_f, keep_s) for q in (0, 1)]
    leaving = []

    def leave(i, value, out):
        slot = i % len(stages)
        if len(leaving) >= len(stages):
            leaving[i - len(stages)].wait()
        stages[slot][...] = value.astype(BF16)
        copy = pltpu.make_async_copy(stages[slot], out, drained.at[slot])
        copy.start()
        leaving.append(copy)

    for i in range(width // rows):
        at = pl.ds(i * rows, rows)
        leave(2 * i, acc_g[at], grad_gelu.at[at])
        leave(2 * i + 1, acc_l[at], grad_linear.at[at])
    events = swap.events()
    events.pop(0)()
    relay(g.nz - 1, events)
    own = pltpu.make_async_copy(cot_full.at[g.t], cot.at[0], fetched.at[0])
    own.start()
    own.wait()
    arrive(5)
    lines = 32
    g_gain[...] = jnp.zeros_like(g_gain)

    def rows_of(i):
        at = span(i, lines)
        back, terms = norm_grad(residual[at], gain[...].astype(F32), acc[at])
        value = cot[0, at].astype(F32) + back
        acc[at] = value
        cot[1, at] = value.astype(BF16)
        g_gain[...] += jnp.sum(terms, axis=0, keepdims=True)

    loop(rows // lines, rows_of)
    last = [
        pltpu.make_async_copy(acc, g_residual, saved.at[0]),
        pltpu.make_async_copy(cot.at[1], g_low, saved.at[1]),
    ]
    swap.finish()
    for i in range(depth):
        at = pl.ds(i * rows, rows)
        last.append(pltpu.make_async_copy(full.at[depth + i], grad_down.at[at], drained.at[len(stages) + i]))
    for copy in last:
        copy.start()
    for copy in leaving[-len(stages) :] + last:
        copy.wait()

    def done(k):
        @pl.when(k != g.j)
        def _():
            for p in range(PARTS):
                line_copy(k, k, p, g.sib).wait_send()

    loop(g.nz, done)


def mlp(n, copies, normed, cot_full, w_gelu, w_linear, w_down, residual, gain):
    rows, width = normed.shape
    columns = w_gelu.shape[1]
    kept = pltpu.VMEM((2, rows, columns), BF16)
    sems = pltpu.SemaphoreType.DMA
    inputs, which = (normed, cot_full, w_gelu, w_linear, w_down, residual, gain), (2, 3, 4, 5)
    specs, held = fetched_specs(inputs, which, (0, 1))
    return pl.pallas_call(
        fetching(functools.partial(mlp_kernel, n, copies), which),
        out_shape=(shape(n, rows, columns, dtype=BF16),)
        + (shape(width, columns, dtype=BF16),) * 2
        + (
            shape(columns, width, dtype=BF16),
            shape(rows, width),
            shape(rows, width, dtype=BF16),
            shape(1, width),
        ),
        in_specs=specs,
        out_specs=(ANY,) * 6 + (VM,),
        scratch_shapes=Gather.scratch(n, rows, width)
        + [pltpu.VMEM((2, rows, width), BF16)]
        + [kept] * 3
        + [pltpu.VMEM((width, columns), F32)] * 2
        + [
            pltpu.VMEM((columns, width), F32),
            pltpu.VMEM((rows, width), BF16),
            pltpu.VMEM((n // 2, rows, width), BF16),
            pltpu.VMEM((n // 2 + 1, rows, width), BF16),
            pltpu.VMEM((rows, width), F32),
            pltpu.VMEM((2, copies - 1, columns // rows, rows, width // (2 * copies)), BF16),
            sems((4, 2, copies - 1)),
            sems((2,)),
            sems((2,)),
            sems((6 + columns // rows,)),
            sems,
            sems((n // 2,)),
            sems((n // 2, PARTS)),
            sems((n // 2 + 1, PARTS)),
        ]
        + held,
        compiler_params=comm_params(3),
        cost_estimate=cost(16 * n * rows * width * columns),
        name="mlp",
    )(*inputs)


def down_kernel(
    n, copies, arrive, hidden, w_down, residual, g_low, w_output, mixture, output, g_mixture, grad_output,
    full, sent, came, acc_o, start_sem, *bufs
):
    g = Place(n)
    gather = Gather(g, full, sent, came)
    width = residual.shape[1]
    wide = tile_of(width, 512)
    scatter = Scatter(g, lambda t, cols: dot(hidden[t], w_down[:, cols]), wide, bufs)
    first = pltpu.make_async_copy(g_low, full.at[g.t], start_sem)
    first.start()
    g.greet()
    first.wait()

    def use(t):
        g_mixture[t] = dot_nt(full[t], w_output[...])

        def part(i):
            at = span(i, wide)
            acc_o[:, at] += dot_tn(mixture[t], full[t, :, at])

        loop(width // wide, part)

    gather.start()
    acc_o[...] = jnp.zeros_like(acc_o)
    arrive(0, 1)
    scatter.offers(g.nz - 1)
    arrive(4, 5)

    def around(i):
        d = g.nz - 1 - i
        scatter.offers(d - 1)
        scatter.step(d)
        gather.each(i, use)
        gather.forward(i + 1)

    loop(g.nz - 1, around)
    gather.each(g.nz - 1, use)
    for i in range(copies):
        part = width // copies
        grad_output[i] = acc_o[:, i * part : (i + 1) * part].astype(BF16)
    scatter.last()
    arrive(2)
    output[...] = (scatter.acc[...] + residual[...]).astype(BF16)
    scatter.finish()
    gather.finish()


def down(n, copies, hidden, w_down, residual, g_low, w_output, mixture):
    rows, width = residual.shape
    channels = w_output.shape[0]
    inputs, which = (hidden, w_down, residual, g_low, w_output, mixture), (0, 1, 4, 5, 2)
    specs, kept = fetched_specs(inputs, which, (3,))
    return pl.pallas_call(
        fetching(functools.partial(down_kernel, n, copies), which),
        out_shape=(
            shape(rows, width, dtype=BF16),
            shape(n, rows, channels),
            shape(copies, channels, width // copies, dtype=BF16),
        ),
        in_specs=specs,
        out_specs=(VM,) * 3,
        scratch_shapes=Gather.scratch(n, rows, width)
        + [pltpu.VMEM((channels, width), F32), pltpu.SemaphoreType.DMA]
        + Scatter.scratch(n, rows, width)
        + kept,
        compiler_params=comm_params(5),
        cost_estimate=cost(2 * n * rows * width * (hidden.shape[-1] + 2 * channels)),
        name="down",
    )(*inputs)


def recur_back_kernel(
    resets, g_mix, branch, states, states_before, u, u_before, conv_low, recall, ingate, init_state, init_conv,
    conv, gate_w, decay, narrow_in,
    g_recur, g_branch, small, g_gates, wide_out,
    g_state, step_buf, root_buf, g_conv, pre_r, pre_i, carry, hist_s, hist_u, sums,
):
    sequence, back = pl.program_id(0), pl.program_id(1)
    last = pl.num_programs(1) - 1
    rows, channels = u.shape
    tile = 32
    wide_out[...] = narrow_in[...].astype(F32)

    @pl.when(jnp.logical_and(sequence == 0, back == 0))
    def _():
        sums[...] = jnp.zeros_like(sums)
        g_gates[...] = jnp.zeros_like(g_gates)

    @pl.when(back == 0)
    def _():
        carry[...] = jnp.zeros_like(carry)
        g_conv[rows : rows + 8] = jnp.zeros((8, channels), F32)

    @pl.when(back > 0)
    def _():
        g_conv[rows : rows + 8] = g_conv[0:8]

    @pl.when(back == last)
    def _():
        starts(
            resets[sequence], pl.ds(sequence, 1), init_state, init_conv, hist_s.at[0:8], hist_u
        )

    @pl.when(back < last)
    def _():
        hist_s[0:8] = states_before[...]
        hist_u[0:8] = u_before[...]

    hist_s[8:] = states[...]
    hist_u[8:] = u[...]

    def first(i):
        at = span(i, tile)
        value, slope = gelu_parts(branch[at])
        gm = g_mix[at]
        g_state[at] = gm * value
        g_branch[at] = (gm * states[at] * slope).astype(BF16)
        log_decay = -8.0 * recall[at] * decay[...][None]
        step = jnp.exp(log_decay)
        step_buf[at] = step
        root_buf[at] = jnp.sqrt(one_minus_square(log_decay, step))

    loop(rows // tile, first)
    row = lax.broadcasted_iota(jnp.int32, (8, channels), 0)
    groups = rows // 32

    def scan(i, after):
        for part in range(4):
            at = pl.ds(pl.multiple_of((groups - 1 - i) * 32 + (3 - part) * 8, 8), 8)
            a, gs = step_buf[at], g_state[at]
            b = a * gs
            for shift in (1, 2, 4):
                inside = row < 8 - shift
                b = b + a * jnp.where(inside, pltpu.roll(b, 8 - shift, 0), 0.0)
                a = a * jnp.where(inside, pltpu.roll(a, 8 - shift, 0), 1.0)
            e = a * after + b
            g_state[at] = gs + jnp.where(row < 7, pltpu.roll(e, 7, 0), after)
            after = jnp.broadcast_to(e[0:1], (8, channels))
        return after

    carry[...] = lax.fori_loop(0, groups, scan, carry[...])

    def fold(x):
        return jnp.sum(x.reshape(tile // 8, 8, channels), axis=0)

    def second(i):
        at = span(i, tile)
        window = hist_s[pl.ds(pl.multiple_of(i * tile, tile), tile + 8)]
        before = window[7 : tile + 7]
        g, r, k = g_state[at], recall[at], ingate[at]
        c = conv_low[at].astype(F32)
        step, root = step_buf[at], root_buf[at]
        kc = k * c
        g_log = g * (before * step - kc * (step * step) / root)
        slow = -8.0 * r
        sums[7] += fold(g_log * slow)
        low_r = (g_log * (slow * decay[...][None]) * (1.0 - r)).astype(BF16)
        low_i = (g * root * kc * (1.0 - k)).astype(BF16)
        pre_r[at] = low_r
        pre_i[at] = low_i
        sums[5] += fold(low_r.astype(F32))
        sums[6] += fold(low_i.astype(F32))
        g_conv[at] = g * root * k

    loop(rows // tile, second)
    low_r, low_i, low_c = pre_r[...], pre_i[...], conv_low[...]
    g_gates[0] += dot_tn(low_c, low_r)
    g_gates[1] += dot_tn(low_c, low_i)
    g_conv[0:rows] += dot_nt(low_r, gate_w[0]) + dot_nt(low_i, gate_w[1])

    def third(i):
        at = span(i, tile)
        start = pl.multiple_of(i * tile, tile)
        window = g_conv[pl.ds(start, tile + 8)]
        value = conv[0:1] * window[0:tile]
        for k in (1, 2, 3):
            value = value + conv[k : k + 1] * window[k : tile + k]
        g_recur[at] = value.astype(BF16)
        past = hist_u[pl.ds(start, tile + 8)]
        gc = window[0:tile]
        for k in range(4):
            sums[k] += fold(gc * past[8 - k : tile + 8 - k])
        sums[4] += fold(gc)

    loop(rows // tile, third)

    @pl.when(jnp.logical_and(sequence == pl.num_programs(0) - 1, back == last))
    def _():
        small[...] = jnp.sum(sums[...], axis=1)


def recur_back(
    resets, g_mix, branch, states, u, conv_low, recall, ingate, init_state, init_conv, conv, gate_w, decay, narrow_in
):
    total, channels = u.shape
    sequences = init_state.shape[0]
    length = total // sequences
    rows = tile_of(length, 256)
    chunks = length // rows
    extra_rows = narrow_in.shape[0] // (sequences * chunks)
    extra = pl.BlockSpec((extra_rows, narrow_in.shape[1]), lambda s, c: (s * chunks + c, 0))
    eights = rows // 8

    def at(s, c):
        return (s * chunks + chunks - 1 - c, 0)

    def earlier(s, c):
        return (jnp.maximum((s * chunks + chunks - 1 - c) * eights - 1, 0), 0)

    block = pl.BlockSpec((rows, channels), at)
    before = pl.BlockSpec((8, channels), earlier)

    def whole(x):
        return pl.BlockSpec(x.shape, lambda s, c: (0,) * x.ndim)

    wide = pltpu.VMEM((rows, channels), F32)
    narrow = pltpu.VMEM((rows, channels), BF16)
    long = pltpu.VMEM((rows + 8, channels), F32)
    return pl.pallas_call(
        recur_back_kernel,
        grid=(sequences, chunks),
        out_shape=(
            shape(total, channels, dtype=BF16),
            shape(total, channels, dtype=BF16),
            shape(8, channels),
            shape(2, channels, channels),
            shape(*narrow_in.shape),
        ),
        in_specs=[
            pl.BlockSpec(memory_space=pltpu.SMEM),
            block, block, block, before, block, before, block, block, block,
            whole(init_state), whole(init_conv), whole(conv), whole(gate_w), whole(decay), extra,
        ],
        out_specs=(
            block,
            block,
            pl.BlockSpec((8, channels), lambda s, c: (0, 0)),
            pl.BlockSpec((2, channels, channels), lambda s, c: (0, 0, 0)),
            extra,
        ),
        scratch_shapes=[
            wide, wide, wide, long, narrow, narrow,
            pltpu.VMEM((8, channels), F32), long, long,
            pltpu.VMEM((8, 8, channels), F32),
        ],
        compiler_params=pltpu.CompilerParams(vmem_limit_bytes=VMEM_LIMIT),
        name="recur_back",
    )(
        resets, g_mix, branch, states, states, u, u, conv_low, recall, ingate, init_state, init_conv,
        conv, gate_w, decay, narrow_in,
    )


def input_back_kernel(
    n, copies, arrive, g_recur, g_branch, w_in, w_br, normed, tokens, g_residual, gain, second_gain, g_gates, small,
    input_grad, in_out, br_out, gates_out, conv_out, bias_out, decay_out, gains_out,
    gain_row, gain_parts, gain_in, gain_sum, gain_dp, gain_sent, gain_came, gain_dp_sent, gain_dp_came, *bufs
):
    g = Place(n)
    me = lax.axis_index("dp")
    rows, width = tokens.shape
    channels = w_in.shape[0]
    blocks, block_width = gates_out.shape[1], gates_out.shape[2]
    segment = width // (2 * copies)
    gain_width = width // n
    weights = Halving.over(me, copies, *bufs[:4])
    rest = Halving.over(me, copies, *bufs[4:8])
    padded = bufs[0].shape[3] // 2
    rest_rows = bufs[4].shape[3]

    def block(ref, t):
        return ref[span(t, rows)]

    def partial(t, cols):
        return dot(block(g_recur, t), w_in[:, cols]) + dot(block(g_branch, t), w_br[:, cols])

    scatter = Scatter(g, partial, tile_of(width, 512), bufs[8:])

    def gain_copy(t, slot):
        return g.copy(gain_parts.at[t], gain_in.at[slot], gain_sent.at[t], gain_came.at[slot], t)

    def gain_dp_copy(i, slot):
        return pltpu.make_async_remote_copy(
            src_ref=gain_sum,
            dst_ref=gain_dp.at[slot],
            send_sem=gain_dp_sent.at[i],
            recv_sem=gain_dp_came.at[slot],
            device_id={"dp": i},
            device_id_type=MESH,
        )

    def others(act):
        loop(n, lambda t: pl.when(t != g.t)(lambda: act(t)))

    def copies_of(act):
        loop(copies, lambda i: pl.when(i != me)(lambda: act(i)))

    barrier = pltpu.get_barrier_semaphore()
    others(
        lambda t: pl.semaphore_signal(barrier, inc=1, device_id={"tensor": t}, device_id_type=MESH)
    )
    copies_of(lambda i: pl.semaphore_signal(barrier, inc=1, device_id={"dp": i}, device_id_type=MESH))
    pl.semaphore_wait(barrier, n - 1 + copies - 1)

    arrive(0, 1, 2, 3)
    scatter.offers(g.nz - 1)

    def around(i):
        d = g.nz - 1 - i
        scatter.offers(d - 1)
        scatter.step(d)

    around(0)
    arrive(4, 9)

    data = bufs[0]

    def weigh(q):
        cols = span(q, 2 * segment)
        first = dot_tn(g_recur[...], normed[:, cols])
        second = dot_tn(g_branch[...], normed[:, cols])
        for half in (0, 1):
            index = 2 * q + half
            track, part = lax.div(index, copies), lax.rem(index, copies)
            for i, value in enumerate((first, second)):
                piece = value[:, half * segment : (half + 1) * segment].astype(BF16)
                data[track, part, 0, i * padded : i * padded + channels] = piece
                if padded > channels:
                    data[track, part, 0, i * padded + channels : (i + 1) * padded] = jnp.zeros(
                        (padded - channels, segment), BF16
                    )
        terms = jnp.sum(w_in[:, cols].astype(F32) * first + w_br[:, cols].astype(F32) * second, axis=0, keepdims=True)
        gain_row[0:1, cols] = terms / gain[0:1, cols].astype(F32)

    loop(copies, weigh)
    weights.start()
    gain_row[1:2] = second_gain[...]
    gain_row[2:8] = jnp.zeros((6, width), F32)
    for t in range(n):
        gain_parts[t] = gain_row[:, t * gain_width : (t + 1) * gain_width]
    others(lambda t: gain_copy(t, g.t).start())
    gain_in[g.t] = gain_parts[g.t]

    flat = jnp.concatenate(
        [
            g_gates[0],
            g_gates[1],
            small[...],
            jnp.zeros((2 * copies * rest_rows - 2 * channels - 8, channels), F32),
        ],
        axis=0,
    ).astype(BF16)
    for i in range(2 * copies):
        bufs[4][i // copies, i % copies, 0] = flat[i * rest_rows : (i + 1) * rest_rows]
    rest.start()

    events = [lambda a=a, b=b: (a(), b()) for a, b in zip(weights.events(), rest.events())]
    for i in range(1, g.nz - 1):
        around(i)
        if events:
            events.pop(0)()
        if i == 1:
            others(lambda t: gain_copy(t, t).wait_recv())
            total = gain_in[0]
            for t in range(1, n):
                total = total + gain_in[t]
            gain_sum[...] = total
            copies_of(lambda i: gain_dp_copy(i, me).start())
            gain_dp[me] = total
    for event in events:
        event()
    scatter.last()
    arrive(5, 6)
    part = 32

    def rows_of(i):
        at = span(i, part)
        back, _ = norm_grad(tokens[at].astype(F32), gain[...].astype(F32), scatter.acc[at])
        input_grad[at] = g_residual[at] + back

    loop(rows // part, rows_of)
    copies_of(lambda i: gain_dp_copy(i, i).wait_recv())
    total = gain_dp[0]
    for i in range(1, copies):
        total = total + gain_dp[i]
    gains_out[...] = total
    rest.finish()
    flat = jnp.concatenate([bufs[6][i // copies, i % copies, 0].astype(F32) for i in range(2 * copies)], axis=0)
    for q in (0, 1):
        for i in range(blocks):
            start = q * channels + i * block_width
            gates_out[q, i] = flat[start : start + block_width, i * block_width : (i + 1) * block_width]
    conv_out[...] = flat[2 * channels : 2 * channels + 5]
    bias_out[...] = flat[2 * channels + 5 : 2 * channels + 7]
    decay_out[...] = flat[2 * channels + 7 : 2 * channels + 8]
    weights.finish()
    for i in range(2 * copies):
        for q, out in enumerate((in_out, br_out)):
            out[:, i * segment : (i + 1) * segment] = bufs[2][
                i // copies, i % copies, 0, q * padded : q * padded + channels
            ]
    others(lambda t: gain_copy(t, t).wait_send())
    copies_of(lambda i: gain_dp_copy(i, i).wait_send())
    scatter.finish()


def up_to(extent, multiple):
    return (extent + multiple - 1) // multiple * multiple


def input_back(
    n, copies, g_recur, g_branch, w_in, w_br, normed, tokens, g_residual, gain, second_gain, g_gates, small, blocks
):
    rows, width = tokens.shape
    channels = w_in.shape[0]
    block = channels // blocks
    rest_rows = up_to((2 * channels + 8 + 2 * copies - 1) // (2 * copies), 16)
    gain_shape = (8, width // n)
    sems = pltpu.SemaphoreType.DMA
    inputs = (g_recur, g_branch, w_in, w_br, normed, tokens, g_residual, gain, second_gain, g_gates, small)
    which = (0, 1, 2, 3, 4, 9, 5, 6)
    specs, kept = fetched_specs(inputs, which)
    return pl.pallas_call(
        fetching(functools.partial(input_back_kernel, n, copies), which),
        out_shape=(shape(rows, width),)
        + (shape(channels, width, dtype=BF16),) * 2
        + (
            shape(2, blocks, block, block),
            shape(5, channels),
            shape(2, channels),
            shape(1, channels),
            shape(*gain_shape),
        ),
        in_specs=specs,
        out_specs=(VM,) * 8,
        scratch_shapes=[
            pltpu.VMEM((8, width), F32),
            pltpu.VMEM((n, *gain_shape), F32),
            pltpu.VMEM((n, *gain_shape), F32),
            pltpu.VMEM(gain_shape, F32),
            pltpu.VMEM((copies, *gain_shape), F32),
            sems((n,)),
            sems((n,)),
            sems((copies,)),
            sems((copies,)),
        ]
        + Halving.scratch(copies, 2 * up_to(channels, 16), width // (2 * copies))
        + Halving.scratch(copies, rest_rows, channels)
        + Scatter.scratch(n, rows, width)
        + kept,
        compiler_params=comm_params(6),
        cost_estimate=cost(8 * n * rows * width * channels),
        name="input_back",
    )(*inputs)


def widen_kernel(*refs):
    half = len(refs) // 2
    for narrow, wide in zip(refs[:half], refs[half:]):
        wide[...] = narrow[...].reshape(wide.shape).astype(F32)


def widen(by_rows, by_columns, in_parts):
    steps = 8
    width = by_columns[0].shape[1]
    tile = width // steps
    per_part = in_parts.shape[2] // tile
    specs, outs = [], []
    for x in by_rows:
        specs.append(pl.BlockSpec((x.shape[0] // steps, x.shape[1]), lambda i: (i, 0)))
        outs.append(shape(*x.shape))
    for x in by_columns:
        specs.append(pl.BlockSpec((x.shape[0], tile), lambda i: (0, i)))
        outs.append(shape(*x.shape))
    last = pl.BlockSpec((1, in_parts.shape[1], tile), lambda i: (i // per_part, 0, i % per_part))
    outs.append(shape(in_parts.shape[1], width))
    wide = pl.BlockSpec((in_parts.shape[1], tile), lambda i: (0, i))
    return pl.pallas_call(
        widen_kernel,
        grid=(steps,),
        out_shape=tuple(outs),
        in_specs=specs + [last],
        out_specs=tuple(specs) + (wide,),
        compiler_params=pltpu.CompilerParams(vmem_limit_bytes=VMEM_LIMIT),
        name="widen",
    )(*by_rows, *by_columns, in_parts)


def body(
    n,
    copies,
    tokens,
    cotangent,
    resets,
    init_state,
    init_conv,
    norm_gain,
    w_input,
    w_branch,
    conv_params,
    gate_weights,
    gate_bias,
    decay_rate,
    w_output,
    mlp_gain,
    w_gelu,
    w_linear,
    w_down,
):
    rows, width = tokens.shape
    total = rows * n
    channels = w_input.shape[1]
    blocks, block = gate_weights.shape[1], gate_weights.shape[2]
    before_conv = init_conv.transpose(1, 0, 2)
    gain_first, gain_second = norm_gain[None], mlp_gain[None]
    gate_w = (gate_weights[:, :, :, None] * jnp.eye(blocks, dtype=BF16)[None, :, None, :, None]).reshape(
        2, channels, channels
    )
    w_in, w_br = w_input.T, w_branch.T

    def flat(x):
        return x.reshape(total, x.shape[-1])

    def blocked(x):
        return x.reshape(n, rows, x.shape[-1])

    normed, recur, branch = project(n, tokens, gain_first, w_in, w_br)
    recur, branch = flat(recur), flat(branch)
    states, mixture, conv_low, recall, ingate, final_state, final_conv = recur_forward(
        resets, recur, branch, init_state, before_conv, conv_params, gate_w, gate_bias, decay_rate
    )
    mixture = blocked(mixture)
    cot_full, residual, normed_mlp = mixer_out(n, mixture, w_output, cotangent, tokens, gain_second)
    hidden, grad_gelu, grad_linear, grad_down, g_residual, g_low, gain_second_grad = mlp(
        n, copies, normed_mlp, cot_full, w_gelu, w_linear, w_down, residual, gain_second
    )
    mlp_sums = lax.psum((grad_gelu, grad_linear), "dp")
    output, g_mixture, grad_output = down(n, copies, hidden, w_down, residual, g_low, w_output, mixture)
    g_recur, g_branch, small, g_gates, grad_down = recur_back(
        resets, flat(g_mixture), branch, states, recur, conv_low, recall, ingate, init_state, before_conv,
        conv_params, gate_w, decay_rate, grad_down,
    )
    mlp_sums, grad_output, small = lax.optimization_barrier((mlp_sums, grad_output, small))
    grad_output = lax.psum(grad_output, "dp")
    input_grad, grad_input, grad_branch, gates, g_conv, g_bias, g_decay, gains = input_back(
        n, copies, g_recur, g_branch, w_in, w_br, flat(normed), tokens, g_residual, gain_first,
        gain_second_grad, g_gates, small, blocks,
    )
    grad_gelu, grad_linear, grad_input, grad_branch, grad_output = widen(
        mlp_sums, (grad_input, grad_branch), grad_output
    )
    return (
        output,
        input_grad,
        final_state,
        final_conv.transpose(1, 0, 2),
        gains[0],
        grad_input.T,
        grad_branch.T,
        g_conv,
        gates,
        g_bias,
        g_decay[0],
        grad_output,
        gains[1],
        grad_gelu,
        grad_linear,
        grad_down,
    )


def solution(mesh):
    in_specs = (
        P(("dp", "tensor"), None),
        P(("dp", "tensor"), None),
        P("dp"),
        P("dp", "tensor"),
        P("dp", None, "tensor"),
        P(),
        P(None, "tensor"),
        P(None, "tensor"),
        P(None, "tensor"),
        P(None, "tensor", None, None),
        P(None, "tensor"),
        P("tensor"),
        P("tensor", None),
        P(),
        P(None, "tensor"),
        P(None, "tensor"),
        P("tensor", None),
    )
    out_specs = (
        P(("dp", "tensor"), None),
        P(("dp", "tensor"), None),
        P("dp", "tensor"),
        P("dp", None, "tensor"),
        P("tensor"),
        P(None, "tensor"),
        P(None, "tensor"),
        P(None, "tensor"),
        P(None, "tensor", None, None),
        P(None, "tensor"),
        P("tensor"),
        P("tensor", None),
        P("tensor"),
        P(None, "tensor"),
        P(None, "tensor"),
        P("tensor", None),
    )
    return jax.shard_map(
        functools.partial(body, mesh.shape["tensor"], mesh.shape["dp"]),
        mesh=mesh,
        in_specs=in_specs,
        out_specs=out_specs,
        check_vma=False,
    )
```

```python
import functools

import jax
import jax.numpy as jnp
from jax import lax
from jax.experimental import pallas as pl
from jax.experimental.pallas import tpu as pltpu
from jax.sharding import PartitionSpec as P

EPSILON = 1e-06
KAPPA = 0.7978845608028654
CUBIC = 0.044715
PIECES = 2
STRIPS = 4
PARTS = 8
F32 = jnp.float32
BF16 = jnp.bfloat16
ANY = pl.BlockSpec(memory_space=pl.ANY)
VM = pl.BlockSpec(memory_space=pltpu.VMEM)
VMEM_LIMIT = 61 * 1024 * 1024
MESH = pl.DeviceIdType.MESH


def dot(a, b):
    return jnp.dot(a, b, preferred_element_type=F32)


def dot_nt(a, b):
    return lax.dot_general(a, b, (((1,), (1,)), ((), ())), preferred_element_type=F32)


def dot_tn(a, b):
    return lax.dot_general(a, b, (((0,), (0,)), ((), ())), preferred_element_type=F32)


def tile_of(extent, wanted):
    while extent % wanted:
        wanted //= 2
    return wanted


def span(i, size):
    return pl.ds(pl.multiple_of(i * size, size), size)


def loop(count, body):
    def step(i, carry):
        body(i)
        return carry

    lax.fori_loop(0, count, step, 0)


class Place:
    def __init__(self, n):
        self.n = n
        self.nz = n // 2
        self.t = lax.axis_index("tensor")
        self.c = lax.rem(self.t, 2)
        self.j = lax.div(self.t, 2)
        self.sib = self.t + 1 - 2 * self.c
        self.has_up = self.j < self.nz - 1
        self.has_down = self.j > 0

    def greet(self, partners=()):
        barrier = pltpu.get_barrier_semaphore()

        def signal(t):
            pl.semaphore_signal(barrier, inc=1, device_id={"tensor": t}, device_id_type=MESH)

        for i in partners:
            pl.semaphore_signal(barrier, inc=1, device_id={"dp": i}, device_id_type=MESH)

        signal(self.sib)
        pl.when(self.has_up)(lambda: signal(self.t + 2))
        pl.when(self.has_down)(lambda: signal(self.t - 2))
        pl.semaphore_wait(
            barrier,
            1 + len(partners) + self.has_up.astype(jnp.int32) + self.has_down.astype(jnp.int32),
        )

    def copy(self, src, dst, send, recv, t):
        return pltpu.make_async_remote_copy(
            src_ref=src,
            dst_ref=dst,
            send_sem=send,
            recv_sem=recv,
            device_id={"tensor": t},
            device_id_type=MESH,
        )


class Gather:
    def __init__(self, place, full, sent, came):
        self.place, self.full, self.sent, self.came = place, full, sent, came
        self.pieces = came.shape[1]
        self.size = full.shape[1] // self.pieces

    @staticmethod
    def scratch(n, rows, width):
        return [
            pltpu.VMEM((n, rows, width), BF16),
            pltpu.SemaphoreType.DMA((n, PIECES, 3)),
            pltpu.SemaphoreType.DMA((n, PIECES)),
        ]

    def copy(self, t, p, way, to):
        piece = self.full.at[t, pl.ds(p * self.size, self.size)]
        return self.place.copy(piece, piece, self.sent.at[t, p, way], self.came.at[t, p], to)

    def start(self):
        g = self.place
        for p in range(self.pieces):
            pl.when(g.has_up)(lambda: self.copy(g.t, p, 0, g.t + 2).start())
            pl.when(g.has_down)(lambda: self.copy(g.t, p, 1, g.t - 2).start())
        for p in range(self.pieces):
            self.copy(g.t, p, 2, g.sib).start()

    def forward(self, d, pieces=None):
        g = self.place
        for p in range(self.pieces) if pieces is None else pieces:

            @pl.when(g.j - d >= 0)
            def _():
                t = g.t - 2 * d
                self.copy(t, p, 0, g.sib).wait_recv()
                pl.when(g.has_up)(lambda: self.copy(t, p, 0, g.t + 2).start())
                self.copy(t, p, 2, g.sib).start()

            @pl.when(g.j + d < g.nz)
            def _():
                t = g.t + 2 * d
                self.copy(t, p, 1, g.sib).wait_recv()
                pl.when(g.has_down)(lambda: self.copy(t, p, 1, g.t - 2).start())
                self.copy(t, p, 2, g.sib).start()

    def each(self, d, use):
        g = self.place

        def visit(q):
            core, way = lax.div(q, 2), 2 * lax.rem(q, 2) - 1
            j = g.j + way * d
            there = jnp.logical_and(j >= 0, j < g.nz)

            @pl.when(jnp.logical_and(there, jnp.logical_or(d > 0, way > 0)))
            def _():
                t = 2 * j + lax.rem(g.c + core, 2)

                @pl.when(core > 0)
                def _():
                    for p in range(self.pieces):
                        self.copy(t, p, 2, g.sib).wait_recv()

                use(t)

        loop(4, visit)

    def finish(self):
        g = self.place

        def done(t):
            for p in range(self.pieces):
                self.copy(t, p, 2, g.sib).wait_send()

                @pl.when(jnp.logical_and(t <= g.t, g.has_up))
                def _():
                    self.copy(t, p, 0, g.sib).wait_send()

                @pl.when(jnp.logical_and(t >= g.t, g.has_down))
                def _():
                    self.copy(t, p, 1, g.sib).wait_send()

        loop(g.nz, lambda k: done(2 * k + g.c))


class Scatter:
    def __init__(self, place, partial, tile, bufs):
        self.place, self.partial, self.tile = place, partial, tile
        self.to_sib, self.from_sib, self.line, self.acc = bufs[:4]
        self.sib_send, self.sib_recv, self.line_send, self.line_recv = bufs[4:]
        self.out = self.from_sib
        self.tiles = self.acc.shape[1] // tile

    @staticmethod
    def scratch(n, rows, width):
        nz = n // 2
        return [
            pltpu.VMEM((nz, rows, width), BF16),
            pltpu.VMEM((nz, rows, width), BF16),
            pltpu.VMEM((nz + 1, rows, width), BF16),
            pltpu.VMEM((rows, width), F32),
            pltpu.SemaphoreType.DMA((nz,)),
            pltpu.SemaphoreType.DMA((nz,)),
            pltpu.SemaphoreType.DMA((nz, STRIPS)),
            pltpu.SemaphoreType.DMA((nz + 1, STRIPS)),
        ]

    def sib_copy(self, k):
        return self.place.copy(
            self.to_sib.at[k],
            self.from_sib.at[k],
            self.sib_send.at[k],
            self.sib_recv.at[k],
            self.place.sib,
        )

    def line_copy(self, k, slot, p, to):
        at = self.strip(p)
        return self.place.copy(
            self.out.at[k, at], self.line.at[slot, at], self.line_send.at[k, p], self.line_recv.at[slot, p], to
        )

    def strip(self, p):
        return span(p, self.acc.shape[0] // STRIPS)

    def offer(self, k):
        t = 2 * k + 1 - self.place.c

        def part(i):
            cols = span(i, self.tile)
            self.to_sib[k, :, cols] = self.partial(t, cols).astype(BF16)

        loop(self.tiles, part)
        self.sib_copy(k).start()

    def pair(self, k):
        self.sib_copy(k).wait_recv()
        t = 2 * k + self.place.c

        def part(i):
            cols = span(i, self.tile)
            self.acc[:, cols] = self.partial(t, cols) + self.from_sib[k, :, cols].astype(F32)

        loop(self.tiles, part)

    def offers(self, d):
        g = self.place

        def way_of(w):
            k = g.j + (1 - 2 * w) * d

            @pl.when(jnp.logical_and(jnp.logical_and(k >= 0, k < g.nz), jnp.logical_or(d > 0, w == 0)))
            def _():
                self.offer(k)

        loop(2, way_of)

    def step(self, d):
        g = self.place

        def way_of(w):
            sign = 1 - 2 * w
            k = g.j + sign * d

            @pl.when(jnp.logical_and(k >= 0, k < g.nz))
            def _():
                self.pair(k)
                upstream = g.j - sign
                more = jnp.logical_and(upstream >= 0, upstream < g.nz)

                slot = jnp.where(jnp.logical_and(d == 1, w == 1), g.nz, k)

                def pass_on(p):
                    at = self.strip(p)

                    @pl.when(more)
                    def _():
                        self.line_copy(k, k, p, g.sib).wait_recv()
                        self.out[k, at] = (self.acc[at] + self.line[k, at].astype(F32)).astype(BF16)

                    @pl.when(jnp.logical_not(more))
                    def _():
                        self.out[k, at] = self.acc[at].astype(BF16)

                    self.line_copy(k, slot, p, g.t + 2 * sign).start()

                loop(STRIPS, pass_on)

        loop(2, way_of)

    def last(self):
        g = self.place
        self.pair(g.j)

        def take(p):
            at = self.strip(p)

            @pl.when(g.has_down)
            def _():
                self.line_copy(g.j, g.j, p, g.sib).wait_recv()
                self.acc[at] += self.line[g.j, at].astype(F32)

            @pl.when(g.has_up)
            def _():
                self.line_copy(g.j, g.nz, p, g.sib).wait_recv()
                self.acc[at] += self.line[g.nz, at].astype(F32)

        loop(STRIPS, take)

    def finish(self):
        g = self.place

        def done(k):
            self.sib_copy(k).wait_send()
            pl.when(g.j != k)(
                lambda: loop(STRIPS, lambda p: self.line_copy(k, k, p, g.sib).wait_send())
            )

        loop(g.nz, done)


class Halving:
    def __init__(self, me, count, data, landed, final, sems):
        self.me, self.count = me, count
        self.data, self.landed, self.final = data, landed, final
        self.out_send, self.out_recv, self.back_send, self.back_recv = (sems.at[q] for q in range(4))
        self.bits = count.bit_length() - 1
        assert count == 1 << self.bits

    @staticmethod
    def scratch(count, rows, columns):
        return [
            pltpu.VMEM((2, count, 1, rows, columns), BF16),
            pltpu.VMEM((2, count - 1, 1, rows, columns), BF16),
            pltpu.VMEM((2, count, 1, rows, columns), BF16),
            pltpu.SemaphoreType.DMA((4, 2, count - 1)),
        ]

    @staticmethod
    def over(me, count, data, landed, final, sems):
        def at(ref):
            return lambda track, index: ref.at[track, index]

        return Halving(me, count, at(data), at(landed), at(final), sems)

    def partners(self):
        return [self.me + (1 - 2 * self.own(b)) * (1 << b) for b in range(self.bits)]

    def own(self, bit):
        return lax.rem(lax.div(self.me, 1 << bit), 2)

    def swaps(self, s):
        for track in (0, 1):
            order = [(i + track) % self.bits for i in range(self.bits)]
            bit = order[s]
            partner = self.me + (1 - 2 * self.own(bit)) * (1 << bit)
            fixed = sum(self.own(b) * (1 << b) for b in order[:s])
            for u in range(self.count >> (s + 1)):
                free = sum(((u >> i) & 1) << b for i, b in enumerate(order[s + 1 :]))
                slot = self.count - (self.count >> s) + u
                kept = fixed + free + self.own(bit) * (1 << bit)
                yield track, slot, partner, fixed + free + (1 - self.own(bit)) * (1 << bit), kept

    def out(self, track, slot, partner, given):
        return pltpu.make_async_remote_copy(
            src_ref=self.data(track, given),
            dst_ref=self.landed(track, slot),
            send_sem=self.out_send.at[track, slot],
            recv_sem=self.out_recv.at[track, slot],
            device_id={"dp": partner},
            device_id_type=MESH,
        )

    def back(self, track, slot, partner, segment):
        return pltpu.make_async_remote_copy(
            src_ref=self.final(track, segment),
            dst_ref=self.final(track, segment),
            send_sem=self.back_send.at[track, slot],
            recv_sem=self.back_recv.at[track, slot],
            device_id={"dp": partner},
            device_id_type=MESH,
        )

    def start(self, s=0):
        for track, slot, partner, given, _ in self.swaps(s):
            self.out(track, slot, partner, given).start()

    def turn(self, s):
        for track, slot, partner, given, kept in self.swaps(s):
            self.out(track, slot, partner, given).wait_recv()
            mine, theirs = self.data(track, kept), self.landed(track, slot)
            result = self.final(track, kept) if s == self.bits - 1 else mine
            blocks, rows, _ = mine.shape
            tile = tile_of(rows, 32)

            def add(r):
                block, at = lax.div(r, rows // tile), span(lax.rem(r, rows // tile), tile)
                result[block, at] = (mine[block, at].astype(F32) + theirs[block, at].astype(F32)).astype(BF16)

            loop(blocks * (rows // tile), add)
        if s < self.bits - 1:
            self.start(s + 1)
        else:
            self.start_back(s)

    def start_back(self, s):
        for track, slot, partner, _, kept in self.swaps(s):
            self.back(track, slot, partner, kept).start()

    def turn_back(self, s):
        for track, slot, partner, given, _ in self.swaps(s):
            self.back(track, slot, partner, given).wait_recv()
        if s > 0:
            self.start_back(s - 1)

    def events(self):
        steps = [functools.partial(self.turn, s) for s in range(self.bits)]
        return steps + [functools.partial(self.turn_back, s) for s in range(self.bits - 1, 0, -1)]

    def finish(self):
        self.turn_back(0)
        for s in range(self.bits):
            for track, slot, partner, given, kept in self.swaps(s):
                self.out(track, slot, partner, given).wait_send()
                self.back(track, slot, partner, kept).wait_send()


def fetching(kernel, which):
    def wrapped(*refs):
        refs = list(refs)
        sems = refs.pop()
        kept = refs[len(refs) - len(which) :]
        del refs[len(refs) - len(which) :]
        copies = {}
        for q, i in enumerate(which):
            copies[i] = pltpu.make_async_copy(refs[i], kept[q], sems.at[q])
            copies[i].start()
            refs[i] = kept[q]

        def arrive(*wanted):
            for i in wanted:
                copies[i].wait()

        return kernel(arrive, *refs)

    return wrapped


def fetched_specs(inputs, which, plain=()):
    specs = [ANY if i in which or i in plain else VM for i in range(len(inputs))]
    scratch = [pltpu.VMEM(inputs[i].shape, inputs[i].dtype) for i in which]
    return specs, scratch + [pltpu.SemaphoreType.DMA((len(which),))]


def comm_params(collective_id):
    return pltpu.CompilerParams(
        collective_id=collective_id, has_side_effects=True, vmem_limit_bytes=VMEM_LIMIT
    )


def cost(flops):
    return pl.CostEstimate(flops=int(flops), bytes_accessed=200_000_000, transcendentals=0)


def shape(*dims, dtype=F32):
    return jax.ShapeDtypeStruct(dims, dtype)


def inv_rms(values):
    return lax.rsqrt(jnp.mean(values * values, axis=-1, keepdims=True) + EPSILON)


def norm_grad(values, gain, gradient):
    inv = inv_rms(values)
    unit = values * inv
    scaled = gradient * gain
    centred = jnp.mean(scaled * unit, axis=-1, keepdims=True)
    return inv * (scaled - unit * centred), gradient * unit


def sigmoid(v):
    return 1.0 / (1.0 + jnp.exp(-v))


def gelu_parts(v):
    square = v * v
    bend = jnp.tanh(KAPPA * v * (1.0 + CUBIC * square))
    half = 0.5 * (1.0 + bend)
    slope = half + 0.5 * v * (1.0 - bend * bend) * (KAPPA * (1.0 + 3.0 * CUBIC * square))
    return v * half, slope


def one_minus_square(log_decay, decay):
    m = -2.0 * log_decay
    series = m * (
        1.0 - m * (1 / 2) * (1.0 - m * (1 / 3) * (1.0 - m * (1 / 4) * (1.0 - m * (1 / 5) * (1.0 - m * (1 / 6)))))
    )
    return jnp.where(m < 0.35, series, 1.0 - decay * decay)


def starts(reset, here, init_state, init_conv, state, hist):
    keep = (1 - reset).astype(F32)
    state[...] = jnp.broadcast_to(init_state[here] * keep, state.shape)
    before = [init_conv[q, here] * keep for q in range(3)]
    hist[0:8] = jnp.concatenate([jnp.zeros((5, hist.shape[1]), F32)] + before, axis=0)


def recur_chunk(base, u, branch, conv, gate_w, bias, decay, kept, hist, decay_buf, drive_buf, carry):
    states, mixture, conv_low, recall, ingate = kept
    rows, channels = decay_buf.shape
    tile = 32

    def rows_of(i, size):
        return pl.ds(pl.multiple_of(base + i * size, size), size)

    whole = rows_of(0, rows)
    hist[8:] = u[whole]

    def convolve(i):
        window = hist[pl.ds(pl.multiple_of(i * tile, tile), tile + 8)]
        value = conv[4:5] + conv[0:1] * window[8:] + conv[1:2] * window[7 : tile + 7]
        value = value + conv[2:3] * window[6 : tile + 6] + conv[3:4] * window[5 : tile + 5]
        conv_low[rows_of(i, tile)] = value.astype(BF16)

    loop(rows // tile, convolve)
    hist[0:8] = hist[rows : rows + 8]
    low = conv_low[whole]
    recall[whole] = dot(low, gate_w[0])
    ingate[whole] = dot(low, gate_w[1])

    def gates(i):
        at, here = rows_of(i, tile), span(i, tile)
        r = sigmoid(recall[at] + bias[0:1])
        k = sigmoid(ingate[at] + bias[1:2])
        recall[at] = r
        ingate[at] = k
        log_decay = -8.0 * r * decay[...][None]
        step = jnp.exp(log_decay)
        decay_buf[here] = step
        drive_buf[here] = jnp.sqrt(one_minus_square(log_decay, step)) * k * conv_low[at].astype(F32)

    loop(rows // tile, gates)
    row = lax.broadcasted_iota(jnp.int32, (8, channels), 0)

    def scan(i, before):
        for part in range(4):
            at = pl.ds(pl.multiple_of(i * 32 + part * 8, 8), 8)
            a, b = decay_buf[at], drive_buf[at]
            for shift in (1, 2, 4):
                inside = row >= shift
                b = b + a * jnp.where(inside, pltpu.roll(b, shift, 0), 0.0)
                a = a * jnp.where(inside, pltpu.roll(a, shift, 0), 1.0)
            h = a * before + b
            states[pl.ds(pl.multiple_of(base + i * 32 + part * 8, 8), 8)] = h
            before = jnp.broadcast_to(h[7:8], (8, channels))
        return before

    carry[...] = lax.fori_loop(0, rows // 32, scan, carry[...])

    def mix(i):
        at = rows_of(i, tile)
        value, _ = gelu_parts(branch[at])
        mixture[at] = (states[at] * value).astype(BF16)

    loop(rows // tile, mix)


def project_kernel(
    n, arrive, tokens, gain, w_in, w_br, resets, init_state, init_conv, conv, gate_w, bias, decay,
    normed, recur, branch, states, mixture, conv_low, recall, ingate, final_state, final_conv,
    full, sent, came, held_a, held_b, kept_s, kept_m, kept_c, kept_r, kept_i,
    hist, decay_buf, drive_buf, carry, saved, written,
):
    g = Place(n)
    gather = Gather(g, full, sent, came)
    rows = full.shape[1]
    part = 64

    def normalize(i):
        at = span(i, part)
        values = tokens[at].astype(F32)
        full[g.t, at] = (values * inv_rms(values) * gain[...].astype(F32)).astype(BF16)

    loop(rows // part, normalize)
    g.greet()
    gather.start()
    arrive(2, 3)

    def out(t):
        return pltpu.make_async_copy(full.at[t], normed.at[t], saved.at[t])

    def use(t):
        out(t).start()
        at = span(t, rows)
        held_a[at] = dot_nt(full[t], w_in[...])
        held_b[at] = dot_nt(full[t], w_br[...])

    kept = (kept_s, kept_m, kept_c, kept_r, kept_i)
    pairs = ((held_a, recur), (held_b, branch)) + tuple(zip(kept, (states, mixture, conv_low, recall, ingate)))
    sequences = init_state.shape[0]
    length = n * rows // sequences
    size = decay_buf.shape[0]
    chunks = length // size

    def leave(c, act):
        at = span(c, size)
        for q, (held, target) in enumerate(pairs):
            act(pltpu.make_async_copy(held.at[at], target.at[at], written.at[c, q]))

    def sequence(s):
        here = pl.ds(s, 1)
        starts(resets[s], here, init_state, init_conv, carry, hist)

        def chunk(c):
            index = s * chunks + c
            base = index * size
            recur_chunk(base, held_a, held_b, conv, gate_w, bias, decay, kept, hist, decay_buf, drive_buf, carry)
            leave(index, lambda copy: copy.start())

        loop(chunks, chunk)
        final_state[here] = carry[0:1]
        for q in range(3):
            final_conv[q, here] = hist[5 + q : 6 + q]

    def step(d):
        pl.when(d > 0)(lambda: gather.forward(d))
        gather.each(d, use)

        def whole(s):
            first = lax.div(s * length, 2 * rows)
            last = lax.div((s + 1) * length - 1, 2 * rows)
            pl.when(jnp.maximum(jnp.abs(first - g.j), jnp.abs(last - g.j)) == d)(lambda: sequence(s))

        loop(sequences, whole)

    loop(g.nz, step)
    loop(n, lambda t: out(t).wait())
    loop(sequences * chunks, lambda c: leave(c, lambda copy: copy.wait()))
    gather.finish()


def project(n, tokens, gain, w_in, w_br, resets, init_state, init_conv, conv, gate_w, bias, decay):
    rows, width = tokens.shape
    channels = w_in.shape[0]
    sequences = init_state.shape[0]
    total = n * rows
    size = tile_of(total // sequences, 256)
    inputs = (tokens, gain, w_in, w_br, resets, init_state, init_conv, conv, gate_w, bias, decay)
    specs, kept = fetched_specs(inputs, (2, 3))
    specs[4] = pl.BlockSpec(memory_space=pltpu.SMEM)
    wide, narrow = (total, channels), pltpu.VMEM((total, channels), BF16)
    return pl.pallas_call(
        fetching(functools.partial(project_kernel, n), (2, 3)),
        out_shape=(
            shape(n, rows, width, dtype=BF16),
            shape(*wide),
            shape(*wide),
            shape(*wide),
            shape(*wide, dtype=BF16),
            shape(*wide, dtype=BF16),
            shape(*wide),
            shape(*wide),
            shape(sequences, channels),
            shape(3, sequences, channels),
        ),
        in_specs=specs,
        out_specs=(ANY,) * 8 + (VM,) * 2,
        scratch_shapes=Gather.scratch(n, rows, width)
        + [pltpu.VMEM(wide, F32)] * 3
        + [narrow] * 2
        + [pltpu.VMEM(wide, F32)] * 2
        + [
            pltpu.VMEM((size + 8, channels), F32),
            pltpu.VMEM((size, channels), F32),
            pltpu.VMEM((size, channels), F32),
            pltpu.VMEM((8, channels), F32),
            pltpu.SemaphoreType.DMA((n,)),
            pltpu.SemaphoreType.DMA((total // size, 7)),
        ]
        + kept,
        compiler_params=comm_params(1),
        cost_estimate=cost(4 * n * rows * width * channels),
        name="project",
    )(*inputs)


def mixer_out_kernel(
    n, arrive, mixture, w_output, cotangent, tokens, gain, cot_full, residual, normed,
    full, sent, came, saved, *bufs
):
    g = Place(n)
    gather = Gather(g, full, sent, came)
    scatter = Scatter(g, lambda t, cols: dot(mixture[t], w_output[:, cols]), tile_of(residual.shape[1], 512), bufs)
    first = pltpu.make_async_copy(cotangent, full.at[g.t], saved.at[0])
    first.start()
    g.greet()
    first.wait()
    gather.start()
    arrive(0, 1)

    def use(t):
        pltpu.make_async_copy(full.at[t], cot_full.at[t], saved.at[t]).start()

    scatter.offers(g.nz - 1)

    def around(i):
        d = g.nz - 1 - i
        scatter.offers(d - 1)
        scatter.step(d)
        gather.each(i, use)
        gather.forward(i + 1)

    loop(g.nz - 1, around)
    scatter.last()
    arrive(3)
    part = 64

    def rows_of(i):
        at = span(i, part)
        values = scatter.acc[at] + tokens[at].astype(F32)
        residual[at] = values
        normed[at] = (values * inv_rms(values) * gain[...].astype(F32)).astype(BF16)

    loop(residual.shape[0] // part, rows_of)
    gather.each(g.nz - 1, use)
    loop(n, lambda t: pltpu.make_async_copy(full.at[t], cot_full.at[t], saved.at[t]).wait())
    scatter.finish()
    gather.finish()


def mixer_out(n, mixture, w_output, cotangent, tokens, gain):
    rows, width = tokens.shape
    inputs, which = (mixture, w_output, cotangent, tokens, gain), (0, 1, 3)
    specs, kept = fetched_specs(inputs, which, (2,))
    return pl.pallas_call(
        fetching(functools.partial(mixer_out_kernel, n), which),
        out_shape=(
            shape(n, rows, width, dtype=BF16),
            shape(rows, width),
            shape(rows, width, dtype=BF16),
        ),
        in_specs=specs,
        out_specs=(ANY, VM, VM),
        scratch_shapes=Gather.scratch(n, rows, width)
        + [pltpu.SemaphoreType.DMA((n,))]
        + Scatter.scratch(n, rows, width)
        + kept,
        compiler_params=comm_params(2),
        cost_estimate=cost(2 * n * rows * width * mixture.shape[-1]),
        name="mixer_out",
    )(*inputs)


def mlp_kernel(
    n, copies, arrive, normed, cot_full, w_gelu, w_linear, w_down, residual, gain,
    hidden, grad_gelu, grad_linear, grad_down, g_residual, g_low, g_gain,
    full, sent, came, cot, keep_h, keep_f, keep_s, acc_g, acc_l, acc_d,
    to_sib, sums, line, acc, landed, swap_sems, saved, fetched, drained, sib_sent, sib_came, line_sent, line_came,
):
    g = Place(n)
    gather = Gather(g, full, sent, came)
    columns = w_gelu.shape[1]
    rows, width = acc.shape
    tile = tile_of(columns, 256)
    wide = tile_of(width, 512)
    strip = rows // PARTS
    me = lax.axis_index("dp")
    start = pltpu.make_async_copy(normed, full.at[g.t], saved.at[0])
    start.start()
    part_width = width // (2 * copies)
    depth = columns // rows

    def segment(track, index):
        return pl.ds(pl.multiple_of((track * copies + index) * part_width, part_width), part_width)

    swap = Halving(
        me,
        copies,
        lambda track, index: full.at[0:depth, :, segment(track, index)],
        lambda track, slot: landed.at[track, slot],
        lambda track, index: full.at[depth : 2 * depth, :, segment(track, index)],
        swap_sems,
    )
    def fetch(t, q):
        return pltpu.make_async_copy(cot_full.at[t], cot.at[q], fetched.at[q])

    g.greet(swap.partners())
    start.wait()
    gather.start()
    fetch(2 * g.j, 0).start()
    fetch(2 * g.j + 1, 1).start()
    arrive(2, 3, 4)
    acc_g[...] = jnp.zeros_like(acc_g)
    acc_l[...] = jnp.zeros_like(acc_l)
    acc_d[...] = jnp.zeros_like(acc_d)

    def save(t, q):
        return pltpu.make_async_copy(keep_h.at[q], hidden.at[t], saved.at[q])

    def layer(t, q):
        fetch(t, q).wait()

        def part(i):
            cols = span(i, tile)
            first = dot(full[t], w_gelu[:, cols])
            second = dot(full[t], w_linear[:, cols])
            back = dot_nt(cot[q], w_down[cols])
            value, slope = gelu_parts(first)
            keep_h[q, :, cols] = (value * second).astype(BF16)
            keep_f[q, :, cols] = (back * second * slope).astype(BF16)
            keep_s[q, :, cols] = (back * value).astype(BF16)

        loop(columns // tile, part)
        save(t, q).start()

    def partial(q, cols):
        return dot_nt(keep_f[q], w_gelu[cols]) + dot_nt(keep_s[q], w_linear[cols])

    def sib_copy(k):
        return g.copy(to_sib, sums.at[k], sib_sent, sib_came.at[k], g.sib)

    def line_copy(k, slot, p, to):
        at = pl.ds(pl.multiple_of(p * strip, strip), strip)
        return g.copy(
            sums.at[k, at], line.at[slot, at], line_sent.at[k, p], line_came.at[slot, p], to
        )

    def chip(d, way):
        k = g.j + way * d
        mine, its = g.c, 1 - g.c
        own, other = 2 * k + mine, 2 * k + its
        for p in range(gather.pieces):
            gather.copy(other, p, 2, g.sib).wait_recv()
        layer(other, its)

        def offer(i):
            cols = span(i, wide)
            to_sib[:, cols] = partial(its, cols).astype(BF16)

        loop(width // wide, offer)
        sib_copy(k).start()
        layer(own, mine)
        sib_copy(k).wait()

        @pl.when(d == 0)
        def _():
            def part(i):
                cols = span(i, wide)
                acc[:, cols] = partial(mine, cols) + sums[k, :, cols].astype(F32)

            loop(width // wide, part)

        @pl.when(d > 0)
        def _():
            def part(i):
                cols = span(i, wide)
                sums[k, :, cols] = (partial(mine, cols) + sums[k, :, cols].astype(F32)).astype(BF16)

            loop(width // wide, part)
            first = jnp.logical_or(
                jnp.logical_and(way > 0, jnp.logical_not(g.has_down)),
                jnp.logical_and(way < 0, jnp.logical_not(g.has_up)),
            )

            @pl.when(first)
            def _():
                slot = jnp.where(jnp.logical_and(way < 0, d == 1), g.nz, k)
                for p in range(PARTS):
                    line_copy(k, slot, p, g.t + 2 * way).start()

        def part(i):
            at = span(i, wide)
            both = full[pl.ds(2 * k, 2), :, at].reshape(2 * rows, wide)
            acc_g[at] += dot_tn(both, keep_f[...].reshape(2 * rows, columns))
            acc_l[at] += dot_tn(both, keep_s[...].reshape(2 * rows, columns))
            acc_d[:, at] += dot_tn(
                keep_h[...].reshape(2 * rows, columns), cot[:, :, at].reshape(2 * rows, wide)
            )

        loop(width // wide, part)
        both_ways = jnp.logical_and(g.j + d < g.nz, g.j - d >= 0)
        again = jnp.logical_and(both_ways, jnp.logical_and(way > 0, d > 0))
        later = jnp.where(g.j + d + 1 < g.nz, g.j + d + 1, g.j - d - 1)
        following = jnp.where(again, g.j - d, later)

        @pl.when(following >= 0)
        def _():
            fetch(2 * following, 0).start()
            fetch(2 * following + 1, 1).start()

        save(other, its).wait()
        save(own, mine).wait()

    def relay(m, events=()):
        def take(k, slot, sign, p):
            at = pl.ds(pl.multiple_of(p * strip, strip), strip)
            line_copy(k, slot, p, g.sib).wait_recv()

            @pl.when(k == g.j)
            def _():
                acc[at] += line[slot, at].astype(F32)

            @pl.when(k != g.j)
            def _():
                sums[k, at] = (sums[k, at].astype(F32) + line[slot, at].astype(F32)).astype(BF16)
                there = jnp.where(jnp.logical_and(sign < 0, k == g.j - 1), g.nz, k)
                line_copy(k, there, p, g.t + 2 * sign).start()

        def rise(p):
            pl.when(jnp.logical_and(g.has_down, m >= g.j))(lambda: take(m, m, 1, p))

        def fall(p):
            k = g.nz - 1 - m
            pl.when(jnp.logical_and(g.has_up, k <= g.j))(
                lambda: take(k, jnp.where(k == g.j, g.nz, k), -1, p)
            )

        lower = 2 * g.j < g.nz

        def strips(i):
            @pl.when(i < PARTS)
            def _():
                pl.when(lower)(lambda: rise(i))
                pl.when(jnp.logical_not(lower))(lambda: fall(i))

            @pl.when(i > 0)
            def _():
                pl.when(lower)(lambda: fall(i - 1))
                pl.when(jnp.logical_not(lower))(lambda: rise(i - 1))

        def between(i):
            strips(i)
            for q, event in enumerate(events):
                pl.when(i == (q + 1) * PARTS // len(events))(event)

        loop(PARTS + 1, between)

    def cores(d):
        up, down = g.j + d < g.nz, g.j - d >= 0

        def way_of(w):
            both = jnp.logical_and(up, down)
            way = jnp.where(jnp.logical_and(w == 0, up), 1, -1)
            wanted = jnp.where(w == 0, jnp.logical_or(up, down), jnp.logical_and(both, d > 0))
            pl.when(wanted)(lambda: chip(d, way))

            @pl.when(d < g.nz - 1)
            def _():
                for p in range(gather.pieces):
                    pl.when(w == min(p, 1))(lambda: gather.forward(d + 1, (p,)))

        loop(2, way_of)

    def step(d):
        @pl.when(d < g.nz)
        def _():
            cores(d)

        @pl.when(d == g.nz - 1)
        def _():
            gather.finish()
            for i in range(depth):
                full[i] = acc_d[pl.ds(i * rows, rows)].astype(BF16)
            swap.start()

        pl.when(d > 1)(lambda: relay(d - 1))

    loop(g.nz, step)

    stages = [held.at[q] for held in (keep_h, keep_f, keep_s) for q in (0, 1)]
    leaving = []

    def leave(i, value, out):
        slot = i % len(stages)
        if len(leaving) >= len(stages):
            leaving[i - len(stages)].wait()
        stages[slot][...] = value.astype(BF16)
        copy = pltpu.make_async_copy(stages[slot], out, drained.at[slot])
        copy.start()
        leaving.append(copy)

    for i in range(width // rows):
        at = pl.ds(i * rows, rows)
        leave(2 * i, acc_g[at], grad_gelu.at[at])
        leave(2 * i + 1, acc_l[at], grad_linear.at[at])
    events = swap.events()
    events.pop(0)()
    relay(g.nz - 1, events)
    own = pltpu.make_async_copy(cot_full.at[g.t], cot.at[0], fetched.at[0])
    own.start()
    own.wait()
    arrive(5)
    lines = 32
    g_gain[...] = jnp.zeros_like(g_gain)

    def rows_of(i):
        at = span(i, lines)
        back, terms = norm_grad(residual[at], gain[...].astype(F32), acc[at])
        value = cot[0, at].astype(F32) + back
        acc[at] = value
        cot[1, at] = value.astype(BF16)
        g_gain[...] += jnp.sum(terms, axis=0, keepdims=True)

    loop(rows // lines, rows_of)
    last = [
        pltpu.make_async_copy(acc, g_residual, saved.at[0]),
        pltpu.make_async_copy(cot.at[1], g_low, saved.at[1]),
    ]
    swap.finish()
    for i in range(depth):
        at = pl.ds(i * rows, rows)
        last.append(pltpu.make_async_copy(full.at[depth + i], grad_down.at[at], drained.at[len(stages) + i]))
    for copy in last:
        copy.start()
    for copy in leaving[-len(stages) :] + last:
        copy.wait()

    def done(k):
        @pl.when(k != g.j)
        def _():
            for p in range(PARTS):
                line_copy(k, k, p, g.sib).wait_send()

    loop(g.nz, done)


def mlp(n, copies, normed, cot_full, w_gelu, w_linear, w_down, residual, gain):
    rows, width = normed.shape
    columns = w_gelu.shape[1]
    kept = pltpu.VMEM((2, rows, columns), BF16)
    sems = pltpu.SemaphoreType.DMA
    inputs, which = (normed, cot_full, w_gelu, w_linear, w_down, residual, gain), (2, 3, 4, 5)
    specs, held = fetched_specs(inputs, which, (0, 1))
    return pl.pallas_call(
        fetching(functools.partial(mlp_kernel, n, copies), which),
        out_shape=(shape(n, rows, columns, dtype=BF16),)
        + (shape(width, columns, dtype=BF16),) * 2
        + (
            shape(columns, width, dtype=BF16),
            shape(rows, width),
            shape(rows, width, dtype=BF16),
            shape(1, width),
        ),
        in_specs=specs,
        out_specs=(ANY,) * 6 + (VM,),
        scratch_shapes=Gather.scratch(n, rows, width)
        + [pltpu.VMEM((2, rows, width), BF16)]
        + [kept] * 3
        + [pltpu.VMEM((width, columns), F32)] * 2
        + [
            pltpu.VMEM((columns, width), F32),
            pltpu.VMEM((rows, width), BF16),
            pltpu.VMEM((n // 2, rows, width), BF16),
            pltpu.VMEM((n // 2 + 1, rows, width), BF16),
            pltpu.VMEM((rows, width), F32),
            pltpu.VMEM((2, copies - 1, columns // rows, rows, width // (2 * copies)), BF16),
            sems((4, 2, copies - 1)),
            sems((2,)),
            sems((2,)),
            sems((6 + columns // rows,)),
            sems,
            sems((n // 2,)),
            sems((n // 2, PARTS)),
            sems((n // 2 + 1, PARTS)),
        ]
        + held,
        compiler_params=comm_params(3),
        cost_estimate=cost(16 * n * rows * width * columns),
        name="mlp",
    )(*inputs)


def down_kernel(
    n, copies, arrive, hidden, w_down, residual, g_low, w_output, mixture, output, g_mixture, grad_output,
    full, sent, came, acc_o, start_sem, *bufs
):
    g = Place(n)
    gather = Gather(g, full, sent, came)
    width = residual.shape[1]
    wide = tile_of(width, 512)
    scatter = Scatter(g, lambda t, cols: dot(hidden[t], w_down[:, cols]), wide, bufs)
    first = pltpu.make_async_copy(g_low, full.at[g.t], start_sem)
    first.start()
    g.greet()
    first.wait()

    def use(t):
        g_mixture[t] = dot_nt(full[t], w_output[...])

        def part(i):
            at = span(i, wide)
            acc_o[:, at] += dot_tn(mixture[t], full[t, :, at])

        loop(width // wide, part)

    gather.start()
    acc_o[...] = jnp.zeros_like(acc_o)
    arrive(0, 1)
    scatter.offers(g.nz - 1)
    arrive(4, 5)

    def around(i):
        d = g.nz - 1 - i
        scatter.offers(d - 1)
        scatter.step(d)
        gather.each(i, use)
        gather.forward(i + 1)

    loop(g.nz - 1, around)
    gather.each(g.nz - 1, use)
    for i in range(copies):
        part = width // copies
        grad_output[i] = acc_o[:, i * part : (i + 1) * part].astype(BF16)
    scatter.last()
    arrive(2)
    output[...] = (scatter.acc[...] + residual[...]).astype(BF16)
    scatter.finish()
    gather.finish()


def down(n, copies, hidden, w_down, residual, g_low, w_output, mixture):
    rows, width = residual.shape
    channels = w_output.shape[0]
    inputs, which = (hidden, w_down, residual, g_low, w_output, mixture), (0, 1, 4, 5, 2)
    specs, kept = fetched_specs(inputs, which, (3,))
    return pl.pallas_call(
        fetching(functools.partial(down_kernel, n, copies), which),
        out_shape=(
            shape(rows, width, dtype=BF16),
            shape(n, rows, channels),
            shape(copies, channels, width // copies, dtype=BF16),
        ),
        in_specs=specs,
        out_specs=(VM,) * 3,
        scratch_shapes=Gather.scratch(n, rows, width)
        + [pltpu.VMEM((channels, width), F32), pltpu.SemaphoreType.DMA]
        + Scatter.scratch(n, rows, width)
        + kept,
        compiler_params=comm_params(5),
        cost_estimate=cost(2 * n * rows * width * (hidden.shape[-1] + 2 * channels)),
        name="down",
    )(*inputs)


def recur_back_kernel(
    resets, g_mix, branch, states, states_before, u, u_before, conv_low, recall, ingate, init_state, init_conv,
    conv, gate_w, decay, narrow_in,
    g_recur, g_branch, small, g_gates, wide_out,
    g_state, step_buf, root_buf, g_conv, pre_r, pre_i, carry, hist_s, hist_u, sums,
):
    sequence, back = pl.program_id(0), pl.program_id(1)
    last = pl.num_programs(1) - 1
    rows, channels = u.shape
    tile = 32
    wide_out[...] = narrow_in[...].astype(F32)

    @pl.when(jnp.logical_and(sequence == 0, back == 0))
    def _():
        sums[...] = jnp.zeros_like(sums)
        g_gates[...] = jnp.zeros_like(g_gates)

    @pl.when(back == 0)
    def _():
        carry[...] = jnp.zeros_like(carry)
        g_conv[rows : rows + 8] = jnp.zeros((8, channels), F32)

    @pl.when(back > 0)
    def _():
        g_conv[rows : rows + 8] = g_conv[0:8]

    @pl.when(back == last)
    def _():
        starts(
            resets[sequence], pl.ds(sequence, 1), init_state, init_conv, hist_s.at[0:8], hist_u
        )

    @pl.when(back < last)
    def _():
        hist_s[0:8] = states_before[...]
        hist_u[0:8] = u_before[...]

    hist_s[8:] = states[...]
    hist_u[8:] = u[...]

    def first(i):
        at = span(i, tile)
        value, slope = gelu_parts(branch[at])
        gm = g_mix[at]
        g_state[at] = gm * value
        g_branch[at] = (gm * states[at] * slope).astype(BF16)
        log_decay = -8.0 * recall[at] * decay[...][None]
        step = jnp.exp(log_decay)
        step_buf[at] = step
        root_buf[at] = jnp.sqrt(one_minus_square(log_decay, step))

    loop(rows // tile, first)
    row = lax.broadcasted_iota(jnp.int32, (8, channels), 0)
    groups = rows // 32

    def scan(i, after):
        for part in range(4):
            at = pl.ds(pl.multiple_of((groups - 1 - i) * 32 + (3 - part) * 8, 8), 8)
            a, gs = step_buf[at], g_state[at]
            b = a * gs
            for shift in (1, 2, 4):
                inside = row < 8 - shift
                b = b + a * jnp.where(inside, pltpu.roll(b, 8 - shift, 0), 0.0)
                a = a * jnp.where(inside, pltpu.roll(a, 8 - shift, 0), 1.0)
            e = a * after + b
            g_state[at] = gs + jnp.where(row < 7, pltpu.roll(e, 7, 0), after)
            after = jnp.broadcast_to(e[0:1], (8, channels))
        return after

    carry[...] = lax.fori_loop(0, groups, scan, carry[...])

    def fold(x):
        return jnp.sum(x.reshape(tile // 8, 8, channels), axis=0)

    def second(i):
        at = span(i, tile)
        window = hist_s[pl.ds(pl.multiple_of(i * tile, tile), tile + 8)]
        before = window[7 : tile + 7]
        g, r, k = g_state[at], recall[at], ingate[at]
        c = conv_low[at].astype(F32)
        step, root = step_buf[at], root_buf[at]
        kc = k * c
        g_log = g * (before * step - kc * (step * step) / root)
        slow = -8.0 * r
        sums[7] += fold(g_log * slow)
        low_r = (g_log * (slow * decay[...][None]) * (1.0 - r)).astype(BF16)
        low_i = (g * root * kc * (1.0 - k)).astype(BF16)
        pre_r[at] = low_r
        pre_i[at] = low_i
        sums[5] += fold(low_r.astype(F32))
        sums[6] += fold(low_i.astype(F32))
        g_conv[at] = g * root * k

    loop(rows // tile, second)
    low_r, low_i, low_c = pre_r[...], pre_i[...], conv_low[...]
    g_gates[0] += dot_tn(low_c, low_r)
    g_gates[1] += dot_tn(low_c, low_i)
    g_conv[0:rows] += dot_nt(low_r, gate_w[0]) + dot_nt(low_i, gate_w[1])

    def third(i):
        at = span(i, tile)
        start = pl.multiple_of(i * tile, tile)
        window = g_conv[pl.ds(start, tile + 8)]
        value = conv[0:1] * window[0:tile]
        for k in (1, 2, 3):
            value = value + conv[k : k + 1] * window[k : tile + k]
        g_recur[at] = value.astype(BF16)
        past = hist_u[pl.ds(start, tile + 8)]
        gc = window[0:tile]
        for k in range(4):
            sums[k] += fold(gc * past[8 - k : tile + 8 - k])
        sums[4] += fold(gc)

    loop(rows // tile, third)

    @pl.when(jnp.logical_and(sequence == pl.num_programs(0) - 1, back == last))
    def _():
        small[...] = jnp.sum(sums[...], axis=1)


def recur_back(
    resets, g_mix, branch, states, u, conv_low, recall, ingate, init_state, init_conv, conv, gate_w, decay, narrow_in
):
    total, channels = u.shape
    sequences = init_state.shape[0]
    length = total // sequences
    rows = tile_of(length, 256)
    chunks = length // rows
    extra_rows = narrow_in.shape[0] // (sequences * chunks)
    extra = pl.BlockSpec((extra_rows, narrow_in.shape[1]), lambda s, c: (s * chunks + c, 0))
    eights = rows // 8

    def at(s, c):
        return (s * chunks + chunks - 1 - c, 0)

    def earlier(s, c):
        return (jnp.maximum((s * chunks + chunks - 1 - c) * eights - 1, 0), 0)

    block = pl.BlockSpec((rows, channels), at)
    before = pl.BlockSpec((8, channels), earlier)

    def whole(x):
        return pl.BlockSpec(x.shape, lambda s, c: (0,) * x.ndim)

    wide = pltpu.VMEM((rows, channels), F32)
    narrow = pltpu.VMEM((rows, channels), BF16)
    long = pltpu.VMEM((rows + 8, channels), F32)
    return pl.pallas_call(
        recur_back_kernel,
        grid=(sequences, chunks),
        out_shape=(
            shape(total, channels, dtype=BF16),
            shape(total, channels, dtype=BF16),
            shape(8, channels),
            shape(2, channels, channels),
            shape(*narrow_in.shape),
        ),
        in_specs=[
            pl.BlockSpec(memory_space=pltpu.SMEM),
            block, block, block, before, block, before, block, block, block,
            whole(init_state), whole(init_conv), whole(conv), whole(gate_w), whole(decay), extra,
        ],
        out_specs=(
            block,
            block,
            pl.BlockSpec((8, channels), lambda s, c: (0, 0)),
            pl.BlockSpec((2, channels, channels), lambda s, c: (0, 0, 0)),
            extra,
        ),
        scratch_shapes=[
            wide, wide, wide, long, narrow, narrow,
            pltpu.VMEM((8, channels), F32), long, long,
            pltpu.VMEM((8, 8, channels), F32),
        ],
        compiler_params=pltpu.CompilerParams(vmem_limit_bytes=VMEM_LIMIT),
        name="recur_back",
    )(
        resets, g_mix, branch, states, states, u, u, conv_low, recall, ingate, init_state, init_conv,
        conv, gate_w, decay, narrow_in,
    )


def input_back_kernel(
    n, copies, arrive, g_recur, g_branch, w_in, w_br, normed, tokens, g_residual, gain, second_gain, g_gates, small,
    input_grad, in_out, br_out, gates_out, conv_out, bias_out, decay_out, gains_out,
    gain_row, gain_parts, gain_in, gain_sum, gain_dp, gain_sent, gain_came, gain_dp_sent, gain_dp_came, *bufs
):
    g = Place(n)
    me = lax.axis_index("dp")
    rows, width = tokens.shape
    channels = w_in.shape[0]
    blocks, block_width = gates_out.shape[1], gates_out.shape[2]
    segment = width // (2 * copies)
    gain_width = width // n
    weights = Halving.over(me, copies, *bufs[:4])
    rest = Halving.over(me, copies, *bufs[4:8])
    padded = bufs[0].shape[3] // 2
    rest_rows = bufs[4].shape[3]

    def block(ref, t):
        return ref[span(t, rows)]

    def partial(t, cols):
        return dot(block(g_recur, t), w_in[:, cols]) + dot(block(g_branch, t), w_br[:, cols])

    scatter = Scatter(g, partial, tile_of(width, 512), bufs[8:])

    def gain_copy(t, slot):
        return g.copy(gain_parts.at[t], gain_in.at[slot], gain_sent.at[t], gain_came.at[slot], t)

    def gain_dp_copy(i, slot):
        return pltpu.make_async_remote_copy(
            src_ref=gain_sum,
            dst_ref=gain_dp.at[slot],
            send_sem=gain_dp_sent.at[i],
            recv_sem=gain_dp_came.at[slot],
            device_id={"dp": i},
            device_id_type=MESH,
        )

    def others(act):
        loop(n, lambda t: pl.when(t != g.t)(lambda: act(t)))

    def copies_of(act):
        loop(copies, lambda i: pl.when(i != me)(lambda: act(i)))

    barrier = pltpu.get_barrier_semaphore()
    others(
        lambda t: pl.semaphore_signal(barrier, inc=1, device_id={"tensor": t}, device_id_type=MESH)
    )
    copies_of(lambda i: pl.semaphore_signal(barrier, inc=1, device_id={"dp": i}, device_id_type=MESH))
    pl.semaphore_wait(barrier, n - 1 + copies - 1)

    arrive(0, 1, 2, 3)
    scatter.offers(g.nz - 1)

    def around(i):
        d = g.nz - 1 - i
        scatter.offers(d - 1)
        scatter.step(d)

    around(0)
    arrive(4, 9)

    data = bufs[0]

    def weigh(q):
        cols = span(q, 2 * segment)
        first = dot_tn(g_recur[...], normed[:, cols])
        second = dot_tn(g_branch[...], normed[:, cols])
        for half in (0, 1):
            index = 2 * q + half
            track, part = lax.div(index, copies), lax.rem(index, copies)
            for i, value in enumerate((first, second)):
                piece = value[:, half * segment : (half + 1) * segment].astype(BF16)
                data[track, part, 0, i * padded : i * padded + channels] = piece
                if padded > channels:
                    data[track, part, 0, i * padded + channels : (i + 1) * padded] = jnp.zeros(
                        (padded - channels, segment), BF16
                    )
        terms = jnp.sum(w_in[:, cols].astype(F32) * first + w_br[:, cols].astype(F32) * second, axis=0, keepdims=True)
        gain_row[0:1, cols] = terms / gain[0:1, cols].astype(F32)

    loop(copies, weigh)
    weights.start()
    gain_row[1:2] = second_gain[...]
    gain_row[2:8] = jnp.zeros((6, width), F32)
    for t in range(n):
        gain_parts[t] = gain_row[:, t * gain_width : (t + 1) * gain_width]
    others(lambda t: gain_copy(t, g.t).start())
    gain_in[g.t] = gain_parts[g.t]

    flat = jnp.concatenate(
        [
            g_gates[0],
            g_gates[1],
            small[...],
            jnp.zeros((2 * copies * rest_rows - 2 * channels - 8, channels), F32),
        ],
        axis=0,
    ).astype(BF16)
    for i in range(2 * copies):
        bufs[4][i // copies, i % copies, 0] = flat[i * rest_rows : (i + 1) * rest_rows]
    rest.start()

    events = [lambda a=a, b=b: (a(), b()) for a, b in zip(weights.events(), rest.events())]
    for i in range(1, g.nz - 1):
        around(i)
        if events:
            events.pop(0)()
        if i == 1:
            others(lambda t: gain_copy(t, t).wait_recv())
            total = gain_in[0]
            for t in range(1, n):
                total = total + gain_in[t]
            gain_sum[...] = total
            copies_of(lambda i: gain_dp_copy(i, me).start())
            gain_dp[me] = total
    for event in events:
        event()
    scatter.last()
    arrive(5, 6)
    part = 32

    def rows_of(i):
        at = span(i, part)
        back, _ = norm_grad(tokens[at].astype(F32), gain[...].astype(F32), scatter.acc[at])
        input_grad[at] = g_residual[at] + back

    loop(rows // part, rows_of)
    copies_of(lambda i: gain_dp_copy(i, i).wait_recv())
    total = gain_dp[0]
    for i in range(1, copies):
        total = total + gain_dp[i]
    gains_out[...] = total
    rest.finish()
    flat = jnp.concatenate([bufs[6][i // copies, i % copies, 0].astype(F32) for i in range(2 * copies)], axis=0)
    for q in (0, 1):
        for i in range(blocks):
            start = q * channels + i * block_width
            gates_out[q, i] = flat[start : start + block_width, i * block_width : (i + 1) * block_width]
    conv_out[...] = flat[2 * channels : 2 * channels + 5]
    bias_out[...] = flat[2 * channels + 5 : 2 * channels + 7]
    decay_out[...] = flat[2 * channels + 7 : 2 * channels + 8]
    weights.finish()
    for i in range(2 * copies):
        for q, out in enumerate((in_out, br_out)):
            out[:, i * segment : (i + 1) * segment] = bufs[2][
                i // copies, i % copies, 0, q * padded : q * padded + channels
            ]
    others(lambda t: gain_copy(t, t).wait_send())
    copies_of(lambda i: gain_dp_copy(i, i).wait_send())
    scatter.finish()


def up_to(extent, multiple):
    return (extent + multiple - 1) // multiple * multiple


def input_back(
    n, copies, g_recur, g_branch, w_in, w_br, normed, tokens, g_residual, gain, second_gain, g_gates, small, blocks
):
    rows, width = tokens.shape
    channels = w_in.shape[0]
    block = channels // blocks
    rest_rows = up_to((2 * channels + 8 + 2 * copies - 1) // (2 * copies), 16)
    gain_shape = (8, width // n)
    sems = pltpu.SemaphoreType.DMA
    inputs = (g_recur, g_branch, w_in, w_br, normed, tokens, g_residual, gain, second_gain, g_gates, small)
    which = (0, 1, 2, 3, 4, 9, 5, 6)
    specs, kept = fetched_specs(inputs, which)
    return pl.pallas_call(
        fetching(functools.partial(input_back_kernel, n, copies), which),
        out_shape=(shape(rows, width),)
        + (shape(channels, width, dtype=BF16),) * 2
        + (
            shape(2, blocks, block, block),
            shape(5, channels),
            shape(2, channels),
            shape(1, channels),
            shape(*gain_shape),
        ),
        in_specs=specs,
        out_specs=(VM,) * 8,
        scratch_shapes=[
            pltpu.VMEM((8, width), F32),
            pltpu.VMEM((n, *gain_shape), F32),
            pltpu.VMEM((n, *gain_shape), F32),
            pltpu.VMEM(gain_shape, F32),
            pltpu.VMEM((copies, *gain_shape), F32),
            sems((n,)),
            sems((n,)),
            sems((copies,)),
            sems((copies,)),
        ]
        + Halving.scratch(copies, 2 * up_to(channels, 16), width // (2 * copies))
        + Halving.scratch(copies, rest_rows, channels)
        + Scatter.scratch(n, rows, width)
        + kept,
        compiler_params=comm_params(6),
        cost_estimate=cost(8 * n * rows * width * channels),
        name="input_back",
    )(*inputs)


def widen_kernel(*refs):
    half = len(refs) // 2
    for narrow, wide in zip(refs[:half], refs[half:]):
        wide[...] = narrow[...].reshape(wide.shape).astype(F32)


def widen(by_rows, by_columns, in_parts):
    steps = 8
    width = by_columns[0].shape[1]
    tile = width // steps
    per_part = in_parts.shape[2] // tile
    specs, outs = [], []
    for x in by_rows:
        specs.append(pl.BlockSpec((x.shape[0] // steps, x.shape[1]), lambda i: (i, 0)))
        outs.append(shape(*x.shape))
    for x in by_columns:
        specs.append(pl.BlockSpec((x.shape[0], tile), lambda i: (0, i)))
        outs.append(shape(*x.shape))
    last = pl.BlockSpec((1, in_parts.shape[1], tile), lambda i: (i // per_part, 0, i % per_part))
    outs.append(shape(in_parts.shape[1], width))
    wide = pl.BlockSpec((in_parts.shape[1], tile), lambda i: (0, i))
    return pl.pallas_call(
        widen_kernel,
        grid=(steps,),
        out_shape=tuple(outs),
        in_specs=specs + [last],
        out_specs=tuple(specs) + (wide,),
        compiler_params=pltpu.CompilerParams(vmem_limit_bytes=VMEM_LIMIT),
        name="widen",
    )(*by_rows, *by_columns, in_parts)


def body(
    n,
    copies,
    tokens,
    cotangent,
    resets,
    init_state,
    init_conv,
    norm_gain,
    w_input,
    w_branch,
    conv_params,
    gate_weights,
    gate_bias,
    decay_rate,
    w_output,
    mlp_gain,
    w_gelu,
    w_linear,
    w_down,
):
    rows, width = tokens.shape
    total = rows * n
    channels = w_input.shape[1]
    blocks, block = gate_weights.shape[1], gate_weights.shape[2]
    before_conv = init_conv.transpose(1, 0, 2)
    gain_first, gain_second = norm_gain[None], mlp_gain[None]
    gate_w = (gate_weights[:, :, :, None] * jnp.eye(blocks, dtype=BF16)[None, :, None, :, None]).reshape(
        2, channels, channels
    )
    w_in, w_br = w_input.T, w_branch.T

    def flat(x):
        return x.reshape(total, x.shape[-1])

    def blocked(x):
        return x.reshape(n, rows, x.shape[-1])

    normed, recur, branch, states, mixture, conv_low, recall, ingate, final_state, final_conv = project(
        n, tokens, gain_first, w_in, w_br, resets, init_state, before_conv, conv_params, gate_w, gate_bias, decay_rate
    )
    mixture = blocked(mixture)
    cot_full, residual, normed_mlp = mixer_out(n, mixture, w_output, cotangent, tokens, gain_second)
    hidden, grad_gelu, grad_linear, grad_down, g_residual, g_low, gain_second_grad = mlp(
        n, copies, normed_mlp, cot_full, w_gelu, w_linear, w_down, residual, gain_second
    )
    mlp_sums = lax.psum((grad_gelu, grad_linear), "dp")
    output, g_mixture, grad_output = down(n, copies, hidden, w_down, residual, g_low, w_output, mixture)
    g_recur, g_branch, small, g_gates, grad_down = recur_back(
        resets, flat(g_mixture), branch, states, recur, conv_low, recall, ingate, init_state, before_conv,
        conv_params, gate_w, decay_rate, grad_down,
    )
    mlp_sums, grad_output, small = lax.optimization_barrier((mlp_sums, grad_output, small))
    grad_output = lax.psum(grad_output, "dp")
    input_grad, grad_input, grad_branch, gates, g_conv, g_bias, g_decay, gains = input_back(
        n, copies, g_recur, g_branch, w_in, w_br, flat(normed), tokens, g_residual, gain_first,
        gain_second_grad, g_gates, small, blocks,
    )
    grad_gelu, grad_linear, grad_input, grad_branch, grad_output = widen(
        mlp_sums, (grad_input, grad_branch), grad_output
    )
    return (
        output,
        input_grad,
        final_state,
        final_conv.transpose(1, 0, 2),
        gains[0],
        grad_input.T,
        grad_branch.T,
        g_conv,
        gates,
        g_bias,
        g_decay[0],
        grad_output,
        gains[1],
        grad_gelu,
        grad_linear,
        grad_down,
    )


def solution(mesh):
    in_specs = (
        P(("dp", "tensor"), None),
        P(("dp", "tensor"), None),
        P("dp"),
        P("dp", "tensor"),
        P("dp", None, "tensor"),
        P(),
        P(None, "tensor"),
        P(None, "tensor"),
        P(None, "tensor"),
        P(None, "tensor", None, None),
        P(None, "tensor"),
        P("tensor"),
        P("tensor", None),
        P(),
        P(None, "tensor"),
        P(None, "tensor"),
        P("tensor", None),
    )
    out_specs = (
        P(("dp", "tensor"), None),
        P(("dp", "tensor"), None),
        P("dp", "tensor"),
        P("dp", None, "tensor"),
        P("tensor"),
        P(None, "tensor"),
        P(None, "tensor"),
        P(None, "tensor"),
        P(None, "tensor", None, None),
        P(None, "tensor"),
        P("tensor"),
        P("tensor", None),
        P("tensor"),
        P(None, "tensor"),
        P(None, "tensor"),
        P("tensor", None),
    )
    return jax.shard_map(
        functools.partial(body, mesh.shape["tensor"], mesh.shape["dp"]),
        mesh=mesh,
        in_specs=in_specs,
        out_specs=out_specs,
        check_vma=False,
    )
```

```python
import functools

import jax
import jax.numpy as jnp
from jax import lax
from jax.experimental import pallas as pl
from jax.experimental.pallas import tpu as pltpu
from jax.sharding import PartitionSpec as P

EPSILON = 1e-06
KAPPA = 0.7978845608028654
CUBIC = 0.044715
PIECES = 2
STRIPS = 4
PARTS = 8
F32 = jnp.float32
BF16 = jnp.bfloat16
ANY = pl.BlockSpec(memory_space=pl.ANY)
VM = pl.BlockSpec(memory_space=pltpu.VMEM)
VMEM_LIMIT = 61 * 1024 * 1024
MESH = pl.DeviceIdType.MESH


def dot(a, b):
    return jnp.dot(a, b, preferred_element_type=F32)


def dot_nt(a, b):
    return lax.dot_general(a, b, (((1,), (1,)), ((), ())), preferred_element_type=F32)


def dot_tn(a, b):
    return lax.dot_general(a, b, (((0,), (0,)), ((), ())), preferred_element_type=F32)


def tile_of(extent, wanted):
    while extent % wanted:
        wanted //= 2
    return wanted


def span(i, size):
    return pl.ds(pl.multiple_of(i * size, size), size)


def loop(count, body):
    def step(i, carry):
        body(i)
        return carry

    lax.fori_loop(0, count, step, 0)


class Place:
    def __init__(self, n):
        self.n = n
        self.nz = n // 2
        self.t = lax.axis_index("tensor")
        self.c = lax.rem(self.t, 2)
        self.j = lax.div(self.t, 2)
        self.sib = self.t + 1 - 2 * self.c
        self.has_up = self.j < self.nz - 1
        self.has_down = self.j > 0

    def greet(self, partners=()):
        barrier = pltpu.get_barrier_semaphore()

        def signal(t):
            pl.semaphore_signal(barrier, inc=1, device_id={"tensor": t}, device_id_type=MESH)

        for i in partners:
            pl.semaphore_signal(barrier, inc=1, device_id={"dp": i}, device_id_type=MESH)

        signal(self.sib)
        pl.when(self.has_up)(lambda: signal(self.t + 2))
        pl.when(self.has_down)(lambda: signal(self.t - 2))
        pl.semaphore_wait(
            barrier,
            1 + len(partners) + self.has_up.astype(jnp.int32) + self.has_down.astype(jnp.int32),
        )

    def copy(self, src, dst, send, recv, t):
        return pltpu.make_async_remote_copy(
            src_ref=src,
            dst_ref=dst,
            send_sem=send,
            recv_sem=recv,
            device_id={"tensor": t},
            device_id_type=MESH,
        )


class Gather:
    def __init__(self, place, full, sent, came):
        self.place, self.full, self.sent, self.came = place, full, sent, came
        self.pieces = came.shape[1]
        self.size = full.shape[1] // self.pieces

    @staticmethod
    def scratch(n, rows, width):
        return [
            pltpu.VMEM((n, rows, width), BF16),
            pltpu.SemaphoreType.DMA((n, PIECES, 3)),
            pltpu.SemaphoreType.DMA((n, PIECES)),
        ]

    def copy(self, t, p, way, to):
        piece = self.full.at[t, pl.ds(p * self.size, self.size)]
        return self.place.copy(piece, piece, self.sent.at[t, p, way], self.came.at[t, p], to)

    def start(self):
        g = self.place
        for p in range(self.pieces):
            pl.when(g.has_up)(lambda: self.copy(g.t, p, 0, g.t + 2).start())
            pl.when(g.has_down)(lambda: self.copy(g.t, p, 1, g.t - 2).start())
        for p in range(self.pieces):
            self.copy(g.t, p, 2, g.sib).start()

    def forward(self, d, pieces=None):
        g = self.place
        for p in range(self.pieces) if pieces is None else pieces:

            @pl.when(g.j - d >= 0)
            def _():
                t = g.t - 2 * d
                self.copy(t, p, 0, g.sib).wait_recv()
                pl.when(g.has_up)(lambda: self.copy(t, p, 0, g.t + 2).start())
                self.copy(t, p, 2, g.sib).start()

            @pl.when(g.j + d < g.nz)
            def _():
                t = g.t + 2 * d
                self.copy(t, p, 1, g.sib).wait_recv()
                pl.when(g.has_down)(lambda: self.copy(t, p, 1, g.t - 2).start())
                self.copy(t, p, 2, g.sib).start()

    def each(self, d, use):
        g = self.place

        def visit(q):
            core, way = lax.div(q, 2), 2 * lax.rem(q, 2) - 1
            j = g.j + way * d
            there = jnp.logical_and(j >= 0, j < g.nz)

            @pl.when(jnp.logical_and(there, jnp.logical_or(d > 0, way > 0)))
            def _():
                t = 2 * j + lax.rem(g.c + core, 2)

                @pl.when(core > 0)
                def _():
                    for p in range(self.pieces):
                        self.copy(t, p, 2, g.sib).wait_recv()

                use(t)

        loop(4, visit)

    def finish(self):
        g = self.place

        def done(t):
            for p in range(self.pieces):
                self.copy(t, p, 2, g.sib).wait_send()

                @pl.when(jnp.logical_and(t <= g.t, g.has_up))
                def _():
                    self.copy(t, p, 0, g.sib).wait_send()

                @pl.when(jnp.logical_and(t >= g.t, g.has_down))
                def _():
                    self.copy(t, p, 1, g.sib).wait_send()

        loop(g.nz, lambda k: done(2 * k + g.c))


class Scatter:
    def __init__(self, place, partial, tile, bufs):
        self.place, self.partial, self.tile = place, partial, tile
        self.to_sib, self.from_sib, self.line, self.acc = bufs[:4]
        self.sib_send, self.sib_recv, self.line_send, self.line_recv = bufs[4:]
        self.out = self.from_sib
        self.tiles = self.acc.shape[1] // tile

    @staticmethod
    def scratch(n, rows, width):
        nz = n // 2
        return [
            pltpu.VMEM((nz, rows, width), BF16),
            pltpu.VMEM((nz, rows, width), BF16),
            pltpu.VMEM((nz + 1, rows, width), BF16),
            pltpu.VMEM((rows, width), F32),
            pltpu.SemaphoreType.DMA((nz,)),
            pltpu.SemaphoreType.DMA((nz,)),
            pltpu.SemaphoreType.DMA((nz, STRIPS)),
            pltpu.SemaphoreType.DMA((nz + 1, STRIPS)),
        ]

    def sib_copy(self, k):
        return self.place.copy(
            self.to_sib.at[k],
            self.from_sib.at[k],
            self.sib_send.at[k],
            self.sib_recv.at[k],
            self.place.sib,
        )

    def line_copy(self, k, slot, p, to):
        at = self.strip(p)
        return self.place.copy(
            self.out.at[k, at], self.line.at[slot, at], self.line_send.at[k, p], self.line_recv.at[slot, p], to
        )

    def strip(self, p):
        return span(p, self.acc.shape[0] // STRIPS)

    def offer(self, k):
        t = 2 * k + 1 - self.place.c

        def part(i):
            cols = span(i, self.tile)
            self.to_sib[k, :, cols] = self.partial(t, cols).astype(BF16)

        loop(self.tiles, part)
        self.sib_copy(k).start()

    def pair(self, k):
        self.sib_copy(k).wait_recv()
        t = 2 * k + self.place.c

        def part(i):
            cols = span(i, self.tile)
            self.acc[:, cols] = self.partial(t, cols) + self.from_sib[k, :, cols].astype(F32)

        loop(self.tiles, part)

    def offers(self, d):
        g = self.place

        def way_of(w):
            k = g.j + (1 - 2 * w) * d

            @pl.when(jnp.logical_and(jnp.logical_and(k >= 0, k < g.nz), jnp.logical_or(d > 0, w == 0)))
            def _():
                self.offer(k)

        loop(2, way_of)

    def step(self, d):
        g = self.place

        def way_of(w):
            sign = 1 - 2 * w
            k = g.j + sign * d

            @pl.when(jnp.logical_and(k >= 0, k < g.nz))
            def _():
                self.pair(k)
                upstream = g.j - sign
                more = jnp.logical_and(upstream >= 0, upstream < g.nz)

                slot = jnp.where(jnp.logical_and(d == 1, w == 1), g.nz, k)

                def pass_on(p):
                    at = self.strip(p)

                    @pl.when(more)
                    def _():
                        self.line_copy(k, k, p, g.sib).wait_recv()
                        self.out[k, at] = (self.acc[at] + self.line[k, at].astype(F32)).astype(BF16)

                    @pl.when(jnp.logical_not(more))
                    def _():
                        self.out[k, at] = self.acc[at].astype(BF16)

                    self.line_copy(k, slot, p, g.t + 2 * sign).start()

                loop(STRIPS, pass_on)

        loop(2, way_of)

    def last(self):
        g = self.place
        self.pair(g.j)

        def take(p):
            at = self.strip(p)

            @pl.when(g.has_down)
            def _():
                self.line_copy(g.j, g.j, p, g.sib).wait_recv()
                self.acc[at] += self.line[g.j, at].astype(F32)

            @pl.when(g.has_up)
            def _():
                self.line_copy(g.j, g.nz, p, g.sib).wait_recv()
                self.acc[at] += self.line[g.nz, at].astype(F32)

        loop(STRIPS, take)

    def finish(self):
        g = self.place

        def done(k):
            self.sib_copy(k).wait_send()
            pl.when(g.j != k)(
                lambda: loop(STRIPS, lambda p: self.line_copy(k, k, p, g.sib).wait_send())
            )

        loop(g.nz, done)


class Halving:
    def __init__(self, me, count, data, landed, final, sems):
        self.me, self.count = me, count
        self.data, self.landed, self.final = data, landed, final
        self.out_send, self.out_recv, self.back_send, self.back_recv = (sems.at[q] for q in range(4))
        self.bits = count.bit_length() - 1
        assert count == 1 << self.bits

    @staticmethod
    def scratch(count, rows, columns):
        return [
            pltpu.VMEM((2, count, 1, rows, columns), BF16),
            pltpu.VMEM((2, count - 1, 1, rows, columns), BF16),
            pltpu.VMEM((2, count, 1, rows, columns), BF16),
            pltpu.SemaphoreType.DMA((4, 2, count - 1)),
        ]

    @staticmethod
    def over(me, count, data, landed, final, sems):
        def at(ref):
            return lambda track, index: ref.at[track, index]

        return Halving(me, count, at(data), at(landed), at(final), sems)

    def partners(self):
        return [self.me + (1 - 2 * self.own(b)) * (1 << b) for b in range(self.bits)]

    def own(self, bit):
        return lax.rem(lax.div(self.me, 1 << bit), 2)

    def swaps(self, s):
        for track in (0, 1):
            order = [(i + track) % self.bits for i in range(self.bits)]
            bit = order[s]
            partner = self.me + (1 - 2 * self.own(bit)) * (1 << bit)
            fixed = sum(self.own(b) * (1 << b) for b in order[:s])
            for u in range(self.count >> (s + 1)):
                free = sum(((u >> i) & 1) << b for i, b in enumerate(order[s + 1 :]))
                slot = self.count - (self.count >> s) + u
                kept = fixed + free + self.own(bit) * (1 << bit)
                yield track, slot, partner, fixed + free + (1 - self.own(bit)) * (1 << bit), kept

    def out(self, track, slot, partner, given):
        return pltpu.make_async_remote_copy(
            src_ref=self.data(track, given),
            dst_ref=self.landed(track, slot),
            send_sem=self.out_send.at[track, slot],
            recv_sem=self.out_recv.at[track, slot],
            device_id={"dp": partner},
            device_id_type=MESH,
        )

    def back(self, track, slot, partner, segment):
        return pltpu.make_async_remote_copy(
            src_ref=self.final(track, segment),
            dst_ref=self.final(track, segment),
            send_sem=self.back_send.at[track, slot],
            recv_sem=self.back_recv.at[track, slot],
            device_id={"dp": partner},
            device_id_type=MESH,
        )

    def start(self, s=0):
        for track, slot, partner, given, _ in self.swaps(s):
            self.out(track, slot, partner, given).start()

    def turn(self, s):
        for track, slot, partner, given, kept in self.swaps(s):
            self.out(track, slot, partner, given).wait_recv()
            mine, theirs = self.data(track, kept), self.landed(track, slot)
            result = self.final(track, kept) if s == self.bits - 1 else mine
            blocks, rows, _ = mine.shape
            tile = tile_of(rows, 32)

            def add(r):
                block, at = lax.div(r, rows // tile), span(lax.rem(r, rows // tile), tile)
                result[block, at] = (mine[block, at].astype(F32) + theirs[block, at].astype(F32)).astype(BF16)

            loop(blocks * (rows // tile), add)
        if s < self.bits - 1:
            self.start(s + 1)
        else:
            self.start_back(s)

    def start_back(self, s):
        for track, slot, partner, _, kept in self.swaps(s):
            self.back(track, slot, partner, kept).start()

    def turn_back(self, s):
        for track, slot, partner, given, _ in self.swaps(s):
            self.back(track, slot, partner, given).wait_recv()
        if s > 0:
            self.start_back(s - 1)

    def events(self):
        steps = [functools.partial(self.turn, s) for s in range(self.bits)]
        return steps + [functools.partial(self.turn_back, s) for s in range(self.bits - 1, 0, -1)]

    def finish(self):
        self.turn_back(0)
        for s in range(self.bits):
            for track, slot, partner, given, kept in self.swaps(s):
                self.out(track, slot, partner, given).wait_send()
                self.back(track, slot, partner, kept).wait_send()


def fetching(kernel, which):
    def wrapped(*refs):
        refs = list(refs)
        sems = refs.pop()
        kept = refs[len(refs) - len(which) :]
        del refs[len(refs) - len(which) :]
        copies = {}
        for q, i in enumerate(which):
            copies[i] = pltpu.make_async_copy(refs[i], kept[q], sems.at[q])
            copies[i].start()
            refs[i] = kept[q]

        def arrive(*wanted):
            for i in wanted:
                copies[i].wait()

        return kernel(arrive, *refs)

    return wrapped


def fetched_specs(inputs, which, plain=()):
    specs = [ANY if i in which or i in plain else VM for i in range(len(inputs))]
    scratch = [pltpu.VMEM(inputs[i].shape, inputs[i].dtype) for i in which]
    return specs, scratch + [pltpu.SemaphoreType.DMA((len(which),))]


def comm_params(collective_id):
    return pltpu.CompilerParams(
        collective_id=collective_id, has_side_effects=True, vmem_limit_bytes=VMEM_LIMIT
    )


def cost(flops):
    return pl.CostEstimate(flops=int(flops), bytes_accessed=200_000_000, transcendentals=0)


def shape(*dims, dtype=F32):
    return jax.ShapeDtypeStruct(dims, dtype)


def inv_rms(values):
    return lax.rsqrt(jnp.mean(values * values, axis=-1, keepdims=True) + EPSILON)


def norm_grad(values, gain, gradient):
    inv = inv_rms(values)
    unit = values * inv
    scaled = gradient * gain
    centred = jnp.mean(scaled * unit, axis=-1, keepdims=True)
    return inv * (scaled - unit * centred), gradient * unit


def sigmoid(v):
    return 1.0 / (1.0 + jnp.exp(-v))


def gelu_parts(v):
    square = v * v
    bend = jnp.tanh(KAPPA * v * (1.0 + CUBIC * square))
    half = 0.5 * (1.0 + bend)
    slope = half + 0.5 * v * (1.0 - bend * bend) * (KAPPA * (1.0 + 3.0 * CUBIC * square))
    return v * half, slope


def one_minus_square(log_decay, decay):
    m = -2.0 * log_decay
    series = m * (
        1.0 - m * (1 / 2) * (1.0 - m * (1 / 3) * (1.0 - m * (1 / 4) * (1.0 - m * (1 / 5) * (1.0 - m * (1 / 6)))))
    )
    return jnp.where(m < 0.35, series, 1.0 - decay * decay)


def starts(reset, here, init_state, init_conv, state, hist):
    keep = (1 - reset).astype(F32)
    state[...] = jnp.broadcast_to(init_state[here] * keep, state.shape)
    before = [init_conv[q, here] * keep for q in range(3)]
    hist[0:8] = jnp.concatenate([jnp.zeros((5, hist.shape[1]), F32)] + before, axis=0)


def recur_chunk(base, u, branch, conv, gate_w, bias, decay, kept, hist, decay_buf, drive_buf, carry):
    states, mixture, conv_low, recall, ingate = kept
    rows, channels = decay_buf.shape
    tile = 32

    def rows_of(i, size):
        return pl.ds(pl.multiple_of(base + i * size, size), size)

    whole = rows_of(0, rows)
    hist[8:] = u[whole]

    def convolve(i):
        window = hist[pl.ds(pl.multiple_of(i * tile, tile), tile + 8)]
        value = conv[4:5] + conv[0:1] * window[8:] + conv[1:2] * window[7 : tile + 7]
        value = value + conv[2:3] * window[6 : tile + 6] + conv[3:4] * window[5 : tile + 5]
        conv_low[rows_of(i, tile)] = value.astype(BF16)

    loop(rows // tile, convolve)
    hist[0:8] = hist[rows : rows + 8]
    low = conv_low[whole]
    recall[whole] = dot(low, gate_w[0])
    ingate[whole] = dot(low, gate_w[1])

    def gates(i):
        at, here = rows_of(i, tile), span(i, tile)
        r = sigmoid(recall[at] + bias[0:1])
        k = sigmoid(ingate[at] + bias[1:2])
        recall[at] = r
        ingate[at] = k
        log_decay = -8.0 * r * decay[...][None]
        step = jnp.exp(log_decay)
        decay_buf[here] = step
        drive_buf[here] = jnp.sqrt(one_minus_square(log_decay, step)) * k * conv_low[at].astype(F32)

    loop(rows // tile, gates)
    row = lax.broadcasted_iota(jnp.int32, (8, channels), 0)

    def scan(i, before):
        for part in range(4):
            at = pl.ds(pl.multiple_of(i * 32 + part * 8, 8), 8)
            a, b = decay_buf[at], drive_buf[at]
            for shift in (1, 2, 4):
                inside = row >= shift
                b = b + a * jnp.where(inside, pltpu.roll(b, shift, 0), 0.0)
                a = a * jnp.where(inside, pltpu.roll(a, shift, 0), 1.0)
            h = a * before + b
            states[pl.ds(pl.multiple_of(base + i * 32 + part * 8, 8), 8)] = h
            before = jnp.broadcast_to(h[7:8], (8, channels))
        return before

    carry[...] = lax.fori_loop(0, rows // 32, scan, carry[...])

    def mix(i):
        at = rows_of(i, tile)
        value, _ = gelu_parts(branch[at])
        mixture[at] = (states[at] * value).astype(BF16)

    loop(rows // tile, mix)


def project_kernel(
    n, arrive, tokens, gain, w_in, w_br, resets, init_state, init_conv, conv, gate_w, bias, decay,
    normed, recur, branch, states, mixture, conv_low, recall, ingate, final_state, final_conv,
    full, sent, came, held_a, held_b, kept_s, kept_m, kept_c, kept_r, kept_i,
    hist, decay_buf, drive_buf, carry, saved, written,
):
    g = Place(n)
    gather = Gather(g, full, sent, came)
    rows = full.shape[1]
    part = 64

    def normalize(i):
        at = span(i, part)
        values = tokens[at].astype(F32)
        full[g.t, at] = (values * inv_rms(values) * gain[...].astype(F32)[None]).astype(BF16)

    loop(rows // part, normalize)
    g.greet()
    gather.start()
    arrive(2, 3)

    def out(t):
        return pltpu.make_async_copy(full.at[t], normed.at[t], saved.at[t])

    def use(t):
        out(t).start()
        at = span(t, rows)
        held_a[at] = dot_nt(full[t], w_in[...])
        held_b[at] = dot_nt(full[t], w_br[...])

    kept = (kept_s, kept_m, kept_c, kept_r, kept_i)
    pairs = ((held_a, recur), (held_b, branch)) + tuple(zip(kept, (states, mixture, conv_low, recall, ingate)))
    sequences = init_state.shape[0]
    length = n * rows // sequences
    size = decay_buf.shape[0]
    chunks = length // size

    def leave(c, act):
        at = span(c, size)
        for q, (held, target) in enumerate(pairs):
            act(pltpu.make_async_copy(held.at[at], target.at[at], written.at[c, q]))

    def sequence(s):
        here = pl.ds(s, 1)
        starts(resets[s], here, init_state, init_conv, carry, hist)

        def chunk(c):
            index = s * chunks + c
            base = index * size
            recur_chunk(base, held_a, held_b, conv, gate_w, bias, decay, kept, hist, decay_buf, drive_buf, carry)
            leave(index, lambda copy: copy.start())

        loop(chunks, chunk)
        final_state[here] = carry[0:1]
        for q in range(3):
            final_conv[q, here] = hist[5 + q : 6 + q]

    def step(d):
        pl.when(d > 0)(lambda: gather.forward(d))
        gather.each(d, use)

        def whole(s):
            first = lax.div(s * length, 2 * rows)
            last = lax.div((s + 1) * length - 1, 2 * rows)
            pl.when(jnp.maximum(jnp.abs(first - g.j), jnp.abs(last - g.j)) == d)(lambda: sequence(s))

        loop(sequences, whole)

    loop(g.nz, step)
    loop(n, lambda t: out(t).wait())
    loop(sequences * chunks, lambda c: leave(c, lambda copy: copy.wait()))
    gather.finish()


def project(n, tokens, gain, w_in, w_br, resets, init_state, init_conv, conv, gate_w, bias, decay):
    rows, width = tokens.shape
    channels = w_in.shape[0]
    sequences = init_state.shape[0]
    total = n * rows
    size = tile_of(total // sequences, 256)
    inputs = (tokens, gain, w_in, w_br, resets, init_state, init_conv, conv, gate_w, bias, decay)
    specs, kept = fetched_specs(inputs, (2, 3))
    specs[4] = pl.BlockSpec(memory_space=pltpu.SMEM)
    wide, narrow = (total, channels), pltpu.VMEM((total, channels), BF16)
    return pl.pallas_call(
        fetching(functools.partial(project_kernel, n), (2, 3)),
        out_shape=(
            shape(n, rows, width, dtype=BF16),
            shape(*wide),
            shape(*wide),
            shape(*wide),
            shape(*wide, dtype=BF16),
            shape(*wide, dtype=BF16),
            shape(*wide),
            shape(*wide),
            shape(sequences, channels),
            shape(3, sequences, channels),
        ),
        in_specs=specs,
        out_specs=(ANY,) * 8 + (VM,) * 2,
        scratch_shapes=Gather.scratch(n, rows, width)
        + [pltpu.VMEM(wide, F32)] * 3
        + [narrow] * 2
        + [pltpu.VMEM(wide, F32)] * 2
        + [
            pltpu.VMEM((size + 8, channels), F32),
            pltpu.VMEM((size, channels), F32),
            pltpu.VMEM((size, channels), F32),
            pltpu.VMEM((8, channels), F32),
            pltpu.SemaphoreType.DMA((n,)),
            pltpu.SemaphoreType.DMA((total // size, 7)),
        ]
        + kept,
        compiler_params=comm_params(1),
        cost_estimate=cost(4 * n * rows * width * channels),
        name="project",
    )(*inputs)


def mixer_out_kernel(
    n, arrive, mixture, w_output, cotangent, tokens, gain, cot_full, residual, normed,
    full, sent, came, saved, *bufs
):
    g = Place(n)
    gather = Gather(g, full, sent, came)
    scatter = Scatter(g, lambda t, cols: dot(mixture[t], w_output[:, cols]), tile_of(residual.shape[1], 512), bufs)
    first = pltpu.make_async_copy(cotangent, full.at[g.t], saved.at[0])
    first.start()
    g.greet()
    first.wait()
    gather.start()
    arrive(0, 1)

    def use(t):
        pltpu.make_async_copy(full.at[t], cot_full.at[t], saved.at[t]).start()

    scatter.offers(g.nz - 1)

    def around(i):
        d = g.nz - 1 - i
        scatter.offers(d - 1)
        scatter.step(d)
        gather.each(i, use)
        gather.forward(i + 1)

    loop(g.nz - 1, around)
    scatter.last()
    arrive(3)
    part = 64

    def rows_of(i):
        at = span(i, part)
        values = scatter.acc[at] + tokens[at].astype(F32)
        residual[at] = values
        normed[at] = (values * inv_rms(values) * gain[...].astype(F32)[None]).astype(BF16)

    loop(residual.shape[0] // part, rows_of)
    gather.each(g.nz - 1, use)
    loop(n, lambda t: pltpu.make_async_copy(full.at[t], cot_full.at[t], saved.at[t]).wait())
    scatter.finish()
    gather.finish()


def mixer_out(n, mixture, w_output, cotangent, tokens, gain):
    rows, width = tokens.shape
    inputs, which = (mixture, w_output, cotangent, tokens, gain), (0, 1, 3)
    specs, kept = fetched_specs(inputs, which, (2,))
    return pl.pallas_call(
        fetching(functools.partial(mixer_out_kernel, n), which),
        out_shape=(
            shape(n, rows, width, dtype=BF16),
            shape(rows, width),
            shape(rows, width, dtype=BF16),
        ),
        in_specs=specs,
        out_specs=(ANY, VM, VM),
        scratch_shapes=Gather.scratch(n, rows, width)
        + [pltpu.SemaphoreType.DMA((n,))]
        + Scatter.scratch(n, rows, width)
        + kept,
        compiler_params=comm_params(2),
        cost_estimate=cost(2 * n * rows * width * mixture.shape[-1]),
        name="mixer_out",
    )(*inputs)


def mlp_kernel(
    n, copies, arrive, normed, cot_full, w_gelu, w_linear, w_down, residual, gain,
    hidden, grad_gelu, grad_linear, grad_down, g_residual, g_low, g_gain,
    full, sent, came, cot, keep_h, keep_f, keep_s, acc_g, acc_l, acc_d,
    to_sib, sums, line, acc, landed, swap_sems, saved, fetched, drained, sib_sent, sib_came, line_sent, line_came,
):
    g = Place(n)
    gather = Gather(g, full, sent, came)
    columns = w_gelu.shape[1]
    rows, width = acc.shape
    tile = tile_of(columns, 256)
    wide = tile_of(width, 512)
    strip = rows // PARTS
    me = lax.axis_index("dp")
    start = pltpu.make_async_copy(normed, full.at[g.t], saved.at[0])
    start.start()
    part_width = width // (2 * copies)
    depth = columns // rows

    def segment(track, index):
        return pl.ds(pl.multiple_of((track * copies + index) * part_width, part_width), part_width)

    swap = Halving(
        me,
        copies,
        lambda track, index: full.at[0:depth, :, segment(track, index)],
        lambda track, slot: landed.at[track, slot],
        lambda track, index: full.at[depth : 2 * depth, :, segment(track, index)],
        swap_sems,
    )
    def fetch(t, q):
        return pltpu.make_async_copy(cot_full.at[t], cot.at[q], fetched.at[q])

    g.greet(swap.partners())
    start.wait()
    gather.start()
    fetch(2 * g.j, 0).start()
    fetch(2 * g.j + 1, 1).start()
    arrive(2, 3, 4)
    acc_g[...] = jnp.zeros_like(acc_g)
    acc_l[...] = jnp.zeros_like(acc_l)
    acc_d[...] = jnp.zeros_like(acc_d)

    def save(t, q):
        return pltpu.make_async_copy(keep_h.at[q], hidden.at[t], saved.at[q])

    def layer(t, q):
        fetch(t, q).wait()

        def part(i):
            cols = span(i, tile)
            first = dot(full[t], w_gelu[:, cols])
            second = dot(full[t], w_linear[:, cols])
            back = dot_nt(cot[q], w_down[cols])
            value, slope = gelu_parts(first)
            keep_h[q, :, cols] = (value * second).astype(BF16)
            keep_f[q, :, cols] = (back * second * slope).astype(BF16)
            keep_s[q, :, cols] = (back * value).astype(BF16)

        loop(columns // tile, part)
        save(t, q).start()

    def partial(q, cols):
        return dot_nt(keep_f[q], w_gelu[cols]) + dot_nt(keep_s[q], w_linear[cols])

    def sib_copy(k):
        return g.copy(to_sib, sums.at[k], sib_sent, sib_came.at[k], g.sib)

    def line_copy(k, slot, p, to):
        at = pl.ds(pl.multiple_of(p * strip, strip), strip)
        return g.copy(
            sums.at[k, at], line.at[slot, at], line_sent.at[k, p], line_came.at[slot, p], to
        )

    def chip(d, way):
        k = g.j + way * d
        mine, its = g.c, 1 - g.c
        own, other = 2 * k + mine, 2 * k + its
        for p in range(gather.pieces):
            gather.copy(other, p, 2, g.sib).wait_recv()
        layer(other, its)

        def offer(i):
            cols = span(i, wide)
            to_sib[:, cols] = partial(its, cols).astype(BF16)

        loop(width // wide, offer)
        sib_copy(k).start()
        layer(own, mine)
        sib_copy(k).wait()

        @pl.when(d == 0)
        def _():
            def part(i):
                cols = span(i, wide)
                acc[:, cols] = partial(mine, cols) + sums[k, :, cols].astype(F32)

            loop(width // wide, part)

        @pl.when(d > 0)
        def _():
            def part(i):
                cols = span(i, wide)
                sums[k, :, cols] = (partial(mine, cols) + sums[k, :, cols].astype(F32)).astype(BF16)

            loop(width // wide, part)
            first = jnp.logical_or(
                jnp.logical_and(way > 0, jnp.logical_not(g.has_down)),
                jnp.logical_and(way < 0, jnp.logical_not(g.has_up)),
            )

            @pl.when(first)
            def _():
                slot = jnp.where(jnp.logical_and(way < 0, d == 1), g.nz, k)
                for p in range(PARTS):
                    line_copy(k, slot, p, g.t + 2 * way).start()

        def part(i):
            at = span(i, wide)
            both = full[pl.ds(2 * k, 2), :, at].reshape(2 * rows, wide)
            acc_g[at] += dot_tn(both, keep_f[...].reshape(2 * rows, columns))
            acc_l[at] += dot_tn(both, keep_s[...].reshape(2 * rows, columns))
            acc_d[:, at] += dot_tn(
                keep_h[...].reshape(2 * rows, columns), cot[:, :, at].reshape(2 * rows, wide)
            )

        loop(width // wide, part)
        both_ways = jnp.logical_and(g.j + d < g.nz, g.j - d >= 0)
        again = jnp.logical_and(both_ways, jnp.logical_and(way > 0, d > 0))
        later = jnp.where(g.j + d + 1 < g.nz, g.j + d + 1, g.j - d - 1)
        following = jnp.where(again, g.j - d, later)

        @pl.when(following >= 0)
        def _():
            fetch(2 * following, 0).start()
            fetch(2 * following + 1, 1).start()

        save(other, its).wait()
        save(own, mine).wait()

    def relay(m, events=()):
        def take(k, slot, sign, p):
            at = pl.ds(pl.multiple_of(p * strip, strip), strip)
            line_copy(k, slot, p, g.sib).wait_recv()

            @pl.when(k == g.j)
            def _():
                acc[at] += line[slot, at].astype(F32)

            @pl.when(k != g.j)
            def _():
                sums[k, at] = (sums[k, at].astype(F32) + line[slot, at].astype(F32)).astype(BF16)
                there = jnp.where(jnp.logical_and(sign < 0, k == g.j - 1), g.nz, k)
                line_copy(k, there, p, g.t + 2 * sign).start()

        def rise(p):
            pl.when(jnp.logical_and(g.has_down, m >= g.j))(lambda: take(m, m, 1, p))

        def fall(p):
            k = g.nz - 1 - m
            pl.when(jnp.logical_and(g.has_up, k <= g.j))(
                lambda: take(k, jnp.where(k == g.j, g.nz, k), -1, p)
            )

        lower = 2 * g.j < g.nz

        def strips(i):
            @pl.when(i < PARTS)
            def _():
                pl.when(lower)(lambda: rise(i))
                pl.when(jnp.logical_not(lower))(lambda: fall(i))

            @pl.when(i > 0)
            def _():
                pl.when(lower)(lambda: fall(i - 1))
                pl.when(jnp.logical_not(lower))(lambda: rise(i - 1))

        middle = jnp.logical_and(g.has_up, g.has_down)
        for event in events:
            pl.when(jnp.logical_not(middle))(event)

        def between(i):
            strips(i)
            for q, event in enumerate(events):
                pl.when(jnp.logical_and(middle, i == min(2 * q + 2, PARTS)))(event)

        loop(PARTS + 1, between)

    def cores(d):
        up, down = g.j + d < g.nz, g.j - d >= 0

        def way_of(w):
            both = jnp.logical_and(up, down)
            way = jnp.where(jnp.logical_and(w == 0, up), 1, -1)
            wanted = jnp.where(w == 0, jnp.logical_or(up, down), jnp.logical_and(both, d > 0))
            pl.when(wanted)(lambda: chip(d, way))

            @pl.when(d < g.nz - 1)
            def _():
                for p in range(gather.pieces):
                    pl.when(w == min(p, 1))(lambda: gather.forward(d + 1, (p,)))

        loop(2, way_of)

    def step(d):
        @pl.when(d < g.nz)
        def _():
            cores(d)

        @pl.when(d == g.nz - 1)
        def _():
            gather.finish()
            for i in range(depth):
                full[i] = acc_d[pl.ds(i * rows, rows)].astype(BF16)
            swap.start()

        pl.when(d > 1)(lambda: relay(d - 1))

    loop(g.nz, step)

    stages = [held.at[q] for held in (keep_h, keep_f, keep_s) for q in (0, 1)]
    leaving = []

    def leave(i, value, out):
        slot = i % len(stages)
        if len(leaving) >= len(stages):
            leaving[i - len(stages)].wait()
        stages[slot][...] = value.astype(BF16)
        copy = pltpu.make_async_copy(stages[slot], out, drained.at[slot])
        copy.start()
        leaving.append(copy)

    for i in range(width // rows):
        at = pl.ds(i * rows, rows)
        leave(2 * i, acc_g[at], grad_gelu.at[at])
        leave(2 * i + 1, acc_l[at], grad_linear.at[at])
    events = swap.events()
    events.pop(0)()
    relay(g.nz - 1, events)
    own = pltpu.make_async_copy(cot_full.at[g.t], cot.at[0], fetched.at[0])
    own.start()
    own.wait()
    arrive(5)
    lines = 32
    g_gain[...] = jnp.zeros_like(g_gain)

    def rows_of(i):
        at = span(i, lines)
        back, terms = norm_grad(residual[at], gain[...].astype(F32)[None], acc[at])
        value = cot[0, at].astype(F32) + back
        acc[at] = value
        cot[1, at] = value.astype(BF16)
        g_gain[...] += jnp.sum(terms, axis=0, keepdims=True)

    loop(rows // lines, rows_of)
    last = [
        pltpu.make_async_copy(acc, g_residual, saved.at[0]),
        pltpu.make_async_copy(cot.at[1], g_low, saved.at[1]),
    ]
    swap.finish()
    for i in range(depth):
        at = pl.ds(i * rows, rows)
        last.append(pltpu.make_async_copy(full.at[depth + i], grad_down.at[at], drained.at[len(stages) + i]))
    for copy in last:
        copy.start()
    for copy in leaving[-len(stages) :] + last:
        copy.wait()

    def done(k):
        @pl.when(k != g.j)
        def _():
            for p in range(PARTS):
                line_copy(k, k, p, g.sib).wait_send()

    loop(g.nz, done)


def mlp(n, copies, normed, cot_full, w_gelu, w_linear, w_down, residual, gain):
    rows, width = normed.shape
    columns = w_gelu.shape[1]
    kept = pltpu.VMEM((2, rows, columns), BF16)
    sems = pltpu.SemaphoreType.DMA
    inputs, which = (normed, cot_full, w_gelu, w_linear, w_down, residual, gain), (2, 3, 4, 5)
    specs, held = fetched_specs(inputs, which, (0, 1))
    return pl.pallas_call(
        fetching(functools.partial(mlp_kernel, n, copies), which),
        out_shape=(shape(n, rows, columns, dtype=BF16),)
        + (shape(width, columns, dtype=BF16),) * 2
        + (
            shape(columns, width, dtype=BF16),
            shape(rows, width),
            shape(rows, width, dtype=BF16),
            shape(1, width),
        ),
        in_specs=specs,
        out_specs=(ANY,) * 6 + (VM,),
        scratch_shapes=Gather.scratch(n, rows, width)
        + [pltpu.VMEM((2, rows, width), BF16)]
        + [kept] * 3
        + [pltpu.VMEM((width, columns), F32)] * 2
        + [
            pltpu.VMEM((columns, width), F32),
            pltpu.VMEM((rows, width), BF16),
            pltpu.VMEM((n // 2, rows, width), BF16),
            pltpu.VMEM((n // 2 + 1, rows, width), BF16),
            pltpu.VMEM((rows, width), F32),
            pltpu.VMEM((2, copies - 1, columns // rows, rows, width // (2 * copies)), BF16),
            sems((4, 2, copies - 1)),
            sems((2,)),
            sems((2,)),
            sems((6 + columns // rows,)),
            sems,
            sems((n // 2,)),
            sems((n // 2, PARTS)),
            sems((n // 2 + 1, PARTS)),
        ]
        + held,
        compiler_params=comm_params(3),
        cost_estimate=cost(16 * n * rows * width * columns),
        name="mlp",
    )(*inputs)


def down_kernel(
    n, copies, arrive, hidden, w_down, residual, g_low, w_output, mixture, output, g_mixture, grad_output,
    full, sent, came, acc_o, start_sem, *bufs
):
    g = Place(n)
    gather = Gather(g, full, sent, came)
    width = residual.shape[1]
    wide = tile_of(width, 512)
    scatter = Scatter(g, lambda t, cols: dot(hidden[t], w_down[:, cols]), wide, bufs)
    first = pltpu.make_async_copy(g_low, full.at[g.t], start_sem)
    first.start()
    g.greet()
    first.wait()

    def use(t):
        g_mixture[t] = dot_nt(full[t], w_output[...])

        def part(i):
            at = span(i, wide)
            acc_o[:, at] += dot_tn(mixture[t], full[t, :, at])

        loop(width // wide, part)

    gather.start()
    acc_o[...] = jnp.zeros_like(acc_o)
    arrive(0, 1)
    scatter.offers(g.nz - 1)
    arrive(4, 5)

    def around(i):
        d = g.nz - 1 - i
        scatter.offers(d - 1)
        scatter.step(d)
        gather.each(i, use)
        gather.forward(i + 1)

    loop(g.nz - 1, around)
    gather.each(g.nz - 1, use)
    for i in range(copies):
        part = width // copies
        grad_output[i] = acc_o[:, i * part : (i + 1) * part].astype(BF16)
    scatter.last()
    arrive(2)
    output[...] = (scatter.acc[...] + residual[...]).astype(BF16)
    scatter.finish()
    gather.finish()


def down(n, copies, hidden, w_down, residual, g_low, w_output, mixture):
    rows, width = residual.shape
    channels = w_output.shape[0]
    inputs, which = (hidden, w_down, residual, g_low, w_output, mixture), (0, 1, 4, 5, 2)
    specs, kept = fetched_specs(inputs, which, (3,))
    return pl.pallas_call(
        fetching(functools.partial(down_kernel, n, copies), which),
        out_shape=(
            shape(rows, width, dtype=BF16),
            shape(n, rows, channels),
            shape(copies, channels, width // copies, dtype=BF16),
        ),
        in_specs=specs,
        out_specs=(VM,) * 3,
        scratch_shapes=Gather.scratch(n, rows, width)
        + [pltpu.VMEM((channels, width), F32), pltpu.SemaphoreType.DMA]
        + Scatter.scratch(n, rows, width)
        + kept,
        compiler_params=comm_params(5),
        cost_estimate=cost(2 * n * rows * width * (hidden.shape[-1] + 2 * channels)),
        name="down",
    )(*inputs)


def recur_back_kernel(
    resets, g_mix, branch, states, states_before, u, u_before, conv_low, recall, ingate, init_state, init_conv,
    conv, gate_w, decay, narrow_in,
    g_recur, g_branch, small, g_gates, wide_out,
    g_state, step_buf, root_buf, g_conv, pre_r, pre_i, carry, hist_s, hist_u, sums,
):
    sequence, back = pl.program_id(0), pl.program_id(1)
    last = pl.num_programs(1) - 1
    rows, channels = u.shape
    tile = 32
    wide_out[...] = narrow_in[...].astype(F32)

    @pl.when(jnp.logical_and(sequence == 0, back == 0))
    def _():
        sums[...] = jnp.zeros_like(sums)
        g_gates[...] = jnp.zeros_like(g_gates)

    @pl.when(back == 0)
    def _():
        carry[...] = jnp.zeros_like(carry)
        g_conv[rows : rows + 8] = jnp.zeros((8, channels), F32)

    @pl.when(back > 0)
    def _():
        g_conv[rows : rows + 8] = g_conv[0:8]

    @pl.when(back == last)
    def _():
        starts(
            resets[sequence], pl.ds(sequence, 1), init_state, init_conv, hist_s.at[0:8], hist_u
        )

    @pl.when(back < last)
    def _():
        hist_s[0:8] = states_before[...]
        hist_u[0:8] = u_before[...]

    hist_s[8:] = states[...]
    hist_u[8:] = u[...]

    def first(i):
        at = span(i, tile)
        value, slope = gelu_parts(branch[at])
        gm = g_mix[at]
        g_state[at] = gm * value
        g_branch[at] = (gm * states[at] * slope).astype(BF16)
        log_decay = -8.0 * recall[at] * decay[...][None]
        step = jnp.exp(log_decay)
        step_buf[at] = step
        root_buf[at] = jnp.sqrt(one_minus_square(log_decay, step))

    loop(rows // tile, first)
    row = lax.broadcasted_iota(jnp.int32, (8, channels), 0)
    groups = rows // 32

    def scan(i, after):
        for part in range(4):
            at = pl.ds(pl.multiple_of((groups - 1 - i) * 32 + (3 - part) * 8, 8), 8)
            a, gs = step_buf[at], g_state[at]
            b = a * gs
            for shift in (1, 2, 4):
                inside = row < 8 - shift
                b = b + a * jnp.where(inside, pltpu.roll(b, 8 - shift, 0), 0.0)
                a = a * jnp.where(inside, pltpu.roll(a, 8 - shift, 0), 1.0)
            e = a * after + b
            g_state[at] = gs + jnp.where(row < 7, pltpu.roll(e, 7, 0), after)
            after = jnp.broadcast_to(e[0:1], (8, channels))
        return after

    carry[...] = lax.fori_loop(0, groups, scan, carry[...])

    def fold(x):
        return jnp.sum(x.reshape(tile // 8, 8, channels), axis=0)

    def second(i):
        at = span(i, tile)
        window = hist_s[pl.ds(pl.multiple_of(i * tile, tile), tile + 8)]
        before = window[7 : tile + 7]
        g, r, k = g_state[at], recall[at], ingate[at]
        c = conv_low[at].astype(F32)
        step, root = step_buf[at], root_buf[at]
        kc = k * c
        g_log = g * (before * step - kc * (step * step) / root)
        slow = -8.0 * r
        sums[7] += fold(g_log * slow)
        low_r = (g_log * (slow * decay[...][None]) * (1.0 - r)).astype(BF16)
        low_i = (g * root * kc * (1.0 - k)).astype(BF16)
        pre_r[at] = low_r
        pre_i[at] = low_i
        sums[5] += fold(low_r.astype(F32))
        sums[6] += fold(low_i.astype(F32))
        g_conv[at] = g * root * k

    loop(rows // tile, second)
    low_r, low_i, low_c = pre_r[...], pre_i[...], conv_low[...]
    g_gates[0] += dot_tn(low_c, low_r)
    g_gates[1] += dot_tn(low_c, low_i)
    g_conv[0:rows] += dot_nt(low_r, gate_w[0]) + dot_nt(low_i, gate_w[1])

    def third(i):
        at = span(i, tile)
        start = pl.multiple_of(i * tile, tile)
        window = g_conv[pl.ds(start, tile + 8)]
        value = conv[0:1] * window[0:tile]
        for k in (1, 2, 3):
            value = value + conv[k : k + 1] * window[k : tile + k]
        g_recur[at] = value.astype(BF16)
        past = hist_u[pl.ds(start, tile + 8)]
        gc = window[0:tile]
        for k in range(4):
            sums[k] += fold(gc * past[8 - k : tile + 8 - k])
        sums[4] += fold(gc)

    loop(rows // tile, third)

    @pl.when(jnp.logical_and(sequence == pl.num_programs(0) - 1, back == last))
    def _():
        small[...] = jnp.sum(sums[...], axis=1)


def recur_back(
    resets, g_mix, branch, states, u, conv_low, recall, ingate, init_state, init_conv, conv, gate_w, decay, narrow_in
):
    total, channels = u.shape
    sequences = init_state.shape[0]
    length = total // sequences
    rows = tile_of(length, 256)
    chunks = length // rows
    extra_rows = narrow_in.shape[0] // (sequences * chunks)
    extra = pl.BlockSpec((extra_rows, narrow_in.shape[1]), lambda s, c: (s * chunks + c, 0))
    eights = rows // 8

    def at(s, c):
        return (s * chunks + chunks - 1 - c, 0)

    def earlier(s, c):
        return (jnp.maximum((s * chunks + chunks - 1 - c) * eights - 1, 0), 0)

    block = pl.BlockSpec((rows, channels), at)
    before = pl.BlockSpec((8, channels), earlier)

    def whole(x):
        return pl.BlockSpec(x.shape, lambda s, c: (0,) * x.ndim)

    wide = pltpu.VMEM((rows, channels), F32)
    narrow = pltpu.VMEM((rows, channels), BF16)
    long = pltpu.VMEM((rows + 8, channels), F32)
    return pl.pallas_call(
        recur_back_kernel,
        grid=(sequences, chunks),
        out_shape=(
            shape(total, channels, dtype=BF16),
            shape(total, channels, dtype=BF16),
            shape(8, channels),
            shape(2, channels, channels),
            shape(*narrow_in.shape),
        ),
        in_specs=[
            pl.BlockSpec(memory_space=pltpu.SMEM),
            block, block, block, before, block, before, block, block, block,
            whole(init_state), whole(init_conv), whole(conv), whole(gate_w), whole(decay), extra,
        ],
        out_specs=(
            block,
            block,
            pl.BlockSpec((8, channels), lambda s, c: (0, 0)),
            pl.BlockSpec((2, channels, channels), lambda s, c: (0, 0, 0)),
            extra,
        ),
        scratch_shapes=[
            wide, wide, wide, long, narrow, narrow,
            pltpu.VMEM((8, channels), F32), long, long,
            pltpu.VMEM((8, 8, channels), F32),
        ],
        compiler_params=pltpu.CompilerParams(vmem_limit_bytes=VMEM_LIMIT),
        name="recur_back",
    )(
        resets, g_mix, branch, states, states, u, u, conv_low, recall, ingate, init_state, init_conv,
        conv, gate_w, decay, narrow_in,
    )


def input_back_kernel(
    n, copies, arrive, g_recur, g_branch, w_in, w_br, normed, tokens, g_residual, gain, second_gain, g_gates, small,
    input_grad, in_out, br_out, gates_out, conv_out, bias_out, decay_out, first_out, second_out,
    gain_row, gain_parts, gain_in, gain_sum, gain_dp, gain_sent, gain_came, gain_dp_sent, gain_dp_came, *bufs
):
    g = Place(n)
    me = lax.axis_index("dp")
    rows, width = tokens.shape
    channels = w_in.shape[0]
    block_width, blocks = gates_out.shape[1], gates_out.shape[2]
    segment = width // (2 * copies)
    gain_width = width // n
    weights = Halving.over(me, copies, *bufs[:4])
    rest = Halving.over(me, copies, *bufs[4:8])
    padded = bufs[0].shape[3] // 2
    rest_rows = bufs[4].shape[3]

    def block(ref, t):
        return ref[span(t, rows)]

    def partial(t, cols):
        return dot(block(g_recur, t), w_in[:, cols]) + dot(block(g_branch, t), w_br[:, cols])

    scatter = Scatter(g, partial, tile_of(width, 512), bufs[8:])

    def gain_copy(t, slot):
        return g.copy(gain_parts.at[t], gain_in.at[slot], gain_sent.at[t], gain_came.at[slot], t)

    def gain_dp_copy(i, slot):
        return pltpu.make_async_remote_copy(
            src_ref=gain_sum,
            dst_ref=gain_dp.at[slot],
            send_sem=gain_dp_sent.at[i],
            recv_sem=gain_dp_came.at[slot],
            device_id={"dp": i},
            device_id_type=MESH,
        )

    def others(act):
        loop(n, lambda t: pl.when(t != g.t)(lambda: act(t)))

    def copies_of(act):
        loop(copies, lambda i: pl.when(i != me)(lambda: act(i)))

    barrier = pltpu.get_barrier_semaphore()
    others(
        lambda t: pl.semaphore_signal(barrier, inc=1, device_id={"tensor": t}, device_id_type=MESH)
    )
    copies_of(lambda i: pl.semaphore_signal(barrier, inc=1, device_id={"dp": i}, device_id_type=MESH))
    pl.semaphore_wait(barrier, n - 1 + copies - 1)

    arrive(0, 1, 2, 3)
    scatter.offers(g.nz - 1)

    def around(i):
        d = g.nz - 1 - i
        scatter.offers(d - 1)
        scatter.step(d)

    around(0)
    arrive(4, 9)

    data = bufs[0]

    def weigh(q):
        cols = span(q, 2 * segment)
        first = dot_tn(g_recur[...], normed[:, cols])
        second = dot_tn(g_branch[...], normed[:, cols])
        for half in (0, 1):
            index = 2 * q + half
            track, part = lax.div(index, copies), lax.rem(index, copies)
            for i, value in enumerate((first, second)):
                piece = value[:, half * segment : (half + 1) * segment].astype(BF16)
                data[track, part, 0, i * padded : i * padded + channels] = piece
                if padded > channels:
                    data[track, part, 0, i * padded + channels : (i + 1) * padded] = jnp.zeros(
                        (padded - channels, segment), BF16
                    )
        terms = jnp.sum(w_in[:, cols].astype(F32) * first + w_br[:, cols].astype(F32) * second, axis=0, keepdims=True)
        gain_row[0:1, cols] = terms

    loop(copies, weigh)
    gain_row[0:1] = gain_row[0:1] / gain[...].astype(F32)[None]
    weights.start()
    gain_row[1:2] = second_gain[...]
    gain_row[2:8] = jnp.zeros((6, width), F32)
    for t in range(n):
        gain_parts[t] = gain_row[:, t * gain_width : (t + 1) * gain_width]
    others(lambda t: gain_copy(t, g.t).start())
    gain_in[g.t] = gain_parts[g.t]

    flat = jnp.concatenate(
        [
            g_gates[0],
            g_gates[1],
            small[...],
            jnp.zeros((2 * copies * rest_rows - 2 * channels - 8, channels), F32),
        ],
        axis=0,
    ).astype(BF16)
    for i in range(2 * copies):
        bufs[4][i // copies, i % copies, 0] = flat[i * rest_rows : (i + 1) * rest_rows]
    rest.start()

    events = [lambda a=a, b=b: (a(), b()) for a, b in zip(weights.events(), rest.events())]
    for i in range(1, g.nz - 1):
        around(i)
        if events:
            events.pop(0)()
        if i == 1:
            others(lambda t: gain_copy(t, t).wait_recv())
            total = gain_in[0]
            for t in range(1, n):
                total = total + gain_in[t]
            gain_sum[...] = total
            copies_of(lambda i: gain_dp_copy(i, me).start())
            gain_dp[me] = total
    for event in events:
        event()
    scatter.last()
    arrive(5, 6)
    part = 32

    def rows_of(i):
        at = span(i, part)
        back, _ = norm_grad(tokens[at].astype(F32), gain[...].astype(F32)[None], scatter.acc[at])
        input_grad[at] = g_residual[at] + back

    loop(rows // part, rows_of)
    copies_of(lambda i: gain_dp_copy(i, i).wait_recv())
    total = gain_dp[0]
    for i in range(1, copies):
        total = total + gain_dp[i]
    first_out[...] = total[0]
    second_out[...] = total[1]
    rest.finish()
    flat = jnp.concatenate([bufs[6][i // copies, i % copies, 0].astype(F32) for i in range(2 * copies)], axis=0)
    for q in (0, 1):
        for i in range(blocks):
            start = q * channels + i * block_width
            gates_out[q, :, i] = flat[start : start + block_width, i * block_width : (i + 1) * block_width]
    conv_out[...] = flat[2 * channels : 2 * channels + 5]
    bias_out[...] = flat[2 * channels + 5 : 2 * channels + 7]
    decay_out[...] = flat[2 * channels + 7]
    weights.finish()
    for i in range(2 * copies):
        for q, out in enumerate((in_out, br_out)):
            out[:, i * segment : (i + 1) * segment] = bufs[2][
                i // copies, i % copies, 0, q * padded : q * padded + channels
            ]
    others(lambda t: gain_copy(t, t).wait_send())
    copies_of(lambda i: gain_dp_copy(i, i).wait_send())
    scatter.finish()


def up_to(extent, multiple):
    return (extent + multiple - 1) // multiple * multiple


def input_back(
    n, copies, g_recur, g_branch, w_in, w_br, normed, tokens, g_residual, gain, second_gain, g_gates, small, blocks
):
    rows, width = tokens.shape
    channels = w_in.shape[0]
    block = channels // blocks
    rest_rows = up_to((2 * channels + 8 + 2 * copies - 1) // (2 * copies), 16)
    gain_shape = (8, width // n)
    sems = pltpu.SemaphoreType.DMA
    inputs = (g_recur, g_branch, w_in, w_br, normed, tokens, g_residual, gain, second_gain, g_gates, small)
    which = (0, 1, 2, 3, 4, 9, 5, 6)
    specs, kept = fetched_specs(inputs, which)
    return pl.pallas_call(
        fetching(functools.partial(input_back_kernel, n, copies), which),
        out_shape=(shape(rows, width),)
        + (shape(channels, width, dtype=BF16),) * 2
        + (
            shape(2, block, blocks, block),
            shape(5, channels),
            shape(2, channels),
            shape(channels),
            shape(width // n),
            shape(width // n),
        ),
        in_specs=specs,
        out_specs=(VM,) * 9,
        scratch_shapes=[
            pltpu.VMEM((8, width), F32),
            pltpu.VMEM((n, *gain_shape), F32),
            pltpu.VMEM((n, *gain_shape), F32),
            pltpu.VMEM(gain_shape, F32),
            pltpu.VMEM((copies, *gain_shape), F32),
            sems((n,)),
            sems((n,)),
            sems((copies,)),
            sems((copies,)),
        ]
        + Halving.scratch(copies, 2 * up_to(channels, 16), width // (2 * copies))
        + Halving.scratch(copies, rest_rows, channels)
        + Scatter.scratch(n, rows, width)
        + kept,
        compiler_params=comm_params(6),
        cost_estimate=cost(8 * n * rows * width * channels),
        name="input_back",
    )(*inputs)


def widen_kernel(small, *refs):
    half = len(refs) // 2
    for q, (narrow, wide) in enumerate(zip(refs[:half], refs[half:])):

        def pass_on(narrow=narrow, wide=wide):
            wide[...] = narrow[...].reshape(wide.shape).astype(wide.dtype)

        if q < small:
            pl.when(pl.program_id(0) == 0)(pass_on)
        else:
            pass_on()


def widen(small, as_is, by_rows, by_columns, in_parts):
    steps = 8
    width = by_columns[0].shape[1]
    tile = width // steps
    per_part = in_parts.shape[2] // tile
    specs, outs = [], []

    def whole(x):
        return pl.BlockSpec(x.shape, lambda i: (0,) * x.ndim)

    for x in small:
        specs.append(whole(x))
        outs.append(shape(*x.shape))
    for x in as_is:
        specs.append(pl.BlockSpec((x.shape[0] // steps, x.shape[1]), lambda i: (i, 0)))
        outs.append(shape(*x.shape, dtype=x.dtype))
    for x in by_rows:
        specs.append(pl.BlockSpec((x.shape[0] // steps, x.shape[1]), lambda i: (i, 0)))
        outs.append(shape(*x.shape))
    for x in by_columns:
        specs.append(pl.BlockSpec((x.shape[0], tile), lambda i: (0, i)))
        outs.append(shape(*x.shape))
    last = pl.BlockSpec((1, in_parts.shape[1], tile), lambda i: (i // per_part, 0, i % per_part))
    outs.append(shape(in_parts.shape[1], width))
    wide = pl.BlockSpec((in_parts.shape[1], tile), lambda i: (0, i))
    return pl.pallas_call(
        functools.partial(widen_kernel, len(small)),
        grid=(steps,),
        out_shape=tuple(outs),
        in_specs=specs + [last],
        out_specs=tuple(specs) + (wide,),
        compiler_params=pltpu.CompilerParams(vmem_limit_bytes=VMEM_LIMIT),
        name="widen",
    )(*small, *as_is, *by_rows, *by_columns, in_parts)


def body(
    n,
    copies,
    tokens,
    cotangent,
    resets,
    init_state,
    init_conv,
    norm_gain,
    w_input,
    w_branch,
    conv_params,
    gate_weights,
    gate_bias,
    decay_rate,
    w_output,
    mlp_gain,
    w_gelu,
    w_linear,
    w_down,
):
    rows, width = tokens.shape
    total = rows * n
    channels = w_input.shape[1]
    blocks, block = gate_weights.shape[1], gate_weights.shape[2]
    before_conv = init_conv.transpose(1, 0, 2)
    gain_first, gain_second = norm_gain, mlp_gain
    gate_w = (gate_weights[:, :, :, None] * jnp.eye(blocks, dtype=BF16)[None, :, None, :, None]).reshape(
        2, channels, channels
    )
    w_in, w_br = w_input.T, w_branch.T

    def flat(x):
        return x.reshape(total, x.shape[-1])

    def blocked(x):
        return x.reshape(n, rows, x.shape[-1])

    normed, recur, branch, states, mixture, conv_low, recall, ingate, final_state, final_conv = project(
        n, tokens, gain_first, w_in, w_br, resets, init_state, before_conv, conv_params, gate_w, gate_bias, decay_rate
    )
    mixture = blocked(mixture)
    cot_full, residual, normed_mlp = mixer_out(n, mixture, w_output, cotangent, tokens, gain_second)
    hidden, grad_gelu, grad_linear, grad_down, g_residual, g_low, gain_second_grad = mlp(
        n, copies, normed_mlp, cot_full, w_gelu, w_linear, w_down, residual, gain_second
    )
    mlp_sums = lax.psum((grad_gelu, grad_linear), "dp")
    output, g_mixture, grad_output = down(n, copies, hidden, w_down, residual, g_low, w_output, mixture)
    g_recur, g_branch, small, g_gates, grad_down = recur_back(
        resets, flat(g_mixture), branch, states, recur, conv_low, recall, ingate, init_state, before_conv,
        conv_params, gate_w, decay_rate, grad_down,
    )
    mlp_sums, grad_output, small = lax.optimization_barrier((mlp_sums, grad_output, small))
    grad_output = lax.psum(grad_output, "dp")
    input_grad, grad_input, grad_branch, gates, g_conv, g_bias, g_decay, g_first_gain, g_second_gain = input_back(
        n, copies, g_recur, g_branch, w_in, w_br, flat(normed), tokens, g_residual, gain_first,
        gain_second_grad, g_gates, small, blocks,
    )
    (
        final_state, final_conv, gates, g_conv, g_bias, g_decay, g_first_gain, g_second_gain, output, input_grad,
        grad_gelu, grad_linear, grad_input, grad_branch, grad_output,
    ) = widen(
        (final_state, final_conv, gates, g_conv, g_bias, g_decay, g_first_gain, g_second_gain),
        (output, input_grad),
        mlp_sums,
        (grad_input, grad_branch),
        grad_output,
    )
    return (
        output,
        input_grad,
        final_state,
        final_conv.transpose(1, 0, 2),
        g_first_gain,
        grad_input.T,
        grad_branch.T,
        g_conv,
        gates.transpose(0, 2, 1, 3),
        g_bias,
        g_decay,
        grad_output,
        g_second_gain,
        grad_gelu,
        grad_linear,
        grad_down,
    )


def solution(mesh):
    in_specs = (
        P(("dp", "tensor"), None),
        P(("dp", "tensor"), None),
        P("dp"),
        P("dp", "tensor"),
        P("dp", None, "tensor"),
        P(),
        P(None, "tensor"),
        P(None, "tensor"),
        P(None, "tensor"),
        P(None, "tensor", None, None),
        P(None, "tensor"),
        P("tensor"),
        P("tensor", None),
        P(),
        P(None, "tensor"),
        P(None, "tensor"),
        P("tensor", None),
    )
    out_specs = (
        P(("dp", "tensor"), None),
        P(("dp", "tensor"), None),
        P("dp", "tensor"),
        P("dp", None, "tensor"),
        P("tensor"),
        P(None, "tensor"),
        P(None, "tensor"),
        P(None, "tensor"),
        P(None, "tensor", None, None),
        P(None, "tensor"),
        P("tensor"),
        P("tensor", None),
        P("tensor"),
        P(None, "tensor"),
        P(None, "tensor"),
        P("tensor", None),
    )
    return jax.shard_map(
        functools.partial(body, mesh.shape["tensor"], mesh.shape["dp"]),
        mesh=mesh,
        in_specs=in_specs,
        out_specs=out_specs,
        check_vma=False,
    )
```

```python
import functools

import jax
import jax.numpy as jnp
from jax import lax
from jax.experimental import pallas as pl
from jax.experimental.pallas import tpu as pltpu
from jax.sharding import PartitionSpec as P

EPSILON = 1e-06
KAPPA = 0.7978845608028654
CUBIC = 0.044715
PIECES = 2
STRIPS = 4
PARTS = 8
F32 = jnp.float32
BF16 = jnp.bfloat16
ANY = pl.BlockSpec(memory_space=pl.ANY)
VM = pl.BlockSpec(memory_space=pltpu.VMEM)
VMEM_LIMIT = 61 * 1024 * 1024
MESH = pl.DeviceIdType.MESH


def dot(a, b):
    return jnp.dot(a, b, preferred_element_type=F32)


def dot_nt(a, b):
    return lax.dot_general(a, b, (((1,), (1,)), ((), ())), preferred_element_type=F32)


def dot_tn(a, b):
    return lax.dot_general(a, b, (((0,), (0,)), ((), ())), preferred_element_type=F32)


def tile_of(extent, wanted):
    while extent % wanted:
        wanted //= 2
    return wanted


def span(i, size):
    return pl.ds(pl.multiple_of(i * size, size), size)


def loop(count, body):
    def step(i, carry):
        body(i)
        return carry

    lax.fori_loop(0, count, step, 0)


class Place:
    def __init__(self, n):
        self.n = n
        self.nz = n // 2
        self.t = lax.axis_index("tensor")
        self.c = lax.rem(self.t, 2)
        self.j = lax.div(self.t, 2)
        self.sib = self.t + 1 - 2 * self.c
        self.has_up = self.j < self.nz - 1
        self.has_down = self.j > 0

    def greet(self, partners=()):
        barrier = pltpu.get_barrier_semaphore()

        def signal(t):
            pl.semaphore_signal(barrier, inc=1, device_id={"tensor": t}, device_id_type=MESH)

        for i in partners:
            pl.semaphore_signal(barrier, inc=1, device_id={"dp": i}, device_id_type=MESH)

        signal(self.sib)
        pl.when(self.has_up)(lambda: signal(self.t + 2))
        pl.when(self.has_down)(lambda: signal(self.t - 2))
        pl.semaphore_wait(
            barrier,
            1 + len(partners) + self.has_up.astype(jnp.int32) + self.has_down.astype(jnp.int32),
        )

    def copy(self, src, dst, send, recv, t):
        return pltpu.make_async_remote_copy(
            src_ref=src,
            dst_ref=dst,
            send_sem=send,
            recv_sem=recv,
            device_id={"tensor": t},
            device_id_type=MESH,
        )


class Gather:
    def __init__(self, place, full, sent, came):
        self.place, self.full, self.sent, self.came = place, full, sent, came
        self.pieces = came.shape[1]
        self.size = full.shape[1] // self.pieces

    @staticmethod
    def scratch(n, rows, width):
        return [
            pltpu.VMEM((n, rows, width), BF16),
            pltpu.SemaphoreType.DMA((n, PIECES, 3)),
            pltpu.SemaphoreType.DMA((n, PIECES)),
        ]

    def copy(self, t, p, way, to):
        piece = self.full.at[t, pl.ds(p * self.size, self.size)]
        return self.place.copy(piece, piece, self.sent.at[t, p, way], self.came.at[t, p], to)

    def start(self):
        g = self.place
        for p in range(self.pieces):
            pl.when(g.has_up)(lambda: self.copy(g.t, p, 0, g.t + 2).start())
            pl.when(g.has_down)(lambda: self.copy(g.t, p, 1, g.t - 2).start())
        for p in range(self.pieces):
            self.copy(g.t, p, 2, g.sib).start()

    def forward(self, d, pieces=None):
        g = self.place
        for p in range(self.pieces) if pieces is None else pieces:

            @pl.when(g.j - d >= 0)
            def _():
                t = g.t - 2 * d
                self.copy(t, p, 0, g.sib).wait_recv()
                pl.when(g.has_up)(lambda: self.copy(t, p, 0, g.t + 2).start())
                self.copy(t, p, 2, g.sib).start()

            @pl.when(g.j + d < g.nz)
            def _():
                t = g.t + 2 * d
                self.copy(t, p, 1, g.sib).wait_recv()
                pl.when(g.has_down)(lambda: self.copy(t, p, 1, g.t - 2).start())
                self.copy(t, p, 2, g.sib).start()

    def each(self, d, use):
        g = self.place

        def visit(q):
            core, way = lax.div(q, 2), 2 * lax.rem(q, 2) - 1
            j = g.j + way * d
            there = jnp.logical_and(j >= 0, j < g.nz)

            @pl.when(jnp.logical_and(there, jnp.logical_or(d > 0, way > 0)))
            def _():
                t = 2 * j + lax.rem(g.c + core, 2)

                @pl.when(core > 0)
                def _():
                    for p in range(self.pieces):
                        self.copy(t, p, 2, g.sib).wait_recv()

                use(t)

        loop(4, visit)

    def finish(self):
        g = self.place

        def done(t):
            for p in range(self.pieces):
                self.copy(t, p, 2, g.sib).wait_send()

                @pl.when(jnp.logical_and(t <= g.t, g.has_up))
                def _():
                    self.copy(t, p, 0, g.sib).wait_send()

                @pl.when(jnp.logical_and(t >= g.t, g.has_down))
                def _():
                    self.copy(t, p, 1, g.sib).wait_send()

        loop(g.nz, lambda k: done(2 * k + g.c))


class Scatter:
    def __init__(self, place, partial, tile, bufs):
        self.place, self.partial, self.tile = place, partial, tile
        self.to_sib, self.from_sib, self.line, self.acc = bufs[:4]
        self.sib_send, self.sib_recv, self.line_send, self.line_recv = bufs[4:]
        self.out = self.from_sib
        self.tiles = self.acc.shape[1] // tile

    @staticmethod
    def scratch(n, rows, width):
        nz = n // 2
        return [
            pltpu.VMEM((nz, rows, width), BF16),
            pltpu.VMEM((nz, rows, width), BF16),
            pltpu.VMEM((nz + 1, rows, width), BF16),
            pltpu.VMEM((rows, width), F32),
            pltpu.SemaphoreType.DMA((nz,)),
            pltpu.SemaphoreType.DMA((nz,)),
            pltpu.SemaphoreType.DMA((nz, STRIPS)),
            pltpu.SemaphoreType.DMA((nz + 1, STRIPS)),
        ]

    def sib_copy(self, k):
        return self.place.copy(
            self.to_sib.at[k],
            self.from_sib.at[k],
            self.sib_send.at[k],
            self.sib_recv.at[k],
            self.place.sib,
        )

    def line_copy(self, k, slot, p, to):
        at = self.strip(p)
        return self.place.copy(
            self.out.at[k, at], self.line.at[slot, at], self.line_send.at[k, p], self.line_recv.at[slot, p], to
        )

    def strip(self, p):
        return span(p, self.acc.shape[0] // STRIPS)

    def offer(self, k):
        t = 2 * k + 1 - self.place.c

        def part(i):
            cols = span(i, self.tile)
            self.to_sib[k, :, cols] = self.partial(t, cols).astype(BF16)

        loop(self.tiles, part)
        self.sib_copy(k).start()

    def pair(self, k):
        self.sib_copy(k).wait_recv()
        t = 2 * k + self.place.c

        def part(i):
            cols = span(i, self.tile)
            self.acc[:, cols] = self.partial(t, cols) + self.from_sib[k, :, cols].astype(F32)

        loop(self.tiles, part)

    def offers(self, d):
        g = self.place

        def way_of(w):
            k = g.j + (1 - 2 * w) * d

            @pl.when(jnp.logical_and(jnp.logical_and(k >= 0, k < g.nz), jnp.logical_or(d > 0, w == 0)))
            def _():
                self.offer(k)

        loop(2, way_of)

    def step(self, d):
        g = self.place

        def way_of(w):
            sign = 1 - 2 * w
            k = g.j + sign * d

            @pl.when(jnp.logical_and(k >= 0, k < g.nz))
            def _():
                self.pair(k)
                upstream = g.j - sign
                more = jnp.logical_and(upstream >= 0, upstream < g.nz)

                slot = jnp.where(jnp.logical_and(d == 1, w == 1), g.nz, k)

                def pass_on(p):
                    at = self.strip(p)

                    @pl.when(more)
                    def _():
                        self.line_copy(k, k, p, g.sib).wait_recv()
                        self.out[k, at] = (self.acc[at] + self.line[k, at].astype(F32)).astype(BF16)

                    @pl.when(jnp.logical_not(more))
                    def _():
                        self.out[k, at] = self.acc[at].astype(BF16)

                    self.line_copy(k, slot, p, g.t + 2 * sign).start()

                loop(STRIPS, pass_on)

        loop(2, way_of)

    def last(self):
        g = self.place
        self.pair(g.j)

        def take(p):
            at = self.strip(p)

            @pl.when(g.has_down)
            def _():
                self.line_copy(g.j, g.j, p, g.sib).wait_recv()
                self.acc[at] += self.line[g.j, at].astype(F32)

            @pl.when(g.has_up)
            def _():
                self.line_copy(g.j, g.nz, p, g.sib).wait_recv()
                self.acc[at] += self.line[g.nz, at].astype(F32)

        loop(STRIPS, take)

    def finish(self):
        g = self.place

        def done(k):
            self.sib_copy(k).wait_send()
            pl.when(g.j != k)(
                lambda: loop(STRIPS, lambda p: self.line_copy(k, k, p, g.sib).wait_send())
            )

        loop(g.nz, done)


class Halving:
    def __init__(self, me, count, data, landed, final, sems):
        self.me, self.count = me, count
        self.data, self.landed, self.final = data, landed, final
        self.out_send, self.out_recv, self.back_send, self.back_recv = (sems.at[q] for q in range(4))
        self.bits = count.bit_length() - 1
        assert count == 1 << self.bits

    @staticmethod
    def scratch(count, rows, columns):
        return [
            pltpu.VMEM((2, count, 1, rows, columns), BF16),
            pltpu.VMEM((2, count - 1, 1, rows, columns), BF16),
            pltpu.VMEM((2, count, 1, rows, columns), BF16),
            pltpu.SemaphoreType.DMA((4, 2, count - 1)),
        ]

    @staticmethod
    def over(me, count, data, landed, final, sems):
        def at(ref):
            return lambda track, index: ref.at[track, index]

        return Halving(me, count, at(data), at(landed), at(final), sems)

    def partners(self):
        return [self.me + (1 - 2 * self.own(b)) * (1 << b) for b in range(self.bits)]

    def own(self, bit):
        return lax.rem(lax.div(self.me, 1 << bit), 2)

    def swaps(self, s):
        for track in (0, 1):
            order = [(i + track) % self.bits for i in range(self.bits)]
            bit = order[s]
            partner = self.me + (1 - 2 * self.own(bit)) * (1 << bit)
            fixed = sum(self.own(b) * (1 << b) for b in order[:s])
            for u in range(self.count >> (s + 1)):
                free = sum(((u >> i) & 1) << b for i, b in enumerate(order[s + 1 :]))
                slot = self.count - (self.count >> s) + u
                kept = fixed + free + self.own(bit) * (1 << bit)
                yield track, slot, partner, fixed + free + (1 - self.own(bit)) * (1 << bit), kept

    def out(self, track, slot, partner, given):
        return pltpu.make_async_remote_copy(
            src_ref=self.data(track, given),
            dst_ref=self.landed(track, slot),
            send_sem=self.out_send.at[track, slot],
            recv_sem=self.out_recv.at[track, slot],
            device_id={"dp": partner},
            device_id_type=MESH,
        )

    def back(self, track, slot, partner, segment):
        return pltpu.make_async_remote_copy(
            src_ref=self.final(track, segment),
            dst_ref=self.final(track, segment),
            send_sem=self.back_send.at[track, slot],
            recv_sem=self.back_recv.at[track, slot],
            device_id={"dp": partner},
            device_id_type=MESH,
        )

    def start(self, s=0):
        for track, slot, partner, given, _ in self.swaps(s):
            self.out(track, slot, partner, given).start()

    def turn(self, s):
        for track, slot, partner, given, kept in self.swaps(s):
            self.out(track, slot, partner, given).wait_recv()
            mine, theirs = self.data(track, kept), self.landed(track, slot)
            result = self.final(track, kept) if s == self.bits - 1 else mine
            blocks, rows, _ = mine.shape
            tile = tile_of(rows, 32)

            def add(r):
                block, at = lax.div(r, rows // tile), span(lax.rem(r, rows // tile), tile)
                result[block, at] = (mine[block, at].astype(F32) + theirs[block, at].astype(F32)).astype(BF16)

            loop(blocks * (rows // tile), add)
        if s < self.bits - 1:
            self.start(s + 1)
        else:
            self.start_back(s)

    def start_back(self, s):
        for track, slot, partner, _, kept in self.swaps(s):
            self.back(track, slot, partner, kept).start()

    def turn_back(self, s):
        for track, slot, partner, given, _ in self.swaps(s):
            self.back(track, slot, partner, given).wait_recv()
        if s > 0:
            self.start_back(s - 1)

    def events(self):
        steps = [functools.partial(self.turn, s) for s in range(self.bits)]
        return steps + [functools.partial(self.turn_back, s) for s in range(self.bits - 1, 0, -1)]

    def finish(self):
        self.turn_back(0)
        for s in range(self.bits):
            for track, slot, partner, given, kept in self.swaps(s):
                self.out(track, slot, partner, given).wait_send()
                self.back(track, slot, partner, kept).wait_send()


def fetching(kernel, which):
    def wrapped(*refs):
        refs = list(refs)
        sems = refs.pop()
        kept = refs[len(refs) - len(which) :]
        del refs[len(refs) - len(which) :]
        copies = {}
        for q, i in enumerate(which):
            copies[i] = pltpu.make_async_copy(refs[i], kept[q], sems.at[q])
            copies[i].start()
            refs[i] = kept[q]

        def arrive(*wanted):
            for i in wanted:
                copies[i].wait()

        return kernel(arrive, *refs)

    return wrapped


def fetched_specs(inputs, which, plain=()):
    specs = [ANY if i in which or i in plain else VM for i in range(len(inputs))]
    scratch = [pltpu.VMEM(inputs[i].shape, inputs[i].dtype) for i in which]
    return specs, scratch + [pltpu.SemaphoreType.DMA((len(which),))]


def comm_params(collective_id):
    return pltpu.CompilerParams(
        collective_id=collective_id, has_side_effects=True, vmem_limit_bytes=VMEM_LIMIT
    )


def cost(flops):
    return pl.CostEstimate(flops=int(flops), bytes_accessed=200_000_000, transcendentals=0)


def shape(*dims, dtype=F32):
    return jax.ShapeDtypeStruct(dims, dtype)


def inv_rms(values):
    return lax.rsqrt(jnp.mean(values * values, axis=-1, keepdims=True) + EPSILON)


def norm_grad(values, gain, gradient):
    inv = inv_rms(values)
    unit = values * inv
    scaled = gradient * gain
    centred = jnp.mean(scaled * unit, axis=-1, keepdims=True)
    return inv * (scaled - unit * centred), gradient * unit


def sigmoid(v):
    return 1.0 / (1.0 + jnp.exp(-v))


def gelu_parts(v):
    square = v * v
    bend = jnp.tanh(KAPPA * v * (1.0 + CUBIC * square))
    half = 0.5 * (1.0 + bend)
    slope = half + 0.5 * v * (1.0 - bend * bend) * (KAPPA * (1.0 + 3.0 * CUBIC * square))
    return v * half, slope


def one_minus_square(log_decay, decay):
    m = -2.0 * log_decay
    series = m * (
        1.0 - m * (1 / 2) * (1.0 - m * (1 / 3) * (1.0 - m * (1 / 4) * (1.0 - m * (1 / 5) * (1.0 - m * (1 / 6)))))
    )
    return jnp.where(m < 0.35, series, 1.0 - decay * decay)


def starts(reset, here, init_state, init_conv, state, hist):
    keep = (1 - reset).astype(F32)
    state[...] = jnp.broadcast_to(init_state[here] * keep, state.shape)
    before = [init_conv[q, here] * keep for q in range(3)]
    hist[0:8] = jnp.concatenate([jnp.zeros((5, hist.shape[1]), F32)] + before, axis=0)


def recur_chunk(base, u, branch, conv, gate_w, bias, decay, kept, hist, decay_buf, drive_buf, carry):
    states, mixture, conv_low, recall, ingate = kept
    rows, channels = decay_buf.shape
    tile = 32

    def rows_of(i, size):
        return pl.ds(pl.multiple_of(base + i * size, size), size)

    whole = rows_of(0, rows)
    hist[8:] = u[whole]

    def convolve(i):
        window = hist[pl.ds(pl.multiple_of(i * tile, tile), tile + 8)]
        value = conv[4:5] + conv[0:1] * window[8:] + conv[1:2] * window[7 : tile + 7]
        value = value + conv[2:3] * window[6 : tile + 6] + conv[3:4] * window[5 : tile + 5]
        conv_low[rows_of(i, tile)] = value.astype(BF16)

    loop(rows // tile, convolve)
    hist[0:8] = hist[rows : rows + 8]
    low = conv_low[whole]
    recall[whole] = dot(low, gate_w[0])
    ingate[whole] = dot(low, gate_w[1])

    def gates(i):
        at, here = rows_of(i, tile), span(i, tile)
        r = sigmoid(recall[at] + bias[0:1])
        k = sigmoid(ingate[at] + bias[1:2])
        recall[at] = r
        ingate[at] = k
        log_decay = -8.0 * r * decay[...][None]
        step = jnp.exp(log_decay)
        decay_buf[here] = step
        drive_buf[here] = jnp.sqrt(one_minus_square(log_decay, step)) * k * conv_low[at].astype(F32)

    loop(rows // tile, gates)
    row = lax.broadcasted_iota(jnp.int32, (8, channels), 0)

    def scan(i, before):
        for part in range(4):
            at = pl.ds(pl.multiple_of(i * 32 + part * 8, 8), 8)
            a, b = decay_buf[at], drive_buf[at]
            for shift in (1, 2, 4):
                inside = row >= shift
                b = b + a * jnp.where(inside, pltpu.roll(b, shift, 0), 0.0)
                a = a * jnp.where(inside, pltpu.roll(a, shift, 0), 1.0)
            h = a * before + b
            states[pl.ds(pl.multiple_of(base + i * 32 + part * 8, 8), 8)] = h
            before = jnp.broadcast_to(h[7:8], (8, channels))
        return before

    carry[...] = lax.fori_loop(0, rows // 32, scan, carry[...])

    def mix(i):
        at = rows_of(i, tile)
        value, _ = gelu_parts(branch[at])
        mixture[at] = (states[at] * value).astype(BF16)

    loop(rows // tile, mix)


def project_kernel(
    n, arrive, tokens, gain, w_in, w_br, resets, init_state, init_conv, conv, gate_w, bias, decay,
    normed, recur, branch, states, mixture, conv_low, recall, ingate, final_state, final_conv,
    full, sent, came, held_a, held_b, kept_s, kept_m, kept_c, kept_r, kept_i,
    hist, decay_buf, drive_buf, carry, saved, written,
):
    g = Place(n)
    gather = Gather(g, full, sent, came)
    rows = full.shape[1]
    part = 64

    def normalize(i):
        at = span(i, part)
        values = tokens[at].astype(F32)
        full[g.t, at] = (values * inv_rms(values) * gain[...].astype(F32)[None]).astype(BF16)

    loop(rows // part, normalize)
    g.greet()
    gather.start()
    arrive(2, 3)

    def out(t):
        return pltpu.make_async_copy(full.at[t], normed.at[t], saved.at[t])

    def use(t):
        out(t).start()
        at = span(t, rows)
        held_a[at] = dot_nt(full[t], w_in[...])
        held_b[at] = dot_nt(full[t], w_br[...])

    kept = (kept_s, kept_m, kept_c, kept_r, kept_i)
    pairs = ((held_a, recur), (held_b, branch)) + tuple(zip(kept, (states, mixture, conv_low, recall, ingate)))
    sequences = init_state.shape[0]
    length = n * rows // sequences
    size = decay_buf.shape[0]
    chunks = length // size

    def leave(c, act):
        at = span(c, size)
        for q, (held, target) in enumerate(pairs):
            act(pltpu.make_async_copy(held.at[at], target.at[at], written.at[c, q]))

    def sequence(s):
        here = pl.ds(s, 1)
        starts(resets[s], here, init_state, init_conv, carry, hist)

        def chunk(c):
            index = s * chunks + c
            base = index * size
            recur_chunk(base, held_a, held_b, conv, gate_w, bias, decay, kept, hist, decay_buf, drive_buf, carry)
            leave(index, lambda copy: copy.start())

        loop(chunks, chunk)
        final_state[here] = carry[0:1]
        for q in range(3):
            final_conv[q, here] = hist[5 + q : 6 + q]

    def step(d):
        pl.when(d > 0)(lambda: gather.forward(d))
        gather.each(d, use)

        def whole(s):
            first = lax.div(s * length, 2 * rows)
            last = lax.div((s + 1) * length - 1, 2 * rows)
            pl.when(jnp.maximum(jnp.abs(first - g.j), jnp.abs(last - g.j)) == d)(lambda: sequence(s))

        loop(sequences, whole)

    loop(g.nz, step)
    loop(n, lambda t: out(t).wait())
    loop(sequences * chunks, lambda c: leave(c, lambda copy: copy.wait()))
    gather.finish()


def project(n, tokens, gain, w_in, w_br, resets, init_state, init_conv, conv, gate_w, bias, decay):
    rows, width = tokens.shape
    channels = w_in.shape[0]
    sequences = init_state.shape[0]
    total = n * rows
    size = tile_of(total // sequences, 256)
    inputs = (tokens, gain, w_in, w_br, resets, init_state, init_conv, conv, gate_w, bias, decay)
    specs, kept = fetched_specs(inputs, (2, 3))
    specs[4] = pl.BlockSpec(memory_space=pltpu.SMEM)
    wide, narrow = (total, channels), pltpu.VMEM((total, channels), BF16)
    return pl.pallas_call(
        fetching(functools.partial(project_kernel, n), (2, 3)),
        out_shape=(
            shape(n, rows, width, dtype=BF16),
            shape(*wide),
            shape(*wide),
            shape(*wide),
            shape(*wide, dtype=BF16),
            shape(*wide, dtype=BF16),
            shape(*wide),
            shape(*wide),
            shape(sequences, channels),
            shape(3, sequences, channels),
        ),
        in_specs=specs,
        out_specs=(ANY,) * 8 + (VM,) * 2,
        scratch_shapes=Gather.scratch(n, rows, width)
        + [pltpu.VMEM(wide, F32)] * 3
        + [narrow] * 2
        + [pltpu.VMEM(wide, F32)] * 2
        + [
            pltpu.VMEM((size + 8, channels), F32),
            pltpu.VMEM((size, channels), F32),
            pltpu.VMEM((size, channels), F32),
            pltpu.VMEM((8, channels), F32),
            pltpu.SemaphoreType.DMA((n,)),
            pltpu.SemaphoreType.DMA((total // size, 7)),
        ]
        + kept,
        compiler_params=comm_params(1),
        cost_estimate=cost(4 * n * rows * width * channels),
        name="project",
    )(*inputs)


def mixer_out_kernel(
    n, arrive, mixture, w_output, cotangent, tokens, gain, cot_full, residual, normed,
    full, sent, came, saved, *bufs
):
    g = Place(n)
    gather = Gather(g, full, sent, came)
    scatter = Scatter(g, lambda t, cols: dot(mixture[t], w_output[:, cols]), tile_of(residual.shape[1], 512), bufs)
    first = pltpu.make_async_copy(cotangent, full.at[g.t], saved.at[0])
    first.start()
    g.greet()
    first.wait()
    gather.start()
    arrive(0, 1)

    def use(t):
        pltpu.make_async_copy(full.at[t], cot_full.at[t], saved.at[t]).start()

    scatter.offers(g.nz - 1)

    def around(i):
        d = g.nz - 1 - i
        scatter.offers(d - 1)
        scatter.step(d)
        gather.each(i, use)
        gather.forward(i + 1)

    loop(g.nz - 1, around)
    scatter.last()
    arrive(3)
    part = 64

    def rows_of(i):
        at = span(i, part)
        values = scatter.acc[at] + tokens[at].astype(F32)
        residual[at] = values
        normed[at] = (values * inv_rms(values) * gain[...].astype(F32)[None]).astype(BF16)

    loop(residual.shape[0] // part, rows_of)
    gather.each(g.nz - 1, use)
    loop(n, lambda t: pltpu.make_async_copy(full.at[t], cot_full.at[t], saved.at[t]).wait())
    scatter.finish()
    gather.finish()


def mixer_out(n, mixture, w_output, cotangent, tokens, gain):
    rows, width = tokens.shape
    inputs, which = (mixture, w_output, cotangent, tokens, gain), (0, 1, 3)
    specs, kept = fetched_specs(inputs, which, (2,))
    return pl.pallas_call(
        fetching(functools.partial(mixer_out_kernel, n), which),
        out_shape=(
            shape(n, rows, width, dtype=BF16),
            shape(rows, width),
            shape(rows, width, dtype=BF16),
        ),
        in_specs=specs,
        out_specs=(ANY, VM, VM),
        scratch_shapes=Gather.scratch(n, rows, width)
        + [pltpu.SemaphoreType.DMA((n,))]
        + Scatter.scratch(n, rows, width)
        + kept,
        compiler_params=comm_params(2),
        cost_estimate=cost(2 * n * rows * width * mixture.shape[-1]),
        name="mixer_out",
    )(*inputs)


def mlp_kernel(
    n, copies, arrive, normed, cot_full, w_gelu, w_linear, w_down, residual, gain,
    hidden, grad_gelu, grad_linear, grad_down, g_residual, g_low, g_gain,
    full, sent, came, cot, keep_h, keep_f, keep_s, acc_g, acc_l, acc_d,
    to_sib, sums, line, acc, landed, swap_sems, saved, fetched, drained, sib_sent, sib_came, line_sent, line_came,
):
    g = Place(n)
    gather = Gather(g, full, sent, came)
    columns = w_gelu.shape[1]
    rows, width = acc.shape
    tile = tile_of(columns, 256)
    wide = tile_of(width, 1024)
    strip = rows // PARTS
    me = lax.axis_index("dp")
    start = pltpu.make_async_copy(normed, full.at[g.t], saved.at[0])
    start.start()
    part_width = width // (2 * copies)
    depth = columns // rows

    def segment(track, index):
        return pl.ds(pl.multiple_of((track * copies + index) * part_width, part_width), part_width)

    swap = Halving(
        me,
        copies,
        lambda track, index: full.at[0:depth, :, segment(track, index)],
        lambda track, slot: landed.at[track, slot],
        lambda track, index: full.at[depth : 2 * depth, :, segment(track, index)],
        swap_sems,
    )
    def fetch(t, q):
        return pltpu.make_async_copy(cot_full.at[t], cot.at[q], fetched.at[q])

    g.greet(swap.partners())
    start.wait()
    gather.start()
    fetch(2 * g.j, 0).start()
    fetch(2 * g.j + 1, 1).start()
    arrive(2, 3, 4)
    acc_g[...] = jnp.zeros_like(acc_g)
    acc_l[...] = jnp.zeros_like(acc_l)
    acc_d[...] = jnp.zeros_like(acc_d)

    def save(t, q):
        return pltpu.make_async_copy(keep_h.at[q], hidden.at[t], saved.at[q])

    def layer(t, q):
        fetch(t, q).wait()

        def part(i):
            cols = span(i, tile)
            first = dot(full[t], w_gelu[:, cols])
            second = dot(full[t], w_linear[:, cols])
            back = dot_nt(cot[q], w_down[cols])
            value, slope = gelu_parts(first)
            keep_h[q, :, cols] = (value * second).astype(BF16)
            keep_f[q, :, cols] = (back * second * slope).astype(BF16)
            keep_s[q, :, cols] = (back * value).astype(BF16)

        loop(columns // tile, part)
        save(t, q).start()

    def partial(q, cols):
        return dot_nt(keep_f[q], w_gelu[cols]) + dot_nt(keep_s[q], w_linear[cols])

    def sib_copy(k):
        return g.copy(to_sib, sums.at[k], sib_sent, sib_came.at[k], g.sib)

    def line_copy(k, slot, p, to):
        at = pl.ds(pl.multiple_of(p * strip, strip), strip)
        return g.copy(
            sums.at[k, at], line.at[slot, at], line_sent.at[k, p], line_came.at[slot, p], to
        )

    def chip(d, way):
        k = g.j + way * d
        mine, its = g.c, 1 - g.c
        own, other = 2 * k + mine, 2 * k + its
        for p in range(gather.pieces):
            gather.copy(other, p, 2, g.sib).wait_recv()
        layer(other, its)

        def offer(i):
            cols = span(i, wide)
            to_sib[:, cols] = partial(its, cols).astype(BF16)

        loop(width // wide, offer)
        sib_copy(k).start()
        layer(own, mine)
        sib_copy(k).wait()

        @pl.when(d == 0)
        def _():
            def part(i):
                cols = span(i, wide)
                acc[:, cols] = partial(mine, cols) + sums[k, :, cols].astype(F32)

            loop(width // wide, part)

        @pl.when(d > 0)
        def _():
            def part(i):
                cols = span(i, wide)
                sums[k, :, cols] = (partial(mine, cols) + sums[k, :, cols].astype(F32)).astype(BF16)

            loop(width // wide, part)
            first = jnp.logical_or(
                jnp.logical_and(way > 0, jnp.logical_not(g.has_down)),
                jnp.logical_and(way < 0, jnp.logical_not(g.has_up)),
            )

            @pl.when(first)
            def _():
                slot = jnp.where(jnp.logical_and(way < 0, d == 1), g.nz, k)
                for p in range(PARTS):
                    line_copy(k, slot, p, g.t + 2 * way).start()

        def part(i):
            at = span(i, wide)
            both = full[pl.ds(2 * k, 2), :, at].reshape(2 * rows, wide)
            acc_g[at] += dot_tn(both, keep_f[...].reshape(2 * rows, columns))
            acc_l[at] += dot_tn(both, keep_s[...].reshape(2 * rows, columns))
            acc_d[:, at] += dot_tn(
                keep_h[...].reshape(2 * rows, columns), cot[:, :, at].reshape(2 * rows, wide)
            )

        loop(width // wide, part)
        both_ways = jnp.logical_and(g.j + d < g.nz, g.j - d >= 0)
        again = jnp.logical_and(both_ways, jnp.logical_and(way > 0, d > 0))
        later = jnp.where(g.j + d + 1 < g.nz, g.j + d + 1, g.j - d - 1)
        following = jnp.where(again, g.j - d, later)

        @pl.when(following >= 0)
        def _():
            fetch(2 * following, 0).start()
            fetch(2 * following + 1, 1).start()

        save(other, its).wait()
        save(own, mine).wait()

    def relay(m, events=()):
        def take(k, slot, sign, p):
            at = pl.ds(pl.multiple_of(p * strip, strip), strip)
            line_copy(k, slot, p, g.sib).wait_recv()

            @pl.when(k == g.j)
            def _():
                acc[at] += line[slot, at].astype(F32)

            @pl.when(k != g.j)
            def _():
                sums[k, at] = (sums[k, at].astype(F32) + line[slot, at].astype(F32)).astype(BF16)
                there = jnp.where(jnp.logical_and(sign < 0, k == g.j - 1), g.nz, k)
                line_copy(k, there, p, g.t + 2 * sign).start()

        def rise(p):
            pl.when(jnp.logical_and(g.has_down, m >= g.j))(lambda: take(m, m, 1, p))

        def fall(p):
            k = g.nz - 1 - m
            pl.when(jnp.logical_and(g.has_up, k <= g.j))(
                lambda: take(k, jnp.where(k == g.j, g.nz, k), -1, p)
            )

        lower = 2 * g.j < g.nz

        def strips(i):
            @pl.when(i < PARTS)
            def _():
                pl.when(lower)(lambda: rise(i))
                pl.when(jnp.logical_not(lower))(lambda: fall(i))

            @pl.when(i > 0)
            def _():
                pl.when(lower)(lambda: fall(i - 1))
                pl.when(jnp.logical_not(lower))(lambda: rise(i - 1))

        middle = jnp.logical_and(g.has_up, g.has_down)
        for event in events:
            pl.when(jnp.logical_not(middle))(event)

        def between(i):
            strips(i)
            for q, event in enumerate(events):
                pl.when(jnp.logical_and(middle, i == min(2 * q + 2, PARTS)))(event)

        loop(PARTS + 1, between)

    def cores(d):
        up, down = g.j + d < g.nz, g.j - d >= 0

        def way_of(w):
            both = jnp.logical_and(up, down)
            way = jnp.where(jnp.logical_and(w == 0, up), 1, -1)
            wanted = jnp.where(w == 0, jnp.logical_or(up, down), jnp.logical_and(both, d > 0))
            pl.when(wanted)(lambda: chip(d, way))

            @pl.when(d < g.nz - 1)
            def _():
                for p in range(gather.pieces):
                    pl.when(w == min(p, 1))(lambda: gather.forward(d + 1, (p,)))

        loop(2, way_of)

    def step(d):
        @pl.when(d < g.nz)
        def _():
            cores(d)

        @pl.when(d == g.nz - 1)
        def _():
            gather.finish()
            for i in range(depth):
                full[i] = acc_d[pl.ds(i * rows, rows)].astype(BF16)
            swap.start()

        pl.when(d > 1)(lambda: relay(d - 1))

    loop(g.nz, step)

    stages = [held.at[q] for held in (keep_h, keep_f, keep_s) for q in (0, 1)]
    leaving = []

    def leave(i, value, out):
        slot = i % len(stages)
        if len(leaving) >= len(stages):
            leaving[i - len(stages)].wait()
        stages[slot][...] = value.astype(BF16)
        copy = pltpu.make_async_copy(stages[slot], out, drained.at[slot])
        copy.start()
        leaving.append(copy)

    for i in range(width // rows):
        at = pl.ds(i * rows, rows)
        leave(2 * i, acc_g[at], grad_gelu.at[at])
        leave(2 * i + 1, acc_l[at], grad_linear.at[at])
    events = swap.events()
    events.pop(0)()
    relay(g.nz - 1, events)
    own = pltpu.make_async_copy(cot_full.at[g.t], cot.at[0], fetched.at[0])
    own.start()
    own.wait()
    arrive(5)
    lines = 32
    g_gain[...] = jnp.zeros_like(g_gain)

    def rows_of(i):
        at = span(i, lines)
        back, terms = norm_grad(residual[at], gain[...].astype(F32)[None], acc[at])
        value = cot[0, at].astype(F32) + back
        acc[at] = value
        cot[1, at] = value.astype(BF16)
        g_gain[...] += jnp.sum(terms, axis=0, keepdims=True)

    loop(rows // lines, rows_of)
    last = [
        pltpu.make_async_copy(acc, g_residual, saved.at[0]),
        pltpu.make_async_copy(cot.at[1], g_low, saved.at[1]),
    ]
    swap.finish()
    for i in range(depth):
        at = pl.ds(i * rows, rows)
        last.append(pltpu.make_async_copy(full.at[depth + i], grad_down.at[at], drained.at[len(stages) + i]))
    for copy in last:
        copy.start()
    for copy in leaving[-len(stages) :] + last:
        copy.wait()

    def done(k):
        @pl.when(k != g.j)
        def _():
            for p in range(PARTS):
                line_copy(k, k, p, g.sib).wait_send()

    loop(g.nz, done)


def mlp(n, copies, normed, cot_full, w_gelu, w_linear, w_down, residual, gain):
    rows, width = normed.shape
    columns = w_gelu.shape[1]
    kept = pltpu.VMEM((2, rows, columns), BF16)
    sems = pltpu.SemaphoreType.DMA
    inputs, which = (normed, cot_full, w_gelu, w_linear, w_down, residual, gain), (2, 3, 4, 5)
    specs, held = fetched_specs(inputs, which, (0, 1))
    return pl.pallas_call(
        fetching(functools.partial(mlp_kernel, n, copies), which),
        out_shape=(shape(n, rows, columns, dtype=BF16),)
        + (shape(width, columns, dtype=BF16),) * 2
        + (
            shape(columns, width, dtype=BF16),
            shape(rows, width),
            shape(rows, width, dtype=BF16),
            shape(1, width),
        ),
        in_specs=specs,
        out_specs=(ANY,) * 6 + (VM,),
        scratch_shapes=Gather.scratch(n, rows, width)
        + [pltpu.VMEM((2, rows, width), BF16)]
        + [kept] * 3
        + [pltpu.VMEM((width, columns), F32)] * 2
        + [
            pltpu.VMEM((columns, width), F32),
            pltpu.VMEM((rows, width), BF16),
            pltpu.VMEM((n // 2, rows, width), BF16),
            pltpu.VMEM((n // 2 + 1, rows, width), BF16),
            pltpu.VMEM((rows, width), F32),
            pltpu.VMEM((2, copies - 1, columns // rows, rows, width // (2 * copies)), BF16),
            sems((4, 2, copies - 1)),
            sems((2,)),
            sems((2,)),
            sems((6 + columns // rows,)),
            sems,
            sems((n // 2,)),
            sems((n // 2, PARTS)),
            sems((n // 2 + 1, PARTS)),
        ]
        + held,
        compiler_params=comm_params(3),
        cost_estimate=cost(16 * n * rows * width * columns),
        name="mlp",
    )(*inputs)


def down_kernel(
    n, copies, arrive, hidden, w_down, residual, g_low, w_output, mixture, output, g_mixture, grad_output,
    full, sent, came, acc_o, start_sem, *bufs
):
    g = Place(n)
    gather = Gather(g, full, sent, came)
    width = residual.shape[1]
    wide = tile_of(width, 512)
    scatter = Scatter(g, lambda t, cols: dot(hidden[t], w_down[:, cols]), wide, bufs)
    first = pltpu.make_async_copy(g_low, full.at[g.t], start_sem)
    first.start()
    g.greet()
    first.wait()

    def use(t):
        g_mixture[t] = dot_nt(full[t], w_output[...])

        def part(i):
            at = span(i, wide)
            acc_o[:, at] += dot_tn(mixture[t], full[t, :, at])

        loop(width // wide, part)

    gather.start()
    acc_o[...] = jnp.zeros_like(acc_o)
    arrive(0, 1)
    scatter.offers(g.nz - 1)
    arrive(4, 5)

    def around(i):
        d = g.nz - 1 - i
        scatter.offers(d - 1)
        scatter.step(d)
        gather.each(i, use)
        gather.forward(i + 1)

    loop(g.nz - 1, around)
    gather.each(g.nz - 1, use)
    for i in range(copies):
        part = width // copies
        grad_output[i] = acc_o[:, i * part : (i + 1) * part].astype(BF16)
    scatter.last()
    arrive(2)
    output[...] = (scatter.acc[...] + residual[...]).astype(BF16)
    scatter.finish()
    gather.finish()


def down(n, copies, hidden, w_down, residual, g_low, w_output, mixture):
    rows, width = residual.shape
    channels = w_output.shape[0]
    inputs, which = (hidden, w_down, residual, g_low, w_output, mixture), (0, 1, 4, 5, 2)
    specs, kept = fetched_specs(inputs, which, (3,))
    return pl.pallas_call(
        fetching(functools.partial(down_kernel, n, copies), which),
        out_shape=(
            shape(rows, width, dtype=BF16),
            shape(n, rows, channels),
            shape(copies, channels, width // copies, dtype=BF16),
        ),
        in_specs=specs,
        out_specs=(VM,) * 3,
        scratch_shapes=Gather.scratch(n, rows, width)
        + [pltpu.VMEM((channels, width), F32), pltpu.SemaphoreType.DMA]
        + Scatter.scratch(n, rows, width)
        + kept,
        compiler_params=comm_params(5),
        cost_estimate=cost(2 * n * rows * width * (hidden.shape[-1] + 2 * channels)),
        name="down",
    )(*inputs)


def recur_back_kernel(
    resets, g_mix, branch, states, states_before, u, u_before, conv_low, recall, ingate, init_state, init_conv,
    conv, gate_w, decay, narrow_in,
    g_recur, g_branch, small, g_gates, wide_out,
    g_state, step_buf, root_buf, g_conv, pre_r, pre_i, carry, hist_s, hist_u, sums,
):
    sequence, back = pl.program_id(0), pl.program_id(1)
    last = pl.num_programs(1) - 1
    rows, channels = u.shape
    tile = 32
    wide_out[...] = narrow_in[...].astype(F32)

    @pl.when(jnp.logical_and(sequence == 0, back == 0))
    def _():
        sums[...] = jnp.zeros_like(sums)
        g_gates[...] = jnp.zeros_like(g_gates)

    @pl.when(back == 0)
    def _():
        carry[...] = jnp.zeros_like(carry)
        g_conv[rows : rows + 8] = jnp.zeros((8, channels), F32)

    @pl.when(back > 0)
    def _():
        g_conv[rows : rows + 8] = g_conv[0:8]

    @pl.when(back == last)
    def _():
        starts(
            resets[sequence], pl.ds(sequence, 1), init_state, init_conv, hist_s.at[0:8], hist_u
        )

    @pl.when(back < last)
    def _():
        hist_s[0:8] = states_before[...]
        hist_u[0:8] = u_before[...]

    hist_s[8:] = states[...]
    hist_u[8:] = u[...]

    def first(i):
        at = span(i, tile)
        value, slope = gelu_parts(branch[at])
        gm = g_mix[at]
        g_state[at] = gm * value
        g_branch[at] = (gm * states[at] * slope).astype(BF16)
        log_decay = -8.0 * recall[at] * decay[...][None]
        step = jnp.exp(log_decay)
        step_buf[at] = step
        root_buf[at] = jnp.sqrt(one_minus_square(log_decay, step))

    loop(rows // tile, first)
    row = lax.broadcasted_iota(jnp.int32, (8, channels), 0)
    groups = rows // 32

    def scan(i, after):
        for part in range(4):
            at = pl.ds(pl.multiple_of((groups - 1 - i) * 32 + (3 - part) * 8, 8), 8)
            a, gs = step_buf[at], g_state[at]
            b = a * gs
            for shift in (1, 2, 4):
                inside = row < 8 - shift
                b = b + a * jnp.where(inside, pltpu.roll(b, 8 - shift, 0), 0.0)
                a = a * jnp.where(inside, pltpu.roll(a, 8 - shift, 0), 1.0)
            e = a * after + b
            g_state[at] = gs + jnp.where(row < 7, pltpu.roll(e, 7, 0), after)
            after = jnp.broadcast_to(e[0:1], (8, channels))
        return after

    carry[...] = lax.fori_loop(0, groups, scan, carry[...])

    def fold(x):
        return jnp.sum(x.reshape(tile // 8, 8, channels), axis=0)

    def second(i):
        at = span(i, tile)
        window = hist_s[pl.ds(pl.multiple_of(i * tile, tile), tile + 8)]
        before = window[7 : tile + 7]
        g, r, k = g_state[at], recall[at], ingate[at]
        c = conv_low[at].astype(F32)
        step, root = step_buf[at], root_buf[at]
        kc = k * c
        g_log = g * (before * step - kc * (step * step) / root)
        slow = -8.0 * r
        sums[7] += fold(g_log * slow)
        low_r = (g_log * (slow * decay[...][None]) * (1.0 - r)).astype(BF16)
        low_i = (g * root * kc * (1.0 - k)).astype(BF16)
        pre_r[at] = low_r
        pre_i[at] = low_i
        sums[5] += fold(low_r.astype(F32))
        sums[6] += fold(low_i.astype(F32))
        g_conv[at] = g * root * k

    loop(rows // tile, second)
    low_r, low_i, low_c = pre_r[...], pre_i[...], conv_low[...]
    g_gates[0] += dot_tn(low_c, low_r)
    g_gates[1] += dot_tn(low_c, low_i)
    g_conv[0:rows] += dot_nt(low_r, gate_w[0]) + dot_nt(low_i, gate_w[1])

    def third(i):
        at = span(i, tile)
        start = pl.multiple_of(i * tile, tile)
        window = g_conv[pl.ds(start, tile + 8)]
        value = conv[0:1] * window[0:tile]
        for k in (1, 2, 3):
            value = value + conv[k : k + 1] * window[k : tile + k]
        g_recur[at] = value.astype(BF16)
        past = hist_u[pl.ds(start, tile + 8)]
        gc = window[0:tile]
        for k in range(4):
            sums[k] += fold(gc * past[8 - k : tile + 8 - k])
        sums[4] += fold(gc)

    loop(rows // tile, third)

    @pl.when(jnp.logical_and(sequence == pl.num_programs(0) - 1, back == last))
    def _():
        small[...] = jnp.sum(sums[...], axis=1)


def recur_back(
    resets, g_mix, branch, states, u, conv_low, recall, ingate, init_state, init_conv, conv, gate_w, decay, narrow_in
):
    total, channels = u.shape
    sequences = init_state.shape[0]
    length = total // sequences
    rows = tile_of(length, 256)
    chunks = length // rows
    extra_rows = narrow_in.shape[0] // (sequences * chunks)
    extra = pl.BlockSpec((extra_rows, narrow_in.shape[1]), lambda s, c: (s * chunks + c, 0))
    eights = rows // 8

    def at(s, c):
        return (s * chunks + chunks - 1 - c, 0)

    def earlier(s, c):
        return (jnp.maximum((s * chunks + chunks - 1 - c) * eights - 1, 0), 0)

    block = pl.BlockSpec((rows, channels), at)
    before = pl.BlockSpec((8, channels), earlier)

    def whole(x):
        return pl.BlockSpec(x.shape, lambda s, c: (0,) * x.ndim)

    wide = pltpu.VMEM((rows, channels), F32)
    narrow = pltpu.VMEM((rows, channels), BF16)
    long = pltpu.VMEM((rows + 8, channels), F32)
    return pl.pallas_call(
        recur_back_kernel,
        grid=(sequences, chunks),
        out_shape=(
            shape(total, channels, dtype=BF16),
            shape(total, channels, dtype=BF16),
            shape(8, channels),
            shape(2, channels, channels),
            shape(*narrow_in.shape),
        ),
        in_specs=[
            pl.BlockSpec(memory_space=pltpu.SMEM),
            block, block, block, before, block, before, block, block, block,
            whole(init_state), whole(init_conv), whole(conv), whole(gate_w), whole(decay), extra,
        ],
        out_specs=(
            block,
            block,
            pl.BlockSpec((8, channels), lambda s, c: (0, 0)),
            pl.BlockSpec((2, channels, channels), lambda s, c: (0, 0, 0)),
            extra,
        ),
        scratch_shapes=[
            wide, wide, wide, long, narrow, narrow,
            pltpu.VMEM((8, channels), F32), long, long,
            pltpu.VMEM((8, 8, channels), F32),
        ],
        compiler_params=pltpu.CompilerParams(vmem_limit_bytes=VMEM_LIMIT),
        name="recur_back",
    )(
        resets, g_mix, branch, states, states, u, u, conv_low, recall, ingate, init_state, init_conv,
        conv, gate_w, decay, narrow_in,
    )


def input_back_kernel(
    n, copies, arrive, g_recur, g_branch, w_in, w_br, normed, tokens, g_residual, gain, second_gain, g_gates, small,
    input_grad, in_out, br_out, gates_out, conv_out, bias_out, decay_out, first_out, second_out,
    gain_row, gain_parts, gain_in, gain_sum, gain_dp, gain_sent, gain_came, gain_dp_sent, gain_dp_came, *bufs
):
    g = Place(n)
    me = lax.axis_index("dp")
    rows, width = tokens.shape
    channels = w_in.shape[0]
    block_width, blocks = gates_out.shape[1], gates_out.shape[2]
    segment = width // (2 * copies)
    gain_width = width // n
    weights = Halving.over(me, copies, *bufs[:4])
    rest = Halving.over(me, copies, *bufs[4:8])
    padded = bufs[0].shape[3] // 2
    rest_rows = bufs[4].shape[3]

    def block(ref, t):
        return ref[span(t, rows)]

    def partial(t, cols):
        return dot(block(g_recur, t), w_in[:, cols]) + dot(block(g_branch, t), w_br[:, cols])

    scatter = Scatter(g, partial, tile_of(width, 512), bufs[8:])

    def gain_copy(t, slot):
        return g.copy(gain_parts.at[t], gain_in.at[slot], gain_sent.at[t], gain_came.at[slot], t)

    def gain_dp_copy(i, slot):
        return pltpu.make_async_remote_copy(
            src_ref=gain_sum,
            dst_ref=gain_dp.at[slot],
            send_sem=gain_dp_sent.at[i],
            recv_sem=gain_dp_came.at[slot],
            device_id={"dp": i},
            device_id_type=MESH,
        )

    def others(act):
        loop(n, lambda t: pl.when(t != g.t)(lambda: act(t)))

    def copies_of(act):
        loop(copies, lambda i: pl.when(i != me)(lambda: act(i)))

    barrier = pltpu.get_barrier_semaphore()
    others(
        lambda t: pl.semaphore_signal(barrier, inc=1, device_id={"tensor": t}, device_id_type=MESH)
    )
    copies_of(lambda i: pl.semaphore_signal(barrier, inc=1, device_id={"dp": i}, device_id_type=MESH))
    pl.semaphore_wait(barrier, n - 1 + copies - 1)

    arrive(0, 1, 2, 3)
    scatter.offers(g.nz - 1)

    def around(i):
        d = g.nz - 1 - i
        scatter.offers(d - 1)
        scatter.step(d)

    around(0)
    arrive(4, 9)

    data = bufs[0]

    def weigh(q):
        cols = span(q, 2 * segment)
        first = dot_tn(g_recur[...], normed[:, cols])
        second = dot_tn(g_branch[...], normed[:, cols])
        for half in (0, 1):
            index = 2 * q + half
            track, part = lax.div(index, copies), lax.rem(index, copies)
            for i, value in enumerate((first, second)):
                piece = value[:, half * segment : (half + 1) * segment].astype(BF16)
                data[track, part, 0, i * padded : i * padded + channels] = piece
                if padded > channels:
                    data[track, part, 0, i * padded + channels : (i + 1) * padded] = jnp.zeros(
                        (padded - channels, segment), BF16
                    )
        terms = jnp.sum(w_in[:, cols].astype(F32) * first + w_br[:, cols].astype(F32) * second, axis=0, keepdims=True)
        gain_row[0:1, cols] = terms

    loop(copies, weigh)
    gain_row[0:1] = gain_row[0:1] / gain[...].astype(F32)[None]
    weights.start()
    gain_row[1:2] = second_gain[...]
    gain_row[2:8] = jnp.zeros((6, width), F32)
    for t in range(n):
        gain_parts[t] = gain_row[:, t * gain_width : (t + 1) * gain_width]
    others(lambda t: gain_copy(t, g.t).start())
    gain_in[g.t] = gain_parts[g.t]

    flat = jnp.concatenate(
        [
            g_gates[0],
            g_gates[1],
            small[...],
            jnp.zeros((2 * copies * rest_rows - 2 * channels - 8, channels), F32),
        ],
        axis=0,
    ).astype(BF16)
    for i in range(2 * copies):
        bufs[4][i // copies, i % copies, 0] = flat[i * rest_rows : (i + 1) * rest_rows]
    rest.start()

    events = [lambda a=a, b=b: (a(), b()) for a, b in zip(weights.events(), rest.events())]
    for i in range(1, g.nz - 1):
        around(i)
        if events:
            events.pop(0)()
        if i == 1:
            others(lambda t: gain_copy(t, t).wait_recv())
            total = gain_in[0]
            for t in range(1, n):
                total = total + gain_in[t]
            gain_sum[...] = total
            copies_of(lambda i: gain_dp_copy(i, me).start())
            gain_dp[me] = total
    for event in events:
        event()
    scatter.last()
    arrive(5, 6)
    part = 32

    def rows_of(i):
        at = span(i, part)
        back, _ = norm_grad(tokens[at].astype(F32), gain[...].astype(F32)[None], scatter.acc[at])
        input_grad[at] = g_residual[at] + back

    loop(rows // part, rows_of)
    copies_of(lambda i: gain_dp_copy(i, i).wait_recv())
    total = gain_dp[0]
    for i in range(1, copies):
        total = total + gain_dp[i]
    first_out[...] = total[0]
    second_out[...] = total[1]
    rest.finish()
    flat = jnp.concatenate([bufs[6][i // copies, i % copies, 0].astype(F32) for i in range(2 * copies)], axis=0)
    for q in (0, 1):
        for i in range(blocks):
            start = q * channels + i * block_width
            gates_out[q, :, i] = flat[start : start + block_width, i * block_width : (i + 1) * block_width]
    conv_out[...] = flat[2 * channels : 2 * channels + 5]
    bias_out[...] = flat[2 * channels + 5 : 2 * channels + 7]
    decay_out[...] = flat[2 * channels + 7]
    weights.finish()
    for i in range(2 * copies):
        for q, out in enumerate((in_out, br_out)):
            out[:, i * segment : (i + 1) * segment] = bufs[2][
                i // copies, i % copies, 0, q * padded : q * padded + channels
            ]
    others(lambda t: gain_copy(t, t).wait_send())
    copies_of(lambda i: gain_dp_copy(i, i).wait_send())
    scatter.finish()


def up_to(extent, multiple):
    return (extent + multiple - 1) // multiple * multiple


def input_back(
    n, copies, g_recur, g_branch, w_in, w_br, normed, tokens, g_residual, gain, second_gain, g_gates, small, blocks
):
    rows, width = tokens.shape
    channels = w_in.shape[0]
    block = channels // blocks
    rest_rows = up_to((2 * channels + 8 + 2 * copies - 1) // (2 * copies), 16)
    gain_shape = (8, width // n)
    sems = pltpu.SemaphoreType.DMA
    inputs = (g_recur, g_branch, w_in, w_br, normed, tokens, g_residual, gain, second_gain, g_gates, small)
    which = (0, 1, 2, 3, 4, 9, 5, 6)
    specs, kept = fetched_specs(inputs, which)
    return pl.pallas_call(
        fetching(functools.partial(input_back_kernel, n, copies), which),
        out_shape=(shape(rows, width),)
        + (shape(channels, width, dtype=BF16),) * 2
        + (
            shape(2, block, blocks, block),
            shape(5, channels),
            shape(2, channels),
            shape(channels),
            shape(width // n),
            shape(width // n),
        ),
        in_specs=specs,
        out_specs=(VM,) * 9,
        scratch_shapes=[
            pltpu.VMEM((8, width), F32),
            pltpu.VMEM((n, *gain_shape), F32),
            pltpu.VMEM((n, *gain_shape), F32),
            pltpu.VMEM(gain_shape, F32),
            pltpu.VMEM((copies, *gain_shape), F32),
            sems((n,)),
            sems((n,)),
            sems((copies,)),
            sems((copies,)),
        ]
        + Halving.scratch(copies, 2 * up_to(channels, 16), width // (2 * copies))
        + Halving.scratch(copies, rest_rows, channels)
        + Scatter.scratch(n, rows, width)
        + kept,
        compiler_params=comm_params(6),
        cost_estimate=cost(8 * n * rows * width * channels),
        name="input_back",
    )(*inputs)


def widen_kernel(small, *refs):
    half = len(refs) // 2
    for q, (narrow, wide) in enumerate(zip(refs[:half], refs[half:])):

        def pass_on(narrow=narrow, wide=wide):
            wide[...] = narrow[...].reshape(wide.shape).astype(wide.dtype)

        if q < small:
            pl.when(pl.program_id(0) == 0)(pass_on)
        else:
            pass_on()


def widen(small, as_is, by_rows, by_columns, in_parts):
    steps = 8
    width = by_columns[0].shape[1]
    tile = width // steps
    per_part = in_parts.shape[2] // tile
    specs, outs = [], []

    def whole(x):
        return pl.BlockSpec(x.shape, lambda i: (0,) * x.ndim)

    for x in small:
        specs.append(whole(x))
        outs.append(shape(*x.shape))
    for x in as_is:
        specs.append(pl.BlockSpec((x.shape[0] // steps, x.shape[1]), lambda i: (i, 0)))
        outs.append(shape(*x.shape, dtype=x.dtype))
    for x in by_rows:
        specs.append(pl.BlockSpec((x.shape[0] // steps, x.shape[1]), lambda i: (i, 0)))
        outs.append(shape(*x.shape))
    for x in by_columns:
        specs.append(pl.BlockSpec((x.shape[0], tile), lambda i: (0, i)))
        outs.append(shape(*x.shape))
    last = pl.BlockSpec((1, in_parts.shape[1], tile), lambda i: (i // per_part, 0, i % per_part))
    outs.append(shape(in_parts.shape[1], width))
    wide = pl.BlockSpec((in_parts.shape[1], tile), lambda i: (0, i))
    return pl.pallas_call(
        functools.partial(widen_kernel, len(small)),
        grid=(steps,),
        out_shape=tuple(outs),
        in_specs=specs + [last],
        out_specs=tuple(specs) + (wide,),
        compiler_params=pltpu.CompilerParams(vmem_limit_bytes=VMEM_LIMIT),
        name="widen",
    )(*small, *as_is, *by_rows, *by_columns, in_parts)


def body(
    n,
    copies,
    tokens,
    cotangent,
    resets,
    init_state,
    init_conv,
    norm_gain,
    w_input,
    w_branch,
    conv_params,
    gate_weights,
    gate_bias,
    decay_rate,
    w_output,
    mlp_gain,
    w_gelu,
    w_linear,
    w_down,
):
    rows, width = tokens.shape
    total = rows * n
    channels = w_input.shape[1]
    blocks, block = gate_weights.shape[1], gate_weights.shape[2]
    before_conv = init_conv.transpose(1, 0, 2)
    gain_first, gain_second = norm_gain, mlp_gain
    gate_w = (gate_weights[:, :, :, None] * jnp.eye(blocks, dtype=BF16)[None, :, None, :, None]).reshape(
        2, channels, channels
    )
    w_in, w_br = w_input.T, w_branch.T

    def flat(x):
        return x.reshape(total, x.shape[-1])

    def blocked(x):
        return x.reshape(n, rows, x.shape[-1])

    normed, recur, branch, states, mixture, conv_low, recall, ingate, final_state, final_conv = project(
        n, tokens, gain_first, w_in, w_br, resets, init_state, before_conv, conv_params, gate_w, gate_bias, decay_rate
    )
    mixture = blocked(mixture)
    cot_full, residual, normed_mlp = mixer_out(n, mixture, w_output, cotangent, tokens, gain_second)
    hidden, grad_gelu, grad_linear, grad_down, g_residual, g_low, gain_second_grad = mlp(
        n, copies, normed_mlp, cot_full, w_gelu, w_linear, w_down, residual, gain_second
    )
    mlp_sums = lax.psum((grad_gelu, grad_linear), "dp")
    output, g_mixture, grad_output = down(n, copies, hidden, w_down, residual, g_low, w_output, mixture)
    g_recur, g_branch, small, g_gates, grad_down = recur_back(
        resets, flat(g_mixture), branch, states, recur, conv_low, recall, ingate, init_state, before_conv,
        conv_params, gate_w, decay_rate, grad_down,
    )
    mlp_sums, grad_output, small = lax.optimization_barrier((mlp_sums, grad_output, small))
    grad_output = lax.psum(grad_output, "dp")
    input_grad, grad_input, grad_branch, gates, g_conv, g_bias, g_decay, g_first_gain, g_second_gain = input_back(
        n, copies, g_recur, g_branch, w_in, w_br, flat(normed), tokens, g_residual, gain_first,
        gain_second_grad, g_gates, small, blocks,
    )
    (
        final_state, final_conv, gates, g_conv, g_bias, g_decay, g_first_gain, g_second_gain, output, input_grad,
        grad_gelu, grad_linear, grad_input, grad_branch, grad_output,
    ) = widen(
        (final_state, final_conv, gates, g_conv, g_bias, g_decay, g_first_gain, g_second_gain),
        (output, input_grad),
        mlp_sums,
        (grad_input, grad_branch),
        grad_output,
    )
    return (
        output,
        input_grad,
        final_state,
        final_conv.transpose(1, 0, 2),
        g_first_gain,
        grad_input.T,
        grad_branch.T,
        g_conv,
        gates.transpose(0, 2, 1, 3),
        g_bias,
        g_decay,
        grad_output,
        g_second_gain,
        grad_gelu,
        grad_linear,
        grad_down,
    )


def solution(mesh):
    in_specs = (
        P(("dp", "tensor"), None),
        P(("dp", "tensor"), None),
        P("dp"),
        P("dp", "tensor"),
        P("dp", None, "tensor"),
        P(),
        P(None, "tensor"),
        P(None, "tensor"),
        P(None, "tensor"),
        P(None, "tensor", None, None),
        P(None, "tensor"),
        P("tensor"),
        P("tensor", None),
        P(),
        P(None, "tensor"),
        P(None, "tensor"),
        P("tensor", None),
    )
    out_specs = (
        P(("dp", "tensor"), None),
        P(("dp", "tensor"), None),
        P("dp", "tensor"),
        P("dp", None, "tensor"),
        P("tensor"),
        P(None, "tensor"),
        P(None, "tensor"),
        P(None, "tensor"),
        P(None, "tensor", None, None),
        P(None, "tensor"),
        P("tensor"),
        P("tensor", None),
        P("tensor"),
        P(None, "tensor"),
        P(None, "tensor"),
        P("tensor", None),
    )
    return jax.shard_map(
        functools.partial(body, mesh.shape["tensor"], mesh.shape["dp"]),
        mesh=mesh,
        in_specs=in_specs,
        out_specs=out_specs,
        check_vma=False,
    )
```

```python
import functools

import jax
import jax.numpy as jnp
from jax import lax
from jax.experimental import pallas as pl
from jax.experimental.pallas import tpu as pltpu
from jax.sharding import PartitionSpec as P

EPSILON = 1e-06
KAPPA = 0.7978845608028654
CUBIC = 0.044715
PIECES = 2
STRIPS = 4
PARTS = 8
F32 = jnp.float32
BF16 = jnp.bfloat16
ANY = pl.BlockSpec(memory_space=pl.ANY)
VM = pl.BlockSpec(memory_space=pltpu.VMEM)
VMEM_LIMIT = 61 * 1024 * 1024
MESH = pl.DeviceIdType.MESH


def dot(a, b):
    return jnp.dot(a, b, preferred_element_type=F32)


def dot_nt(a, b):
    return lax.dot_general(a, b, (((1,), (1,)), ((), ())), preferred_element_type=F32)


def dot_tn(a, b):
    return lax.dot_general(a, b, (((0,), (0,)), ((), ())), preferred_element_type=F32)


def tile_of(extent, wanted):
    while extent % wanted:
        wanted //= 2
    return wanted


def span(i, size):
    return pl.ds(pl.multiple_of(i * size, size), size)


def loop(count, body):
    def step(i, carry):
        body(i)
        return carry

    lax.fori_loop(0, count, step, 0)


class Place:
    def __init__(self, n):
        self.n = n
        self.nz = n // 2
        self.t = lax.axis_index("tensor")
        self.c = lax.rem(self.t, 2)
        self.j = lax.div(self.t, 2)
        self.sib = self.t + 1 - 2 * self.c
        self.has_up = self.j < self.nz - 1
        self.has_down = self.j > 0

    def greet(self, partners=()):
        barrier = pltpu.get_barrier_semaphore()

        def signal(t):
            pl.semaphore_signal(barrier, inc=1, device_id={"tensor": t}, device_id_type=MESH)

        for i in partners:
            pl.semaphore_signal(barrier, inc=1, device_id={"dp": i}, device_id_type=MESH)

        signal(self.sib)
        pl.when(self.has_up)(lambda: signal(self.t + 2))
        pl.when(self.has_down)(lambda: signal(self.t - 2))
        pl.semaphore_wait(
            barrier,
            1 + len(partners) + self.has_up.astype(jnp.int32) + self.has_down.astype(jnp.int32),
        )

    def copy(self, src, dst, send, recv, t):
        return pltpu.make_async_remote_copy(
            src_ref=src,
            dst_ref=dst,
            send_sem=send,
            recv_sem=recv,
            device_id={"tensor": t},
            device_id_type=MESH,
        )


class Gather:
    def __init__(self, place, full, sent, came):
        self.place, self.full, self.sent, self.came = place, full, sent, came
        self.pieces = came.shape[1]
        self.size = full.shape[1] // self.pieces

    @staticmethod
    def scratch(n, rows, width):
        return [
            pltpu.VMEM((n, rows, width), BF16),
            pltpu.SemaphoreType.DMA((n, PIECES, 3)),
            pltpu.SemaphoreType.DMA((n, PIECES)),
        ]

    def copy(self, t, p, way, to):
        piece = self.full.at[t, pl.ds(p * self.size, self.size)]
        return self.place.copy(piece, piece, self.sent.at[t, p, way], self.came.at[t, p], to)

    def start(self):
        g = self.place
        for p in range(self.pieces):
            pl.when(g.has_up)(lambda: self.copy(g.t, p, 0, g.t + 2).start())
            pl.when(g.has_down)(lambda: self.copy(g.t, p, 1, g.t - 2).start())
        for p in range(self.pieces):
            self.copy(g.t, p, 2, g.sib).start()

    def forward(self, d, pieces=None):
        g = self.place
        for p in range(self.pieces) if pieces is None else pieces:

            @pl.when(g.j - d >= 0)
            def _():
                t = g.t - 2 * d
                self.copy(t, p, 0, g.sib).wait_recv()
                pl.when(g.has_up)(lambda: self.copy(t, p, 0, g.t + 2).start())
                self.copy(t, p, 2, g.sib).start()

            @pl.when(g.j + d < g.nz)
            def _():
                t = g.t + 2 * d
                self.copy(t, p, 1, g.sib).wait_recv()
                pl.when(g.has_down)(lambda: self.copy(t, p, 1, g.t - 2).start())
                self.copy(t, p, 2, g.sib).start()

    def each(self, d, use):
        g = self.place

        def visit(q):
            core, way = lax.div(q, 2), 2 * lax.rem(q, 2) - 1
            j = g.j + way * d
            there = jnp.logical_and(j >= 0, j < g.nz)

            @pl.when(jnp.logical_and(there, jnp.logical_or(d > 0, way > 0)))
            def _():
                t = 2 * j + lax.rem(g.c + core, 2)

                @pl.when(core > 0)
                def _():
                    for p in range(self.pieces):
                        self.copy(t, p, 2, g.sib).wait_recv()

                use(t)

        loop(4, visit)

    def finish(self):
        g = self.place

        def done(t):
            for p in range(self.pieces):
                self.copy(t, p, 2, g.sib).wait_send()

                @pl.when(jnp.logical_and(t <= g.t, g.has_up))
                def _():
                    self.copy(t, p, 0, g.sib).wait_send()

                @pl.when(jnp.logical_and(t >= g.t, g.has_down))
                def _():
                    self.copy(t, p, 1, g.sib).wait_send()

        loop(g.nz, lambda k: done(2 * k + g.c))


class Scatter:
    def __init__(self, place, partial, tile, bufs):
        self.place, self.partial, self.tile = place, partial, tile
        self.to_sib, self.from_sib, self.line, self.acc = bufs[:4]
        self.sib_send, self.sib_recv, self.line_send, self.line_recv = bufs[4:]
        self.out = self.from_sib
        self.tiles = self.acc.shape[1] // tile

    @staticmethod
    def scratch(n, rows, width):
        nz = n // 2
        return [
            pltpu.VMEM((nz, rows, width), BF16),
            pltpu.VMEM((nz, rows, width), BF16),
            pltpu.VMEM((nz + 1, rows, width), BF16),
            pltpu.VMEM((rows, width), F32),
            pltpu.SemaphoreType.DMA((nz,)),
            pltpu.SemaphoreType.DMA((nz,)),
            pltpu.SemaphoreType.DMA((nz, STRIPS)),
            pltpu.SemaphoreType.DMA((nz + 1, STRIPS)),
        ]

    def sib_copy(self, k):
        return self.place.copy(
            self.to_sib.at[k],
            self.from_sib.at[k],
            self.sib_send.at[k],
            self.sib_recv.at[k],
            self.place.sib,
        )

    def line_copy(self, k, slot, p, to):
        at = self.strip(p)
        return self.place.copy(
            self.out.at[k, at], self.line.at[slot, at], self.line_send.at[k, p], self.line_recv.at[slot, p], to
        )

    def strip(self, p):
        return span(p, self.acc.shape[0] // STRIPS)

    def offer(self, k):
        t = 2 * k + 1 - self.place.c

        def part(i):
            cols = span(i, self.tile)
            self.to_sib[k, :, cols] = self.partial(t, cols).astype(BF16)

        loop(self.tiles, part)
        self.sib_copy(k).start()

    def pair(self, k):
        self.sib_copy(k).wait_recv()
        t = 2 * k + self.place.c

        def part(i):
            cols = span(i, self.tile)
            self.acc[:, cols] = self.partial(t, cols) + self.from_sib[k, :, cols].astype(F32)

        loop(self.tiles, part)

    def offers(self, d):
        g = self.place

        def way_of(w):
            k = g.j + (1 - 2 * w) * d

            @pl.when(jnp.logical_and(jnp.logical_and(k >= 0, k < g.nz), jnp.logical_or(d > 0, w == 0)))
            def _():
                self.offer(k)

        loop(2, way_of)

    def step(self, d):
        g = self.place

        def way_of(w):
            sign = 1 - 2 * w
            k = g.j + sign * d

            @pl.when(jnp.logical_and(k >= 0, k < g.nz))
            def _():
                self.pair(k)
                upstream = g.j - sign
                more = jnp.logical_and(upstream >= 0, upstream < g.nz)

                slot = jnp.where(jnp.logical_and(d == 1, w == 1), g.nz, k)

                def pass_on(p):
                    at = self.strip(p)

                    @pl.when(more)
                    def _():
                        self.line_copy(k, k, p, g.sib).wait_recv()
                        self.out[k, at] = (self.acc[at] + self.line[k, at].astype(F32)).astype(BF16)

                    @pl.when(jnp.logical_not(more))
                    def _():
                        self.out[k, at] = self.acc[at].astype(BF16)

                    self.line_copy(k, slot, p, g.t + 2 * sign).start()

                loop(STRIPS, pass_on)

        loop(2, way_of)

    def last(self):
        g = self.place
        self.pair(g.j)

        def take(p):
            at = self.strip(p)

            @pl.when(g.has_down)
            def _():
                self.line_copy(g.j, g.j, p, g.sib).wait_recv()
                self.acc[at] += self.line[g.j, at].astype(F32)

            @pl.when(g.has_up)
            def _():
                self.line_copy(g.j, g.nz, p, g.sib).wait_recv()
                self.acc[at] += self.line[g.nz, at].astype(F32)

        loop(STRIPS, take)

    def finish(self):
        g = self.place

        def done(k):
            self.sib_copy(k).wait_send()
            pl.when(g.j != k)(
                lambda: loop(STRIPS, lambda p: self.line_copy(k, k, p, g.sib).wait_send())
            )

        loop(g.nz, done)


class Halving:
    def __init__(self, me, count, data, landed, final, sems):
        self.me, self.count = me, count
        self.data, self.landed, self.final = data, landed, final
        self.out_send, self.out_recv, self.back_send, self.back_recv = (sems.at[q] for q in range(4))
        self.bits = count.bit_length() - 1
        assert count == 1 << self.bits

    @staticmethod
    def scratch(count, rows, columns):
        return [
            pltpu.VMEM((2, count, 1, rows, columns), BF16),
            pltpu.VMEM((2, count - 1, 1, rows, columns), BF16),
            pltpu.VMEM((2, count, 1, rows, columns), BF16),
            pltpu.SemaphoreType.DMA((4, 2, count - 1)),
        ]

    @staticmethod
    def over(me, count, data, landed, final, sems):
        def at(ref):
            return lambda track, index: ref.at[track, index]

        return Halving(me, count, at(data), at(landed), at(final), sems)

    def partners(self):
        return [self.me + (1 - 2 * self.own(b)) * (1 << b) for b in range(self.bits)]

    def own(self, bit):
        return lax.rem(lax.div(self.me, 1 << bit), 2)

    def swaps(self, s):
        for track in (0, 1):
            order = [(i + track) % self.bits for i in range(self.bits)]
            bit = order[s]
            partner = self.me + (1 - 2 * self.own(bit)) * (1 << bit)
            fixed = sum(self.own(b) * (1 << b) for b in order[:s])
            for u in range(self.count >> (s + 1)):
                free = sum(((u >> i) & 1) << b for i, b in enumerate(order[s + 1 :]))
                slot = self.count - (self.count >> s) + u
                kept = fixed + free + self.own(bit) * (1 << bit)
                yield track, slot, partner, fixed + free + (1 - self.own(bit)) * (1 << bit), kept

    def out(self, track, slot, partner, given):
        return pltpu.make_async_remote_copy(
            src_ref=self.data(track, given),
            dst_ref=self.landed(track, slot),
            send_sem=self.out_send.at[track, slot],
            recv_sem=self.out_recv.at[track, slot],
            device_id={"dp": partner},
            device_id_type=MESH,
        )

    def back(self, track, slot, partner, segment):
        return pltpu.make_async_remote_copy(
            src_ref=self.final(track, segment),
            dst_ref=self.final(track, segment),
            send_sem=self.back_send.at[track, slot],
            recv_sem=self.back_recv.at[track, slot],
            device_id={"dp": partner},
            device_id_type=MESH,
        )

    def start(self, s=0):
        for track, slot, partner, given, _ in self.swaps(s):
            self.out(track, slot, partner, given).start()

    def turn(self, s):
        for track, slot, partner, given, kept in self.swaps(s):
            self.out(track, slot, partner, given).wait_recv()
            mine, theirs = self.data(track, kept), self.landed(track, slot)
            result = self.final(track, kept) if s == self.bits - 1 else mine
            blocks, rows, _ = mine.shape
            tile = tile_of(rows, 32)

            def add(r):
                block, at = lax.div(r, rows // tile), span(lax.rem(r, rows // tile), tile)
                result[block, at] = (mine[block, at].astype(F32) + theirs[block, at].astype(F32)).astype(BF16)

            loop(blocks * (rows // tile), add)
        if s < self.bits - 1:
            self.start(s + 1)
        else:
            self.start_back(s)

    def start_back(self, s):
        for track, slot, partner, _, kept in self.swaps(s):
            self.back(track, slot, partner, kept).start()

    def turn_back(self, s):
        for track, slot, partner, given, _ in self.swaps(s):
            self.back(track, slot, partner, given).wait_recv()
        if s > 0:
            self.start_back(s - 1)

    def events(self):
        steps = [functools.partial(self.turn, s) for s in range(self.bits)]
        return steps + [functools.partial(self.turn_back, s) for s in range(self.bits - 1, 0, -1)]

    def finish(self):
        self.turn_back(0)
        for s in range(self.bits):
            for track, slot, partner, given, kept in self.swaps(s):
                self.out(track, slot, partner, given).wait_send()
                self.back(track, slot, partner, kept).wait_send()


def fetching(kernel, which):
    def wrapped(*refs):
        refs = list(refs)
        sems = refs.pop()
        kept = refs[len(refs) - len(which) :]
        del refs[len(refs) - len(which) :]
        copies = {}
        for q, i in enumerate(which):
            copies[i] = pltpu.make_async_copy(refs[i], kept[q], sems.at[q])
            copies[i].start()
            refs[i] = kept[q]

        def arrive(*wanted):
            for i in wanted:
                copies[i].wait()

        return kernel(arrive, *refs)

    return wrapped


def fetched_specs(inputs, which, plain=()):
    specs = [ANY if i in which or i in plain else VM for i in range(len(inputs))]
    scratch = [pltpu.VMEM(inputs[i].shape, inputs[i].dtype) for i in which]
    return specs, scratch + [pltpu.SemaphoreType.DMA((len(which),))]


def comm_params(collective_id):
    return pltpu.CompilerParams(
        collective_id=collective_id, has_side_effects=True, vmem_limit_bytes=VMEM_LIMIT
    )


def cost(flops):
    return pl.CostEstimate(flops=int(flops), bytes_accessed=200_000_000, transcendentals=0)


def shape(*dims, dtype=F32):
    return jax.ShapeDtypeStruct(dims, dtype)


def inv_rms(values):
    return lax.rsqrt(jnp.mean(values * values, axis=-1, keepdims=True) + EPSILON)


def norm_grad(values, gain, gradient):
    inv = inv_rms(values)
    unit = values * inv
    scaled = gradient * gain
    centred = jnp.mean(scaled * unit, axis=-1, keepdims=True)
    return inv * (scaled - unit * centred), gradient * unit


def sigmoid(v):
    return 1.0 / (1.0 + jnp.exp(-v))


def gelu_parts(v):
    square = v * v
    bend = jnp.tanh(KAPPA * v * (1.0 + CUBIC * square))
    half = 0.5 * (1.0 + bend)
    slope = half + 0.5 * v * (1.0 - bend * bend) * (KAPPA * (1.0 + 3.0 * CUBIC * square))
    return v * half, slope


def one_minus_square(log_decay, decay):
    m = -2.0 * log_decay
    series = m * (
        1.0 - m * (1 / 2) * (1.0 - m * (1 / 3) * (1.0 - m * (1 / 4) * (1.0 - m * (1 / 5) * (1.0 - m * (1 / 6)))))
    )
    return jnp.where(m < 0.35, series, 1.0 - decay * decay)


def starts(reset, here, init_state, init_conv, state, hist):
    keep = (1 - reset).astype(F32)
    state[...] = jnp.broadcast_to(init_state[here] * keep, state.shape)
    before = [init_conv[q, here] * keep for q in range(3)]
    hist[0:8] = jnp.concatenate([jnp.zeros((5, hist.shape[1]), F32)] + before, axis=0)


def recur_chunk(base, u, branch, conv, gate_w, bias, decay, kept, hist, decay_buf, drive_buf, carry):
    states, mixture, conv_low, recall, ingate = kept
    rows, channels = decay_buf.shape
    tile = 32

    def rows_of(i, size):
        return pl.ds(pl.multiple_of(base + i * size, size), size)

    whole = rows_of(0, rows)
    hist[8:] = u[whole]

    def convolve(i):
        window = hist[pl.ds(pl.multiple_of(i * tile, tile), tile + 8)]
        value = conv[4:5] + conv[0:1] * window[8:] + conv[1:2] * window[7 : tile + 7]
        value = value + conv[2:3] * window[6 : tile + 6] + conv[3:4] * window[5 : tile + 5]
        conv_low[rows_of(i, tile)] = value.astype(BF16)

    loop(rows // tile, convolve)
    hist[0:8] = hist[rows : rows + 8]
    low = conv_low[whole]
    recall[whole] = dot(low, gate_w[0])
    ingate[whole] = dot(low, gate_w[1])

    def gates(i):
        at, here = rows_of(i, tile), span(i, tile)
        r = sigmoid(recall[at] + bias[0:1])
        k = sigmoid(ingate[at] + bias[1:2])
        recall[at] = r
        ingate[at] = k
        log_decay = -8.0 * r * decay[...][None]
        step = jnp.exp(log_decay)
        decay_buf[here] = step
        drive_buf[here] = jnp.sqrt(one_minus_square(log_decay, step)) * k * conv_low[at].astype(F32)

    loop(rows // tile, gates)
    row = lax.broadcasted_iota(jnp.int32, (8, channels), 0)

    def scan(i, before):
        for part in range(4):
            at = pl.ds(pl.multiple_of(i * 32 + part * 8, 8), 8)
            a, b = decay_buf[at], drive_buf[at]
            for shift in (1, 2, 4):
                inside = row >= shift
                b = b + a * jnp.where(inside, pltpu.roll(b, shift, 0), 0.0)
                a = a * jnp.where(inside, pltpu.roll(a, shift, 0), 1.0)
            h = a * before + b
            states[pl.ds(pl.multiple_of(base + i * 32 + part * 8, 8), 8)] = h
            before = jnp.broadcast_to(h[7:8], (8, channels))
        return before

    carry[...] = lax.fori_loop(0, rows // 32, scan, carry[...])

    def mix(i):
        at = rows_of(i, tile)
        value, _ = gelu_parts(branch[at])
        mixture[at] = (states[at] * value).astype(BF16)

    loop(rows // tile, mix)


def project_kernel(
    n, arrive, tokens, gain, w_in, w_br, resets, init_state, init_conv, conv, gate_w, bias, decay,
    normed, recur, branch, states, mixture, conv_low, recall, ingate, final_state, final_conv,
    full, sent, came, held_a, held_b, kept_s, kept_m, kept_c, kept_r, kept_i,
    hist, decay_buf, drive_buf, carry, saved, written,
):
    g = Place(n)
    gather = Gather(g, full, sent, came)
    rows = full.shape[1]
    part = 64

    def normalize(i):
        at = span(i, part)
        values = tokens[at].astype(F32)
        full[g.t, at] = (values * inv_rms(values) * gain[...].astype(F32)[None]).astype(BF16)

    loop(rows // part, normalize)
    g.greet()
    gather.start()
    arrive(2, 3)

    def out(t):
        return pltpu.make_async_copy(full.at[t], normed.at[t], saved.at[t])

    def use(t):
        out(t).start()
        at = span(t, rows)
        held_a[at] = dot_nt(full[t], w_in[...])
        held_b[at] = dot_nt(full[t], w_br[...])

    kept = (kept_s, kept_m, kept_c, kept_r, kept_i)
    pairs = ((held_a, recur), (held_b, branch)) + tuple(zip(kept, (states, mixture, conv_low, recall, ingate)))
    sequences = init_state.shape[0]
    length = n * rows // sequences
    size = decay_buf.shape[0]
    chunks = length // size

    def leave(c, act):
        at = span(c, size)
        for q, (held, target) in enumerate(pairs):
            act(pltpu.make_async_copy(held.at[at], target.at[at], written.at[c, q]))

    def sequence(s):
        here = pl.ds(s, 1)
        starts(resets[s], here, init_state, init_conv, carry, hist)

        def chunk(c):
            index = s * chunks + c
            base = index * size
            recur_chunk(base, held_a, held_b, conv, gate_w, bias, decay, kept, hist, decay_buf, drive_buf, carry)
            leave(index, lambda copy: copy.start())

        loop(chunks, chunk)
        final_state[here] = carry[0:1]
        for q in range(3):
            final_conv[q, here] = hist[5 + q : 6 + q]

    def step(d):
        pl.when(d > 0)(lambda: gather.forward(d))
        gather.each(d, use)

        def whole(s):
            first = lax.div(s * length, 2 * rows)
            last = lax.div((s + 1) * length - 1, 2 * rows)
            pl.when(jnp.maximum(jnp.abs(first - g.j), jnp.abs(last - g.j)) == d)(lambda: sequence(s))

        loop(sequences, whole)

    loop(g.nz, step)
    loop(n, lambda t: out(t).wait())
    loop(sequences * chunks, lambda c: leave(c, lambda copy: copy.wait()))
    gather.finish()


def project(n, tokens, gain, w_in, w_br, resets, init_state, init_conv, conv, gate_w, bias, decay):
    rows, width = tokens.shape
    channels = w_in.shape[0]
    sequences = init_state.shape[0]
    total = n * rows
    size = tile_of(total // sequences, 256)
    inputs = (tokens, gain, w_in, w_br, resets, init_state, init_conv, conv, gate_w, bias, decay)
    specs, kept = fetched_specs(inputs, (2, 3))
    specs[4] = pl.BlockSpec(memory_space=pltpu.SMEM)
    wide, narrow = (total, channels), pltpu.VMEM((total, channels), BF16)
    return pl.pallas_call(
        fetching(functools.partial(project_kernel, n), (2, 3)),
        out_shape=(
            shape(n, rows, width, dtype=BF16),
            shape(*wide),
            shape(*wide),
            shape(*wide),
            shape(*wide, dtype=BF16),
            shape(*wide, dtype=BF16),
            shape(*wide),
            shape(*wide),
            shape(sequences, channels),
            shape(3, sequences, channels),
        ),
        in_specs=specs,
        out_specs=(ANY,) * 8 + (VM,) * 2,
        scratch_shapes=Gather.scratch(n, rows, width)
        + [pltpu.VMEM(wide, F32)] * 3
        + [narrow] * 2
        + [pltpu.VMEM(wide, F32)] * 2
        + [
            pltpu.VMEM((size + 8, channels), F32),
            pltpu.VMEM((size, channels), F32),
            pltpu.VMEM((size, channels), F32),
            pltpu.VMEM((8, channels), F32),
            pltpu.SemaphoreType.DMA((n,)),
            pltpu.SemaphoreType.DMA((total // size, 7)),
        ]
        + kept,
        compiler_params=comm_params(1),
        cost_estimate=cost(4 * n * rows * width * channels),
        name="project",
    )(*inputs)


def mixer_out_kernel(
    n, arrive, mixture, w_output, cotangent, tokens, gain, cot_full, residual, normed,
    full, sent, came, saved, *bufs
):
    g = Place(n)
    gather = Gather(g, full, sent, came)
    scatter = Scatter(g, lambda t, cols: dot(mixture[t], w_output[:, cols]), tile_of(residual.shape[1], 512), bufs)
    first = pltpu.make_async_copy(cotangent, full.at[g.t], saved.at[0])
    first.start()
    g.greet()
    first.wait()
    gather.start()
    arrive(0, 1)

    def use(t):
        pltpu.make_async_copy(full.at[t], cot_full.at[t], saved.at[t]).start()

    scatter.offers(g.nz - 1)

    def around(i):
        d = g.nz - 1 - i
        scatter.offers(d - 1)
        scatter.step(d)
        gather.each(i, use)
        gather.forward(i + 1)

    loop(g.nz - 1, around)
    scatter.last()
    arrive(3)
    part = 64

    def rows_of(i):
        at = span(i, part)
        values = scatter.acc[at] + tokens[at].astype(F32)
        residual[at] = values
        normed[at] = (values * inv_rms(values) * gain[...].astype(F32)[None]).astype(BF16)

    loop(residual.shape[0] // part, rows_of)
    gather.each(g.nz - 1, use)
    loop(n, lambda t: pltpu.make_async_copy(full.at[t], cot_full.at[t], saved.at[t]).wait())
    scatter.finish()
    gather.finish()


def mixer_out(n, mixture, w_output, cotangent, tokens, gain):
    rows, width = tokens.shape
    inputs, which = (mixture, w_output, cotangent, tokens, gain), (0, 1, 3)
    specs, kept = fetched_specs(inputs, which, (2,))
    return pl.pallas_call(
        fetching(functools.partial(mixer_out_kernel, n), which),
        out_shape=(
            shape(n, rows, width, dtype=BF16),
            shape(rows, width),
            shape(rows, width, dtype=BF16),
        ),
        in_specs=specs,
        out_specs=(ANY, VM, VM),
        scratch_shapes=Gather.scratch(n, rows, width)
        + [pltpu.SemaphoreType.DMA((n,))]
        + Scatter.scratch(n, rows, width)
        + kept,
        compiler_params=comm_params(2),
        cost_estimate=cost(2 * n * rows * width * mixture.shape[-1]),
        name="mixer_out",
    )(*inputs)


def mlp_kernel(
    n, copies, arrive, normed, cot_full, w_gelu, w_linear, w_down, residual, gain,
    hidden, grad_gelu, grad_linear, grad_down, g_residual, g_low, g_gain,
    full, sent, came, cot, keep_h, keep_f, keep_s, acc_g, acc_l, acc_d,
    to_sib, sums, line, acc, landed, swap_sems, saved, fetched, drained, sib_sent, sib_came, line_sent, line_came,
):
    g = Place(n)
    gather = Gather(g, full, sent, came)
    columns = w_gelu.shape[1]
    rows, width = acc.shape
    tile = tile_of(columns, 256)
    wide = tile_of(width, 1024)
    strip = rows // PARTS
    me = lax.axis_index("dp")
    start = pltpu.make_async_copy(normed, full.at[g.t], saved.at[0])
    start.start()
    part_width = width // (2 * copies)
    depth = columns // rows

    def segment(track, index):
        return pl.ds(pl.multiple_of((track * copies + index) * part_width, part_width), part_width)

    swap = Halving(
        me,
        copies,
        lambda track, index: full.at[0:depth, :, segment(track, index)],
        lambda track, slot: landed.at[track, slot],
        lambda track, index: full.at[depth : 2 * depth, :, segment(track, index)],
        swap_sems,
    )
    def fetch(t, q):
        return pltpu.make_async_copy(cot_full.at[t], cot.at[q], fetched.at[q])

    g.greet(swap.partners())
    start.wait()
    gather.start()
    fetch(2 * g.j, 0).start()
    fetch(2 * g.j + 1, 1).start()
    arrive(2, 3, 4)
    acc_g[...] = jnp.zeros_like(acc_g)
    acc_l[...] = jnp.zeros_like(acc_l)
    acc_d[...] = jnp.zeros_like(acc_d)

    def save(t, q):
        return pltpu.make_async_copy(keep_h.at[q], hidden.at[t], saved.at[q])

    def layer(t, q):
        fetch(t, q).wait()

        def part(i):
            cols = span(i, tile)
            first = dot(full[t], w_gelu[:, cols])
            second = dot(full[t], w_linear[:, cols])
            back = dot_nt(cot[q], w_down[cols])
            value, slope = gelu_parts(first)
            keep_h[q, :, cols] = (value * second).astype(BF16)
            keep_f[q, :, cols] = (back * second * slope).astype(BF16)
            keep_s[q, :, cols] = (back * value).astype(BF16)

        loop(columns // tile, part)
        save(t, q).start()

    def partial(q, cols):
        return dot_nt(keep_f[q], w_gelu[cols]) + dot_nt(keep_s[q], w_linear[cols])

    def sib_copy(k):
        return g.copy(to_sib, sums.at[k], sib_sent, sib_came.at[k], g.sib)

    def line_copy(k, slot, p, to):
        at = pl.ds(pl.multiple_of(p * strip, strip), strip)
        return g.copy(
            sums.at[k, at], line.at[slot, at], line_sent.at[k, p], line_came.at[slot, p], to
        )

    def chip(d, way):
        k = g.j + way * d
        mine, its = g.c, 1 - g.c
        own, other = 2 * k + mine, 2 * k + its
        for p in range(gather.pieces):
            gather.copy(other, p, 2, g.sib).wait_recv()
        layer(other, its)

        def offer(i):
            cols = span(i, width)
            to_sib[:, cols] = partial(its, cols).astype(BF16)

        loop(1, offer)
        sib_copy(k).start()
        layer(own, mine)
        sib_copy(k).wait()

        @pl.when(d == 0)
        def _():
            def part(i):
                cols = span(i, width)
                acc[:, cols] = partial(mine, cols) + sums[k, :, cols].astype(F32)

            loop(1, part)

        @pl.when(d > 0)
        def _():
            def part(i):
                cols = span(i, width)
                sums[k, :, cols] = (partial(mine, cols) + sums[k, :, cols].astype(F32)).astype(BF16)

            loop(1, part)
            first = jnp.logical_or(
                jnp.logical_and(way > 0, jnp.logical_not(g.has_down)),
                jnp.logical_and(way < 0, jnp.logical_not(g.has_up)),
            )

            @pl.when(first)
            def _():
                slot = jnp.where(jnp.logical_and(way < 0, d == 1), g.nz, k)
                for p in range(PARTS):
                    line_copy(k, slot, p, g.t + 2 * way).start()

        def part(i):
            at = span(i, wide)
            both = full[pl.ds(2 * k, 2), :, at].reshape(2 * rows, wide)
            acc_g[at] += dot_tn(both, keep_f[...].reshape(2 * rows, columns))
            acc_l[at] += dot_tn(both, keep_s[...].reshape(2 * rows, columns))
            acc_d[:, at] += dot_tn(
                keep_h[...].reshape(2 * rows, columns), cot[:, :, at].reshape(2 * rows, wide)
            )

        loop(width // wide, part)
        both_ways = jnp.logical_and(g.j + d < g.nz, g.j - d >= 0)
        again = jnp.logical_and(both_ways, jnp.logical_and(way > 0, d > 0))
        later = jnp.where(g.j + d + 1 < g.nz, g.j + d + 1, g.j - d - 1)
        following = jnp.where(again, g.j - d, later)

        @pl.when(following >= 0)
        def _():
            fetch(2 * following, 0).start()
            fetch(2 * following + 1, 1).start()

        save(other, its).wait()
        save(own, mine).wait()

    def relay(m, events=()):
        def take(k, slot, sign, p):
            at = pl.ds(pl.multiple_of(p * strip, strip), strip)
            line_copy(k, slot, p, g.sib).wait_recv()

            @pl.when(k == g.j)
            def _():
                acc[at] += line[slot, at].astype(F32)

            @pl.when(k != g.j)
            def _():
                sums[k, at] = (sums[k, at].astype(F32) + line[slot, at].astype(F32)).astype(BF16)
                there = jnp.where(jnp.logical_and(sign < 0, k == g.j - 1), g.nz, k)
                line_copy(k, there, p, g.t + 2 * sign).start()

        def rise(p):
            pl.when(jnp.logical_and(g.has_down, m >= g.j))(lambda: take(m, m, 1, p))

        def fall(p):
            k = g.nz - 1 - m
            pl.when(jnp.logical_and(g.has_up, k <= g.j))(
                lambda: take(k, jnp.where(k == g.j, g.nz, k), -1, p)
            )

        lower = 2 * g.j < g.nz

        def strips(i):
            @pl.when(i < PARTS)
            def _():
                pl.when(lower)(lambda: rise(i))
                pl.when(jnp.logical_not(lower))(lambda: fall(i))

            @pl.when(i > 0)
            def _():
                pl.when(lower)(lambda: fall(i - 1))
                pl.when(jnp.logical_not(lower))(lambda: rise(i - 1))

        middle = jnp.logical_and(g.has_up, g.has_down)
        for event in events:
            pl.when(jnp.logical_not(middle))(event)

        def between(i):
            strips(i)
            for q, event in enumerate(events):
                pl.when(jnp.logical_and(middle, i == min(2 * q + 2, PARTS)))(event)

        loop(PARTS + 1, between)

    def cores(d):
        up, down = g.j + d < g.nz, g.j - d >= 0

        def way_of(w):
            both = jnp.logical_and(up, down)
            way = jnp.where(jnp.logical_and(w == 0, up), 1, -1)
            wanted = jnp.where(w == 0, jnp.logical_or(up, down), jnp.logical_and(both, d > 0))
            pl.when(wanted)(lambda: chip(d, way))

            @pl.when(d < g.nz - 1)
            def _():
                for p in range(gather.pieces):
                    pl.when(w == min(p, 1))(lambda: gather.forward(d + 1, (p,)))

        loop(2, way_of)

    def step(d):
        @pl.when(d < g.nz)
        def _():
            cores(d)

        @pl.when(d == g.nz - 1)
        def _():
            gather.finish()
            for i in range(depth):
                full[i] = acc_d[pl.ds(i * rows, rows)].astype(BF16)
            swap.start()

        pl.when(d > 1)(lambda: relay(d - 1))

    loop(g.nz, step)

    stages = [held.at[q] for held in (keep_h, keep_f, keep_s) for q in (0, 1)]
    leaving = []

    def leave(i, value, out):
        slot = i % len(stages)
        if len(leaving) >= len(stages):
            leaving[i - len(stages)].wait()
        stages[slot][...] = value.astype(BF16)
        copy = pltpu.make_async_copy(stages[slot], out, drained.at[slot])
        copy.start()
        leaving.append(copy)

    for i in range(width // rows):
        at = pl.ds(i * rows, rows)
        leave(2 * i, acc_g[at], grad_gelu.at[at])
        leave(2 * i + 1, acc_l[at], grad_linear.at[at])
    events = swap.events()
    events.pop(0)()
    relay(g.nz - 1, events)
    own = pltpu.make_async_copy(cot_full.at[g.t], cot.at[0], fetched.at[0])
    own.start()
    own.wait()
    arrive(5)
    lines = 32
    g_gain[...] = jnp.zeros_like(g_gain)

    def rows_of(i):
        at = span(i, lines)
        back, terms = norm_grad(residual[at], gain[...].astype(F32)[None], acc[at])
        value = cot[0, at].astype(F32) + back
        acc[at] = value
        cot[1, at] = value.astype(BF16)
        g_gain[...] += jnp.sum(terms, axis=0, keepdims=True)

    loop(rows // lines, rows_of)
    last = [
        pltpu.make_async_copy(acc, g_residual, saved.at[0]),
        pltpu.make_async_copy(cot.at[1], g_low, saved.at[1]),
    ]
    swap.finish()
    for i in range(depth):
        at = pl.ds(i * rows, rows)
        last.append(pltpu.make_async_copy(full.at[depth + i], grad_down.at[at], drained.at[len(stages) + i]))
    for copy in last:
        copy.start()
    for copy in leaving[-len(stages) :] + last:
        copy.wait()

    def done(k):
        @pl.when(k != g.j)
        def _():
            for p in range(PARTS):
                line_copy(k, k, p, g.sib).wait_send()

    loop(g.nz, done)


def mlp(n, copies, normed, cot_full, w_gelu, w_linear, w_down, residual, gain):
    rows, width = normed.shape
    columns = w_gelu.shape[1]
    kept = pltpu.VMEM((2, rows, columns), BF16)
    sems = pltpu.SemaphoreType.DMA
    inputs, which = (normed, cot_full, w_gelu, w_linear, w_down, residual, gain), (2, 3, 4, 5)
    specs, held = fetched_specs(inputs, which, (0, 1))
    return pl.pallas_call(
        fetching(functools.partial(mlp_kernel, n, copies), which),
        out_shape=(shape(n, rows, columns, dtype=BF16),)
        + (shape(width, columns, dtype=BF16),) * 2
        + (
            shape(columns, width, dtype=BF16),
            shape(rows, width),
            shape(rows, width, dtype=BF16),
            shape(1, width),
        ),
        in_specs=specs,
        out_specs=(ANY,) * 6 + (VM,),
        scratch_shapes=Gather.scratch(n, rows, width)
        + [pltpu.VMEM((2, rows, width), BF16)]
        + [kept] * 3
        + [pltpu.VMEM((width, columns), F32)] * 2
        + [
            pltpu.VMEM((columns, width), F32),
            pltpu.VMEM((rows, width), BF16),
            pltpu.VMEM((n // 2, rows, width), BF16),
            pltpu.VMEM((n // 2 + 1, rows, width), BF16),
            pltpu.VMEM((rows, width), F32),
            pltpu.VMEM((2, copies - 1, columns // rows, rows, width // (2 * copies)), BF16),
            sems((4, 2, copies - 1)),
            sems((2,)),
            sems((2,)),
            sems((6 + columns // rows,)),
            sems,
            sems((n // 2,)),
            sems((n // 2, PARTS)),
            sems((n // 2 + 1, PARTS)),
        ]
        + held,
        compiler_params=comm_params(3),
        cost_estimate=cost(16 * n * rows * width * columns),
        name="mlp",
    )(*inputs)


def down_kernel(
    n, copies, arrive, hidden, w_down, residual, g_low, w_output, mixture, output, g_mixture, grad_output,
    full, sent, came, acc_o, start_sem, *bufs
):
    g = Place(n)
    gather = Gather(g, full, sent, came)
    width = residual.shape[1]
    wide = tile_of(width, 512)
    scatter = Scatter(g, lambda t, cols: dot(hidden[t], w_down[:, cols]), wide, bufs)
    first = pltpu.make_async_copy(g_low, full.at[g.t], start_sem)
    first.start()
    g.greet()
    first.wait()

    def use(t):
        g_mixture[t] = dot_nt(full[t], w_output[...])

        def part(i):
            at = span(i, wide)
            acc_o[:, at] += dot_tn(mixture[t], full[t, :, at])

        loop(width // wide, part)

    gather.start()
    acc_o[...] = jnp.zeros_like(acc_o)
    arrive(0, 1)
    scatter.offers(g.nz - 1)
    arrive(4, 5)

    def around(i):
        d = g.nz - 1 - i
        scatter.offers(d - 1)
        scatter.step(d)
        gather.each(i, use)
        gather.forward(i + 1)

    loop(g.nz - 1, around)
    gather.each(g.nz - 1, use)
    for i in range(copies):
        part = width // copies
        grad_output[i] = acc_o[:, i * part : (i + 1) * part].astype(BF16)
    scatter.last()
    arrive(2)
    output[...] = (scatter.acc[...] + residual[...]).astype(BF16)
    scatter.finish()
    gather.finish()


def down(n, copies, hidden, w_down, residual, g_low, w_output, mixture):
    rows, width = residual.shape
    channels = w_output.shape[0]
    inputs, which = (hidden, w_down, residual, g_low, w_output, mixture), (0, 1, 4, 5, 2)
    specs, kept = fetched_specs(inputs, which, (3,))
    return pl.pallas_call(
        fetching(functools.partial(down_kernel, n, copies), which),
        out_shape=(
            shape(rows, width, dtype=BF16),
            shape(n, rows, channels),
            shape(copies, channels, width // copies, dtype=BF16),
        ),
        in_specs=specs,
        out_specs=(VM,) * 3,
        scratch_shapes=Gather.scratch(n, rows, width)
        + [pltpu.VMEM((channels, width), F32), pltpu.SemaphoreType.DMA]
        + Scatter.scratch(n, rows, width)
        + kept,
        compiler_params=comm_params(5),
        cost_estimate=cost(2 * n * rows * width * (hidden.shape[-1] + 2 * channels)),
        name="down",
    )(*inputs)


def recur_back_kernel(
    resets, g_mix, branch, states, states_before, u, u_before, conv_low, recall, ingate, init_state, init_conv,
    conv, gate_w, decay, narrow_in,
    g_recur, g_branch, small, g_gates, wide_out,
    g_state, step_buf, root_buf, g_conv, pre_r, pre_i, carry, hist_s, hist_u, sums,
):
    sequence, back = pl.program_id(0), pl.program_id(1)
    last = pl.num_programs(1) - 1
    rows, channels = u.shape
    tile = 32
    wide_out[...] = narrow_in[...].astype(F32)

    @pl.when(jnp.logical_and(sequence == 0, back == 0))
    def _():
        sums[...] = jnp.zeros_like(sums)
        g_gates[...] = jnp.zeros_like(g_gates)

    @pl.when(back == 0)
    def _():
        carry[...] = jnp.zeros_like(carry)
        g_conv[rows : rows + 8] = jnp.zeros((8, channels), F32)

    @pl.when(back > 0)
    def _():
        g_conv[rows : rows + 8] = g_conv[0:8]

    @pl.when(back == last)
    def _():
        starts(
            resets[sequence], pl.ds(sequence, 1), init_state, init_conv, hist_s.at[0:8], hist_u
        )

    @pl.when(back < last)
    def _():
        hist_s[0:8] = states_before[...]
        hist_u[0:8] = u_before[...]

    hist_s[8:] = states[...]
    hist_u[8:] = u[...]

    def first(i):
        at = span(i, tile)
        value, slope = gelu_parts(branch[at])
        gm = g_mix[at]
        g_state[at] = gm * value
        g_branch[at] = (gm * states[at] * slope).astype(BF16)
        log_decay = -8.0 * recall[at] * decay[...][None]
        step = jnp.exp(log_decay)
        step_buf[at] = step
        root_buf[at] = jnp.sqrt(one_minus_square(log_decay, step))

    loop(rows // tile, first)
    row = lax.broadcasted_iota(jnp.int32, (8, channels), 0)
    groups = rows // 32

    def scan(i, after):
        for part in range(4):
            at = pl.ds(pl.multiple_of((groups - 1 - i) * 32 + (3 - part) * 8, 8), 8)
            a, gs = step_buf[at], g_state[at]
            b = a * gs
            for shift in (1, 2, 4):
                inside = row < 8 - shift
                b = b + a * jnp.where(inside, pltpu.roll(b, 8 - shift, 0), 0.0)
                a = a * jnp.where(inside, pltpu.roll(a, 8 - shift, 0), 1.0)
            e = a * after + b
            g_state[at] = gs + jnp.where(row < 7, pltpu.roll(e, 7, 0), after)
            after = jnp.broadcast_to(e[0:1], (8, channels))
        return after

    carry[...] = lax.fori_loop(0, groups, scan, carry[...])

    def fold(x):
        return jnp.sum(x.reshape(tile // 8, 8, channels), axis=0)

    def second(i):
        at = span(i, tile)
        window = hist_s[pl.ds(pl.multiple_of(i * tile, tile), tile + 8)]
        before = window[7 : tile + 7]
        g, r, k = g_state[at], recall[at], ingate[at]
        c = conv_low[at].astype(F32)
        step, root = step_buf[at], root_buf[at]
        kc = k * c
        g_log = g * (before * step - kc * (step * step) / root)
        slow = -8.0 * r
        sums[7] += fold(g_log * slow)
        low_r = (g_log * (slow * decay[...][None]) * (1.0 - r)).astype(BF16)
        low_i = (g * root * kc * (1.0 - k)).astype(BF16)
        pre_r[at] = low_r
        pre_i[at] = low_i
        sums[5] += fold(low_r.astype(F32))
        sums[6] += fold(low_i.astype(F32))
        g_conv[at] = g * root * k

    loop(rows // tile, second)
    low_r, low_i, low_c = pre_r[...], pre_i[...], conv_low[...]
    g_gates[0] += dot_tn(low_c, low_r)
    g_gates[1] += dot_tn(low_c, low_i)
    g_conv[0:rows] += dot_nt(low_r, gate_w[0]) + dot_nt(low_i, gate_w[1])

    def third(i):
        at = span(i, tile)
        start = pl.multiple_of(i * tile, tile)
        window = g_conv[pl.ds(start, tile + 8)]
        value = conv[0:1] * window[0:tile]
        for k in (1, 2, 3):
            value = value + conv[k : k + 1] * window[k : tile + k]
        g_recur[at] = value.astype(BF16)
        past = hist_u[pl.ds(start, tile + 8)]
        gc = window[0:tile]
        for k in range(4):
            sums[k] += fold(gc * past[8 - k : tile + 8 - k])
        sums[4] += fold(gc)

    loop(rows // tile, third)

    @pl.when(jnp.logical_and(sequence == pl.num_programs(0) - 1, back == last))
    def _():
        small[...] = jnp.sum(sums[...], axis=1)


def recur_back(
    resets, g_mix, branch, states, u, conv_low, recall, ingate, init_state, init_conv, conv, gate_w, decay, narrow_in
):
    total, channels = u.shape
    sequences = init_state.shape[0]
    length = total // sequences
    rows = tile_of(length, 256)
    chunks = length // rows
    extra_rows = narrow_in.shape[0] // (sequences * chunks)
    extra = pl.BlockSpec((extra_rows, narrow_in.shape[1]), lambda s, c: (s * chunks + c, 0))
    eights = rows // 8

    def at(s, c):
        return (s * chunks + chunks - 1 - c, 0)

    def earlier(s, c):
        return (jnp.maximum((s * chunks + chunks - 1 - c) * eights - 1, 0), 0)

    block = pl.BlockSpec((rows, channels), at)
    before = pl.BlockSpec((8, channels), earlier)

    def whole(x):
        return pl.BlockSpec(x.shape, lambda s, c: (0,) * x.ndim)

    wide = pltpu.VMEM((rows, channels), F32)
    narrow = pltpu.VMEM((rows, channels), BF16)
    long = pltpu.VMEM((rows + 8, channels), F32)
    return pl.pallas_call(
        recur_back_kernel,
        grid=(sequences, chunks),
        out_shape=(
            shape(total, channels, dtype=BF16),
            shape(total, channels, dtype=BF16),
            shape(8, channels),
            shape(2, channels, channels),
            shape(*narrow_in.shape),
        ),
        in_specs=[
            pl.BlockSpec(memory_space=pltpu.SMEM),
            block, block, block, before, block, before, block, block, block,
            whole(init_state), whole(init_conv), whole(conv), whole(gate_w), whole(decay), extra,
        ],
        out_specs=(
            block,
            block,
            pl.BlockSpec((8, channels), lambda s, c: (0, 0)),
            pl.BlockSpec((2, channels, channels), lambda s, c: (0, 0, 0)),
            extra,
        ),
        scratch_shapes=[
            wide, wide, wide, long, narrow, narrow,
            pltpu.VMEM((8, channels), F32), long, long,
            pltpu.VMEM((8, 8, channels), F32),
        ],
        compiler_params=pltpu.CompilerParams(vmem_limit_bytes=VMEM_LIMIT),
        name="recur_back",
    )(
        resets, g_mix, branch, states, states, u, u, conv_low, recall, ingate, init_state, init_conv,
        conv, gate_w, decay, narrow_in,
    )


def input_back_kernel(
    n, copies, arrive, g_recur, g_branch, w_in, w_br, normed, tokens, g_residual, gain, second_gain, g_gates, small,
    input_grad, in_out, br_out, gates_out, conv_out, bias_out, decay_out, first_out, second_out,
    gain_row, gain_parts, gain_in, gain_sum, gain_dp, gain_sent, gain_came, gain_dp_sent, gain_dp_came, *bufs
):
    g = Place(n)
    me = lax.axis_index("dp")
    rows, width = tokens.shape
    channels = w_in.shape[0]
    block_width, blocks = gates_out.shape[1], gates_out.shape[2]
    segment = width // (2 * copies)
    gain_width = width // n
    weights = Halving.over(me, copies, *bufs[:4])
    rest = Halving.over(me, copies, *bufs[4:8])
    padded = bufs[0].shape[3] // 2
    rest_rows = bufs[4].shape[3]

    def block(ref, t):
        return ref[span(t, rows)]

    def partial(t, cols):
        return dot(block(g_recur, t), w_in[:, cols]) + dot(block(g_branch, t), w_br[:, cols])

    scatter = Scatter(g, partial, tile_of(width, 512), bufs[8:])

    def gain_copy(t, slot):
        return g.copy(gain_parts.at[t], gain_in.at[slot], gain_sent.at[t], gain_came.at[slot], t)

    def gain_dp_copy(i, slot):
        return pltpu.make_async_remote_copy(
            src_ref=gain_sum,
            dst_ref=gain_dp.at[slot],
            send_sem=gain_dp_sent.at[i],
            recv_sem=gain_dp_came.at[slot],
            device_id={"dp": i},
            device_id_type=MESH,
        )

    def others(act):
        loop(n, lambda t: pl.when(t != g.t)(lambda: act(t)))

    def copies_of(act):
        loop(copies, lambda i: pl.when(i != me)(lambda: act(i)))

    barrier = pltpu.get_barrier_semaphore()
    others(
        lambda t: pl.semaphore_signal(barrier, inc=1, device_id={"tensor": t}, device_id_type=MESH)
    )
    copies_of(lambda i: pl.semaphore_signal(barrier, inc=1, device_id={"dp": i}, device_id_type=MESH))
    pl.semaphore_wait(barrier, n - 1 + copies - 1)

    arrive(0, 1, 2, 3)
    scatter.offers(g.nz - 1)

    def around(i):
        d = g.nz - 1 - i
        scatter.offers(d - 1)
        scatter.step(d)

    around(0)
    arrive(4, 9)

    data = bufs[0]

    def weigh(q):
        cols = span(q, 2 * segment)
        first = dot_tn(g_recur[...], normed[:, cols])
        second = dot_tn(g_branch[...], normed[:, cols])
        for half in (0, 1):
            index = 2 * q + half
            track, part = lax.div(index, copies), lax.rem(index, copies)
            for i, value in enumerate((first, second)):
                piece = value[:, half * segment : (half + 1) * segment].astype(BF16)
                data[track, part, 0, i * padded : i * padded + channels] = piece
                if padded > channels:
                    data[track, part, 0, i * padded + channels : (i + 1) * padded] = jnp.zeros(
                        (padded - channels, segment), BF16
                    )
        terms = jnp.sum(w_in[:, cols].astype(F32) * first + w_br[:, cols].astype(F32) * second, axis=0, keepdims=True)
        gain_row[0:1, cols] = terms

    loop(copies, weigh)
    gain_row[0:1] = gain_row[0:1] / gain[...].astype(F32)[None]
    weights.start()
    gain_row[1:2] = second_gain[...]
    gain_row[2:8] = jnp.zeros((6, width), F32)
    for t in range(n):
        gain_parts[t] = gain_row[:, t * gain_width : (t + 1) * gain_width]
    others(lambda t: gain_copy(t, g.t).start())
    gain_in[g.t] = gain_parts[g.t]

    flat = jnp.concatenate(
        [
            g_gates[0],
            g_gates[1],
            small[...],
            jnp.zeros((2 * copies * rest_rows - 2 * channels - 8, channels), F32),
        ],
        axis=0,
    ).astype(BF16)
    for i in range(2 * copies):
        bufs[4][i // copies, i % copies, 0] = flat[i * rest_rows : (i + 1) * rest_rows]
    rest.start()

    events = [lambda a=a, b=b: (a(), b()) for a, b in zip(weights.events(), rest.events())]
    for i in range(1, g.nz - 1):
        around(i)
        if events:
            events.pop(0)()
        if i == 1:
            others(lambda t: gain_copy(t, t).wait_recv())
            total = gain_in[0]
            for t in range(1, n):
                total = total + gain_in[t]
            gain_sum[...] = total
            copies_of(lambda i: gain_dp_copy(i, me).start())
            gain_dp[me] = total
    for event in events:
        event()
    scatter.last()
    arrive(5, 6)
    part = 32

    def rows_of(i):
        at = span(i, part)
        back, _ = norm_grad(tokens[at].astype(F32), gain[...].astype(F32)[None], scatter.acc[at])
        input_grad[at] = g_residual[at] + back

    loop(rows // part, rows_of)
    copies_of(lambda i: gain_dp_copy(i, i).wait_recv())
    total = gain_dp[0]
    for i in range(1, copies):
        total = total + gain_dp[i]
    first_out[...] = total[0]
    second_out[...] = total[1]
    rest.finish()
    flat = jnp.concatenate([bufs[6][i // copies, i % copies, 0].astype(F32) for i in range(2 * copies)], axis=0)
    for q in (0, 1):
        for i in range(blocks):
            start = q * channels + i * block_width
            gates_out[q, :, i] = flat[start : start + block_width, i * block_width : (i + 1) * block_width]
    conv_out[...] = flat[2 * channels : 2 * channels + 5]
    bias_out[...] = flat[2 * channels + 5 : 2 * channels + 7]
    decay_out[...] = flat[2 * channels + 7]
    weights.finish()
    for i in range(2 * copies):
        for q, out in enumerate((in_out, br_out)):
            out[:, i * segment : (i + 1) * segment] = bufs[2][
                i // copies, i % copies, 0, q * padded : q * padded + channels
            ]
    others(lambda t: gain_copy(t, t).wait_send())
    copies_of(lambda i: gain_dp_copy(i, i).wait_send())
    scatter.finish()


def up_to(extent, multiple):
    return (extent + multiple - 1) // multiple * multiple


def input_back(
    n, copies, g_recur, g_branch, w_in, w_br, normed, tokens, g_residual, gain, second_gain, g_gates, small, blocks
):
    rows, width = tokens.shape
    channels = w_in.shape[0]
    block = channels // blocks
    rest_rows = up_to((2 * channels + 8 + 2 * copies - 1) // (2 * copies), 16)
    gain_shape = (8, width // n)
    sems = pltpu.SemaphoreType.DMA
    inputs = (g_recur, g_branch, w_in, w_br, normed, tokens, g_residual, gain, second_gain, g_gates, small)
    which = (0, 1, 2, 3, 4, 9, 5, 6)
    specs, kept = fetched_specs(inputs, which)
    return pl.pallas_call(
        fetching(functools.partial(input_back_kernel, n, copies), which),
        out_shape=(shape(rows, width),)
        + (shape(channels, width, dtype=BF16),) * 2
        + (
            shape(2, block, blocks, block),
            shape(5, channels),
            shape(2, channels),
            shape(channels),
            shape(width // n),
            shape(width // n),
        ),
        in_specs=specs,
        out_specs=(VM,) * 9,
        scratch_shapes=[
            pltpu.VMEM((8, width), F32),
            pltpu.VMEM((n, *gain_shape), F32),
            pltpu.VMEM((n, *gain_shape), F32),
            pltpu.VMEM(gain_shape, F32),
            pltpu.VMEM((copies, *gain_shape), F32),
            sems((n,)),
            sems((n,)),
            sems((copies,)),
            sems((copies,)),
        ]
        + Halving.scratch(copies, 2 * up_to(channels, 16), width // (2 * copies))
        + Halving.scratch(copies, rest_rows, channels)
        + Scatter.scratch(n, rows, width)
        + kept,
        compiler_params=comm_params(6),
        cost_estimate=cost(8 * n * rows * width * channels),
        name="input_back",
    )(*inputs)


def widen_kernel(small, *refs):
    half = len(refs) // 2
    for q, (narrow, wide) in enumerate(zip(refs[:half], refs[half:])):

        def pass_on(narrow=narrow, wide=wide):
            wide[...] = narrow[...].reshape(wide.shape).astype(wide.dtype)

        if q < small:
            pl.when(pl.program_id(0) == 0)(pass_on)
        else:
            pass_on()


def widen(small, as_is, by_rows, by_columns, in_parts):
    steps = 8
    width = by_columns[0].shape[1]
    tile = width // steps
    per_part = in_parts.shape[2] // tile
    specs, outs = [], []

    def whole(x):
        return pl.BlockSpec(x.shape, lambda i: (0,) * x.ndim)

    for x in small:
        specs.append(whole(x))
        outs.append(shape(*x.shape))
    for x in as_is:
        specs.append(pl.BlockSpec((x.shape[0] // steps, x.shape[1]), lambda i: (i, 0)))
        outs.append(shape(*x.shape, dtype=x.dtype))
    for x in by_rows:
        specs.append(pl.BlockSpec((x.shape[0] // steps, x.shape[1]), lambda i: (i, 0)))
        outs.append(shape(*x.shape))
    for x in by_columns:
        specs.append(pl.BlockSpec((x.shape[0], tile), lambda i: (0, i)))
        outs.append(shape(*x.shape))
    last = pl.BlockSpec((1, in_parts.shape[1], tile), lambda i: (i // per_part, 0, i % per_part))
    outs.append(shape(in_parts.shape[1], width))
    wide = pl.BlockSpec((in_parts.shape[1], tile), lambda i: (0, i))
    return pl.pallas_call(
        functools.partial(widen_kernel, len(small)),
        grid=(steps,),
        out_shape=tuple(outs),
        in_specs=specs + [last],
        out_specs=tuple(specs) + (wide,),
        compiler_params=pltpu.CompilerParams(vmem_limit_bytes=VMEM_LIMIT),
        name="widen",
    )(*small, *as_is, *by_rows, *by_columns, in_parts)


def body(
    n,
    copies,
    tokens,
    cotangent,
    resets,
    init_state,
    init_conv,
    norm_gain,
    w_input,
    w_branch,
    conv_params,
    gate_weights,
    gate_bias,
    decay_rate,
    w_output,
    mlp_gain,
    w_gelu,
    w_linear,
    w_down,
):
    rows, width = tokens.shape
    total = rows * n
    channels = w_input.shape[1]
    blocks, block = gate_weights.shape[1], gate_weights.shape[2]
    before_conv = init_conv.transpose(1, 0, 2)
    gain_first, gain_second = norm_gain, mlp_gain
    gate_w = (gate_weights[:, :, :, None] * jnp.eye(blocks, dtype=BF16)[None, :, None, :, None]).reshape(
        2, channels, channels
    )
    w_in, w_br = w_input.T, w_branch.T

    def flat(x):
        return x.reshape(total, x.shape[-1])

    def blocked(x):
        return x.reshape(n, rows, x.shape[-1])

    normed, recur, branch, states, mixture, conv_low, recall, ingate, final_state, final_conv = project(
        n, tokens, gain_first, w_in, w_br, resets, init_state, before_conv, conv_params, gate_w, gate_bias, decay_rate
    )
    mixture = blocked(mixture)
    cot_full, residual, normed_mlp = mixer_out(n, mixture, w_output, cotangent, tokens, gain_second)
    hidden, grad_gelu, grad_linear, grad_down, g_residual, g_low, gain_second_grad = mlp(
        n, copies, normed_mlp, cot_full, w_gelu, w_linear, w_down, residual, gain_second
    )
    mlp_sums = lax.psum((grad_gelu, grad_linear), "dp")
    output, g_mixture, grad_output = down(n, copies, hidden, w_down, residual, g_low, w_output, mixture)
    g_recur, g_branch, small, g_gates, grad_down = recur_back(
        resets, flat(g_mixture), branch, states, recur, conv_low, recall, ingate, init_state, before_conv,
        conv_params, gate_w, decay_rate, grad_down,
    )
    mlp_sums, grad_output, small = lax.optimization_barrier((mlp_sums, grad_output, small))
    grad_output = lax.psum(grad_output, "dp")
    input_grad, grad_input, grad_branch, gates, g_conv, g_bias, g_decay, g_first_gain, g_second_gain = input_back(
        n, copies, g_recur, g_branch, w_in, w_br, flat(normed), tokens, g_residual, gain_first,
        gain_second_grad, g_gates, small, blocks,
    )
    (
        final_state, final_conv, gates, g_conv, g_bias, g_decay, g_first_gain, g_second_gain, output, input_grad,
        grad_gelu, grad_linear, grad_input, grad_branch, grad_output,
    ) = widen(
        (final_state, final_conv, gates, g_conv, g_bias, g_decay, g_first_gain, g_second_gain),
        (output, input_grad),
        mlp_sums,
        (grad_input, grad_branch),
        grad_output,
    )
    return (
        output,
        input_grad,
        final_state,
        final_conv.transpose(1, 0, 2),
        g_first_gain,
        grad_input.T,
        grad_branch.T,
        g_conv,
        gates.transpose(0, 2, 1, 3),
        g_bias,
        g_decay,
        grad_output,
        g_second_gain,
        grad_gelu,
        grad_linear,
        grad_down,
    )


def solution(mesh):
    in_specs = (
        P(("dp", "tensor"), None),
        P(("dp", "tensor"), None),
        P("dp"),
        P("dp", "tensor"),
        P("dp", None, "tensor"),
        P(),
        P(None, "tensor"),
        P(None, "tensor"),
        P(None, "tensor"),
        P(None, "tensor", None, None),
        P(None, "tensor"),
        P("tensor"),
        P("tensor", None),
        P(),
        P(None, "tensor"),
        P(None, "tensor"),
        P("tensor", None),
    )
    out_specs = (
        P(("dp", "tensor"), None),
        P(("dp", "tensor"), None),
        P("dp", "tensor"),
        P("dp", None, "tensor"),
        P("tensor"),
        P(None, "tensor"),
        P(None, "tensor"),
        P(None, "tensor"),
        P(None, "tensor", None, None),
        P(None, "tensor"),
        P("tensor"),
        P("tensor", None),
        P("tensor"),
        P(None, "tensor"),
        P(None, "tensor"),
        P("tensor", None),
    )
    return jax.shard_map(
        functools.partial(body, mesh.shape["tensor"], mesh.shape["dp"]),
        mesh=mesh,
        in_specs=in_specs,
        out_specs=out_specs,
        check_vma=False,
    )
```
